32 devices in a mesh: gx: 4 (over x, core), gy: 8 (over z, y).
Axes of the slice: x: 2, y: 2, z: 4, core: 2. Of those that a mesh axis runs over, the one named last changes fastest.
Arguments:
- phase: float32 [4, 16, 32, 32, 128], P('gx', 'gy'), may hold values from -1 to 1
- solute: float32 [4, 16, 32, 32, 128], P('gx', 'gy'), may hold values from -2.5 to 2.5
- undercool: float32 [4, 16], P('gx', 'gy'), may hold values from -0.5 to 0.5
- mobility: float32 [4, 16], P('gx', 'gy'), may hold values from 0.03 to 0.08
- diffusivity: float32 [4, 16], P('gx', 'gy'), may hold values from 0.04 to 0.14
- owner: int32 [4, 16], P('gx', 'gy'), may hold values from 0 to 31, as said below
Outputs:
- phase_out: float32 [32, 2, 32, 32, 128], P(('gx', 'gy'))
- solute_out: float32 [32, 2, 32, 32, 128], P(('gx', 'gy'))
The draws below stay inside these ranges and needn't reach their ends.
Inputs may be any that keep to these rules, and one draw needn't show every extreme that they name: A tile (p, q) is owned by one of the owners i*8 to i*8+8-1 with i = p. Each owner receives exactly 2 tiles; no device's tiles include more than 1 tiles of one owner, and some device's include exactly 1.
All inputs are finite; a program needn't handle non-finite values.
Results may differ from the reference program's by a relative error of at most 0.0003.
Values sent between devices are 32-bit elements; how exact they have to be, the bound alone decides.
No kernel may reach another device: no remote copies, remote signals or barrier semaphores. Data moves between devices by JAX's collectives and lax.ppermute only.
A program may use at most 192 MiB of HBM per device.

```python
import math
import jax
import jax.numpy as jnp

TE = 32
NZ = 128
BX = 1
BY = 2
NSTEPS = 4
TILES_X = 4
TILES_Y = 16
TPD = 2
OWNERS = 32
N_GX = 4
N_GY = 8


def draw_owner(key, part):
    relabel_key, shift_key, tile_key = jax.random.split(key, 3)
    rows_mesh = TILES_X // BX
    cols_mesh = TILES_Y // BY
    tile_perm = jax.random.permutation(tile_key, TPD)
    shift_table = jax.vmap(lambda k: jax.random.permutation(k, cols_mesh))(jax.random.split(shift_key, rows_mesh))
    relabel_table = jax.vmap(lambda k: jax.random.permutation(k, cols_mesh))(jax.random.split(relabel_key, rows_mesh))
    row_index = jnp.arange(TILES_X, dtype=jnp.int32)[:, None]
    col_index = jnp.arange(TILES_Y, dtype=jnp.int32)[None, :]
    mesh_row = row_index // BX + 0 * col_index
    mesh_col = col_index // BY + 0 * row_index
    local_index = row_index % BX * BY + col_index % BY
    within = (shift_table[mesh_row, mesh_col] + tile_perm[local_index]) % cols_mesh
    return (mesh_row * cols_mesh + relabel_table[mesh_row, within]).astype(jnp.int32)


def steps_of(rng, dims, pieces, least, largest):
    factor_of = 1.0
    for position, parts in pieces:
        steps = jax.random.uniform(jax.random.fold_in(jax.random.fold_in(rng, 6), position), (parts,), jnp.float32, least / len(pieces), largest / len(pieces))
        factor_of = factor_of * jnp.repeat(jnp.exp(steps), dims[position] // parts).reshape((-1,) + (1,) * (len(dims) - 1 - position))
    return factor_of


def noise(own_key, extent, deviation, reach, cuts=(), kind=jnp.bfloat16):
    factor_of = steps_of(own_key, extent, cuts, -0.22, 0.18) if cuts else 1.0
    drawn = jax.random.normal(own_key, extent, jnp.float32) * deviation * factor_of
    return jnp.minimum(jnp.maximum(drawn, -reach), reach).astype(kind)


def setup_inputs(seed: int = 0) -> dict:
    seeds = jax.random.split(jax.random.key(seed), 7)
    return {
        "phase": jnp.clip(jax.random.uniform(seeds[0], (TILES_X, TILES_Y, TE, TE, NZ), jnp.float32, -1.0, 1.0) * steps_of(seeds[0], (TILES_X, TILES_Y, TE, TE, NZ), ((0, 4), (1, 8)), -0.4, 0.0), -1.0, 1.0),
        "solute": noise(seeds[1], (TILES_X, TILES_Y, TE, TE, NZ), 0.3, 2.5, ((0, 4), (1, 8)), jnp.float32),
        "undercool": jnp.clip(jax.random.uniform(seeds[2], (TILES_X, TILES_Y), jnp.float32, -0.5, 0.5) * steps_of(seeds[2], (TILES_X, TILES_Y), ((0, 4), (1, 8)), -0.4, 0.0), -0.5, 0.5),
        "mobility": jnp.clip(jnp.exp(math.log(0.08) - 0.98082925 * jax.random.uniform(seeds[3], (TILES_X, TILES_Y), jnp.float32) ** steps_of(seeds[3], (TILES_X, TILES_Y), ((0, 4), (1, 8)), -0.2, 0.2)), 0.03, 0.08),
        "diffusivity": jnp.clip(jnp.exp(math.log(0.14) - 1.252763 * jax.random.uniform(seeds[4], (TILES_X, TILES_Y), jnp.float32) ** steps_of(seeds[4], (TILES_X, TILES_Y), ((0, 4), (1, 8)), -0.2, 0.2)), 0.04, 0.14),
        "owner": draw_owner(jax.random.fold_in(seeds[6], 71), 0),
    }


aniso_strength = 0.05
coupling = 2.0


def step_cells(phase, solute, phase_near, solute_near, under, mobile, spread):
    lower_first, upper_first, lower_second, upper_second, lower_third, upper_third = phase_near
    slope_first = 0.5 * (upper_first - lower_first)
    slope_second = 0.5 * (upper_second - lower_second)
    slope_third = 0.5 * (upper_third - lower_third)
    lap_phase = upper_first + lower_first + upper_second + lower_second + upper_third + lower_third - 6.0 * phase
    sol_lf, sol_uf, sol_ls, sol_us, sol_lt, sol_ut = solute_near
    lap_solute = sol_uf + sol_lf + sol_us + sol_ls + sol_ut + sol_lt - 6.0 * solute
    square_first = slope_first * slope_first
    square_second = slope_second * slope_second
    square_third = slope_third * slope_third
    grad_two = square_first + square_second + square_third
    grad_four = square_first * square_first + square_second * square_second + square_third * square_third
    aniso = 1.0 + aniso_strength * (4.0 * grad_four - 3.0 * grad_two * grad_two) / ((1.0 + grad_two) * (1.0 + grad_two))
    well = 1.0 - phase * phase
    new_phase = phase + mobile * (aniso * lap_phase + phase - phase * phase * phase - coupling * well * well * (under + solute))
    new_solute = solute + spread * lap_solute + 0.5 * (new_phase - phase)
    return new_phase, new_solute


def near_cells(field):
    return (jnp.roll(field, 1, 0), jnp.roll(field, -1, 0), jnp.roll(field, 1, 1), jnp.roll(field, -1, 1),
            jnp.concatenate([field[:, :, :1], field[:, :, :-1]], 2),
            jnp.concatenate([field[:, :, 1:], field[:, :, -1:]], 2))


def assemble(tiles):
    return jnp.transpose(tiles, (0, 2, 1, 3, 4)).reshape(TILES_X * TE, TILES_Y * TE, NZ)


def split_tiles(field):
    return jnp.transpose(field.reshape(TILES_X, TE, TILES_Y, TE, NZ), (0, 2, 1, 3, 4))


def home_order(values):
    rest = values.shape[2:]
    grouped = values.reshape((N_GX, BX, N_GY, BY) + rest)
    grouped = jnp.moveaxis(grouped, 2, 1)
    return grouped.reshape((OWNERS * TPD,) + rest)


def spread_cells(coeff):
    return jnp.repeat(jnp.repeat(coeff, TE, 0), TE, 1)[:, :, None]


def reference(phase, solute, undercool, mobility, diffusivity, owner):
    phase_field = assemble(phase)
    solute_field = assemble(solute)
    under = spread_cells(undercool)
    mobile = spread_cells(mobility)
    spread = spread_cells(diffusivity)
    for iteration in range(NSTEPS):
        phase_field, solute_field = step_cells(phase_field, solute_field, near_cells(phase_field),
                                               near_cells(solute_field), under, mobile, spread)
    owner_flat = home_order(owner)
    ordering = jnp.argsort(owner_flat, stable=True)
    phase_home = home_order(split_tiles(phase_field))[ordering]
    solute_home = home_order(split_tiles(solute_field))[ordering]
    return (phase_home.reshape(OWNERS, TPD, TE, TE, NZ), solute_home.reshape(OWNERS, TPD, TE, TE, NZ))
```

```python
import functools

import jax
import jax.numpy as jnp
from jax import lax
from jax.experimental import pallas as pl
from jax.experimental.pallas import tpu as pltpu
from jax.sharding import PartitionSpec as P

NSTEPS = 4
W = NSTEPS
PAD = 8

aniso_strength = 0.05


def pack_y_kernel(coef_ref, phase_lo, phase_hi, solute_lo, solute_hi, to_prev, to_next):
    edge = phase_lo.shape[2]
    to_prev[:edge, :W, :] = phase_lo[0, 0, :, :W, :]
    to_prev[:edge, W:, :] = solute_lo[0, 0, :, :W, :]
    to_next[:edge, :W, :] = phase_hi[0, 0, :, W:, :]
    to_next[:edge, W:, :] = solute_hi[0, 0, :, W:, :]
    to_prev[edge] = jnp.zeros((2 * W, to_prev.shape[2]), jnp.float32)
    to_next[edge] = jnp.zeros((2 * W, to_prev.shape[2]), jnp.float32)
    for kind in range(3):
        to_prev[edge, kind, :] = jnp.full((to_prev.shape[2],), coef_ref[0, kind], jnp.float32)
        to_next[edge, kind, :] = jnp.full((to_prev.shape[2],), coef_ref[1, kind], jnp.float32)


def pack_y(phase, solute, coef):
    _, tiles, edge, _, depth = phase.shape
    low = pl.BlockSpec((1, 1, edge, 2 * W, depth), lambda i: (0, 0, 0, 0, 0))
    high = pl.BlockSpec((1, 1, edge, 2 * W, depth), lambda i: (0, tiles - 1, 0, edge // (2 * W) - 1, 0))
    out = jax.ShapeDtypeStruct((edge + 1, 2 * W, depth), jnp.float32)
    whole = pl.BlockSpec((edge + 1, 2 * W, depth), lambda i: (0, 0, 0))
    return pl.pallas_call(
        pack_y_kernel,
        grid=(1,),
        in_specs=[pl.BlockSpec(memory_space=pltpu.SMEM), low, high, low, high],
        out_specs=[whole, whole],
        out_shape=[out, out],
        name="pack_y",
    )(coef, phase, phase, solute, solute)


def fill_row(dst, row, phase_row, solute_row, lo, hi):
    start = PAD
    dst[0][row, start : start + W, :] = lo[:W]
    dst[1][row, start : start + W, :] = lo[W:]
    start += W
    for values in phase_row:
        size = values.shape[0]
        dst[0][row, start : start + size, :] = values
        start += size
    dst[0][row, start : start + W, :] = hi[:W]
    dst[1][row, start : start + W, :] = hi[W:]
    start = PAD + W
    for values in solute_row:
        size = values.shape[0]
        dst[1][row, start : start + size, :] = values
        start += size


def pack_x_kernel(coef_ref, phase_lo, phase_hi, solute_lo, solute_hi, y_lo, y_hi, to_prev, to_next):
    tiles, edge, depth = phase_lo.shape[1], phase_lo.shape[3], phase_lo.shape[4]
    width = tiles * edge + 2 * W
    for out, phase, solute, first in (
        (to_prev, phase_lo, solute_lo, 0),
        (to_next, phase_hi, solute_hi, edge - W),
    ):
        for row in range(W):
            for field, values, half in ((0, phase, 0), (1, solute, W)):
                at = (2 * row + field) * width
                out[at : at + W, :] = y_lo[first + row, half : half + W, :]
                for tile in range(tiles):
                    begin = at + W + tile * edge
                    out[begin : begin + edge, :] = values[0, tile, row]
                out[at + width - W : at + width, :] = y_hi[first + row, half : half + W, :]
        at = 2 * W * width
        out[at : at + 8, :] = y_lo[edge]
        out[at + 8 : at + 16, :] = y_hi[edge]
        for tile in range(tiles):
            begin = at + 16 + 8 * tile
            out[begin : begin + 8, :] = jnp.zeros((8, depth), jnp.float32)
            for kind in range(3):
                out[begin + kind : begin + kind + 1, :] = jnp.full((1, depth), coef_ref[tile, kind], jnp.float32)


def pack_x(phase, solute, coef, y_lo, y_hi):
    _, tiles, edge, _, depth = phase.shape
    low = pl.BlockSpec((1, tiles, W, edge, depth), lambda i: (0, 0, 0, 0, 0))
    high = pl.BlockSpec((1, tiles, W, edge, depth), lambda i: (0, 0, edge // W - 1, 0, 0))
    side = pl.BlockSpec((edge + 1, 2 * W, depth), lambda i: (0, 0, 0))
    rows = 2 * W * (tiles * edge + 2 * W) + 8 * (tiles + 2)
    out = jax.ShapeDtypeStruct((rows, depth), jnp.float32)
    whole = pl.BlockSpec((rows, depth), lambda i: (0, 0))
    return pl.pallas_call(
        pack_x_kernel,
        grid=(1,),
        in_specs=[pl.BlockSpec(memory_space=pltpu.SMEM), low, high, low, high, side, side],
        out_specs=[whole, whole],
        out_shape=[out, out],
        name="pack_x",
    )(coef, phase, phase, solute, solute, y_lo, y_hi)


def update(near_p, near_u, under, mobile, spread):
    p, p_xl, p_xh, p_yl, p_yh = near_p
    u, u_xl, u_xh, u_yl, u_yh = near_u
    depth = p.shape[-1]
    lane = lax.broadcasted_iota(jnp.int32, p.shape, 1)
    first, last = lane == 0, lane == depth - 1
    p_zl = jnp.where(first, p, pltpu.roll(p, 1, 1))
    p_zh = jnp.where(last, p, pltpu.roll(p, depth - 1, 1))
    u_zl = jnp.where(first, u, pltpu.roll(u, 1, 1))
    u_zh = jnp.where(last, u, pltpu.roll(u, depth - 1, 1))
    dx, dy, dz = p_xh - p_xl, p_yh - p_yl, p_zh - p_zl
    qx, qy, qz = dx * dx, dy * dy, dz * dz
    total = qx + qy + qz
    fourth = qx * qx + qy * qy + qz * qz
    base = total + 4.0
    guess = pl.reciprocal(base, approx=True)
    inverse = guess * (2.0 - base * guess)
    extra = (4.0 * aniso_strength * fourth - (3.0 * aniso_strength) * total * total) * (inverse * inverse)
    lap_p = (p_xl + p_xh) + (p_yl + p_yh) + (p_zl + p_zh) - 6.0 * p
    lap_u = (u_xl + u_xh) + (u_yl + u_yh) + (u_zl + u_zh) - 6.0 * u
    well = 1.0 - p * p
    drive = well * (under + u)
    change = mobile * (lap_p + extra * lap_p + well * (p - 2.0 * drive))
    return p + change, u + spread * lap_u + 0.5 * change


def steps_kernel(
    coef_ref, phase, solute, y_lo, y_hi, x_lo, x_hi, owner_ref, out, p_a, u_a, p_b, u_b, coefs
):
    tiles, edge, depth = phase.shape[1], phase.shape[2], phase.shape[4]
    width = tiles * edge + 2 * W
    pieces = out.shape[0]
    rows_each = edge // pieces
    for zone, source in ((0, x_lo), (1, None), (2, x_hi)):
        for kind in range(3):
            if source is None:
                parts = [y_lo[edge, kind : kind + 1, :]]
                parts += [jnp.full((1, depth), coef_ref[tile, kind], jnp.float32) for tile in range(tiles)]
                parts += [y_hi[edge, kind : kind + 1, :]]
            else:
                at = 2 * W * width + kind
                parts = [source[at : at + 1, :]]
                parts += [source[at + 16 + 8 * tile : at + 17 + 8 * tile, :] for tile in range(tiles)]
                parts += [source[at + 8 : at + 9, :]]
            coefs[zone, kind, :W, :] = jnp.broadcast_to(parts[0], (W, depth))
            for tile in range(tiles):
                begin = W + tile * edge
                coefs[zone, kind, begin : begin + edge, :] = jnp.broadcast_to(parts[1 + tile], (edge, depth))
            coefs[zone, kind, width - W :, :] = jnp.broadcast_to(parts[-1], (W, depth))
    for source, first in ((x_lo, 0), (x_hi, edge + W)):
        for row in range(W):
            for field, buffer in ((0, p_a), (1, u_a)):
                at = (2 * row + field) * width
                buffer[first + row, PAD : PAD + width, :] = source[at : at + width, :]

    def load_row(row, carry):
        fill_row(
            (p_a, u_a),
            W + row,
            [phase[0, tile, row] for tile in range(tiles)],
            [solute[0, tile, row] for tile in range(tiles)],
            y_lo[row],
            y_hi[row],
        )
        return carry

    lax.fori_loop(0, edge, load_row, 0)

    def cell_block(src_p, src_u, row, start, zone):
        size = 8
        near = []
        for src in (src_p, src_u):
            near.append(
                (
                    src[row, start : start + size, :],
                    src[row - 1, start : start + size, :],
                    src[row + 1, start : start + size, :],
                    src[row, start - 1 : start - 1 + size, :],
                    src[row, start + 1 : start + 1 + size, :],
                )
            )
        kinds = [coefs[zone, kind, start - PAD : start - PAD + size, :] for kind in range(3)]
        return update(near[0], near[1], *kinds)

    for step in range(NSTEPS - 1):
        src_p, src_u, dst_p, dst_u = (p_a, u_a, p_b, u_b) if step % 2 == 0 else (p_b, u_b, p_a, u_a)

        def one_row(row, carry, src_p=src_p, src_u=src_u, dst_p=dst_p, dst_u=dst_u):
            zone = jnp.where(row < W, 0, jnp.where(row < W + edge, 1, 2))
            for start in range(PAD, PAD + width, 8):
                new_p, new_u = cell_block(src_p, src_u, row, start, zone)
                dst_p[row, start : start + 8, :] = new_p
                dst_u[row, start : start + 8, :] = new_u
            return carry

        lax.fori_loop(step + 1, edge + 2 * W - step - 1, one_row, 0)

    src_p, src_u = (p_a, u_a) if (NSTEPS - 1) % 2 == 0 else (p_b, u_b)

    def last_row(row, carry):
        piece, inner = row // rows_each, row % rows_each
        for tile in range(tiles):
            for col in range(0, edge, 8):
                start = PAD + W + tile * edge + col
                new_p, new_u = cell_block(src_p, src_u, row + W, start, 1)
                at = pl.multiple_of(inner * edge, 8) + col
                size = rows_each * edge
                out[piece, pl.ds(pl.multiple_of((2 * tile) * size + at, 8), 8), :] = new_p
                out[piece, pl.ds(pl.multiple_of((2 * tile + 1) * size + at, 8), 8), :] = new_u
        return carry

    lax.fori_loop(0, edge, last_row, 0)
    tail = 2 * tiles * rows_each * edge
    lane = lax.broadcasted_iota(jnp.int32, (8, depth), 1)
    names = jnp.zeros((8, depth), jnp.float32)
    for tile in range(tiles):
        names = jnp.where(lane == tile, owner_ref[0, tile].astype(jnp.float32), names)
    for piece in range(pieces):
        out[piece, tail : tail + 8, :] = names


def run_steps(phase, solute, coef, y_lo, y_hi, x_lo, x_hi, owner, pieces):
    _, tiles, edge, _, depth = phase.shape
    width = tiles * edge + 2 * W
    buffer = pltpu.VMEM((edge + 2 * W, width + 2 * PAD, depth), jnp.float32)
    vmem = pl.BlockSpec(memory_space=pltpu.VMEM)
    smem = pl.BlockSpec(memory_space=pltpu.SMEM)
    rows = 2 * tiles * (edge // pieces) * edge + 8
    return pl.pallas_call(
        steps_kernel,
        in_specs=[smem] + [vmem] * 6 + [smem],
        out_specs=vmem,
        out_shape=jax.ShapeDtypeStruct((pieces, rows, depth), jnp.float32),
        scratch_shapes=[buffer] * 4 + [pltpu.VMEM((3, 3, width, depth), jnp.float32)],
        compiler_params=pltpu.CompilerParams(vmem_limit_bytes=40 * 1024 * 1024),
        name="steps",
    )(coef, phase, solute, y_lo, y_hi, x_lo, x_hi, owner)


def route_kernel(pieces, tiles, arrived, out, names, name_sem, sems):
    size = out.shape[2]
    tail = tiles * size
    names_copy = pltpu.make_async_copy(arrived.at[:, pl.ds(tail, 1), :], names, name_sem)
    names_copy.start()
    names_copy.wait()
    count = pieces * tiles
    owners = []
    for home in range(count):
        owners.append(lax.rem(names[home // tiles, 0, home % tiles].astype(jnp.int32), pieces))
    copies = []
    for home in range(count):
        slot = jnp.int32(0)
        for other in range(home):
            slot = slot + (owners[other] == owners[home]).astype(jnp.int32)
        copy = pltpu.make_async_copy(
            arrived.at[home // tiles, pl.ds((home % tiles) * size, size), :],
            out.at[owners[home], slot],
            sems.at[home],
        )
        copy.start()
        copies.append(copy)
    for copy in copies:
        copy.wait()


def route(arrived, pieces, tiles):
    depth = arrived.shape[2]
    size = (arrived.shape[1] - 8) // tiles
    return pl.pallas_call(
        functools.partial(route_kernel, pieces, tiles),
        in_specs=[pl.BlockSpec(memory_space=pl.ANY)],
        out_specs=pl.BlockSpec(memory_space=pl.ANY),
        out_shape=jax.ShapeDtypeStruct((pieces, tiles, size, depth), jnp.float32),
        scratch_shapes=[
            pltpu.SMEM((pieces, 1, depth), jnp.float32),
            pltpu.SemaphoreType.DMA,
            pltpu.SemaphoreType.DMA((pieces * tiles,)),
        ],
        name="route",
    )(arrived)


def settle_kernel(pieces, arrived, phase, solute, sems):
    tiles, edge, depth = phase.shape[1], phase.shape[2], phase.shape[4]
    rows_each = edge // pieces
    copies = []
    for piece in range(pieces):
        for tile in range(tiles):
            for field, out in ((0, phase), (1, solute)):
                copy = pltpu.make_async_copy(
                    arrived.at[piece, tile, field],
                    out.at[0, tile, pl.ds(piece * rows_each, rows_each)],
                    sems.at[len(copies)],
                )
                copy.start()
                copies.append(copy)
    for copy in copies:
        copy.wait()


def settle(arrived, pieces, tiles, edge, depth):
    arrived = arrived.reshape(pieces, tiles, 2, edge // pieces, edge, depth)
    out = jax.ShapeDtypeStruct((1, tiles, edge, edge, depth), jnp.float32)
    hbm = pl.BlockSpec(memory_space=pl.ANY)
    return pl.pallas_call(
        functools.partial(settle_kernel, pieces),
        in_specs=[hbm],
        out_specs=[hbm, hbm],
        out_shape=[out, out],
        scratch_shapes=[pltpu.SemaphoreType.DMA((pieces * tiles * 2,))],
        name="settle",
    )(arrived)


def ring(axis, step):
    count = lax.axis_size(axis)
    return [(i, (i + step) % count) for i in range(count)]


def per_device(phase, solute, undercool, mobility, diffusivity, owner):
    _, tiles, edge, _, depth = phase.shape
    pieces = lax.axis_size("gy")
    coef = jnp.stack([undercool[0], mobility[0], diffusivity[0]], axis=1)
    to_prev, to_next = pack_y(phase, solute, coef)
    y_lo = lax.ppermute(to_next, "gy", ring("gy", 1))
    y_hi = lax.ppermute(to_prev, "gy", ring("gy", -1))
    to_prev, to_next = pack_x(phase, solute, coef, y_lo, y_hi)
    x_lo = lax.ppermute(to_next, "gx", ring("gx", 1))
    x_hi = lax.ppermute(to_prev, "gx", ring("gx", -1))
    cut = run_steps(phase, solute, coef, y_lo, y_hi, x_lo, x_hi, owner, pieces)
    spread = lax.all_to_all(cut, "gy", split_axis=0, concat_axis=0, tiled=True)
    sent = route(spread, pieces, tiles)
    arrived = lax.all_to_all(sent, "gy", split_axis=0, concat_axis=0, tiled=True)
    return tuple(settle(arrived, pieces, tiles, edge, depth))


def solution(mesh):
    tile_spec = P("gx", "gy", None, None, None)
    in_specs = (tile_spec, tile_spec) + (P("gx", "gy"),) * 4
    out_spec = P(("gx", "gy"), None, None, None, None)
    return jax.shard_map(
        per_device, mesh=mesh, in_specs=in_specs, out_specs=(out_spec, out_spec), check_vma=False
    )
```

```python
import functools

import jax
import jax.numpy as jnp
from jax import lax
from jax.experimental import pallas as pl
from jax.experimental.pallas import tpu as pltpu
from jax.sharding import PartitionSpec as P

NSTEPS = 4
W = NSTEPS
PAD = 8

aniso_strength = 0.05


def pack_y_kernel(under, mobile, spread, phase_lo, phase_hi, solute_lo, solute_hi, to_prev, to_next):
    edge = phase_lo.shape[2]
    to_prev[:edge, :W, :] = phase_lo[0, 0, :, :W, :]
    to_prev[:edge, W:, :] = solute_lo[0, 0, :, :W, :]
    to_next[:edge, :W, :] = phase_hi[0, 0, :, W:, :]
    to_next[:edge, W:, :] = solute_hi[0, 0, :, W:, :]
    to_prev[edge] = jnp.zeros((2 * W, to_prev.shape[2]), jnp.float32)
    to_next[edge] = jnp.zeros((2 * W, to_prev.shape[2]), jnp.float32)
    for kind, own in enumerate((under, mobile, spread)):
        to_prev[edge, kind, :] = jnp.full((to_prev.shape[2],), own[0, 0], jnp.float32)
        to_next[edge, kind, :] = jnp.full((to_prev.shape[2],), own[0, own.shape[1] - 1], jnp.float32)


def pack_y(phase, solute, coef):
    _, tiles, edge, _, depth = phase.shape
    low = pl.BlockSpec((1, 1, edge, 2 * W, depth), lambda i: (0, 0, 0, 0, 0))
    high = pl.BlockSpec((1, 1, edge, 2 * W, depth), lambda i: (0, tiles - 1, 0, edge // (2 * W) - 1, 0))
    out = jax.ShapeDtypeStruct((edge + 1, 2 * W, depth), jnp.float32)
    whole = pl.BlockSpec((edge + 1, 2 * W, depth), lambda i: (0, 0, 0))
    return pl.pallas_call(
        pack_y_kernel,
        grid=(1,),
        in_specs=[pl.BlockSpec(memory_space=pltpu.SMEM)] * 3 + [low, high, low, high],
        out_specs=[whole, whole],
        out_shape=[out, out],
        name="pack_y",
    )(*coef, phase, phase, solute, solute)


def fill_row(dst, row, phase_row, solute_row, lo, hi):
    start = PAD
    dst[0][row, start : start + W, :] = lo[:W]
    dst[1][row, start : start + W, :] = lo[W:]
    start += W
    for values in phase_row:
        size = values.shape[0]
        dst[0][row, start : start + size, :] = values
        start += size
    dst[0][row, start : start + W, :] = hi[:W]
    dst[1][row, start : start + W, :] = hi[W:]
    start = PAD + W
    for values in solute_row:
        size = values.shape[0]
        dst[1][row, start : start + size, :] = values
        start += size


def pack_x_kernel(under, mobile, spread, phase_lo, phase_hi, solute_lo, solute_hi, y_lo, y_hi, to_prev, to_next):
    tiles, edge, depth = phase_lo.shape[1], phase_lo.shape[3], phase_lo.shape[4]
    width = tiles * edge + 2 * W
    for out, phase, solute, first in (
        (to_prev, phase_lo, solute_lo, 0),
        (to_next, phase_hi, solute_hi, edge - W),
    ):
        for row in range(W):
            for field, values, half in ((0, phase, 0), (1, solute, W)):
                at = (2 * row + field) * width
                out[at : at + W, :] = y_lo[first + row, half : half + W, :]
                for tile in range(tiles):
                    begin = at + W + tile * edge
                    out[begin : begin + edge, :] = values[0, tile, row]
                out[at + width - W : at + width, :] = y_hi[first + row, half : half + W, :]
        at = 2 * W * width
        out[at : at + 8, :] = y_lo[edge]
        out[at + 8 : at + 16, :] = y_hi[edge]
        for tile in range(tiles):
            begin = at + 16 + 8 * tile
            out[begin : begin + 8, :] = jnp.zeros((8, depth), jnp.float32)
            for kind, own in enumerate((under, mobile, spread)):
                out[begin + kind : begin + kind + 1, :] = jnp.full((1, depth), own[0, tile], jnp.float32)


def pack_x(phase, solute, coef, y_lo, y_hi):
    _, tiles, edge, _, depth = phase.shape
    low = pl.BlockSpec((1, tiles, W, edge, depth), lambda i: (0, 0, 0, 0, 0))
    high = pl.BlockSpec((1, tiles, W, edge, depth), lambda i: (0, 0, edge // W - 1, 0, 0))
    side = pl.BlockSpec((edge + 1, 2 * W, depth), lambda i: (0, 0, 0))
    rows = 2 * W * (tiles * edge + 2 * W) + 8 * (tiles + 2)
    out = jax.ShapeDtypeStruct((rows, depth), jnp.float32)
    whole = pl.BlockSpec((rows, depth), lambda i: (0, 0))
    return pl.pallas_call(
        pack_x_kernel,
        grid=(1,),
        in_specs=[pl.BlockSpec(memory_space=pltpu.SMEM)] * 3 + [low, high, low, high, side, side],
        out_specs=[whole, whole],
        out_shape=[out, out],
        name="pack_x",
    )(*coef, phase, phase, solute, solute, y_lo, y_hi)


def update(near_p, near_u, under, mobile, spread):
    p, p_xl, p_xh, p_yl, p_yh = near_p
    u, u_xl, u_xh, u_yl, u_yh = near_u
    depth = p.shape[-1]
    lane = lax.broadcasted_iota(jnp.int32, p.shape, 1)
    first, last = lane == 0, lane == depth - 1
    p_zl = jnp.where(first, p, pltpu.roll(p, 1, 1))
    p_zh = jnp.where(last, p, pltpu.roll(p, depth - 1, 1))
    u_zl = jnp.where(first, u, pltpu.roll(u, 1, 1))
    u_zh = jnp.where(last, u, pltpu.roll(u, depth - 1, 1))
    dx, dy, dz = p_xh - p_xl, p_yh - p_yl, p_zh - p_zl
    qx, qy, qz = dx * dx, dy * dy, dz * dz
    total = qx + qy + qz
    fourth = qx * qx + qy * qy + qz * qz
    base = total + 4.0
    guess = pl.reciprocal(base, approx=True)
    inverse = guess * (2.0 - base * guess)
    extra = (4.0 * aniso_strength * fourth - (3.0 * aniso_strength) * total * total) * (inverse * inverse)
    lap_p = (p_xl + p_xh) + (p_yl + p_yh) + (p_zl + p_zh) - 6.0 * p
    lap_u = (u_xl + u_xh) + (u_yl + u_yh) + (u_zl + u_zh) - 6.0 * u
    well = 1.0 - p * p
    drive = well * (under + u)
    change = mobile * (lap_p + extra * lap_p + well * (p - 2.0 * drive))
    return p + change, u + spread * lap_u + 0.5 * change


class Plan:
    def __init__(self, pieces, tiles, edge, depth):
        self.pieces, self.tiles, self.edge, self.depth = pieces, tiles, edge, depth
        self.half = pieces // 2
        self.inner = (edge - 2 * W) // pieces * pieces
        self.low = (edge - self.inner) // 2
        self.rows_a = self.inner // pieces
        self.rows_b = (edge - self.inner) // pieces
        self.cols_a = edge - 8
        self.size_a = self.rows_a * self.cols_a
        self.size_b = self.rows_b * edge + self.rows_a * 8
        self.size = self.size_a + self.size_b


AUX = 8


def cells(src_p, src_u, row, start, coefs):
    near = []
    for src in (src_p, src_u):
        near.append(
            (
                src[row, start : start + 8, :],
                src[row - 1, start : start + 8, :],
                src[row + 1, start : start + 8, :],
                src[row, start - 1 : start + 7, :],
                src[row, start + 1 : start + 9, :],
            )
        )
    return update(near[0], near[1], *coefs)


def inner_kernel(plan, under, mobile, spread, phase, solute, *rest):
    half, tiles, edge = plan.half, plan.tiles, plan.edge
    outs, (p_a, u_a, p_b, u_b) = rest[:half], rest[half:]
    count = half * plan.rows_a
    me = lax.axis_index("gy")
    other = 1 - me // half
    base = plan.low - W + other * count

    def load_row(row, carry):
        for tile in range(tiles):
            start = PAD + tile * edge
            p_a[row, start : start + edge, :] = phase[0, tile, base + row]
            u_a[row, start : start + edge, :] = solute[0, tile, base + row]
        return carry

    lax.fori_loop(0, count + 2 * W, load_row, 0)
    for step in range(NSTEPS):
        src_p, src_u, dst_p, dst_u = (p_a, u_a, p_b, u_b) if step % 2 == 0 else (p_b, u_b, p_a, u_a)

        def one_row(row, carry, src_p=src_p, src_u=src_u, dst_p=dst_p, dst_u=dst_u):
            for start in range(PAD, PAD + tiles * edge, 8):
                tile = (start - PAD) // edge
                kinds = (under[0, tile], mobile[0, tile], spread[0, tile])
                new_p, new_u = cells(src_p, src_u, row, start, kinds)
                dst_p[row, start : start + 8, :] = new_p
                dst_u[row, start : start + 8, :] = new_u
            return carry

        lax.fori_loop(step + 1, count + 2 * W - step - 1, one_row, 0, unroll=UNROLL)
    done_p, done_u = (p_a, u_a) if NSTEPS % 2 == 0 else (p_b, u_b)
    for index, out in enumerate(outs):
        piece = (me ^ (half + index)) - other * half
        for tile in range(tiles):
            start = PAD + tile * edge + (8 if tile == 0 else 0)
            for field, done in ((0, done_p), (1, done_u)):
                for row in range(plan.rows_a):
                    at = (2 * tile + field) * plan.size_a + row * plan.cols_a
                    out[at : at + plan.cols_a, :] = done[
                        W + piece * plan.rows_a + row, start : start + plan.cols_a, :
                    ]


UNROLL = 4


def run_inner(plan, coef, phase, solute):
    rows = plan.half * plan.rows_a + 2 * W
    buffer = pltpu.VMEM((rows, plan.tiles * plan.edge + 2 * PAD, plan.depth), jnp.float32)
    vmem = pl.BlockSpec(memory_space=pltpu.VMEM)
    smem = pl.BlockSpec(memory_space=pltpu.SMEM)
    shape = jax.ShapeDtypeStruct((2 * plan.tiles * plan.size_a, plan.depth), jnp.float32)
    return pl.pallas_call(
        functools.partial(inner_kernel, plan),
        in_specs=[smem] * 3 + [vmem] * 2,
        out_specs=[vmem] * plan.half,
        out_shape=[shape] * plan.half,
        scratch_shapes=[buffer] * 4,
        compiler_params=pltpu.CompilerParams(vmem_limit_bytes=40 * 1024 * 1024),
        cost_estimate=pl.CostEstimate(flops=10**8, bytes_accessed=24 * 1024 * 1024, transcendentals=0),
        name="inner",
    )(*coef, phase, solute)


def steps_kernel(plan, under, mobile, spread, owner_ref, phase, solute, y_lo, y_hi, x_lo, x_hi, *rest):
    tiles, edge, depth, half = plan.tiles, plan.edge, plan.depth, plan.half
    outs, (p_a, u_a, p_b, u_b, coefs) = rest[: plan.pieces], rest[plan.pieces :]
    width = tiles * edge + 2 * W
    me = lax.axis_index("gy")
    for zone, source in ((0, x_lo), (1, None), (2, x_hi)):
        for kind, own in enumerate((under, mobile, spread)):
            if source is None:
                parts = [y_lo[edge, kind : kind + 1, :]]
                parts += [jnp.full((1, depth), own[0, tile], jnp.float32) for tile in range(tiles)]
                parts += [y_hi[edge, kind : kind + 1, :]]
            else:
                at = 2 * W * width + kind
                parts = [source[at : at + 1, :]]
                parts += [source[at + 16 + 8 * tile : at + 17 + 8 * tile, :] for tile in range(tiles)]
                parts += [source[at + 8 : at + 9, :]]
            coefs[zone, kind, :W, :] = jnp.broadcast_to(parts[0], (W, depth))
            for tile in range(tiles):
                begin = W + tile * edge
                coefs[zone, kind, begin : begin + edge, :] = jnp.broadcast_to(parts[1 + tile], (edge, depth))
            coefs[zone, kind, width - W :, :] = jnp.broadcast_to(parts[-1], (W, depth))
    for source, first in ((x_lo, 0), (x_hi, edge + W)):
        for row in range(W):
            for field, buffer in ((0, p_a), (1, u_a)):
                at = (2 * row + field) * width
                buffer[first + row, PAD : PAD + width, :] = source[at : at + width, :]

    def load_row(row, carry):
        fill_row(
            (p_a, u_a),
            W + row,
            [phase[0, tile, row] for tile in range(tiles)],
            [solute[0, tile, row] for tile in range(tiles)],
            y_lo[row],
            y_hi[row],
        )
        return carry

    lax.fori_loop(0, edge, load_row, 0)
    for step in range(NSTEPS):
        src_p, src_u, dst_p, dst_u = (p_a, u_a, p_b, u_b) if step % 2 == 0 else (p_b, u_b, p_a, u_a)

        def one_row(row, carry, src_p=src_p, src_u=src_u, dst_p=dst_p, dst_u=dst_u):
            zone = jnp.where(row < W, 0, jnp.where(row < W + edge, 1, 2))
            for start in range(PAD, PAD + width, 8):
                kinds = [coefs[zone, kind, start - PAD : start - PAD + 8, :] for kind in range(3)]
                new_p, new_u = cells(src_p, src_u, row, start, kinds)
                dst_p[row, start : start + 8, :] = new_p
                dst_u[row, start : start + 8, :] = new_u
            return carry

        lax.fori_loop(step + 1, edge + 2 * W - step - 1, one_row, 0, unroll=UNROLL)
    done_p, done_u = (p_a, u_a) if NSTEPS % 2 == 0 else (p_b, u_b)
    lane = lax.broadcasted_iota(jnp.int32, (AUX, depth), 1)
    names = jnp.zeros((AUX, depth), jnp.float32)
    for tile in range(tiles):
        names = jnp.where(lane == tile, owner_ref[0, tile].astype(jnp.float32), names)
    for mask, out in enumerate(outs):
        piece = me ^ mask
        begin = 0 if mask >= half else plan.size_a
        each = plan.size_b + begin
        for tile in range(tiles):
            start = PAD + W + tile * edge
            start_a, start_e = (start + 8, start) if tile == 0 else (start, start + plan.cols_a)
            for field, done in ((0, done_p), (1, done_u)):
                at = (2 * tile + field) * each
                for row in range(plan.rows_a):
                    x = W + plan.low + piece * plan.rows_a + row
                    if mask < half:
                        to = at + row * plan.cols_a
                        out[to : to + plan.cols_a, :] = done[x, start_a : start_a + plan.cols_a, :]
                    to = at + begin + plan.rows_b * edge + row * 8
                    out[to : to + 8, :] = done[x, start_e : start_e + 8, :]
                for row in range(plan.rows_b):
                    index = piece * plan.rows_b + row
                    x = W + index + jnp.where(index < plan.low, 0, plan.inner)
                    to = at + begin + row * edge
                    out[to : to + edge, :] = done[x, start : start + edge, :]
        tail = 2 * tiles * each
        out[tail : tail + AUX, :] = names


def run_steps(plan, coef, owner, phase, solute, y_lo, y_hi, x_lo, x_hi):
    tiles, edge, depth = plan.tiles, plan.edge, plan.depth
    width = tiles * edge + 2 * W
    buffer = pltpu.VMEM((edge + 2 * W, width + 2 * PAD, depth), jnp.float32)
    vmem = pl.BlockSpec(memory_space=pltpu.VMEM)
    smem = pl.BlockSpec(memory_space=pltpu.SMEM)
    near = jax.ShapeDtypeStruct((2 * tiles * plan.size + AUX, depth), jnp.float32)
    far = jax.ShapeDtypeStruct((2 * tiles * plan.size_b + AUX, depth), jnp.float32)
    return pl.pallas_call(
        functools.partial(steps_kernel, plan),
        in_specs=[smem] * 4 + [vmem] * 6,
        out_specs=[vmem] * plan.pieces,
        out_shape=[near] * plan.half + [far] * plan.half,
        scratch_shapes=[buffer] * 4 + [pltpu.VMEM((3, 3, width, depth), jnp.float32)],
        compiler_params=pltpu.CompilerParams(vmem_limit_bytes=40 * 1024 * 1024),
        cost_estimate=pl.CostEstimate(flops=10**8, bytes_accessed=40 * 1024 * 1024, transcendentals=0),
        name="steps",
    )(*coef, owner, phase, solute, y_lo, y_hi, x_lo, x_hi)


def route_kernel(plan, *refs):
    pieces, tiles, half, each = plan.pieces, plan.tiles, plan.half, 2 * plan.size
    near, far_a, far_b = refs[:half], refs[half : 2 * half], refs[2 * half : 3 * half]
    outs = refs[3 * half : 3 * half + pieces]
    held, names, table, name_sems, in_sems, out_sems = refs[3 * half + pieces :]
    me = lax.axis_index("gy")
    name_copies, copies = [], []
    for mask in range(pieces):
        source = near[mask] if mask < half else far_b[mask - half]
        tail = tiles * (each if mask < half else 2 * plan.size_b)
        copy = pltpu.make_async_copy(source.at[pl.ds(tail, 1), :], names.at[mask], name_sems.at[mask])
        copy.start()
        name_copies.append(copy)
    for mask in range(pieces):
        for tile in range(tiles):
            for field in range(2):
                index = 2 * tile + field
                if mask < half:
                    parts = [(near[mask], index * plan.size, 0, plan.size)]
                else:
                    parts = [
                        (far_a[mask - half], index * plan.size_a, 0, plan.size_a),
                        (far_b[mask - half], index * plan.size_b, plan.size_a, plan.size_b),
                    ]
                for source, begin, to, size in parts:
                    copy = pltpu.make_async_copy(
                        source.at[pl.ds(begin, size), :],
                        held.at[mask * tiles + tile, pl.ds(field * plan.size + to, size), :],
                        in_sems.at[len(copies)],
                    )
                    copy.start()
                    copies.append(copy)
    for mask in range(pieces):
        for tile in range(tiles):
            held[mask * tiles + tile, each : each + AUX, :] = jnp.full((AUX, plan.depth), tile, jnp.float32)
    for copy in name_copies:
        copy.wait()
    peers, homes = [], []
    for mask in range(pieces):
        for tile in range(tiles):
            peers.append(lax.rem(names[mask, 0, tile].astype(jnp.int32), pieces))
            homes.append((me ^ mask) * tiles + tile)
    for index in range(pieces * tiles):
        slot = jnp.int32(0)
        for other in range(pieces * tiles):
            if other != index:
                ahead = (peers[other] == peers[index]) & (homes[other] < homes[index])
                slot = slot + ahead.astype(jnp.int32)
        table[(peers[index] ^ me) * tiles + slot] = index
    for copy in copies:
        copy.wait()
    sends = []
    for mask in range(pieces):
        for slot in range(tiles):
            copy = pltpu.make_async_copy(
                held.at[table[mask * tiles + slot]], outs[mask].at[slot], out_sems.at[len(sends)]
            )
            copy.start()
            sends.append(copy)
    for copy in sends:
        copy.wait()


def route(plan, near, far_a, far_b):
    pieces, tiles, depth = plan.pieces, plan.tiles, plan.depth
    rows = 2 * plan.size + AUX
    count = 2 * tiles * (plan.half + 2 * plan.half)
    hbm = pl.BlockSpec(memory_space=pl.ANY)
    return pl.pallas_call(
        functools.partial(route_kernel, plan),
        in_specs=[hbm] * (3 * plan.half),
        out_specs=[hbm] * pieces,
        out_shape=[jax.ShapeDtypeStruct((tiles, rows, depth), jnp.float32)] * pieces,
        scratch_shapes=[
            pltpu.VMEM((pieces * tiles, rows, depth), jnp.float32),
            pltpu.SMEM((pieces, 1, depth), jnp.float32),
            pltpu.SMEM((pieces * tiles,), jnp.int32),
            pltpu.SemaphoreType.DMA((pieces,)),
            pltpu.SemaphoreType.DMA((count,)),
            pltpu.SemaphoreType.DMA((pieces * tiles,)),
        ],
        compiler_params=pltpu.CompilerParams(vmem_limit_bytes=16 * 1024 * 1024),
        name="route",
    )(*near, *far_a, *far_b)


def settle_kernel(plan, *refs):
    pieces, tiles, edge = plan.pieces, plan.tiles, plan.edge
    arrived, (phase, solute), (sides, side_sems, sems) = refs[:pieces], refs[pieces : pieces + 2], refs[pieces + 2 :]
    me = lax.axis_index("gy")
    side_copies = []
    for mask in range(pieces):
        for slot in range(tiles):
            copy = pltpu.make_async_copy(
                arrived[mask].at[slot, pl.ds(2 * plan.size, 1), :],
                sides.at[mask, slot],
                side_sems.at[len(side_copies)],
            )
            copy.start()
            side_copies.append(copy)
    copies = []

    def move(mask, slot, begin, rows, cols, out, row, col):
        copy = pltpu.make_async_copy(
            arrived[mask].at[slot, pl.ds(begin, rows * cols), :].reshape(rows, cols, plan.depth),
            out.at[0, slot, pl.ds(row, rows), pl.ds(col, cols), :],
            sems.at[len(copies)],
        )
        copy.start()
        copies.append(copy)

    for mask in range(pieces):
        piece = me ^ mask
        for slot in range(tiles):
            for field, out in ((0, phase), (1, solute)):
                for row in range(plan.rows_b):
                    index = piece * plan.rows_b + row
                    x = index + jnp.where(index < plan.low, 0, plan.inner)
                    begin = field * plan.size + plan.size_a + row * edge
                    move(mask, slot, begin, 1, edge, out, x, 0)
    for copy in side_copies:
        copy.wait()
    for mask in range(pieces):
        piece = me ^ mask
        for slot in range(tiles):
            side = sides[mask, slot, 0, 0].astype(jnp.int32)
            col_a = pl.multiple_of((1 - side) * 8, 8)
            col_e = pl.multiple_of(side * plan.cols_a, 8)
            x = plan.low + piece * plan.rows_a
            for field, out in ((0, phase), (1, solute)):
                move(mask, slot, field * plan.size, plan.rows_a, plan.cols_a, out, x, col_a)
                begin = field * plan.size + plan.size_a + plan.rows_b * edge
                move(mask, slot, begin, plan.rows_a, 8, out, x, col_e)
    for copy in copies:
        copy.wait()


def settle(plan, arrived):
    pieces, tiles, edge, depth = plan.pieces, plan.tiles, plan.edge, plan.depth
    out = jax.ShapeDtypeStruct((1, tiles, edge, edge, depth), jnp.float32)
    hbm = pl.BlockSpec(memory_space=pl.ANY)
    vmem = pl.BlockSpec(memory_space=pltpu.VMEM)
    return pl.pallas_call(
        functools.partial(settle_kernel, plan),
        in_specs=[hbm] * pieces,
        out_specs=[vmem, vmem],
        out_shape=[out, out],
        scratch_shapes=[
            pltpu.SMEM((pieces, tiles, 1, depth), jnp.float32),
            pltpu.SemaphoreType.DMA((pieces * tiles,)),
            pltpu.SemaphoreType.DMA((pieces * tiles * 2 * (plan.rows_b + 2),)),
        ],
        compiler_params=pltpu.CompilerParams(vmem_limit_bytes=16 * 1024 * 1024),
        name="settle",
    )(*arrived)


def ring(axis, step):
    count = lax.axis_size(axis)
    return [(i, (i + step) % count) for i in range(count)]


def swap(values, mask):
    return lax.ppermute(values, "gy", [(i, i ^ mask) for i in range(lax.axis_size("gy"))])


def per_device(phase, solute, undercool, mobility, diffusivity, owner):
    _, tiles, edge, _, depth = phase.shape
    plan = Plan(lax.axis_size("gy"), tiles, edge, depth)
    half = plan.half
    coef = (undercool, mobility, diffusivity)
    to_prev, to_next = pack_y(phase, solute, coef)
    y_lo = lax.ppermute(to_next, "gy", ring("gy", 1))
    y_hi = lax.ppermute(to_prev, "gy", ring("gy", -1))
    first = run_inner(plan, coef, phase, solute)
    far_a = [swap(values, half + index) for index, values in enumerate(first)]
    to_prev, to_next = pack_x(phase, solute, coef, y_lo, y_hi)
    x_lo = lax.ppermute(to_next, "gx", ring("gx", 1))
    x_hi = lax.ppermute(to_prev, "gx", ring("gx", -1))
    second = run_steps(plan, coef, owner, phase, solute, y_lo, y_hi, x_lo, x_hi)
    spread = [second[0]] + [swap(second[mask], mask) for mask in range(1, plan.pieces)]
    sent = route(plan, spread[:half], far_a, spread[half:])
    arrived = [sent[0]] + [swap(sent[mask], mask) for mask in range(1, plan.pieces)]
    return tuple(settle(plan, arrived))


def solution(mesh):
    tile_spec = P("gx", "gy", None, None, None)
    in_specs = (tile_spec, tile_spec) + (P("gx", "gy"),) * 4
    out_spec = P(("gx", "gy"), None, None, None, None)
    return jax.shard_map(
        per_device, mesh=mesh, in_specs=in_specs, out_specs=(out_spec, out_spec), check_vma=False
    )
```

```python
import functools

import jax
import jax.numpy as jnp
from jax import lax
from jax.experimental import pallas as pl
from jax.experimental.pallas import tpu as pltpu
from jax.sharding import PartitionSpec as P

NSTEPS = 4
W = NSTEPS
PAD = 8

aniso_strength = 0.05


def pack_y_kernel(under, mobile, spread, phase_lo, phase_hi, solute_lo, solute_hi, to_prev, to_next):
    edge = phase_lo.shape[2]
    to_prev[:edge, :W, :] = phase_lo[0, 0, :, :W, :]
    to_prev[:edge, W:, :] = solute_lo[0, 0, :, :W, :]
    to_next[:edge, :W, :] = phase_hi[0, 0, :, W:, :]
    to_next[:edge, W:, :] = solute_hi[0, 0, :, W:, :]
    to_prev[edge] = jnp.zeros((2 * W, to_prev.shape[2]), jnp.float32)
    to_next[edge] = jnp.zeros((2 * W, to_prev.shape[2]), jnp.float32)
    for kind, own in enumerate((under, mobile, spread)):
        to_prev[edge, kind, :] = jnp.full((to_prev.shape[2],), own[0, 0], jnp.float32)
        to_next[edge, kind, :] = jnp.full((to_prev.shape[2],), own[0, own.shape[1] - 1], jnp.float32)


def pack_y(phase, solute, coef):
    _, tiles, edge, _, depth = phase.shape
    low = pl.BlockSpec((1, 1, edge, 2 * W, depth), lambda i: (0, 0, 0, 0, 0))
    high = pl.BlockSpec((1, 1, edge, 2 * W, depth), lambda i: (0, tiles - 1, 0, edge // (2 * W) - 1, 0))
    out = jax.ShapeDtypeStruct((edge + 1, 2 * W, depth), jnp.float32)
    whole = pl.BlockSpec((edge + 1, 2 * W, depth), lambda i: (0, 0, 0))
    return pl.pallas_call(
        pack_y_kernel,
        grid=(1,),
        in_specs=[pl.BlockSpec(memory_space=pltpu.SMEM)] * 3 + [low, high, low, high],
        out_specs=[whole, whole],
        out_shape=[out, out],
        name="pack_y",
    )(*coef, phase, phase, solute, solute)


def pack_x_kernel(under, mobile, spread, phase_lo, phase_hi, solute_lo, solute_hi, y_lo, y_hi, _, to_prev, to_next):
    tiles, edge, depth = phase_lo.shape[1], phase_lo.shape[3], phase_lo.shape[4]
    width = tiles * edge + 2 * W
    for out, phase, solute, first in (
        (to_prev, phase_lo, solute_lo, 0),
        (to_next, phase_hi, solute_hi, edge - W),
    ):
        for row in range(W):
            for field, values, half in ((0, phase, 0), (1, solute, W)):
                at = (2 * row + field) * width
                out[at : at + W, :] = y_lo[first + row, half : half + W, :]
                for tile in range(tiles):
                    begin = at + W + tile * edge
                    out[begin : begin + edge, :] = values[0, tile, row]
                out[at + width - W : at + width, :] = y_hi[first + row, half : half + W, :]
        at = 2 * W * width
        out[at : at + 8, :] = y_lo[edge]
        out[at + 8 : at + 16, :] = y_hi[edge]
        for tile in range(tiles):
            begin = at + 16 + 8 * tile
            out[begin : begin + 8, :] = jnp.zeros((8, depth), jnp.float32)
            for kind, own in enumerate((under, mobile, spread)):
                out[begin + kind : begin + kind + 1, :] = jnp.full((1, depth), own[0, tile], jnp.float32)


def pack_x(phase, solute, coef, y_lo, y_hi, after):
    _, tiles, edge, _, depth = phase.shape
    low = pl.BlockSpec((1, tiles, W, edge, depth), lambda i: (0, 0, 0, 0, 0))
    high = pl.BlockSpec((1, tiles, W, edge, depth), lambda i: (0, 0, edge // W - 1, 0, 0))
    side = pl.BlockSpec((edge + 1, 2 * W, depth), lambda i: (0, 0, 0))
    rows = 2 * W * (tiles * edge + 2 * W) + 8 * (tiles + 2)
    out = jax.ShapeDtypeStruct((rows, depth), jnp.float32)
    whole = pl.BlockSpec((rows, depth), lambda i: (0, 0))
    return pl.pallas_call(
        pack_x_kernel,
        grid=(1,),
        in_specs=[pl.BlockSpec(memory_space=pltpu.SMEM)] * 3 + [low, high, low, high, side, side, pl.BlockSpec(memory_space=pl.ANY)],
        out_specs=[whole, whole],
        out_shape=[out, out],
        name="pack_x",
    )(*coef, phase, phase, solute, solute, y_lo, y_hi, after)


def update(near_p, near_u, under, mobile, spread):
    p, p_xl, p_xh, p_yl, p_yh = near_p
    u, u_xl, u_xh, u_yl, u_yh = near_u
    depth = p.shape[-1]
    lane = lax.broadcasted_iota(jnp.int32, p.shape, 1)
    first, last = lane == 0, lane == depth - 1
    p_zl = jnp.where(first, p, pltpu.roll(p, 1, 1))
    p_zh = jnp.where(last, p, pltpu.roll(p, depth - 1, 1))
    u_zl = jnp.where(first, u, pltpu.roll(u, 1, 1))
    u_zh = jnp.where(last, u, pltpu.roll(u, depth - 1, 1))
    dx, dy, dz = p_xh - p_xl, p_yh - p_yl, p_zh - p_zl
    qx, qy, qz = dx * dx, dy * dy, dz * dz
    total = qx + qy + qz
    fourth = qx * qx + qy * qy + qz * qz
    base = total + 4.0
    guess = pl.reciprocal(base, approx=True)
    inverse = guess * (2.0 - base * guess)
    extra = (4.0 * aniso_strength * fourth - (3.0 * aniso_strength) * total * total) * (inverse * inverse)
    lap_p = (p_xl + p_xh) + (p_yl + p_yh) + (p_zl + p_zh) - 6.0 * p
    lap_u = (u_xl + u_xh) + (u_yl + u_yh) + (u_zl + u_zh) - 6.0 * u
    well = 1.0 - p * p
    drive = well * (under + u)
    change = mobile * (lap_p + extra * lap_p + well * (p - 2.0 * drive))
    return p + change, u + spread * lap_u + 0.5 * change


class Plan:
    def __init__(self, pieces, tiles, edge, depth):
        self.pieces, self.tiles, self.edge, self.depth = pieces, tiles, edge, depth
        self.half = pieces // 2
        self.inner = (edge - 2 * W) // pieces * pieces
        self.low = (edge - self.inner) // 2
        self.rows_a = self.inner // pieces
        self.rows_b = (edge - self.inner) // pieces
        self.cols_a = edge - 8
        self.size_a = self.rows_a * self.cols_a
        self.size_b = self.rows_b * edge + self.rows_a * 8
        self.size = self.size_a + self.size_b


AUX = 8


def cells(src_p, src_u, row, start, coefs):
    near = []
    for src in (src_p, src_u):
        near.append(
            (
                src[row, start : start + 8, :],
                src[row - 1, start : start + 8, :],
                src[row + 1, start : start + 8, :],
                src[row, start - 1 : start + 7, :],
                src[row, start + 1 : start + 9, :],
            )
        )
    return update(near[0], near[1], *coefs)


UNROLL = 4


def march(first, last, starts, source, target, coefs_of):
    def one_row(row, carry):
        for start in starts:
            new_p, new_u = cells(source[0], source[1], row, start, coefs_of(row, start))
            target[0][row, start : start + 8, :] = new_p
            target[1][row, start : start + 8, :] = new_u
        return carry

    lax.fori_loop(first, last, one_row, 0, unroll=UNROLL)


def inner_kernel(plan, under, mobile, spread, owner, phase, solute, *rest):
    tiles, edge, depth, pieces = plan.tiles, plan.edge, plan.depth, plan.pieces
    outs, fields = rest[:pieces], rest[pieces:]
    pairs = [fields[2 * NSTEPS - 2 : 2 * NSTEPS]]
    pairs += [fields[2 * step : 2 * step + 2] for step in range(NSTEPS - 1)]
    pairs += [fields[2 * NSTEPS :]]
    me = lax.axis_index("gy")

    def load_row(row, carry):
        for tile in range(tiles):
            start = PAD + tile * edge
            pairs[0][0][row, start : start + edge, :] = phase[0, tile, row]
            pairs[0][1][row, start : start + edge, :] = solute[0, tile, row]
        return carry

    lax.fori_loop(plan.low - W, edge - plan.low + W, load_row, 0, unroll=UNROLL)

    def coefs_of(row, start):
        tile = (start - PAD) // edge
        return under[0, tile], mobile[0, tile], spread[0, tile]

    for step in range(NSTEPS):
        margin = plan.low - W + step + 1
        starts = range(PAD, PAD + tiles * edge, 8)
        march(margin, edge - margin, starts, pairs[step], pairs[step + 1], coefs_of)
    lane = lax.broadcasted_iota(jnp.int32, (AUX, depth), 1)
    names = jnp.zeros((AUX, depth), jnp.float32)
    for tile in range(tiles):
        names = jnp.where(lane == tile, owner[0, tile].astype(jnp.float32), names)
    for mask, out in enumerate(outs):
        piece = me ^ mask
        for tile in range(tiles):
            start = PAD + tile * edge + (8 if tile == 0 else 0)
            for field, done in enumerate(pairs[-1]):
                for row in range(plan.rows_a):
                    at = (2 * tile + field) * plan.size_a + row * plan.cols_a
                    out[at : at + plan.cols_a, :] = done[
                        plan.low + piece * plan.rows_a + row, start : start + plan.cols_a, :
                    ]
        at = 2 * tiles * plan.size_a
        out[at : at + AUX, :] = names


def run_inner(plan, coef, owner, phase, solute):
    shape = (plan.edge, plan.tiles * plan.edge + 2 * PAD, plan.depth)
    vmem = pl.BlockSpec(memory_space=pltpu.VMEM)
    smem = pl.BlockSpec(memory_space=pltpu.SMEM)
    piece = jax.ShapeDtypeStruct((2 * plan.tiles * plan.size_a + AUX, plan.depth), jnp.float32)
    kept = 2 * (NSTEPS - 1)
    results = pl.pallas_call(
        functools.partial(inner_kernel, plan),
        in_specs=[smem] * 4 + [vmem] * 2,
        out_specs=[vmem] * (plan.pieces + kept),
        out_shape=[piece] * plan.pieces + [jax.ShapeDtypeStruct(shape, jnp.float32)] * kept,
        scratch_shapes=[pltpu.VMEM(shape, jnp.float32)] * 4,
        compiler_params=pltpu.CompilerParams(vmem_limit_bytes=40 * 1024 * 1024),
        cost_estimate=pl.CostEstimate(flops=10**8, bytes_accessed=24 * 1024 * 1024, transcendentals=0),
        name="inner",
    )(*coef, owner, phase, solute)
    return results[: plan.pieces], results[plan.pieces :]


def ring_kernel(plan, under, mobile, spread, phase, solute, y_lo, y_hi, x_lo, x_hi, *rest):
    tiles, edge, depth, pieces, low = plan.tiles, plan.edge, plan.depth, plan.pieces, plan.low
    kept = 2 * (NSTEPS - 1)
    fields, outs, scratch = rest[:kept], rest[kept : kept + pieces], rest[kept + pieces :]
    pairs, coefs = [scratch[2 * step : 2 * step + 2] for step in range(NSTEPS + 1)], scratch[-1]
    cols = tiles * edge
    width = cols + 2 * W
    own = 2 * PAD
    me = lax.axis_index("gy")
    for zone, source in ((0, x_lo), (1, None), (2, x_hi)):
        for kind, here in enumerate((under, mobile, spread)):
            if source is None:
                parts = [y_lo[edge, kind : kind + 1, :]]
                parts += [jnp.full((1, depth), here[0, tile], jnp.float32) for tile in range(tiles)]
                parts += [y_hi[edge, kind : kind + 1, :]]
            else:
                at = 2 * W * width + kind
                parts = [source[at : at + 1, :]]
                parts += [source[at + 16 + 8 * tile : at + 17 + 8 * tile, :] for tile in range(tiles)]
                parts += [source[at + 8 : at + 9, :]]
            coefs[zone, kind, :8, :] = jnp.broadcast_to(parts[0], (8, depth))
            for tile in range(tiles):
                begin = 8 + tile * edge
                coefs[zone, kind, begin : begin + edge, :] = jnp.broadcast_to(parts[1 + tile], (edge, depth))
            coefs[zone, kind, 8 + cols :, :] = jnp.broadcast_to(parts[-1], (8, depth))
    for source, first in ((x_lo, 0), (x_hi, edge + W)):
        for row in range(W):
            for field in range(2):
                at = (2 * row + field) * width
                pairs[0][field][first + row, own - W : own + cols + W, :] = source[at : at + width, :]

    def load_sides(row, carry):
        for field, values in ((0, phase), (1, solute)):
            buffer = pairs[0][field]
            half = field * W
            buffer[W + row, own - W : own, :] = y_lo[row, half : half + W, :]
            buffer[W + row, own + cols : own + cols + W, :] = y_hi[row, half : half + W, :]
            buffer[W + row, own : own + 16, :] = values[0, 0, row, :16, :]
            buffer[W + row, own + cols - 16 : own + cols, :] = values[0, tiles - 1, row, edge - 16 :, :]
        return carry

    lax.fori_loop(0, edge, load_sides, 0, unroll=UNROLL)
    for row in list(range(low - 2)) + list(range(edge - low + 2, edge)):
        for field, values in ((0, phase), (1, solute)):
            for tile in range(tiles):
                start = own + tile * edge
                pairs[0][field][W + row, start : start + edge, :] = values[0, tile, row]
    for step in range(1, NSTEPS):
        margin = low - W + step
        for field in range(2):
            kept_field, buffer = fields[2 * (step - 1) + field], pairs[step][field]
            for row in (margin, margin + 1, edge - margin - 2, edge - margin - 1):
                buffer[W + row, own + 8 : own + cols - 8, :] = kept_field[row, PAD + 8 : PAD + cols - 8, :]

            def copy_sides(row, carry, kept_field=kept_field, buffer=buffer):
                for start in (8, cols - 16):
                    buffer[W + row, own + start : own + start + 8, :] = kept_field[
                        row, PAD + start : PAD + start + 8, :
                    ]
                return carry

            lax.fori_loop(margin, edge - margin, copy_sides, 0, unroll=UNROLL)

    def coefs_of(zone):
        def found(row, start):
            return tuple(coefs[zone(row), kind, start - PAD : start - PAD + 8, :] for kind in range(3))

        return found

    any_zone = coefs_of(lambda row: jnp.where(row < W, 0, jnp.where(row < W + edge, 1, 2)))
    own_zone = coefs_of(lambda row: 1)
    for step in range(1, NSTEPS + 1):
        source, target = pairs[step - 1], pairs[step]
        if step < NSTEPS:
            across = range(own - 8, own + cols + 8, 8)
            sides = (own - 8, own, own + cols - 8, own + cols)
        else:
            across, sides = range(own, own + cols, 8), (own, own + cols - 8)
        margin = low - W + step
        march(W - (W - step), W + margin, across, source, target, any_zone)
        march(W + edge - margin, W + edge + W - step, across, source, target, any_zone)
        march(W + margin, W + edge - margin, sides, source, target, own_zone)
    for mask, out in enumerate(outs):
        piece = me ^ mask
        for tile in range(tiles):
            start = own + tile * edge
            side = start if tile == 0 else start + plan.cols_a
            for field, done in enumerate(pairs[NSTEPS]):
                at = (2 * tile + field) * plan.size_b
                for row in range(plan.rows_b):
                    index = piece * plan.rows_b + row
                    x = W + index + jnp.where(index < low, 0, plan.inner)
                    out[at : at + edge, :] = done[x, start : start + edge, :]
                    at += edge
                for row in range(plan.rows_a):
                    x = W + low + piece * plan.rows_a + row
                    out[at : at + 8, :] = done[x, side : side + 8, :]
                    at += 8


def run_ring(plan, coef, phase, solute, halos, fields):
    cols = plan.tiles * plan.edge
    buffer = pltpu.VMEM((plan.edge + 2 * W, cols + 4 * PAD, plan.depth), jnp.float32)
    vmem = pl.BlockSpec(memory_space=pltpu.VMEM)
    smem = pl.BlockSpec(memory_space=pltpu.SMEM)
    piece = jax.ShapeDtypeStruct((2 * plan.tiles * plan.size_b, plan.depth), jnp.float32)
    return pl.pallas_call(
        functools.partial(ring_kernel, plan),
        in_specs=[smem] * 3 + [vmem] * (6 + len(fields)),
        out_specs=[vmem] * plan.pieces,
        out_shape=[piece] * plan.pieces,
        scratch_shapes=[buffer] * (2 * NSTEPS + 2) + [pltpu.VMEM((3, 3, cols + 16, plan.depth), jnp.float32)],
        compiler_params=pltpu.CompilerParams(vmem_limit_bytes=40 * 1024 * 1024),
        cost_estimate=pl.CostEstimate(flops=10**8, bytes_accessed=24 * 1024 * 1024, transcendentals=0),
        name="rest",
    )(*coef, phase, solute, *halos, *fields)


def table_kernel(plan, *refs):
    pieces, tiles = plan.pieces, plan.tiles
    arrived, (table, names, sems) = refs[:pieces], refs[pieces + 1 :]
    me = lax.axis_index("gy")
    copies = []
    for mask in range(pieces):
        tail = 2 * tiles * plan.size_a
        copy = pltpu.make_async_copy(arrived[mask].at[pl.ds(tail, 1), :], names.at[mask], sems.at[mask])
        copy.start()
        copies.append(copy)
    for copy in copies:
        copy.wait()
    peers, homes = [], []
    for mask in range(pieces):
        for tile in range(tiles):
            peers.append(lax.rem(names[mask, 0, tile].astype(jnp.int32), pieces))
            homes.append((me ^ mask) * tiles + tile)
    for index in range(pieces * tiles):
        slot = jnp.int32(0)
        for other in range(pieces * tiles):
            if other != index:
                ahead = (peers[other] == peers[index]) & (homes[other] < homes[index])
                slot = slot + ahead.astype(jnp.int32)
        table[(peers[index] ^ me) * tiles + slot] = index


def find_table(plan, arrived, after):
    pieces, tiles = plan.pieces, plan.tiles
    return pl.pallas_call(
        functools.partial(table_kernel, plan),
        in_specs=[pl.BlockSpec(memory_space=pl.ANY)] * (pieces + 1),
        out_specs=pl.BlockSpec(memory_space=pltpu.SMEM),
        out_shape=jax.ShapeDtypeStruct((pieces * tiles,), jnp.int32),
        scratch_shapes=[
            pltpu.SMEM((pieces, 1, plan.depth), jnp.float32),
            pltpu.SemaphoreType.DMA((pieces,)),
        ],
        name="table",
    )(*arrived, after)


def route_kernel(plan, size, aux, table, *refs):
    pieces, tiles = plan.pieces, plan.tiles
    arrived, outs, (held,) = refs[:pieces], refs[pieces : 2 * pieces], refs[2 * pieces :]
    for mask in range(pieces):
        for tile in range(tiles):
            held[mask * tiles + tile] = arrived[mask][tile * size : (tile + 1) * size, :]
    for mask in range(pieces):
        for slot in range(tiles):
            index = table[mask * tiles + slot]
            outs[mask][slot, :size, :] = held[index]
            if aux:
                side = lax.rem(index, tiles).astype(jnp.float32)
                outs[mask][slot, size : size + aux, :] = jnp.full((aux, plan.depth), side, jnp.float32)


def route(plan, size, aux, table, arrived):
    pieces, tiles, depth = plan.pieces, plan.tiles, plan.depth
    vmem = pl.BlockSpec(memory_space=pltpu.VMEM)
    return pl.pallas_call(
        functools.partial(route_kernel, plan, size, aux),
        in_specs=[pl.BlockSpec(memory_space=pltpu.SMEM)] + [vmem] * pieces,
        out_specs=[vmem] * pieces,
        out_shape=[jax.ShapeDtypeStruct((tiles, size + aux, depth), jnp.float32)] * pieces,
        scratch_shapes=[pltpu.VMEM((pieces * tiles, size, depth), jnp.float32)],
        compiler_params=pltpu.CompilerParams(vmem_limit_bytes=16 * 1024 * 1024),
        name="route",
    )(table, *arrived)


def settle_kernel(plan, *refs):
    pieces, tiles, edge, depth = plan.pieces, plan.tiles, plan.edge, plan.depth
    part_a, part_b, outs = refs[:pieces], refs[pieces : 2 * pieces], refs[2 * pieces :]
    me = lax.axis_index("gy")
    for mask in range(pieces):
        piece = me ^ mask
        for slot in range(tiles):
            last = part_a[mask][slot, 2 * plan.size_a : 2 * plan.size_a + 8, :] > 0.5
            for field, out in enumerate(outs):
                at = field * plan.size_b
                for row in range(plan.rows_b):
                    index = piece * plan.rows_b + row
                    x = index + jnp.where(index < plan.low, 0, plan.inner)
                    out[0, slot, x] = part_b[mask][slot, at : at + edge, :]
                    at += edge
                for row in range(plan.rows_a):
                    x = plan.low + piece * plan.rows_a + row
                    begin = field * plan.size_a + row * plan.cols_a
                    side = part_b[mask][slot, at : at + 8, :]
                    at += 8
                    blocks = [
                        part_a[mask][slot, begin + col : begin + col + 8, :] for col in range(0, plan.cols_a, 8)
                    ]
                    for index, (low, high) in enumerate(zip([side] + blocks, blocks + [side])):
                        out[0, slot, x, 8 * index : 8 * index + 8, :] = jnp.where(last, high, low)


def settle(plan, part_a, part_b):
    out = jax.ShapeDtypeStruct((1, plan.tiles, plan.edge, plan.edge, plan.depth), jnp.float32)
    vmem = pl.BlockSpec(memory_space=pltpu.VMEM)
    return pl.pallas_call(
        functools.partial(settle_kernel, plan),
        in_specs=[vmem] * (2 * plan.pieces),
        out_specs=[vmem, vmem],
        out_shape=[out, out],
        compiler_params=pltpu.CompilerParams(vmem_limit_bytes=16 * 1024 * 1024),
        name="settle",
    )(*part_a, *part_b)


def ring(axis, step):
    count = lax.axis_size(axis)
    return [(i, (i + step) % count) for i in range(count)]


def exchange(plan, values):
    moved = [values[0]] + [None] * (plan.pieces - 1)
    for mask in list(range(plan.half, plan.pieces)) + list(range(1, plan.half)):
        moved[mask] = lax.ppermute(values[mask], "gy", [(i, i ^ mask) for i in range(plan.pieces)])
    return moved


def per_device(phase, solute, undercool, mobility, diffusivity, owner):
    _, tiles, edge, _, depth = phase.shape
    plan = Plan(lax.axis_size("gy"), tiles, edge, depth)
    coef = (undercool, mobility, diffusivity)
    to_prev, to_next = pack_y(phase, solute, coef)
    y_lo = lax.ppermute(to_next, "gy", ring("gy", 1))
    y_hi = lax.ppermute(to_prev, "gy", ring("gy", -1))
    first, fields = run_inner(plan, coef, owner, phase, solute)
    part_a = exchange(plan, first)
    to_prev, to_next = pack_x(phase, solute, coef, y_lo, y_hi, fields[0])
    x_lo = lax.ppermute(to_next, "gx", ring("gx", 1))
    x_hi = lax.ppermute(to_prev, "gx", ring("gx", -1))
    second = run_ring(plan, coef, phase, solute, (y_lo, y_hi, x_lo, x_hi), fields)
    part_b = exchange(plan, second)
    table = find_table(plan, part_a, second[0])
    sent_a = exchange(plan, route(plan, 2 * plan.size_a, AUX, table, part_a))
    sent_b = exchange(plan, route(plan, 2 * plan.size_b, 0, table, part_b))
    return tuple(settle(plan, sent_a, sent_b))


def solution(mesh):
    tile_spec = P("gx", "gy", None, None, None)
    in_specs = (tile_spec, tile_spec) + (P("gx", "gy"),) * 4
    out_spec = P(("gx", "gy"), None, None, None, None)
    return jax.shard_map(
        per_device, mesh=mesh, in_specs=in_specs, out_specs=(out_spec, out_spec), check_vma=False
    )
```

```python
import functools

import jax
import jax.numpy as jnp
from jax import lax
from jax.experimental import pallas as pl
from jax.experimental.pallas import tpu as pltpu
from jax.sharding import PartitionSpec as P

NSTEPS = 4
W = NSTEPS
PAD = 8

aniso_strength = 0.05


def pack_y_kernel(under, mobile, spread, owner, phase_lo, phase_hi, solute_lo, solute_hi, to_prev, to_next, own, *scratch):
    copies = []
    for index, source in enumerate((under, mobile, spread, owner)):
        copies.append(pltpu.make_async_copy(source, scratch[index], scratch[-1].at[index]))
        copies[-1].start()
    edge, depth = phase_lo.shape[2], phase_lo.shape[4]
    tiles = own.shape[0] // 8 - 1
    to_prev[:edge, :W, :] = phase_lo[0, 0, :, :W, :]
    to_prev[:edge, W:, :] = solute_lo[0, 0, :, :W, :]
    to_next[:edge, :W, :] = phase_hi[0, 0, :, W:, :]
    to_next[:edge, W:, :] = solute_hi[0, 0, :, W:, :]
    for copy in copies:
        copy.wait()
    line = lax.broadcasted_iota(jnp.int32, (8, depth), 0)
    lane = lax.broadcasted_iota(jnp.int32, (8, depth), 1)
    names = jnp.zeros((8, depth), jnp.float32)
    for tile in range(tiles):
        rows = jnp.zeros((8, depth), jnp.float32)
        for kind in range(3):
            rows = jnp.where(line == kind, scratch[kind][0, tile], rows)
        own[8 * tile : 8 * tile + 8, :] = rows
        if tile == 0:
            to_prev[edge] = rows
        if tile == tiles - 1:
            to_next[edge] = rows
        names = jnp.where(lane == tile, scratch[3][0, tile].astype(jnp.float32), names)
    own[8 * tiles :, :] = names


def pack_y(phase, solute, coef, owner):
    _, tiles, edge, _, depth = phase.shape
    low = pl.BlockSpec((1, 1, edge, 2 * W, depth), lambda i: (0, 0, 0, 0, 0))
    high = pl.BlockSpec((1, 1, edge, 2 * W, depth), lambda i: (0, tiles - 1, 0, edge // (2 * W) - 1, 0))
    face = jax.ShapeDtypeStruct((edge + 1, 2 * W, depth), jnp.float32)
    own = jax.ShapeDtypeStruct((8 * tiles + 8, depth), jnp.float32)
    whole = pl.BlockSpec((edge + 1, 2 * W, depth), lambda i: (0, 0, 0))
    return pl.pallas_call(
        pack_y_kernel,
        grid=(1,),
        in_specs=[pl.BlockSpec(memory_space=pl.ANY)] * 4 + [low, high, low, high],
        out_specs=[whole, whole, pl.BlockSpec((8 * tiles + 8, depth), lambda i: (0, 0))],
        out_shape=[face, face, own],
        scratch_shapes=[pltpu.SMEM((1, tiles), jnp.float32)] * 3
        + [pltpu.SMEM((1, tiles), jnp.int32), pltpu.SemaphoreType.DMA((4,))],
        compiler_params=pltpu.CompilerParams(vmem_limit_bytes=8 * 1024 * 1024),
        name="pack_y",
    )(*coef, owner, phase, phase, solute, solute)


def pack_x_kernel(own, phase_lo, phase_hi, solute_lo, solute_hi, y_lo, y_hi, _, to_prev, to_next):
    tiles, edge, depth = phase_lo.shape[1], phase_lo.shape[3], phase_lo.shape[4]
    width = tiles * edge + 2 * W
    for out, phase, solute, first in (
        (to_prev, phase_lo, solute_lo, 0),
        (to_next, phase_hi, solute_hi, edge - W),
    ):
        for row in range(W):
            for field, values, half in ((0, phase, 0), (1, solute, W)):
                at = (2 * row + field) * width
                out[at : at + W, :] = y_lo[first + row, half : half + W, :]
                for tile in range(tiles):
                    begin = at + W + tile * edge
                    out[begin : begin + edge, :] = values[0, tile, row]
                out[at + width - W : at + width, :] = y_hi[first + row, half : half + W, :]
        at = 2 * W * width
        out[at : at + 8, :] = y_lo[edge]
        out[at + 8 : at + 16, :] = y_hi[edge]
        out[at + 16 : at + 16 + 8 * tiles, :] = own[: 8 * tiles, :]


def pack_x(phase, solute, own, y_lo, y_hi, after):
    _, tiles, edge, _, depth = phase.shape
    low = pl.BlockSpec((1, tiles, W, edge, depth), lambda i: (0, 0, 0, 0, 0))
    high = pl.BlockSpec((1, tiles, W, edge, depth), lambda i: (0, 0, edge // W - 1, 0, 0))
    side = pl.BlockSpec((edge + 1, 2 * W, depth), lambda i: (0, 0, 0))
    rows = 2 * W * (tiles * edge + 2 * W) + 8 * (tiles + 2)
    out = jax.ShapeDtypeStruct((rows, depth), jnp.float32)
    whole = pl.BlockSpec((rows, depth), lambda i: (0, 0))
    return pl.pallas_call(
        pack_x_kernel,
        grid=(1,),
        in_specs=[pl.BlockSpec((8 * tiles + 8, depth), lambda i: (0, 0)), low, high, low, high, side, side, pl.BlockSpec(memory_space=pl.ANY)],
        out_specs=[whole, whole],
        out_shape=[out, out],
        compiler_params=pltpu.CompilerParams(vmem_limit_bytes=8 * 1024 * 1024),
        name="pack_x",
    )(own, phase, phase, solute, solute, y_lo, y_hi, after)


def update(near_p, near_u, under, mobile, spread):
    p, p_xl, p_xh, p_yl, p_yh = near_p
    u, u_xl, u_xh, u_yl, u_yh = near_u
    depth = p.shape[-1]
    lane = lax.broadcasted_iota(jnp.int32, p.shape, 1)
    first, last = lane == 0, lane == depth - 1
    p_zl = jnp.where(first, p, pltpu.roll(p, 1, 1))
    p_zh = jnp.where(last, p, pltpu.roll(p, depth - 1, 1))
    u_zl = jnp.where(first, u, pltpu.roll(u, 1, 1))
    u_zh = jnp.where(last, u, pltpu.roll(u, depth - 1, 1))
    dx, dy, dz = p_xh - p_xl, p_yh - p_yl, p_zh - p_zl
    qx, qy, qz = dx * dx, dy * dy, dz * dz
    total = qx + qy + qz
    fourth = qx * qx + qy * qy + qz * qz
    base = total + 4.0
    guess = pl.reciprocal(base, approx=True)
    inverse = guess * (2.0 - base * guess)
    extra = (4.0 * aniso_strength * fourth - (3.0 * aniso_strength) * total * total) * (inverse * inverse)
    lap_p = (p_xl + p_xh) + (p_yl + p_yh) + (p_zl + p_zh) - 6.0 * p
    lap_u = (u_xl + u_xh) + (u_yl + u_yh) + (u_zl + u_zh) - 6.0 * u
    well = 1.0 - p * p
    drive = well * (under + u)
    change = mobile * (lap_p + extra * lap_p + well * (p - 2.0 * drive))
    return p + change, u + spread * lap_u + 0.5 * change


class Plan:
    def __init__(self, pieces, tiles, edge, depth):
        self.pieces, self.tiles, self.edge, self.depth = pieces, tiles, edge, depth
        self.half = pieces // 2
        self.inner = (edge - 2 * W) // pieces * pieces
        self.low = (edge - self.inner) // 2
        self.rows_a = self.inner // pieces
        self.rows_b = (edge - self.inner) // pieces
        self.cols_a = edge - 8
        self.size_a = self.rows_a * self.cols_a
        self.size_b = self.rows_b * edge + self.rows_a * 8
        self.size = self.size_a + self.size_b

    def far_first(self, values):
        return [*values[self.half :], *values[1 : self.half], values[0]]

    def by_mask(self, values):
        return [values[-1], *values[self.half : -1], *values[: self.half]]


AUX = 8


def cells(src_p, src_u, row, start, coefs):
    near = []
    for src in (src_p, src_u):
        near.append(
            (
                src[row, start : start + 8, :],
                src[row - 1, start : start + 8, :],
                src[row + 1, start : start + 8, :],
                src[row, start - 1 : start + 7, :],
                src[row, start + 1 : start + 9, :],
            )
        )
    return update(near[0], near[1], *coefs)


UNROLL = 4


def march(first, last, starts, source, target, coefs_of):
    def one_row(row, carry):
        for start in starts:
            new_p, new_u = cells(source[0], source[1], row, start, coefs_of(row, start))
            target[0][row, start : start + 8, :] = new_p
            target[1][row, start : start + 8, :] = new_u
        return carry

    lax.fori_loop(first, last, one_row, 0, unroll=UNROLL)


def inner_kernel(plan, own, phase, solute, *rest):
    tiles, edge, depth, pieces = plan.tiles, plan.edge, plan.depth, plan.pieces
    outs, fields = rest[:pieces], rest[pieces:]
    pairs = [fields[2 * NSTEPS - 2 : 2 * NSTEPS]]
    pairs += [fields[2 * step : 2 * step + 2] for step in range(NSTEPS - 1)]
    pairs += [fields[2 * NSTEPS :]]
    me = lax.axis_index("gy")

    def load_row(row, carry):
        for tile in range(tiles):
            start = PAD + tile * edge
            pairs[0][0][row, start : start + edge, :] = phase[0, tile, row]
            pairs[0][1][row, start : start + edge, :] = solute[0, tile, row]
        return carry

    lax.fori_loop(plan.low - W, edge - plan.low + W, load_row, 0, unroll=UNROLL)

    def coefs_of(row, start):
        tile = (start - PAD) // edge
        return tuple(own[8 * tile + kind : 8 * tile + kind + 1, :] for kind in range(3))

    for step in range(NSTEPS):
        margin = plan.low - W + step + 1
        starts = range(PAD, PAD + tiles * edge, 8)
        march(margin, edge - margin, starts, pairs[step], pairs[step + 1], coefs_of)
    for mask, out in enumerate(outs):
        piece = me ^ mask
        for tile in range(tiles):
            start = PAD + tile * edge + (8 if tile == 0 else 0)
            for field, done in enumerate(pairs[-1]):
                for row in range(plan.rows_a):
                    at = (2 * tile + field) * plan.size_a + row * plan.cols_a
                    out[at : at + plan.cols_a, :] = done[
                        plan.low + piece * plan.rows_a + row, start : start + plan.cols_a, :
                    ]
        at = 2 * tiles * plan.size_a
        out[at : at + AUX, :] = own[8 * tiles : 8 * tiles + AUX, :]


def run_inner(plan, own, phase, solute):
    shape = (plan.edge, plan.tiles * plan.edge + 2 * PAD, plan.depth)
    vmem = pl.BlockSpec(memory_space=pltpu.VMEM)
    piece = jax.ShapeDtypeStruct((2 * plan.tiles * plan.size_a + AUX, plan.depth), jnp.float32)
    kept = 2 * (NSTEPS - 1)
    results = pl.pallas_call(
        functools.partial(inner_kernel, plan),
        in_specs=[vmem] * 3,
        out_specs=[vmem] * (plan.pieces + kept),
        out_shape=[piece] * plan.pieces + [jax.ShapeDtypeStruct(shape, jnp.float32)] * kept,
        scratch_shapes=[pltpu.VMEM(shape, jnp.float32)] * 4,
        compiler_params=pltpu.CompilerParams(vmem_limit_bytes=12 * 1024 * 1024),
        cost_estimate=pl.CostEstimate(flops=10**8, bytes_accessed=24 * 1024 * 1024, transcendentals=0),
        name="inner",
    )(own, phase, solute)
    return results[: plan.pieces], results[plan.pieces :]


def ring_kernel(plan, own_rows, phase, solute, y_lo, y_hi, x_lo, x_hi, *rest):
    tiles, edge, depth, pieces, low = plan.tiles, plan.edge, plan.depth, plan.pieces, plan.low
    kept = 2 * (NSTEPS - 1)
    fields, outs, scratch = rest[:kept], rest[kept : kept + pieces], rest[kept + pieces :]
    pairs = [scratch[2 * (step % 2) : 2 * (step % 2) + 2] for step in range(NSTEPS + 1)]
    coefs = scratch[-1]
    cols = tiles * edge
    width = cols + 2 * W
    own = 2 * PAD
    me = lax.axis_index("gy")
    for zone, source in ((0, x_lo), (1, None), (2, x_hi)):
        for kind in range(3):
            if source is None:
                parts = [y_lo[edge, kind : kind + 1, :]]
                parts += [own_rows[8 * tile + kind : 8 * tile + kind + 1, :] for tile in range(tiles)]
                parts += [y_hi[edge, kind : kind + 1, :]]
            else:
                at = 2 * W * width + kind
                parts = [source[at : at + 1, :]]
                parts += [source[at + 16 + 8 * tile : at + 17 + 8 * tile, :] for tile in range(tiles)]
                parts += [source[at + 8 : at + 9, :]]
            coefs[zone, kind, :8, :] = jnp.broadcast_to(parts[0], (8, depth))
            for tile in range(tiles):
                begin = 8 + tile * edge
                coefs[zone, kind, begin : begin + edge, :] = jnp.broadcast_to(parts[1 + tile], (edge, depth))
            coefs[zone, kind, 8 + cols :, :] = jnp.broadcast_to(parts[-1], (8, depth))
    for source, first in ((x_lo, 0), (x_hi, edge + W)):
        for row in range(W):
            for field in range(2):
                at = (2 * row + field) * width
                pairs[0][field][first + row, own - W : own + cols + W, :] = source[at : at + width, :]

    def load_sides(row, carry):
        for field, values in ((0, phase), (1, solute)):
            buffer = pairs[0][field]
            half = field * W
            buffer[W + row, own - W : own, :] = y_lo[row, half : half + W, :]
            buffer[W + row, own + cols : own + cols + W, :] = y_hi[row, half : half + W, :]
            buffer[W + row, own : own + 16, :] = values[0, 0, row, :16, :]
            buffer[W + row, own + cols - 16 : own + cols, :] = values[0, tiles - 1, row, edge - 16 :, :]
        return carry

    lax.fori_loop(0, edge, load_sides, 0, unroll=UNROLL)
    for row in list(range(low - 2)) + list(range(edge - low + 2, edge)):
        for field, values in ((0, phase), (1, solute)):
            for tile in range(tiles):
                start = own + tile * edge
                pairs[0][field][W + row, start : start + edge, :] = values[0, tile, row]
    def coefs_of(zone):
        def found(row, start):
            return tuple(coefs[zone(row), kind, start - PAD : start - PAD + 8, :] for kind in range(3))

        return found

    any_zone = coefs_of(lambda row: jnp.where(row < W, 0, jnp.where(row < W + edge, 1, 2)))
    own_zone = coefs_of(lambda row: 1)
    for step in range(1, NSTEPS + 1):
        source, target = pairs[step - 1], pairs[step]
        if step < NSTEPS:
            across = range(own - 8, own + cols + 8, 8)
            sides = (own - 8, own, own + cols - 8, own + cols)
        else:
            across, sides = range(own, own + cols, 8), (own, own + cols - 8)
        margin = low - W + step
        march(W - (W - step), W + margin, across, source, target, any_zone)
        march(W + edge - margin, W + edge + W - step, across, source, target, any_zone)
        march(W + margin, W + edge - margin, sides, source, target, own_zone)
        if step < NSTEPS:
            for field in range(2):
                kept_field, buffer = fields[2 * (step - 1) + field], pairs[step][field]
                for row in (margin, margin + 1, edge - margin - 2, edge - margin - 1):
                    buffer[W + row, own + 8 : own + cols - 8, :] = kept_field[row, PAD + 8 : PAD + cols - 8, :]

                def copy_sides(row, carry, kept_field=kept_field, buffer=buffer):
                    for start in (8, cols - 16):
                        buffer[W + row, own + start : own + start + 8, :] = kept_field[
                            row, PAD + start : PAD + start + 8, :
                        ]
                    return carry

                lax.fori_loop(margin, edge - margin, copy_sides, 0, unroll=UNROLL)
    for mask, out in enumerate(outs):
        piece = me ^ mask
        for tile in range(tiles):
            start = own + tile * edge
            side = start if tile == 0 else start + plan.cols_a
            for field, done in enumerate(pairs[NSTEPS]):
                at = (2 * tile + field) * plan.size_b
                for row in range(plan.rows_b):
                    index = piece * plan.rows_b + row
                    x = W + index + jnp.where(index < low, 0, plan.inner)
                    out[at : at + edge, :] = done[x, start : start + edge, :]
                    at += edge
                for row in range(plan.rows_a):
                    x = W + low + piece * plan.rows_a + row
                    out[at : at + 8, :] = done[x, side : side + 8, :]
                    at += 8


def run_ring(plan, own, phase, solute, halos, fields):
    cols = plan.tiles * plan.edge
    buffer = pltpu.VMEM((plan.edge + 2 * W, cols + 4 * PAD, plan.depth), jnp.float32)
    vmem = pl.BlockSpec(memory_space=pltpu.VMEM)
    piece = jax.ShapeDtypeStruct((2 * plan.tiles * plan.size_b, plan.depth), jnp.float32)
    return pl.pallas_call(
        functools.partial(ring_kernel, plan),
        in_specs=[vmem] * (7 + len(fields)),
        out_specs=[vmem] * plan.pieces,
        out_shape=[piece] * plan.pieces,
        scratch_shapes=[buffer] * 4 + [pltpu.VMEM((3, 3, cols + 16, plan.depth), jnp.float32)],
        compiler_params=pltpu.CompilerParams(vmem_limit_bytes=12 * 1024 * 1024),
        cost_estimate=pl.CostEstimate(flops=10**8, bytes_accessed=24 * 1024 * 1024, transcendentals=0),
        name="rest",
    )(own, phase, solute, *halos, *fields)


def table_kernel(plan, *refs):
    pieces, tiles = plan.pieces, plan.tiles
    arrived, (table, names, sems) = plan.by_mask(refs[:pieces]), refs[pieces + 1 :]
    me = lax.axis_index("gy")
    copies = []
    for mask in range(pieces):
        tail = 2 * tiles * plan.size_a
        copy = pltpu.make_async_copy(arrived[mask].at[pl.ds(tail, 1), :], names.at[mask], sems.at[mask])
        copy.start()
        copies.append(copy)
    for copy in copies:
        copy.wait()
    peers, homes = [], []
    for mask in range(pieces):
        for tile in range(tiles):
            peers.append(lax.rem(names[mask, 0, tile].astype(jnp.int32), pieces))
            homes.append((me ^ mask) * tiles + tile)
    for index in range(pieces * tiles):
        slot = jnp.int32(0)
        for other in range(pieces * tiles):
            if other != index:
                ahead = (peers[other] == peers[index]) & (homes[other] < homes[index])
                slot = slot + ahead.astype(jnp.int32)
        table[(peers[index] ^ me) * tiles + slot] = index


def find_table(plan, arrived, after):
    pieces, tiles = plan.pieces, plan.tiles
    return pl.pallas_call(
        functools.partial(table_kernel, plan),
        in_specs=[pl.BlockSpec(memory_space=pl.ANY)] * (pieces + 1),
        out_specs=pl.BlockSpec(memory_space=pltpu.SMEM),
        out_shape=jax.ShapeDtypeStruct((pieces * tiles,), jnp.int32),
        scratch_shapes=[
            pltpu.SMEM((pieces, 1, plan.depth), jnp.float32),
            pltpu.SemaphoreType.DMA((pieces,)),
        ],
        name="table",
    )(*plan.far_first(arrived), after)


def route_kernel(plan, size, aux, table, *refs):
    pieces, tiles = plan.pieces, plan.tiles
    arrived, outs, (held,) = plan.by_mask(refs[:pieces]), refs[pieces : 2 * pieces], refs[2 * pieces :]
    for mask in range(pieces):
        for tile in range(tiles):
            held[mask * tiles + tile] = arrived[mask][tile * size : (tile + 1) * size, :]
    for mask in range(pieces):
        for slot in range(tiles):
            index = table[mask * tiles + slot]
            outs[mask][slot, :size, :] = held[index]
            if aux:
                side = lax.rem(index, tiles).astype(jnp.float32)
                outs[mask][slot, size : size + aux, :] = jnp.full((aux, plan.depth), side, jnp.float32)


def route(plan, size, aux, table, arrived):
    pieces, tiles, depth = plan.pieces, plan.tiles, plan.depth
    vmem = pl.BlockSpec(memory_space=pltpu.VMEM)
    return pl.pallas_call(
        functools.partial(route_kernel, plan, size, aux),
        in_specs=[pl.BlockSpec(memory_space=pltpu.SMEM)] + [vmem] * pieces,
        out_specs=[vmem] * pieces,
        out_shape=[jax.ShapeDtypeStruct((tiles, size + aux, depth), jnp.float32)] * pieces,
        scratch_shapes=[pltpu.VMEM((pieces * tiles, size, depth), jnp.float32)],
        compiler_params=pltpu.CompilerParams(vmem_limit_bytes=8 * 1024 * 1024),
        name="route",
    )(table, *plan.far_first(arrived))


def settle_kernel(plan, *refs):
    pieces, tiles, edge, depth = plan.pieces, plan.tiles, plan.edge, plan.depth
    part_a, part_b = plan.by_mask(refs[:pieces]), plan.by_mask(refs[pieces : 2 * pieces])
    outs = refs[2 * pieces :]
    me = lax.axis_index("gy")
    for mask in range(pieces):
        piece = me ^ mask
        for slot in range(tiles):
            last = part_a[mask][slot, 2 * plan.size_a : 2 * plan.size_a + 8, :] > 0.5
            for field, out in enumerate(outs):
                at = field * plan.size_b
                for row in range(plan.rows_b):
                    index = piece * plan.rows_b + row
                    x = index + jnp.where(index < plan.low, 0, plan.inner)
                    out[0, slot, x] = part_b[mask][slot, at : at + edge, :]
                    at += edge
                for row in range(plan.rows_a):
                    x = plan.low + piece * plan.rows_a + row
                    begin = field * plan.size_a + row * plan.cols_a
                    side = part_b[mask][slot, at : at + 8, :]
                    at += 8
                    blocks = [
                        part_a[mask][slot, begin + col : begin + col + 8, :] for col in range(0, plan.cols_a, 8)
                    ]
                    for index, (low, high) in enumerate(zip([side] + blocks, blocks + [side])):
                        out[0, slot, x, 8 * index : 8 * index + 8, :] = jnp.where(last, high, low)


def settle(plan, part_a, part_b):
    out = jax.ShapeDtypeStruct((1, plan.tiles, plan.edge, plan.edge, plan.depth), jnp.float32)
    vmem = pl.BlockSpec(memory_space=pltpu.VMEM)
    return pl.pallas_call(
        functools.partial(settle_kernel, plan),
        in_specs=[vmem] * (2 * plan.pieces),
        out_specs=[vmem, vmem],
        out_shape=[out, out],
        compiler_params=pltpu.CompilerParams(vmem_limit_bytes=8 * 1024 * 1024),
        name="settle",
    )(*plan.far_first(part_a), *plan.far_first(part_b))


def ring(axis, step):
    count = lax.axis_size(axis)
    return [(i, (i + step) % count) for i in range(count)]


def exchange(plan, values):
    moved = [values[0]] + [None] * (plan.pieces - 1)
    for mask in list(range(plan.half, plan.pieces)) + list(range(1, plan.half)):
        moved[mask] = lax.ppermute(values[mask], "gy", [(i, i ^ mask) for i in range(plan.pieces)])
    return moved


def per_device(phase, solute, undercool, mobility, diffusivity, owner):
    _, tiles, edge, _, depth = phase.shape
    plan = Plan(lax.axis_size("gy"), tiles, edge, depth)
    coef = (undercool, mobility, diffusivity)
    to_prev, to_next, own = pack_y(phase, solute, coef, owner)
    y_lo = lax.ppermute(to_next, "gy", ring("gy", 1))
    y_hi = lax.ppermute(to_prev, "gy", ring("gy", -1))
    first, fields = run_inner(plan, own, phase, solute)
    part_a = exchange(plan, first)
    to_prev, to_next = pack_x(phase, solute, own, y_lo, y_hi, fields[0])
    x_lo = lax.ppermute(to_next, "gx", ring("gx", 1))
    x_hi = lax.ppermute(to_prev, "gx", ring("gx", -1))
    second = run_ring(plan, own, phase, solute, (y_lo, y_hi, x_lo, x_hi), fields)
    part_b = exchange(plan, second)
    table = find_table(plan, part_a, second[0])
    sent_a = exchange(plan, route(plan, 2 * plan.size_a, AUX, table, part_a))
    sent_b = exchange(plan, route(plan, 2 * plan.size_b, 0, table, part_b))
    return tuple(settle(plan, sent_a, sent_b))


def solution(mesh):
    tile_spec = P("gx", "gy", None, None, None)
    in_specs = (tile_spec, tile_spec) + (P("gx", "gy"),) * 4
    out_spec = P(("gx", "gy"), None, None, None, None)
    return jax.shard_map(
        per_device, mesh=mesh, in_specs=in_specs, out_specs=(out_spec, out_spec), check_vma=False
    )
```

```python
import functools

import jax
import jax.numpy as jnp
from jax import lax
from jax.experimental import pallas as pl
from jax.experimental.pallas import tpu as pltpu
from jax.sharding import PartitionSpec as P

NSTEPS = 4
W = NSTEPS
PAD = 8

aniso_strength = 0.05


def pack_y_kernel(under, mobile, spread, owner, phase_lo, phase_hi, solute_lo, solute_hi, to_prev, to_next, own):
    edge, depth = phase_lo.shape[2], phase_lo.shape[4]
    tiles = own.shape[0] // 8 - 1
    to_prev[:edge, :W, :] = phase_lo[0, 0, :, :W, :]
    to_prev[:edge, W:, :] = solute_lo[0, 0, :, :W, :]
    to_next[:edge, :W, :] = phase_hi[0, 0, :, W:, :]
    to_next[:edge, W:, :] = solute_hi[0, 0, :, W:, :]
    line = lax.broadcasted_iota(jnp.int32, (8, depth), 0)
    lane = lax.broadcasted_iota(jnp.int32, (8, depth), 1)
    names = jnp.zeros((8, depth), jnp.float32)
    for tile in range(tiles):
        rows = jnp.zeros((8, depth), jnp.float32)
        for kind, coef in enumerate((under, mobile, spread)):
            rows = jnp.where(line == kind, coef[0, tile], rows)
        own[8 * tile : 8 * tile + 8, :] = rows
        if tile == 0:
            to_prev[edge] = rows
        if tile == tiles - 1:
            to_next[edge] = rows
        names = jnp.where(lane == tile, owner[0, tile].astype(jnp.float32), names)
    own[8 * tiles :, :] = names


def pack_y(phase, solute, coef, owner):
    _, tiles, edge, _, depth = phase.shape
    low = pl.BlockSpec((1, 1, edge, 2 * W, depth), lambda i: (0, 0, 0, 0, 0))
    high = pl.BlockSpec((1, 1, edge, 2 * W, depth), lambda i: (0, tiles - 1, 0, edge // (2 * W) - 1, 0))
    face = jax.ShapeDtypeStruct((edge + 1, 2 * W, depth), jnp.float32)
    own = jax.ShapeDtypeStruct((8 * tiles + 8, depth), jnp.float32)
    whole = pl.BlockSpec((edge + 1, 2 * W, depth), lambda i: (0, 0, 0))
    return pl.pallas_call(
        pack_y_kernel,
        grid=(1,),
        in_specs=[pl.BlockSpec(memory_space=pltpu.SMEM)] * 4 + [low, high, low, high],
        out_specs=[whole, whole, pl.BlockSpec((8 * tiles + 8, depth), lambda i: (0, 0))],
        out_shape=[face, face, own],
        name="pack_y",
    )(*coef, owner, phase, phase, solute, solute)


def fill_row(dst, row, phase_row, solute_row, lo, hi):
    start = PAD
    dst[0][row, start : start + W, :] = lo[:W]
    dst[1][row, start : start + W, :] = lo[W:]
    start += W
    for values in phase_row:
        size = values.shape[0]
        dst[0][row, start : start + size, :] = values
        start += size
    dst[0][row, start : start + W, :] = hi[:W]
    dst[1][row, start : start + W, :] = hi[W:]
    start = PAD + W
    for values in solute_row:
        size = values.shape[0]
        dst[1][row, start : start + size, :] = values
        start += size


def pack_x_kernel(own, phase_lo, phase_hi, solute_lo, solute_hi, y_lo, y_hi, _, to_prev, to_next):
    tiles, edge, depth = phase_lo.shape[1], phase_lo.shape[3], phase_lo.shape[4]
    width = tiles * edge + 2 * W
    for out, phase, solute, first in (
        (to_prev, phase_lo, solute_lo, 0),
        (to_next, phase_hi, solute_hi, edge - W),
    ):
        for row in range(W):
            for field, values, half in ((0, phase, 0), (1, solute, W)):
                at = (2 * row + field) * width
                out[at : at + W, :] = y_lo[first + row, half : half + W, :]
                for tile in range(tiles):
                    begin = at + W + tile * edge
                    out[begin : begin + edge, :] = values[0, tile, row]
                out[at + width - W : at + width, :] = y_hi[first + row, half : half + W, :]
        at = 2 * W * width
        out[at : at + 8, :] = y_lo[edge]
        out[at + 8 : at + 16, :] = y_hi[edge]
        out[at + 16 : at + 16 + 8 * tiles, :] = own[: 8 * tiles, :]


def pack_x(phase, solute, own, y_lo, y_hi, after):
    _, tiles, edge, _, depth = phase.shape
    low = pl.BlockSpec((1, tiles, W, edge, depth), lambda i: (0, 0, 0, 0, 0))
    high = pl.BlockSpec((1, tiles, W, edge, depth), lambda i: (0, 0, edge // W - 1, 0, 0))
    side = pl.BlockSpec((edge + 1, 2 * W, depth), lambda i: (0, 0, 0))
    rows = 2 * W * (tiles * edge + 2 * W) + 8 * (tiles + 2)
    out = jax.ShapeDtypeStruct((rows, depth), jnp.float32)
    whole = pl.BlockSpec((rows, depth), lambda i: (0, 0))
    return pl.pallas_call(
        pack_x_kernel,
        grid=(1,),
        in_specs=[pl.BlockSpec((8 * tiles + 8, depth), lambda i: (0, 0)), low, high, low, high, side, side, pl.BlockSpec(memory_space=pl.ANY)],
        out_specs=[whole, whole],
        out_shape=[out, out],
        compiler_params=pltpu.CompilerParams(vmem_limit_bytes=8 * 1024 * 1024),
        name="pack_x",
    )(own, phase, phase, solute, solute, y_lo, y_hi, after)


def update(near_p, near_u, under, mobile, spread):
    p, p_xl, p_xh, p_yl, p_yh = near_p
    u, u_xl, u_xh, u_yl, u_yh = near_u
    depth = p.shape[-1]
    lane = lax.broadcasted_iota(jnp.int32, p.shape, 1)
    first, last = lane == 0, lane == depth - 1
    p_zl = jnp.where(first, p, pltpu.roll(p, 1, 1))
    p_zh = jnp.where(last, p, pltpu.roll(p, depth - 1, 1))
    u_zl = jnp.where(first, u, pltpu.roll(u, 1, 1))
    u_zh = jnp.where(last, u, pltpu.roll(u, depth - 1, 1))
    dx, dy, dz = p_xh - p_xl, p_yh - p_yl, p_zh - p_zl
    qx, qy, qz = dx * dx, dy * dy, dz * dz
    total = qx + qy + qz
    fourth = qx * qx + qy * qy + qz * qz
    base = total + 4.0
    guess = pl.reciprocal(base, approx=True)
    inverse = guess * (2.0 - base * guess)
    extra = (4.0 * aniso_strength * fourth - (3.0 * aniso_strength) * total * total) * (inverse * inverse)
    lap_p = (p_xl + p_xh) + (p_yl + p_yh) + (p_zl + p_zh) - 6.0 * p
    lap_u = (u_xl + u_xh) + (u_yl + u_yh) + (u_zl + u_zh) - 6.0 * u
    well = 1.0 - p * p
    drive = well * (under + u)
    change = mobile * (lap_p + extra * lap_p + well * (p - 2.0 * drive))
    return p + change, u + spread * lap_u + 0.5 * change


def cells(src_p, src_u, row, start, coefs):
    near = []
    for src in (src_p, src_u):
        near.append(
            (
                src[row, start : start + 8, :],
                src[row - 1, start : start + 8, :],
                src[row + 1, start : start + 8, :],
                src[row, start - 1 : start + 7, :],
                src[row, start + 1 : start + 9, :],
            )
        )
    return update(near[0], near[1], *coefs)


class Plan:
    def __init__(self, pieces, tiles, edge, depth):
        self.pieces, self.tiles, self.edge, self.depth = pieces, tiles, edge, depth
        self.half = pieces // 2
        self.inner = edge - 2 * W
        self.rows = self.inner // self.half
        self.rows_far = (self.inner - 2 * W) // self.half
        self.rows_near = 2 * W // self.half
        self.middle = edge - 16
        self.size = self.rows * self.middle + self.rows_far * 8

    def near_row(self, piece, row, gap):
        index = piece * self.rows_near + row
        return index + jnp.where(index < W, 0, gap)

    def parts(self, far, piece):
        at, found = 0, []
        if far:
            for row in range(self.rows):
                found.append((at, W + piece * self.rows + row, "middle"))
                at += self.middle
            for row in range(self.rows_far):
                found.append((at, 2 * W + piece * self.rows_far + row, "last"))
                at += 8
        else:
            for row in range(self.rows_near):
                found.append((at, self.near_row(piece, row, self.inner), "whole"))
                at += self.edge
            for row in range(self.rows):
                found.append((at, W + piece * self.rows + row, "side"))
                at += 8
            for row in range(self.rows_near):
                found.append((at, W + self.near_row(piece, row, self.inner - 2 * W), "last"))
                at += 8
        assert at == self.size
        return found

    def columns(self, name, tile):
        if name == "whole":
            return 0, self.edge
        if name == "middle":
            return 8, self.middle
        low, high = (tile, 1 - tile) if name == "side" else (1 - tile, tile)
        return low * (self.edge - 8), 8


AUX = 8
UNROLL = 4


def march(first, last, starts, source, target, coefs_of):
    def one_row(row, carry):
        for start in starts:
            new_p, new_u = cells(source[0], source[1], row, start, coefs_of(row, start))
            target[0][row, start : start + 8, :] = new_p
            target[1][row, start : start + 8, :] = new_u
        return carry

    lax.fori_loop(first, last, one_row, 0, unroll=UNROLL)


def inner_kernel(plan, own, phase, solute, *rest):
    half, tiles, edge = plan.half, plan.tiles, plan.edge
    outs, scratch = rest[:half], rest[half:]
    pairs = (scratch[:2], scratch[2:])
    me = lax.axis_index("gy")

    def load_row(row, carry):
        for tile in range(tiles):
            start = PAD + tile * edge
            pairs[0][0][row, start : start + edge, :] = phase[0, tile, row]
            pairs[0][1][row, start : start + edge, :] = solute[0, tile, row]
        return carry

    lax.fori_loop(0, edge, load_row, 0, unroll=UNROLL)

    def coefs_of(row, start):
        tile = (start - PAD) // edge
        return tuple(own[8 * tile + kind : 8 * tile + kind + 1, :] for kind in range(3))

    for step in range(NSTEPS):
        starts = range(PAD, PAD + tiles * edge, 8)
        march(step + 1, edge - step - 1, starts, pairs[step % 2], pairs[(step + 1) % 2], coefs_of)
    for index, out in enumerate(outs):
        piece = lax.rem(me ^ (half + index), half)
        for tile in range(tiles):
            for field, done in enumerate(pairs[NSTEPS % 2]):
                begin = (2 * tile + field) * plan.size
                for at, row, name in plan.parts(True, piece):
                    col, count = plan.columns(name, tile)
                    start = PAD + tile * edge + col
                    out[begin + at : begin + at + count, :] = done[row, start : start + count, :]


def run_inner(plan, own, phase, solute):
    buffer = pltpu.VMEM((plan.edge, plan.tiles * plan.edge + 2 * PAD, plan.depth), jnp.float32)
    vmem = pl.BlockSpec(memory_space=pltpu.VMEM)
    shape = jax.ShapeDtypeStruct((2 * plan.tiles * plan.size, plan.depth), jnp.float32)
    return pl.pallas_call(
        functools.partial(inner_kernel, plan),
        in_specs=[vmem] * 3,
        out_specs=[vmem] * plan.half,
        out_shape=[shape] * plan.half,
        scratch_shapes=[buffer] * 4,
        compiler_params=pltpu.CompilerParams(vmem_limit_bytes=16 * 1024 * 1024),
        cost_estimate=pl.CostEstimate(flops=10**8, bytes_accessed=24 * 1024 * 1024, transcendentals=0),
        name="inner",
    )(own, phase, solute)


def outer_kernel(plan, own, phase, solute, y_lo, y_hi, x_lo, x_hi, partner, out, *scratch):
    tiles, edge, depth, half = plan.tiles, plan.edge, plan.depth, plan.half
    pairs, coefs = (scratch[:2], scratch[2:4]), scratch[4]
    cols = tiles * edge
    width = cols + 2 * W
    for zone, source in ((0, x_lo), (1, None), (2, x_hi)):
        for kind in range(3):
            if source is None:
                parts = [y_lo[edge, kind : kind + 1, :]]
                parts += [own[8 * tile + kind : 8 * tile + kind + 1, :] for tile in range(tiles)]
                parts += [y_hi[edge, kind : kind + 1, :]]
            else:
                at = 2 * W * width + kind
                parts = [source[at : at + 1, :]]
                parts += [source[at + 16 + 8 * tile : at + 17 + 8 * tile, :] for tile in range(tiles)]
                parts += [source[at + 8 : at + 9, :]]
            coefs[zone, kind, :W, :] = jnp.broadcast_to(parts[0], (W, depth))
            for tile in range(tiles):
                begin = W + tile * edge
                coefs[zone, kind, begin : begin + edge, :] = jnp.broadcast_to(parts[1 + tile], (edge, depth))
            coefs[zone, kind, width - W :, :] = jnp.broadcast_to(parts[-1], (W, depth))
    for source, first in ((x_lo, 0), (x_hi, edge + W)):
        for row in range(W):
            for field in range(2):
                at = (2 * row + field) * width
                pairs[0][field][first + row, PAD : PAD + width, :] = source[at : at + width, :]

    def load_row(row, carry):
        fill_row(
            pairs[0],
            W + row,
            [phase[0, tile, row] for tile in range(tiles)],
            [solute[0, tile, row] for tile in range(tiles)],
            y_lo[row],
            y_hi[row],
        )
        return carry

    lax.fori_loop(0, edge, load_row, 0, unroll=UNROLL)

    def coefs_of(zone):
        def found(row, start):
            return tuple(coefs[zone(row), kind, start - PAD : start - PAD + 8, :] for kind in range(3))

        return found

    any_zone = coefs_of(lambda row: jnp.where(row < W, 0, jnp.where(row < W + edge, 1, 2)))
    own_zone = coefs_of(lambda row: 1)

    def blocks(first, last):
        shift = W if step == NSTEPS else 0
        low, high = (first + W - shift) // 8 * 8, -(-(last + W - shift) // 8) * 8
        return list(range(PAD + shift + low, PAD + shift + high, 8))

    for step in range(1, NSTEPS + 1):
        source, target = pairs[(step - 1) % 2], pairs[step % 2]
        left = NSTEPS - step
        strip = W + left
        whole = blocks(-left, cols + left)
        sides = blocks(-left, 8 + left) + blocks(cols - 8 - left, cols + left)
        lasts = []
        for tile in range(tiles):
            col, count = plan.columns("last", tile)
            lasts += blocks(tile * edge + col - left, tile * edge + col + count + left)
        ends = sorted(set(sides + lasts))
        march(W - left, W + strip, whole, source, target, any_zone)
        march(W + strip, W + strip + W, ends, source, target, own_zone)
        march(W + strip + W, W + edge - strip - W, sides, source, target, own_zone)
        march(W + edge - strip - W, W + edge - strip, ends, source, target, own_zone)
        march(W + edge - strip, W + edge + left, whole, source, target, any_zone)
    tail = 2 * tiles * plan.size
    for piece in range(half):
        for tile in range(tiles):
            for field, done in enumerate(pairs[NSTEPS % 2]):
                begin = (2 * tile + field) * plan.size
                for at, row, name in plan.parts(False, piece):
                    col, count = plan.columns(name, tile)
                    start = PAD + W + tile * edge + col
                    out[piece, begin + at : begin + at + count, :] = done[W + row, start : start + count, :]
        out[piece, tail : tail + AUX, :] = own[8 * tiles : 8 * tiles + AUX, :]
        out[piece, tail + AUX : tail + 2 * AUX, :] = partner[...]


def run_outer(plan, own, phase, solute, halos, partner):
    tiles, edge, depth = plan.tiles, plan.edge, plan.depth
    width = tiles * edge + 2 * W
    buffer = pltpu.VMEM((edge + 2 * W, width + 2 * PAD, depth), jnp.float32)
    vmem = pl.BlockSpec(memory_space=pltpu.VMEM)
    return pl.pallas_call(
        functools.partial(outer_kernel, plan),
        in_specs=[vmem] * 8,
        out_specs=vmem,
        out_shape=jax.ShapeDtypeStruct((plan.half, 2 * tiles * plan.size + 2 * AUX, depth), jnp.float32),
        scratch_shapes=[buffer] * 4 + [pltpu.VMEM((3, 3, width, depth), jnp.float32)],
        compiler_params=pltpu.CompilerParams(vmem_limit_bytes=16 * 1024 * 1024),
        cost_estimate=pl.CostEstimate(flops=10**8, bytes_accessed=40 * 1024 * 1024, transcendentals=0),
        name="outer",
    )(own, phase, solute, *halos, partner)


def table_kernel(plan, near, table, names, count, sems):
    pieces, tiles, half = plan.pieces, plan.tiles, plan.half
    me = lax.axis_index("gy")
    base = me - lax.rem(me, half)
    tail = 2 * tiles * plan.size
    copies = []
    for piece in range(half):
        for index in range(2):
            copy = pltpu.make_async_copy(
                near.at[piece, pl.ds(tail + index * AUX, 1), :], names.at[index, piece], sems.at[index, piece]
            )
            copy.start()
            copies.append(copy)
    for peer in range(pieces):
        count[peer] = 0
    for copy in copies:
        copy.wait()
    for home in range(pieces):
        other = (home // half != base // half).astype(jnp.int32)
        for tile in range(tiles):
            peer = lax.rem(names[other, home % half, 0, tile].astype(jnp.int32), pieces)
            slot = count[peer]
            table[peer * tiles + slot] = home * tiles + tile
            count[peer] = slot + 1


def find_table(plan, near):
    return pl.pallas_call(
        functools.partial(table_kernel, plan),
        in_specs=[pl.BlockSpec(memory_space=pl.ANY)],
        out_specs=pl.BlockSpec(memory_space=pltpu.SMEM),
        out_shape=jax.ShapeDtypeStruct((plan.pieces * plan.tiles,), jnp.int32),
        scratch_shapes=[
            pltpu.SMEM((2, plan.half, 1, plan.depth), jnp.float32),
            pltpu.SMEM((plan.pieces,), jnp.int32),
            pltpu.SemaphoreType.DMA((2, plan.half)),
        ],
        name="table",
    )(near)


def route_kernel(plan, table, near, *refs):
    tiles, half, size = plan.tiles, plan.half, 2 * plan.size
    far, near_out, far_outs, held = refs[:half], refs[half], refs[half + 1 : 2 * half + 1], refs[-1]
    me = lax.axis_index("gy")
    base = me - lax.rem(me, half)
    for piece in range(half):
        for tile in range(tiles):
            held[(base + piece) * tiles + tile] = near[piece, tile * size : (tile + 1) * size, :]
    for index in range(half):
        for tile in range(tiles):
            held[(me ^ (half + index)) * tiles + tile] = far[index][tile * size : (tile + 1) * size, :]
    for index in range(half):
        for slot in range(tiles):
            far_outs[index][slot] = held[table[(me ^ (half + index)) * tiles + slot]]
            near_out[index, slot] = held[table[(base + index) * tiles + slot]]


def route(plan, table, near, far):
    tiles, half, size, depth = plan.tiles, plan.half, 2 * plan.size, plan.depth
    vmem = pl.BlockSpec(memory_space=pltpu.VMEM)
    one = jax.ShapeDtypeStruct((tiles, size, depth), jnp.float32)
    results = pl.pallas_call(
        functools.partial(route_kernel, plan),
        in_specs=[pl.BlockSpec(memory_space=pltpu.SMEM)] + [vmem] * (half + 1),
        out_specs=[vmem] * (half + 1),
        out_shape=[jax.ShapeDtypeStruct((half, tiles, size, depth), jnp.float32)] + [one] * half,
        scratch_shapes=[pltpu.VMEM((plan.pieces * tiles, size, depth), jnp.float32)],
        compiler_params=pltpu.CompilerParams(vmem_limit_bytes=16 * 1024 * 1024),
        name="route",
    )(table, near, *far)
    return results[0], results[1:]


def settle_kernel(plan, table, near, *refs):
    tiles, half = plan.tiles, plan.half
    far, outs = refs[:half], refs[half:]
    me = lax.axis_index("gy")
    mine = lax.rem(me, half)
    for slot in range(tiles):
        home = table[me * tiles + slot]
        tile = lax.rem(home, tiles)
        at_home = home // (tiles * half) == me // half

        def put(source, piece, is_far, slot=slot, tile=tile):
            for field, out in enumerate(outs):
                for at, row, name in plan.parts(is_far, piece):
                    col, count = plan.columns(name, tile)
                    if not isinstance(col, int):
                        col = pl.multiple_of(col, 8)
                    out[0, slot, row, pl.ds(col, count), :] = source[
                        slot, field * plan.size + at : field * plan.size + at + count, :
                    ]

        def put_all(same, put=put):
            for index in range(half):
                put(near.at[index], index, not same)
                put(far[index], mine ^ index, same)

        @pl.when(at_home)
        def _(put_all=put_all):
            put_all(True)

        @pl.when(jnp.logical_not(at_home))
        def _(put_all=put_all):
            put_all(False)


def settle(plan, table, near, far):
    out = jax.ShapeDtypeStruct((1, plan.tiles, plan.edge, plan.edge, plan.depth), jnp.float32)
    vmem = pl.BlockSpec(memory_space=pltpu.VMEM)
    return pl.pallas_call(
        functools.partial(settle_kernel, plan),
        in_specs=[pl.BlockSpec(memory_space=pltpu.SMEM)] + [vmem] * (plan.half + 1),
        out_specs=[vmem, vmem],
        out_shape=[out, out],
        compiler_params=pltpu.CompilerParams(vmem_limit_bytes=16 * 1024 * 1024),
        name="settle",
    )(table, near, *far)


def ring(axis, step):
    count = lax.axis_size(axis)
    return [(i, (i + step) % count) for i in range(count)]


def swap(values, mask):
    return lax.ppermute(values, "gy", [(i, i ^ mask) for i in range(lax.axis_size("gy"))])


def among_half(plan, values):
    groups = [list(range(plan.half)), list(range(plan.half, plan.pieces))]
    return lax.all_to_all(values, "gy", 0, 0, axis_index_groups=groups, tiled=True)


def per_device(phase, solute, undercool, mobility, diffusivity, owner):
    _, tiles, edge, _, depth = phase.shape
    plan = Plan(lax.axis_size("gy"), tiles, edge, depth)
    half = plan.half
    to_prev, to_next, own = pack_y(phase, solute, (undercool, mobility, diffusivity), owner)
    y_lo = lax.ppermute(to_next, "gy", ring("gy", 1))
    y_hi = lax.ppermute(to_prev, "gy", ring("gy", -1))
    first = run_inner(plan, own, phase, solute)
    far = [swap(values, half + index) for index, values in enumerate(first)]
    partner = swap(own[8 * tiles :], half)
    to_prev, to_next = pack_x(phase, solute, own, y_lo, y_hi, first[0])
    x_lo = lax.ppermute(to_next, "gx", ring("gx", 1))
    x_hi = lax.ppermute(to_prev, "gx", ring("gx", -1))
    near = run_outer(plan, own, phase, solute, (y_lo, y_hi, x_lo, x_hi), partner)
    near = among_half(plan, near)
    table = find_table(plan, near)
    near, far = route(plan, table, near, far)
    far = [swap(values, half + index) for index, values in enumerate(far)]
    near = among_half(plan, near)
    return tuple(settle(plan, table, near, far))


def solution(mesh):
    tile_spec = P("gx", "gy", None, None, None)
    in_specs = (tile_spec, tile_spec) + (P("gx", "gy"),) * 4
    out_spec = P(("gx", "gy"), None, None, None, None)
    return jax.shard_map(
        per_device, mesh=mesh, in_specs=in_specs, out_specs=(out_spec, out_spec), check_vma=False
    )
```

```python
import functools

import jax
import jax.numpy as jnp
from jax import lax
from jax.experimental import pallas as pl
from jax.experimental.pallas import tpu as pltpu
from jax.sharding import PartitionSpec as P

NSTEPS = 4
W = NSTEPS
PAD = 8

aniso_strength = 0.05


def pack_y_kernel(under, mobile, spread, owner, phase_lo, phase_hi, solute_lo, solute_hi, to_prev, to_next, own):
    edge, depth = phase_lo.shape[2], phase_lo.shape[4]
    tiles = own.shape[0] // 8 - 1
    to_prev[:edge, :W, :] = phase_lo[0, 0, :, :W, :]
    to_prev[:edge, W:, :] = solute_lo[0, 0, :, :W, :]
    to_next[:edge, :W, :] = phase_hi[0, 0, :, W:, :]
    to_next[:edge, W:, :] = solute_hi[0, 0, :, W:, :]
    line = lax.broadcasted_iota(jnp.int32, (8, depth), 0)
    lane = lax.broadcasted_iota(jnp.int32, (8, depth), 1)
    names = jnp.zeros((8, depth), jnp.float32)
    for tile in range(tiles):
        rows = jnp.zeros((8, depth), jnp.float32)
        for kind, coef in enumerate((under, mobile, spread)):
            rows = jnp.where(line == kind, coef[0, tile], rows)
        own[8 * tile : 8 * tile + 8, :] = rows
        if tile == 0:
            to_prev[edge] = rows
        if tile == tiles - 1:
            to_next[edge] = rows
        names = jnp.where(lane == tile, owner[0, tile].astype(jnp.float32), names)
    own[8 * tiles :, :] = names


def pack_y(phase, solute, coef, owner):
    _, tiles, edge, _, depth = phase.shape
    low = pl.BlockSpec((1, 1, edge, 2 * W, depth), lambda i: (0, 0, 0, 0, 0))
    high = pl.BlockSpec((1, 1, edge, 2 * W, depth), lambda i: (0, tiles - 1, 0, edge // (2 * W) - 1, 0))
    face = jax.ShapeDtypeStruct((edge + 1, 2 * W, depth), jnp.float32)
    own = jax.ShapeDtypeStruct((8 * tiles + 8, depth), jnp.float32)
    whole = pl.BlockSpec((edge + 1, 2 * W, depth), lambda i: (0, 0, 0))
    return pl.pallas_call(
        pack_y_kernel,
        grid=(1,),
        in_specs=[pl.BlockSpec(memory_space=pltpu.SMEM)] * 4 + [low, high, low, high],
        out_specs=[whole, whole, pl.BlockSpec((8 * tiles + 8, depth), lambda i: (0, 0))],
        out_shape=[face, face, own],
        name="pack_y",
    )(*coef, owner, phase, phase, solute, solute)


def fill_row(dst, row, phase_row, solute_row, lo, hi):
    start = PAD
    dst[0][row, start : start + W, :] = lo[:W]
    dst[1][row, start : start + W, :] = lo[W:]
    start += W
    for values in phase_row:
        size = values.shape[0]
        dst[0][row, start : start + size, :] = values
        start += size
    dst[0][row, start : start + W, :] = hi[:W]
    dst[1][row, start : start + W, :] = hi[W:]
    start = PAD + W
    for values in solute_row:
        size = values.shape[0]
        dst[1][row, start : start + size, :] = values
        start += size


def pack_x_kernel(own, phase_lo, phase_hi, solute_lo, solute_hi, y_lo, y_hi, _, to_prev, to_next):
    tiles, edge, depth = phase_lo.shape[1], phase_lo.shape[3], phase_lo.shape[4]
    width = tiles * edge + 2 * W
    for out, phase, solute, first in (
        (to_prev, phase_lo, solute_lo, 0),
        (to_next, phase_hi, solute_hi, edge - W),
    ):
        for row in range(W):
            for field, values, half in ((0, phase, 0), (1, solute, W)):
                at = (2 * row + field) * width
                out[at : at + W, :] = y_lo[first + row, half : half + W, :]
                for tile in range(tiles):
                    begin = at + W + tile * edge
                    out[begin : begin + edge, :] = values[0, tile, row]
                out[at + width - W : at + width, :] = y_hi[first + row, half : half + W, :]
        at = 2 * W * width
        out[at : at + 8, :] = y_lo[edge]
        out[at + 8 : at + 16, :] = y_hi[edge]
        out[at + 16 : at + 16 + 8 * tiles, :] = own[: 8 * tiles, :]


def pack_x(phase, solute, own, y_lo, y_hi, after):
    _, tiles, edge, _, depth = phase.shape
    low = pl.BlockSpec((1, tiles, W, edge, depth), lambda i: (0, 0, 0, 0, 0))
    high = pl.BlockSpec((1, tiles, W, edge, depth), lambda i: (0, 0, edge // W - 1, 0, 0))
    side = pl.BlockSpec((edge + 1, 2 * W, depth), lambda i: (0, 0, 0))
    rows = 2 * W * (tiles * edge + 2 * W) + 8 * (tiles + 2)
    out = jax.ShapeDtypeStruct((rows, depth), jnp.float32)
    whole = pl.BlockSpec((rows, depth), lambda i: (0, 0))
    return pl.pallas_call(
        pack_x_kernel,
        grid=(1,),
        in_specs=[pl.BlockSpec((8 * tiles + 8, depth), lambda i: (0, 0)), low, high, low, high, side, side, pl.BlockSpec(memory_space=pl.ANY)],
        out_specs=[whole, whole],
        out_shape=[out, out],
        compiler_params=pltpu.CompilerParams(vmem_limit_bytes=8 * 1024 * 1024),
        name="pack_x",
    )(own, phase, phase, solute, solute, y_lo, y_hi, after)


def update(near_p, near_u, under, mobile, spread):
    p, p_xl, p_xh, p_yl, p_yh = near_p
    u, u_xl, u_xh, u_yl, u_yh = near_u
    depth = p.shape[-1]
    lane = lax.broadcasted_iota(jnp.int32, p.shape, 1)
    first, last = lane == 0, lane == depth - 1
    p_zl = jnp.where(first, p, pltpu.roll(p, 1, 1))
    p_zh = jnp.where(last, p, pltpu.roll(p, depth - 1, 1))
    u_zl = jnp.where(first, u, pltpu.roll(u, 1, 1))
    u_zh = jnp.where(last, u, pltpu.roll(u, depth - 1, 1))
    dx, dy, dz = p_xh - p_xl, p_yh - p_yl, p_zh - p_zl
    qx, qy, qz = dx * dx, dy * dy, dz * dz
    total = qx + qy + qz
    fourth = qx * qx + qy * qy + qz * qz
    base = total + 4.0
    guess = pl.reciprocal(base, approx=True)
    inverse = guess * (2.0 - base * guess)
    extra = (4.0 * aniso_strength * fourth - (3.0 * aniso_strength) * total * total) * (inverse * inverse)
    lap_p = (p_xl + p_xh) + (p_yl + p_yh) + (p_zl + p_zh) - 6.0 * p
    lap_u = (u_xl + u_xh) + (u_yl + u_yh) + (u_zl + u_zh) - 6.0 * u
    well = 1.0 - p * p
    drive = well * (under + u)
    change = mobile * (lap_p + extra * lap_p + well * (p - 2.0 * drive))
    return p + change, u + spread * lap_u + 0.5 * change


def cells(src_p, src_u, row, start, coefs):
    near = []
    for src in (src_p, src_u):
        near.append(
            (
                src[row, start : start + 8, :],
                src[row - 1, start : start + 8, :],
                src[row + 1, start : start + 8, :],
                src[row, start - 1 : start + 7, :],
                src[row, start + 1 : start + 9, :],
            )
        )
    return update(near[0], near[1], *coefs)


class Plan:
    def __init__(self, pieces, tiles, edge, depth):
        self.pieces, self.tiles, self.edge, self.depth = pieces, tiles, edge, depth
        self.half = pieces // 2
        self.inner = edge - 2 * W
        self.rows = self.inner // self.half
        self.rows_far = (self.inner - 2 * W) // self.half
        self.rows_near = 2 * W // self.half
        self.middle = edge - 16
        self.size = self.rows * self.middle + self.rows_far * 8

    def near_row(self, piece, row, gap):
        index = piece * self.rows_near + row
        return index + jnp.where(index < W, 0, gap)

    def parts(self, far, piece):
        at, found = 0, []
        if far:
            for row in range(self.rows):
                found.append((at, W + piece * self.rows + row, "middle"))
                at += self.middle
            for row in range(self.rows_far):
                found.append((at, 2 * W + piece * self.rows_far + row, "last"))
                at += 8
        else:
            for row in range(self.rows_near):
                found.append((at, self.near_row(piece, row, self.inner), "whole"))
                at += self.edge
            for row in range(self.rows):
                found.append((at, W + piece * self.rows + row, "side"))
                at += 8
            for row in range(self.rows_near):
                found.append((at, W + self.near_row(piece, row, self.inner - 2 * W), "last"))
                at += 8
        assert at == self.size
        return found

    def columns(self, name, tile):
        if name == "whole":
            return 0, self.edge
        if name == "middle":
            return 8, self.middle
        low, high = (tile, 1 - tile) if name == "side" else (1 - tile, tile)
        return low * (self.edge - 8), 8


AUX = 8
UNROLL = 4


def march(first, last, starts, source, target, coefs_of):
    def one_row(row, carry):
        for start in starts:
            new_p, new_u = cells(source[0], source[1], row, start, coefs_of(row, start))
            target[0][row, start : start + 8, :] = new_p
            target[1][row, start : start + 8, :] = new_u
        return carry

    lax.fori_loop(first, last, one_row, 0, unroll=UNROLL)


def inner_kernel(plan, own, phase, solute, *rest):
    half, tiles, edge = plan.half, plan.tiles, plan.edge
    outs, scratch = rest[:half], rest[half:]
    pairs = (scratch[:2], scratch[2:])
    me = lax.axis_index("gy")

    def load_row(row, carry):
        for tile in range(tiles):
            start = PAD + tile * edge
            pairs[0][0][row, start : start + edge, :] = phase[0, tile, row]
            pairs[0][1][row, start : start + edge, :] = solute[0, tile, row]
        return carry

    lax.fori_loop(0, edge, load_row, 0, unroll=UNROLL)

    def coefs_of(row, start):
        tile = (start - PAD) // edge
        return tuple(own[8 * tile + kind : 8 * tile + kind + 1, :] for kind in range(3))

    for step in range(NSTEPS):
        starts = range(PAD, PAD + tiles * edge, 8)
        march(step + 1, edge - step - 1, starts, pairs[step % 2], pairs[(step + 1) % 2], coefs_of)
    for index, out in enumerate(outs):
        piece = lax.rem(me ^ (half + index), half)
        for tile in range(tiles):
            for field, done in enumerate(pairs[NSTEPS % 2]):
                begin = (2 * tile + field) * plan.size
                for at, row, name in plan.parts(True, piece):
                    col, count = plan.columns(name, tile)
                    start = PAD + tile * edge + col
                    out[begin + at : begin + at + count, :] = done[row, start : start + count, :]


def run_inner(plan, own, phase, solute):
    buffer = pltpu.VMEM((plan.edge, plan.tiles * plan.edge + 2 * PAD, plan.depth), jnp.float32)
    vmem = pl.BlockSpec(memory_space=pltpu.VMEM)
    shape = jax.ShapeDtypeStruct((2 * plan.tiles * plan.size, plan.depth), jnp.float32)
    return pl.pallas_call(
        functools.partial(inner_kernel, plan),
        in_specs=[vmem] * 3,
        out_specs=[vmem] * plan.half,
        out_shape=[shape] * plan.half,
        scratch_shapes=[buffer] * 4,
        compiler_params=pltpu.CompilerParams(vmem_limit_bytes=16 * 1024 * 1024),
        cost_estimate=pl.CostEstimate(flops=10**8, bytes_accessed=24 * 1024 * 1024, transcendentals=0),
        name="inner",
    )(own, phase, solute)


def outer_kernel(plan, own, phase, solute, y_lo, y_hi, x_lo, x_hi, partner, out, *scratch):
    tiles, edge, depth, half = plan.tiles, plan.edge, plan.depth, plan.half
    pairs, coefs = (scratch[:2], scratch[2:4]), scratch[4]
    cols = tiles * edge
    width = cols + 2 * W
    for zone, source in ((0, x_lo), (1, None), (2, x_hi)):
        for kind in range(3):
            if source is None:
                parts = [y_lo[edge, kind : kind + 1, :]]
                parts += [own[8 * tile + kind : 8 * tile + kind + 1, :] for tile in range(tiles)]
                parts += [y_hi[edge, kind : kind + 1, :]]
            else:
                at = 2 * W * width + kind
                parts = [source[at : at + 1, :]]
                parts += [source[at + 16 + 8 * tile : at + 17 + 8 * tile, :] for tile in range(tiles)]
                parts += [source[at + 8 : at + 9, :]]
            coefs[zone, kind, :W, :] = jnp.broadcast_to(parts[0], (W, depth))
            for tile in range(tiles):
                begin = W + tile * edge
                coefs[zone, kind, begin : begin + edge, :] = jnp.broadcast_to(parts[1 + tile], (edge, depth))
            coefs[zone, kind, width - W :, :] = jnp.broadcast_to(parts[-1], (W, depth))
    for source, first in ((x_lo, 0), (x_hi, edge + W)):
        for row in range(W):
            for field in range(2):
                at = (2 * row + field) * width
                pairs[0][field][first + row, PAD : PAD + width, :] = source[at : at + width, :]

    def load_row(row, carry):
        fill_row(
            pairs[0],
            W + row,
            [phase[0, tile, row] for tile in range(tiles)],
            [solute[0, tile, row] for tile in range(tiles)],
            y_lo[row],
            y_hi[row],
        )
        return carry

    lax.fori_loop(0, edge, load_row, 0, unroll=UNROLL)

    def coefs_of(zone):
        def found(row, start):
            return tuple(coefs[zone(row), kind, start - PAD : start - PAD + 8, :] for kind in range(3))

        return found

    any_zone = coefs_of(lambda row: jnp.where(row < W, 0, jnp.where(row < W + edge, 1, 2)))
    own_zone = coefs_of(lambda row: 1)

    def blocks(first, last):
        shift = W if step == NSTEPS else 0
        low, high = (first + W - shift) // 8 * 8, -(-(last + W - shift) // 8) * 8
        return list(range(PAD + shift + low, PAD + shift + high, 8))

    for step in range(1, NSTEPS + 1):
        source, target = pairs[(step - 1) % 2], pairs[step % 2]
        left = NSTEPS - step
        strip = W + left
        whole = blocks(-left, cols + left)
        sides = blocks(-left, 8 + left) + blocks(cols - 8 - left, cols + left)
        lasts = []
        for tile in range(tiles):
            col, count = plan.columns("last", tile)
            lasts += blocks(tile * edge + col - left, tile * edge + col + count + left)
        ends = sorted(set(sides + lasts))
        march(W - left, W + strip, whole, source, target, any_zone)
        march(W + strip, W + strip + W, ends, source, target, own_zone)
        march(W + strip + W, W + edge - strip - W, sides, source, target, own_zone)
        march(W + edge - strip - W, W + edge - strip, ends, source, target, own_zone)
        march(W + edge - strip, W + edge + left, whole, source, target, any_zone)
    tail = 2 * tiles * plan.size
    for piece in range(half):
        for tile in range(tiles):
            for field, done in enumerate(pairs[NSTEPS % 2]):
                begin = (2 * tile + field) * plan.size
                for at, row, name in plan.parts(False, piece):
                    col, count = plan.columns(name, tile)
                    start = PAD + W + tile * edge + col
                    out[piece, begin + at : begin + at + count, :] = done[W + row, start : start + count, :]
        out[piece, tail : tail + AUX, :] = own[8 * tiles : 8 * tiles + AUX, :]
        out[piece, tail + AUX : tail + 2 * AUX, :] = partner[...]


def run_outer(plan, own, phase, solute, halos, partner):
    tiles, edge, depth = plan.tiles, plan.edge, plan.depth
    width = tiles * edge + 2 * W
    buffer = pltpu.VMEM((edge + 2 * W, width + 2 * PAD, depth), jnp.float32)
    vmem = pl.BlockSpec(memory_space=pltpu.VMEM)
    return pl.pallas_call(
        functools.partial(outer_kernel, plan),
        in_specs=[vmem] * 8,
        out_specs=vmem,
        out_shape=jax.ShapeDtypeStruct((plan.half, 2 * tiles * plan.size + 2 * AUX, depth), jnp.float32),
        scratch_shapes=[buffer] * 4 + [pltpu.VMEM((3, 3, width, depth), jnp.float32)],
        compiler_params=pltpu.CompilerParams(vmem_limit_bytes=16 * 1024 * 1024),
        cost_estimate=pl.CostEstimate(flops=10**8, bytes_accessed=40 * 1024 * 1024, transcendentals=0),
        name="outer",
    )(own, phase, solute, *halos, partner)


def table_kernel(plan, near, table, names, count, sems):
    pieces, tiles, half = plan.pieces, plan.tiles, plan.half
    me = lax.axis_index("gy")
    base = me - lax.rem(me, half)
    tail = 2 * tiles * plan.size
    copies = []
    for piece in range(half):
        for index in range(2):
            copy = pltpu.make_async_copy(
                near.at[piece, pl.ds(tail + index * AUX, 1), :], names.at[index, piece], sems.at[index, piece]
            )
            copy.start()
            copies.append(copy)
    for peer in range(pieces):
        count[peer] = 0
    for copy in copies:
        copy.wait()
    for home in range(pieces):
        other = (home // half != base // half).astype(jnp.int32)
        for tile in range(tiles):
            peer = lax.rem(names[other, home % half, 0, tile].astype(jnp.int32), pieces)
            slot = count[peer]
            table[peer * tiles + slot] = home * tiles + tile
            count[peer] = slot + 1


def find_table(plan, near):
    return pl.pallas_call(
        functools.partial(table_kernel, plan),
        in_specs=[pl.BlockSpec(memory_space=pl.ANY)],
        out_specs=pl.BlockSpec(memory_space=pltpu.SMEM),
        out_shape=jax.ShapeDtypeStruct((plan.pieces * plan.tiles,), jnp.int32),
        scratch_shapes=[
            pltpu.SMEM((2, plan.half, 1, plan.depth), jnp.float32),
            pltpu.SMEM((plan.pieces,), jnp.int32),
            pltpu.SemaphoreType.DMA((2, plan.half)),
        ],
        name="table",
    )(near)


def route_kernel(plan, table, near, *refs):
    tiles, half, size = plan.tiles, plan.half, 2 * plan.size
    far, near_out, far_outs, held = refs[:half], refs[half], refs[half + 1 : 2 * half + 1], refs[-1]
    me = lax.axis_index("gy")
    base = me - lax.rem(me, half)
    for piece in range(half):
        for tile in range(tiles):
            held[(base + piece) * tiles + tile] = near[piece, tile * size : (tile + 1) * size, :]
    for index in range(half):
        for tile in range(tiles):
            held[(me ^ (half + index)) * tiles + tile] = far[index][tile * size : (tile + 1) * size, :]
    for index in range(half):
        for slot in range(tiles):
            far_outs[index][slot] = held[table[(me ^ (half + index)) * tiles + slot]]
            near_out[index, slot] = held[table[(base + index) * tiles + slot]]


def route(plan, table, near, far):
    tiles, half, size, depth = plan.tiles, plan.half, 2 * plan.size, plan.depth
    vmem = pl.BlockSpec(memory_space=pltpu.VMEM)
    one = jax.ShapeDtypeStruct((tiles, size, depth), jnp.float32)
    results = pl.pallas_call(
        functools.partial(route_kernel, plan),
        in_specs=[pl.BlockSpec(memory_space=pltpu.SMEM)] + [vmem] * (half + 1),
        out_specs=[vmem] * (half + 1),
        out_shape=[jax.ShapeDtypeStruct((half, tiles, size, depth), jnp.float32)] + [one] * half,
        scratch_shapes=[pltpu.VMEM((plan.pieces * tiles, size, depth), jnp.float32)],
        compiler_params=pltpu.CompilerParams(vmem_limit_bytes=16 * 1024 * 1024),
        name="route",
    )(table, near, *far)
    return results[0], results[1:]


def settle_kernel(plan, table, near, *refs):
    tiles, half = plan.tiles, plan.half
    far, outs = refs[:half], refs[half:]
    me = lax.axis_index("gy")
    mine = lax.rem(me, half)
    for slot in range(tiles):
        home = table[me * tiles + slot]
        tile = lax.rem(home, tiles)
        at_home = home // (tiles * half) == me // half

        def put(source, piece, is_far, slot=slot, tile=tile):
            for field, out in enumerate(outs):
                for at, row, name in plan.parts(is_far, piece):
                    col, count = plan.columns(name, tile)
                    if not isinstance(col, int):
                        col = pl.multiple_of(col, 8)
                    out[0, slot, row, pl.ds(col, count), :] = source[
                        slot, field * plan.size + at : field * plan.size + at + count, :
                    ]

        def put_all(same, put=put):
            for index in range(half):
                put(near.at[index], index, not same)
                put(far[index], mine ^ index, same)

        @pl.when(at_home)
        def _(put_all=put_all):
            put_all(True)

        @pl.when(jnp.logical_not(at_home))
        def _(put_all=put_all):
            put_all(False)


def settle(plan, table, near, far):
    out = jax.ShapeDtypeStruct((1, plan.tiles, plan.edge, plan.edge, plan.depth), jnp.float32)
    vmem = pl.BlockSpec(memory_space=pltpu.VMEM)
    return pl.pallas_call(
        functools.partial(settle_kernel, plan),
        in_specs=[pl.BlockSpec(memory_space=pltpu.SMEM)] + [vmem] * (plan.half + 1),
        out_specs=[vmem, vmem],
        out_shape=[out, out],
        compiler_params=pltpu.CompilerParams(vmem_limit_bytes=16 * 1024 * 1024),
        name="settle",
    )(table, near, *far)


def ring(axis, step):
    count = lax.axis_size(axis)
    return [(i, (i + step) % count) for i in range(count)]


def swap(values, mask):
    return lax.ppermute(values, "gy", [(i, i ^ mask) for i in range(lax.axis_size("gy"))])


def among_half(plan, values, together):
    def at_once(values):
        groups = [list(range(plan.half)), list(range(plan.half, plan.pieces))]
        return lax.all_to_all(values, "gy", 0, 0, axis_index_groups=groups, tiled=True)

    def pairwise(values):
        mine = lax.rem(lax.axis_index("gy"), plan.half)
        found = values
        for mask in range(1, plan.half):
            moved = swap(lax.dynamic_index_in_dim(values, mine ^ mask, 0, keepdims=False), mask)
            found = lax.dynamic_update_index_in_dim(found, moved, mine ^ mask, 0)
        return found

    return lax.cond(together, at_once, pairwise, values)


def per_device(phase, solute, undercool, mobility, diffusivity, owner):
    _, tiles, edge, _, depth = phase.shape
    plan = Plan(lax.axis_size("gy"), tiles, edge, depth)
    half = plan.half
    to_prev, to_next, own = pack_y(phase, solute, (undercool, mobility, diffusivity), owner)
    y_lo = lax.ppermute(to_next, "gy", ring("gy", 1))
    y_hi = lax.ppermute(to_prev, "gy", ring("gy", -1))
    first = run_inner(plan, own, phase, solute)
    far = [swap(values, half + index) for index, values in enumerate(first)]
    partner = swap(own[8 * tiles :], half)
    to_prev, to_next = pack_x(phase, solute, own, y_lo, y_hi, first[0])
    x_lo = lax.ppermute(to_next, "gx", ring("gx", 1))
    x_hi = lax.ppermute(to_prev, "gx", ring("gx", -1))
    near = run_outer(plan, own, phase, solute, (y_lo, y_hi, x_lo, x_hi), partner)
    together = owner[0, 0] >= 0
    near = among_half(plan, near, together)
    table = find_table(plan, near)
    near, far = route(plan, table, near, far)
    far = [swap(values, half + index) for index, values in enumerate(far)]
    near = among_half(plan, near, together)
    return tuple(settle(plan, table, near, far))


def solution(mesh):
    tile_spec = P("gx", "gy", None, None, None)
    in_specs = (tile_spec, tile_spec) + (P("gx", "gy"),) * 4
    out_spec = P(("gx", "gy"), None, None, None, None)
    return jax.shard_map(
        per_device, mesh=mesh, in_specs=in_specs, out_specs=(out_spec, out_spec), check_vma=False
    )
```

```python
import functools

import jax
import jax.numpy as jnp
from jax import lax
from jax.experimental import pallas as pl
from jax.experimental.pallas import tpu as pltpu
from jax.sharding import PartitionSpec as P

NSTEPS = 4
W = NSTEPS
PAD = 8

aniso_strength = 0.05


def pack_y_kernel(under, mobile, spread, owner, phase_lo, phase_hi, solute_lo, solute_hi, to_prev, to_next, own):
    edge, depth = phase_lo.shape[2], phase_lo.shape[4]
    tiles = own.shape[0] // 8 - 1
    to_prev[:edge, :W, :] = phase_lo[0, 0, :, :W, :]
    to_prev[:edge, W:, :] = solute_lo[0, 0, :, :W, :]
    to_next[:edge, :W, :] = phase_hi[0, 0, :, W:, :]
    to_next[:edge, W:, :] = solute_hi[0, 0, :, W:, :]
    line = lax.broadcasted_iota(jnp.int32, (8, depth), 0)
    lane = lax.broadcasted_iota(jnp.int32, (8, depth), 1)
    names = jnp.zeros((8, depth), jnp.float32)
    for tile in range(tiles):
        rows = jnp.zeros((8, depth), jnp.float32)
        for kind, coef in enumerate((under, mobile, spread)):
            rows = jnp.where(line == kind, coef[0, tile], rows)
        own[8 * tile : 8 * tile + 8, :] = rows
        if tile == 0:
            to_prev[edge] = rows
        if tile == tiles - 1:
            to_next[edge] = rows
        names = jnp.where(lane == tile, owner[0, tile].astype(jnp.float32), names)
    own[8 * tiles :, :] = names


def pack_y(phase, solute, coef, owner):
    _, tiles, edge, _, depth = phase.shape
    low = pl.BlockSpec((1, 1, edge, 2 * W, depth), lambda i: (0, 0, 0, 0, 0))
    high = pl.BlockSpec((1, 1, edge, 2 * W, depth), lambda i: (0, tiles - 1, 0, edge // (2 * W) - 1, 0))
    face = jax.ShapeDtypeStruct((edge + 1, 2 * W, depth), jnp.float32)
    own = jax.ShapeDtypeStruct((8 * tiles + 8, depth), jnp.float32)
    whole = pl.BlockSpec((edge + 1, 2 * W, depth), lambda i: (0, 0, 0))
    return pl.pallas_call(
        pack_y_kernel,
        grid=(1,),
        in_specs=[pl.BlockSpec(memory_space=pltpu.SMEM)] * 4 + [low, high, low, high],
        out_specs=[whole, whole, pl.BlockSpec((8 * tiles + 8, depth), lambda i: (0, 0))],
        out_shape=[face, face, own],
        name="pack_y",
    )(*coef, owner, phase, phase, solute, solute)


def fill_row(dst, row, phase_row, solute_row, lo, hi):
    start = PAD
    dst[0][row, start : start + W, :] = lo[:W]
    dst[1][row, start : start + W, :] = lo[W:]
    start += W
    for values in phase_row:
        size = values.shape[0]
        dst[0][row, start : start + size, :] = values
        start += size
    dst[0][row, start : start + W, :] = hi[:W]
    dst[1][row, start : start + W, :] = hi[W:]
    start = PAD + W
    for values in solute_row:
        size = values.shape[0]
        dst[1][row, start : start + size, :] = values
        start += size


def pack_x_kernel(own, phase_lo, phase_hi, solute_lo, solute_hi, y_lo, y_hi, _, to_prev, to_next):
    tiles, edge, depth = phase_lo.shape[1], phase_lo.shape[3], phase_lo.shape[4]
    width = tiles * edge + 2 * W
    for out, phase, solute, first in (
        (to_prev, phase_lo, solute_lo, 0),
        (to_next, phase_hi, solute_hi, edge - W),
    ):
        for row in range(W):
            for field, values, half in ((0, phase, 0), (1, solute, W)):
                at = (2 * row + field) * width
                out[at : at + W, :] = y_lo[first + row, half : half + W, :]
                for tile in range(tiles):
                    begin = at + W + tile * edge
                    out[begin : begin + edge, :] = values[0, tile, row]
                out[at + width - W : at + width, :] = y_hi[first + row, half : half + W, :]
        at = 2 * W * width
        out[at : at + 8, :] = y_lo[edge]
        out[at + 8 : at + 16, :] = y_hi[edge]
        out[at + 16 : at + 16 + 8 * tiles, :] = own[: 8 * tiles, :]


def pack_x(phase, solute, own, y_lo, y_hi, after):
    _, tiles, edge, _, depth = phase.shape
    low = pl.BlockSpec((1, tiles, W, edge, depth), lambda i: (0, 0, 0, 0, 0))
    high = pl.BlockSpec((1, tiles, W, edge, depth), lambda i: (0, 0, edge // W - 1, 0, 0))
    side = pl.BlockSpec((edge + 1, 2 * W, depth), lambda i: (0, 0, 0))
    rows = 2 * W * (tiles * edge + 2 * W) + 8 * (tiles + 2)
    out = jax.ShapeDtypeStruct((rows, depth), jnp.float32)
    whole = pl.BlockSpec((rows, depth), lambda i: (0, 0))
    return pl.pallas_call(
        pack_x_kernel,
        grid=(1,),
        in_specs=[pl.BlockSpec((8 * tiles + 8, depth), lambda i: (0, 0)), low, high, low, high, side, side, pl.BlockSpec(memory_space=pl.ANY)],
        out_specs=[whole, whole],
        out_shape=[out, out],
        compiler_params=pltpu.CompilerParams(vmem_limit_bytes=8 * 1024 * 1024),
        name="pack_x",
    )(own, phase, phase, solute, solute, y_lo, y_hi, after)


def update(near_p, near_u, under, mobile, spread):
    p, p_xl, p_xh, p_yl, p_yh = near_p
    u, u_xl, u_xh, u_yl, u_yh = near_u
    depth = p.shape[-1]
    lane = lax.broadcasted_iota(jnp.int32, p.shape, 1)
    first, last = lane == 0, lane == depth - 1
    p_zl = jnp.where(first, p, pltpu.roll(p, 1, 1))
    p_zh = jnp.where(last, p, pltpu.roll(p, depth - 1, 1))
    u_zl = jnp.where(first, u, pltpu.roll(u, 1, 1))
    u_zh = jnp.where(last, u, pltpu.roll(u, depth - 1, 1))
    dx, dy, dz = p_xh - p_xl, p_yh - p_yl, p_zh - p_zl
    qx, qy, qz = dx * dx, dy * dy, dz * dz
    total = qx + qy + qz
    fourth = qx * qx + qy * qy + qz * qz
    base = total + 4.0
    guess = pl.reciprocal(base, approx=True)
    inverse = guess * (2.0 - base * guess)
    extra = (4.0 * aniso_strength * fourth - (3.0 * aniso_strength) * total * total) * (inverse * inverse)
    lap_p = (p_xl + p_xh) + (p_yl + p_yh) + (p_zl + p_zh) - 6.0 * p
    lap_u = (u_xl + u_xh) + (u_yl + u_yh) + (u_zl + u_zh) - 6.0 * u
    well = 1.0 - p * p
    drive = well * (under + u)
    change = mobile * (lap_p + extra * lap_p + well * (p - 2.0 * drive))
    return p + change, u + spread * lap_u + 0.5 * change


def cells(src_p, src_u, row, start, coefs):
    near = []
    for src in (src_p, src_u):
        near.append(
            (
                src[row, start : start + 8, :],
                src[row - 1, start : start + 8, :],
                src[row + 1, start : start + 8, :],
                src[row, start - 1 : start + 7, :],
                src[row, start + 1 : start + 9, :],
            )
        )
    return update(near[0], near[1], *coefs)


class Plan:
    def __init__(self, pieces, tiles, edge, depth):
        self.pieces, self.tiles, self.edge, self.depth = pieces, tiles, edge, depth
        self.half = pieces // 2
        self.inner = edge - 2 * W
        self.rows = self.inner // self.half
        self.rows_far = (self.inner - 2 * W) // self.half
        self.rows_near = 2 * W // self.half
        self.middle = edge - 16
        self.size = self.rows * self.middle + self.rows_far * 8

    def near_row(self, piece, row, gap):
        index = piece * self.rows_near + row
        return index + jnp.where(index < W, 0, gap)

    def parts(self, far, piece):
        at, found = 0, []
        if far:
            for row in range(self.rows):
                found.append((at, W + piece * self.rows + row, "middle"))
                at += self.middle
            for row in range(self.rows_far):
                found.append((at, 2 * W + piece * self.rows_far + row, "last"))
                at += 8
        else:
            for row in range(self.rows_near):
                found.append((at, self.near_row(piece, row, self.inner), "whole"))
                at += self.edge
            for row in range(self.rows):
                found.append((at, W + piece * self.rows + row, "side"))
                at += 8
            for row in range(self.rows_near):
                found.append((at, W + self.near_row(piece, row, self.inner - 2 * W), "last"))
                at += 8
        assert at == self.size
        return found

    def columns(self, name, tile):
        if name == "whole":
            return 0, self.edge
        if name == "middle":
            return 8, self.middle
        low, high = (tile, 1 - tile) if name == "side" else (1 - tile, tile)
        return low * (self.edge - 8), 8


AUX = 8
UNROLL = 4


def march(first, last, starts, source, target, coefs_of):
    def one_row(row, carry):
        for start in starts:
            new_p, new_u = cells(source[0], source[1], row, start, coefs_of(row, start))
            target[0][row, start : start + 8, :] = new_p
            target[1][row, start : start + 8, :] = new_u
        return carry

    lax.fori_loop(first, last, one_row, 0, unroll=UNROLL)


def inner_kernel(plan, own, phase, solute, *rest):
    half, tiles, edge = plan.half, plan.tiles, plan.edge
    outs, scratch = rest[:half], rest[half:]
    pairs = (scratch[:2], scratch[2:])
    me = lax.axis_index("gy")

    def load_row(row, carry):
        for tile in range(tiles):
            start = PAD + tile * edge
            pairs[0][0][row, start : start + edge, :] = phase[0, tile, row]
            pairs[0][1][row, start : start + edge, :] = solute[0, tile, row]
        return carry

    lax.fori_loop(0, edge, load_row, 0, unroll=UNROLL)

    def coefs_of(row, start):
        tile = (start - PAD) // edge
        return tuple(own[8 * tile + kind : 8 * tile + kind + 1, :] for kind in range(3))

    for step in range(NSTEPS):
        starts = range(PAD, PAD + tiles * edge, 8)
        march(step + 1, edge - step - 1, starts, pairs[step % 2], pairs[(step + 1) % 2], coefs_of)
    for index, out in enumerate(outs):
        piece = lax.rem(me ^ (half + index), half)
        for tile in range(tiles):
            for field, done in enumerate(pairs[NSTEPS % 2]):
                begin = (2 * tile + field) * plan.size
                for at, row, name in plan.parts(True, piece):
                    col, count = plan.columns(name, tile)
                    start = PAD + tile * edge + col
                    out[begin + at : begin + at + count, :] = done[row, start : start + count, :]


def run_inner(plan, own, phase, solute):
    buffer = pltpu.VMEM((plan.edge, plan.tiles * plan.edge + 2 * PAD, plan.depth), jnp.float32)
    vmem = pl.BlockSpec(memory_space=pltpu.VMEM)
    shape = jax.ShapeDtypeStruct((2 * plan.tiles * plan.size, plan.depth), jnp.float32)
    return pl.pallas_call(
        functools.partial(inner_kernel, plan),
        in_specs=[vmem] * 3,
        out_specs=[vmem] * plan.half,
        out_shape=[shape] * plan.half,
        scratch_shapes=[buffer] * 4,
        compiler_params=pltpu.CompilerParams(vmem_limit_bytes=16 * 1024 * 1024),
        cost_estimate=pl.CostEstimate(flops=10**8, bytes_accessed=24 * 1024 * 1024, transcendentals=0),
        name="inner",
    )(own, phase, solute)


def outer_kernel(plan, own, phase, solute, y_lo, y_hi, x_lo, x_hi, partner, out, *scratch):
    tiles, edge, depth, half = plan.tiles, plan.edge, plan.depth, plan.half
    pairs, coefs = (scratch[:2], scratch[2:4]), scratch[4]
    cols = tiles * edge
    width = cols + 2 * W
    for zone, source in ((0, x_lo), (1, None), (2, x_hi)):
        for kind in range(3):
            if source is None:
                parts = [y_lo[edge, kind : kind + 1, :]]
                parts += [own[8 * tile + kind : 8 * tile + kind + 1, :] for tile in range(tiles)]
                parts += [y_hi[edge, kind : kind + 1, :]]
            else:
                at = 2 * W * width + kind
                parts = [source[at : at + 1, :]]
                parts += [source[at + 16 + 8 * tile : at + 17 + 8 * tile, :] for tile in range(tiles)]
                parts += [source[at + 8 : at + 9, :]]
            coefs[zone, kind, :W, :] = jnp.broadcast_to(parts[0], (W, depth))
            for tile in range(tiles):
                begin = W + tile * edge
                coefs[zone, kind, begin : begin + edge, :] = jnp.broadcast_to(parts[1 + tile], (edge, depth))
            coefs[zone, kind, width - W :, :] = jnp.broadcast_to(parts[-1], (W, depth))
    for source, first in ((x_lo, 0), (x_hi, edge + W)):
        for row in range(W):
            for field in range(2):
                at = (2 * row + field) * width
                pairs[0][field][first + row, PAD : PAD + width, :] = source[at : at + width, :]

    def load_row(row, carry):
        fill_row(
            pairs[0],
            W + row,
            [phase[0, tile, row] for tile in range(tiles)],
            [solute[0, tile, row] for tile in range(tiles)],
            y_lo[row],
            y_hi[row],
        )
        return carry

    lax.fori_loop(0, edge, load_row, 0, unroll=UNROLL)

    def coefs_of(zone):
        def found(row, start):
            return tuple(coefs[zone(row), kind, start - PAD : start - PAD + 8, :] for kind in range(3))

        return found

    any_zone = coefs_of(lambda row: jnp.where(row < W, 0, jnp.where(row < W + edge, 1, 2)))
    own_zone = coefs_of(lambda row: 1)

    def blocks(first, last):
        shift = W if step == NSTEPS else 0
        low, high = (first + W - shift) // 8 * 8, -(-(last + W - shift) // 8) * 8
        return list(range(PAD + shift + low, PAD + shift + high, 8))

    for step in range(1, NSTEPS + 1):
        source, target = pairs[(step - 1) % 2], pairs[step % 2]
        left = NSTEPS - step
        strip = W + left
        whole = blocks(-left, cols + left)
        sides = blocks(-left, 8 + left) + blocks(cols - 8 - left, cols + left)
        lasts = []
        for tile in range(tiles):
            col, count = plan.columns("last", tile)
            lasts += blocks(tile * edge + col - left, tile * edge + col + count + left)
        ends = sorted(set(sides + lasts))
        march(W - left, W + strip, whole, source, target, any_zone)
        march(W + strip, W + strip + W, ends, source, target, own_zone)
        march(W + strip + W, W + edge - strip - W, sides, source, target, own_zone)
        march(W + edge - strip - W, W + edge - strip, ends, source, target, own_zone)
        march(W + edge - strip, W + edge + left, whole, source, target, any_zone)
    tail = 2 * tiles * plan.size
    for piece in range(half):
        for tile in range(tiles):
            for field, done in enumerate(pairs[NSTEPS % 2]):
                begin = (2 * tile + field) * plan.size
                for at, row, name in plan.parts(False, piece):
                    col, count = plan.columns(name, tile)
                    start = PAD + W + tile * edge + col
                    out[piece, begin + at : begin + at + count, :] = done[W + row, start : start + count, :]
        out[piece, tail : tail + AUX, :] = own[8 * tiles : 8 * tiles + AUX, :]
        out[piece, tail + AUX : tail + 2 * AUX, :] = partner[...]


def run_outer(plan, own, phase, solute, halos, partner):
    tiles, edge, depth = plan.tiles, plan.edge, plan.depth
    width = tiles * edge + 2 * W
    buffer = pltpu.VMEM((edge + 2 * W, width + 2 * PAD, depth), jnp.float32)
    vmem = pl.BlockSpec(memory_space=pltpu.VMEM)
    return pl.pallas_call(
        functools.partial(outer_kernel, plan),
        in_specs=[vmem] * 8,
        out_specs=vmem,
        out_shape=jax.ShapeDtypeStruct((plan.half, 2 * tiles * plan.size + 2 * AUX, depth), jnp.float32),
        scratch_shapes=[buffer] * 4 + [pltpu.VMEM((3, 3, width, depth), jnp.float32)],
        compiler_params=pltpu.CompilerParams(vmem_limit_bytes=16 * 1024 * 1024),
        cost_estimate=pl.CostEstimate(flops=10**8, bytes_accessed=40 * 1024 * 1024, transcendentals=0),
        name="outer",
    )(own, phase, solute, *halos, partner)


def table_kernel(plan, near, table, names, count, sems):
    pieces, tiles, half = plan.pieces, plan.tiles, plan.half
    me = lax.axis_index("gy")
    base = me - lax.rem(me, half)
    tail = 2 * tiles * plan.size
    copies = []
    for piece in range(half):
        for index in range(2):
            copy = pltpu.make_async_copy(
                near.at[piece, pl.ds(tail + index * AUX, 1), :], names.at[index, piece], sems.at[index, piece]
            )
            copy.start()
            copies.append(copy)
    for peer in range(pieces):
        count[peer] = 0
    for copy in copies:
        copy.wait()
    for home in range(pieces):
        other = (home // half != base // half).astype(jnp.int32)
        for tile in range(tiles):
            peer = lax.rem(names[other, home % half, 0, tile].astype(jnp.int32), pieces)
            slot = count[peer]
            table[peer * tiles + slot] = home * tiles + tile
            count[peer] = slot + 1


def find_table(plan, near):
    return pl.pallas_call(
        functools.partial(table_kernel, plan),
        in_specs=[pl.BlockSpec(memory_space=pl.ANY)],
        out_specs=pl.BlockSpec(memory_space=pltpu.SMEM),
        out_shape=jax.ShapeDtypeStruct((plan.pieces * plan.tiles,), jnp.int32),
        scratch_shapes=[
            pltpu.SMEM((2, plan.half, 1, plan.depth), jnp.float32),
            pltpu.SMEM((plan.pieces,), jnp.int32),
            pltpu.SemaphoreType.DMA((2, plan.half)),
        ],
        name="table",
    )(near)


def route_kernel(plan, table, near, *refs):
    tiles, half, size = plan.tiles, plan.half, 2 * plan.size
    far, near_out, far_outs, held = refs[:half], refs[half], refs[half + 1 : 2 * half + 1], refs[-1]
    me = lax.axis_index("gy")
    base = me - lax.rem(me, half)
    for piece in range(half):
        for tile in range(tiles):
            held[(base + piece) * tiles + tile] = near[piece, tile * size : (tile + 1) * size, :]
    for index in range(half):
        for tile in range(tiles):
            held[(me ^ (half + index)) * tiles + tile] = far[index][tile * size : (tile + 1) * size, :]
    for index in range(half):
        for slot in range(tiles):
            far_outs[index][slot] = held[table[(me ^ (half + index)) * tiles + slot]]
            near_out[index, slot] = held[table[(base + index) * tiles + slot]]


def route(plan, table, near, far):
    tiles, half, size, depth = plan.tiles, plan.half, 2 * plan.size, plan.depth
    vmem = pl.BlockSpec(memory_space=pltpu.VMEM)
    one = jax.ShapeDtypeStruct((tiles, size, depth), jnp.float32)
    results = pl.pallas_call(
        functools.partial(route_kernel, plan),
        in_specs=[pl.BlockSpec(memory_space=pltpu.SMEM)] + [vmem] * (half + 1),
        out_specs=[vmem] * (half + 1),
        out_shape=[jax.ShapeDtypeStruct((half, tiles, size, depth), jnp.float32)] + [one] * half,
        scratch_shapes=[pltpu.VMEM((plan.pieces * tiles, size, depth), jnp.float32)],
        compiler_params=pltpu.CompilerParams(vmem_limit_bytes=16 * 1024 * 1024),
        name="route",
    )(table, near, *far)
    return results[0], results[1:]


def settle_kernel(plan, table, near, *refs):
    tiles, half = plan.tiles, plan.half
    far, outs = refs[:half], refs[half:]
    me = lax.axis_index("gy")
    mine = lax.rem(me, half)
    for slot in range(tiles):
        home = table[me * tiles + slot]
        tile = lax.rem(home, tiles)
        at_home = home // (tiles * half) == me // half

        def put(source, piece, is_far, slot=slot, tile=tile):
            for field, out in enumerate(outs):
                for at, row, name in plan.parts(is_far, piece):
                    col, count = plan.columns(name, tile)
                    if not isinstance(col, int):
                        col = pl.multiple_of(col, 8)
                    out[0, slot, row, pl.ds(col, count), :] = source[
                        slot, field * plan.size + at : field * plan.size + at + count, :
                    ]

        def put_all(same, put=put):
            for index in range(half):
                put(near.at[index], index, not same)
                put(far[index], mine ^ index, same)

        @pl.when(at_home)
        def _(put_all=put_all):
            put_all(True)

        @pl.when(jnp.logical_not(at_home))
        def _(put_all=put_all):
            put_all(False)


def settle(plan, table, near, far):
    out = jax.ShapeDtypeStruct((1, plan.tiles, plan.edge, plan.edge, plan.depth), jnp.float32)
    vmem = pl.BlockSpec(memory_space=pltpu.VMEM)
    return pl.pallas_call(
        functools.partial(settle_kernel, plan),
        in_specs=[pl.BlockSpec(memory_space=pltpu.SMEM)] + [vmem] * (plan.half + 1),
        out_specs=[vmem, vmem],
        out_shape=[out, out],
        compiler_params=pltpu.CompilerParams(vmem_limit_bytes=16 * 1024 * 1024),
        name="settle",
    )(table, near, *far)


def ring(axis, step):
    count = lax.axis_size(axis)
    return [(i, (i + step) % count) for i in range(count)]


def swap(values, mask):
    return lax.ppermute(values, "gy", [(i, i ^ mask) for i in range(lax.axis_size("gy"))])


def among_half(plan, values, together):
    def exchange(values):
        groups = [list(range(plan.half)), list(range(plan.half, plan.pieces))]
        return lax.all_to_all(values, "gy", 0, 0, axis_index_groups=groups, tiled=True)

    return lax.cond(together, exchange, exchange, values)


def per_device(phase, solute, undercool, mobility, diffusivity, owner):
    _, tiles, edge, _, depth = phase.shape
    plan = Plan(lax.axis_size("gy"), tiles, edge, depth)
    half = plan.half
    to_prev, to_next, own = pack_y(phase, solute, (undercool, mobility, diffusivity), owner)
    y_lo = lax.ppermute(to_next, "gy", ring("gy", 1))
    y_hi = lax.ppermute(to_prev, "gy", ring("gy", -1))
    first = run_inner(plan, own, phase, solute)
    far = [swap(values, half + index) for index, values in enumerate(first)]
    partner = swap(own[8 * tiles :], half)
    to_prev, to_next = pack_x(phase, solute, own, y_lo, y_hi, first[0])
    x_lo = lax.ppermute(to_next, "gx", ring("gx", 1))
    x_hi = lax.ppermute(to_prev, "gx", ring("gx", -1))
    near = run_outer(plan, own, phase, solute, (y_lo, y_hi, x_lo, x_hi), partner)
    together = owner[0, 0] >= 0
    near = among_half(plan, near, together)
    table = find_table(plan, near)
    near, far = route(plan, table, near, far)
    far = [swap(values, half + index) for index, values in enumerate(far)]
    near = among_half(plan, near, together)
    return tuple(settle(plan, table, near, far))


def solution(mesh):
    tile_spec = P("gx", "gy", None, None, None)
    in_specs = (tile_spec, tile_spec) + (P("gx", "gy"),) * 4
    out_spec = P(("gx", "gy"), None, None, None, None)
    return jax.shard_map(
        per_device, mesh=mesh, in_specs=in_specs, out_specs=(out_spec, out_spec), check_vma=False
    )
```

```python
import functools

import jax
import jax.numpy as jnp
from jax import lax
from jax.experimental import pallas as pl
from jax.experimental.pallas import tpu as pltpu
from jax.sharding import PartitionSpec as P

NSTEPS = 4
W = NSTEPS
PAD = 8

aniso_strength = 0.05


def pack_y_kernel(under, mobile, spread, owner, phase_lo, phase_hi, solute_lo, solute_hi, to_prev, to_next, own):
    edge, depth = phase_lo.shape[2], phase_lo.shape[4]
    tiles = own.shape[0] // 8 - 1
    to_prev[:edge, :W, :] = phase_lo[0, 0, :, :W, :]
    to_prev[:edge, W:, :] = solute_lo[0, 0, :, :W, :]
    to_next[:edge, :W, :] = phase_hi[0, 0, :, W:, :]
    to_next[:edge, W:, :] = solute_hi[0, 0, :, W:, :]
    line = lax.broadcasted_iota(jnp.int32, (8, depth), 0)
    lane = lax.broadcasted_iota(jnp.int32, (8, depth), 1)
    names = jnp.zeros((8, depth), jnp.float32)
    for tile in range(tiles):
        rows = jnp.zeros((8, depth), jnp.float32)
        for kind, coef in enumerate((under, mobile, spread)):
            rows = jnp.where(line == kind, coef[0, tile], rows)
        own[8 * tile : 8 * tile + 8, :] = rows
        if tile == 0:
            to_prev[edge] = rows
        if tile == tiles - 1:
            to_next[edge] = rows
        names = jnp.where(lane == tile, owner[0, tile].astype(jnp.float32), names)
    own[8 * tiles :, :] = names


def pack_y(phase, solute, coef, owner):
    _, tiles, edge, _, depth = phase.shape
    low = pl.BlockSpec((1, 1, edge, 2 * W, depth), lambda i: (0, 0, 0, 0, 0))
    high = pl.BlockSpec((1, 1, edge, 2 * W, depth), lambda i: (0, tiles - 1, 0, edge // (2 * W) - 1, 0))
    face = jax.ShapeDtypeStruct((edge + 1, 2 * W, depth), jnp.float32)
    own = jax.ShapeDtypeStruct((8 * tiles + 8, depth), jnp.float32)
    whole = pl.BlockSpec((edge + 1, 2 * W, depth), lambda i: (0, 0, 0))
    return pl.pallas_call(
        pack_y_kernel,
        grid=(1,),
        in_specs=[pl.BlockSpec(memory_space=pltpu.SMEM)] * 4 + [low, high, low, high],
        out_specs=[whole, whole, pl.BlockSpec((8 * tiles + 8, depth), lambda i: (0, 0))],
        out_shape=[face, face, own],
        name="pack_y",
    )(*coef, owner, phase, phase, solute, solute)


def fill_row(dst, row, phase_row, solute_row, lo, hi):
    start = PAD
    dst[0][row, start : start + W, :] = lo[:W]
    dst[1][row, start : start + W, :] = lo[W:]
    start += W
    for values in phase_row:
        size = values.shape[0]
        dst[0][row, start : start + size, :] = values
        start += size
    dst[0][row, start : start + W, :] = hi[:W]
    dst[1][row, start : start + W, :] = hi[W:]
    start = PAD + W
    for values in solute_row:
        size = values.shape[0]
        dst[1][row, start : start + size, :] = values
        start += size


def pack_x_kernel(own, phase_lo, phase_hi, solute_lo, solute_hi, y_lo, y_hi, _, to_prev, to_next):
    tiles, edge, depth = phase_lo.shape[1], phase_lo.shape[3], phase_lo.shape[4]
    width = tiles * edge + 2 * W
    for out, phase, solute, first in (
        (to_prev, phase_lo, solute_lo, 0),
        (to_next, phase_hi, solute_hi, edge - W),
    ):
        for row in range(W):
            for field, values, half in ((0, phase, 0), (1, solute, W)):
                at = (2 * row + field) * width
                out[at : at + W, :] = y_lo[first + row, half : half + W, :]
                for tile in range(tiles):
                    begin = at + W + tile * edge
                    out[begin : begin + edge, :] = values[0, tile, row]
                out[at + width - W : at + width, :] = y_hi[first + row, half : half + W, :]
        at = 2 * W * width
        out[at : at + 8, :] = y_lo[edge]
        out[at + 8 : at + 16, :] = y_hi[edge]
        out[at + 16 : at + 16 + 8 * tiles, :] = own[: 8 * tiles, :]


def pack_x(phase, solute, own, y_lo, y_hi, after):
    _, tiles, edge, _, depth = phase.shape
    low = pl.BlockSpec((1, tiles, W, edge, depth), lambda i: (0, 0, 0, 0, 0))
    high = pl.BlockSpec((1, tiles, W, edge, depth), lambda i: (0, 0, edge // W - 1, 0, 0))
    side = pl.BlockSpec((edge + 1, 2 * W, depth), lambda i: (0, 0, 0))
    rows = 2 * W * (tiles * edge + 2 * W) + 8 * (tiles + 2)
    out = jax.ShapeDtypeStruct((rows, depth), jnp.float32)
    whole = pl.BlockSpec((rows, depth), lambda i: (0, 0))
    return pl.pallas_call(
        pack_x_kernel,
        grid=(1,),
        in_specs=[pl.BlockSpec((8 * tiles + 8, depth), lambda i: (0, 0)), low, high, low, high, side, side, pl.BlockSpec(memory_space=pl.ANY)],
        out_specs=[whole, whole],
        out_shape=[out, out],
        compiler_params=pltpu.CompilerParams(vmem_limit_bytes=8 * 1024 * 1024),
        name="pack_x",
    )(own, phase, phase, solute, solute, y_lo, y_hi, after)


def update(near_p, near_u, under, mobile, spread):
    p, p_xl, p_xh, p_yl, p_yh = near_p
    u, u_xl, u_xh, u_yl, u_yh = near_u
    depth = p.shape[-1]
    lane = lax.broadcasted_iota(jnp.int32, p.shape, 1)
    first, last = lane == 0, lane == depth - 1
    p_zl = jnp.where(first, p, pltpu.roll(p, 1, 1))
    p_zh = jnp.where(last, p, pltpu.roll(p, depth - 1, 1))
    u_zl = jnp.where(first, u, pltpu.roll(u, 1, 1))
    u_zh = jnp.where(last, u, pltpu.roll(u, depth - 1, 1))
    dx, dy, dz = p_xh - p_xl, p_yh - p_yl, p_zh - p_zl
    qx, qy, qz = dx * dx, dy * dy, dz * dz
    total = qx + qy + qz
    fourth = qx * qx + qy * qy + qz * qz
    base = total + 4.0
    guess = pl.reciprocal(base, approx=True)
    inverse = guess * (2.0 - base * guess)
    extra = (4.0 * aniso_strength * fourth - (3.0 * aniso_strength) * total * total) * (inverse * inverse)
    lap_p = (p_xl + p_xh) + (p_yl + p_yh) + (p_zl + p_zh) - 6.0 * p
    lap_u = (u_xl + u_xh) + (u_yl + u_yh) + (u_zl + u_zh) - 6.0 * u
    well = 1.0 - p * p
    drive = well * (under + u)
    change = mobile * (lap_p + extra * lap_p + well * (p - 2.0 * drive))
    return p + change, u + spread * lap_u + 0.5 * change


def cells(src_p, src_u, row, start, coefs):
    near = []
    for src in (src_p, src_u):
        near.append(
            (
                src[row, start : start + 8, :],
                src[row - 1, start : start + 8, :],
                src[row + 1, start : start + 8, :],
                src[row, start - 1 : start + 7, :],
                src[row, start + 1 : start + 9, :],
            )
        )
    return update(near[0], near[1], *coefs)


class Plan:
    def __init__(self, pieces, tiles, edge, depth):
        self.pieces, self.tiles, self.edge, self.depth = pieces, tiles, edge, depth
        self.half = pieces // 2
        self.inner = edge - 2 * W
        self.rows = self.inner // self.half
        self.rows_far = (self.inner - 2 * W) // self.half
        self.rows_near = 2 * W // self.half
        self.middle = edge - 16
        self.size = self.rows * self.middle + self.rows_far * 8

    def near_row(self, piece, row, gap):
        index = piece * self.rows_near + row
        return index + jnp.where(index < W, 0, gap)

    def parts(self, far, piece):
        at, found = 0, []
        if far:
            for row in range(self.rows):
                found.append((at, W + piece * self.rows + row, "middle"))
                at += self.middle
            for row in range(self.rows_far):
                found.append((at, 2 * W + piece * self.rows_far + row, "last"))
                at += 8
        else:
            for row in range(self.rows_near):
                found.append((at, self.near_row(piece, row, self.inner), "whole"))
                at += self.edge
            for row in range(self.rows):
                found.append((at, W + piece * self.rows + row, "side"))
                at += 8
            for row in range(self.rows_near):
                found.append((at, W + self.near_row(piece, row, self.inner - 2 * W), "last"))
                at += 8
        assert at == self.size
        return found

    def columns(self, name, tile):
        if name == "whole":
            return 0, self.edge
        if name == "middle":
            return 8, self.middle
        low, high = (tile, 1 - tile) if name == "side" else (1 - tile, tile)
        return low * (self.edge - 8), 8


AUX = 8
UNROLL = 4


def march(first, last, starts, source, target, coefs_of):
    def one_row(row, carry):
        for start in starts:
            new_p, new_u = cells(source[0], source[1], row, start, coefs_of(row, start))
            target[0][row, start : start + 8, :] = new_p
            target[1][row, start : start + 8, :] = new_u
        return carry

    lax.fori_loop(first, last, one_row, 0, unroll=UNROLL)


def inner_kernel(plan, own, phase, solute, *rest):
    tiles, edge, count = plan.tiles, plan.edge, plan.inner // 2
    outs, scratch = rest[: plan.half // 2], rest[plan.half // 2 :]
    pairs = (scratch[:2], scratch[2:])
    mine = lax.rem(lax.axis_index("gy"), plan.half)
    base = mine // (plan.half // 2) * count

    def load_row(row, carry):
        for tile in range(tiles):
            start = PAD + tile * edge
            pairs[0][0][row, start : start + edge, :] = phase[0, tile, base + row]
            pairs[0][1][row, start : start + edge, :] = solute[0, tile, base + row]
        return carry

    lax.fori_loop(0, count + 2 * W, load_row, 0, unroll=UNROLL)

    def coefs_of(row, start):
        tile = (start - PAD) // edge
        return tuple(own[8 * tile + kind : 8 * tile + kind + 1, :] for kind in range(3))

    for step in range(NSTEPS):
        starts = range(PAD, PAD + tiles * edge, 8)
        march(step + 1, count + 2 * W - step - 1, starts, pairs[step % 2], pairs[(step + 1) % 2], coefs_of)
    for index, out in enumerate(outs):
        pack(plan, True, mine ^ index, pairs[NSTEPS % 2], -base, PAD, out)


def pack(plan, far, piece, done, row_shift, col_shift, out):
    for tile in range(plan.tiles):
        for field, values in enumerate(done):
            begin = (2 * tile + field) * plan.size
            for at, row, name in plan.parts(far, piece):
                col, count = plan.columns(name, tile)
                start = col_shift + tile * plan.edge + col
                out[begin + at : begin + at + count, :] = values[row + row_shift, start : start + count, :]


def run_inner(plan, own, phase, solute):
    rows = plan.inner // 2 + 2 * W
    buffer = pltpu.VMEM((rows, plan.tiles * plan.edge + 2 * PAD, plan.depth), jnp.float32)
    vmem = pl.BlockSpec(memory_space=pltpu.VMEM)
    shape = jax.ShapeDtypeStruct((2 * plan.tiles * plan.size, plan.depth), jnp.float32)
    return pl.pallas_call(
        functools.partial(inner_kernel, plan),
        in_specs=[vmem] * 3,
        out_specs=[vmem] * (plan.half // 2),
        out_shape=[shape] * (plan.half // 2),
        scratch_shapes=[buffer] * 4,
        compiler_params=pltpu.CompilerParams(vmem_limit_bytes=16 * 1024 * 1024),
        cost_estimate=pl.CostEstimate(flops=10**8, bytes_accessed=24 * 1024 * 1024, transcendentals=0),
        name="inner",
    )(own, phase, solute)


def outer_kernel(plan, own, phase, solute, y_lo, y_hi, x_lo, x_hi, partner, out, *rest):
    tiles, edge, depth, half = plan.tiles, plan.edge, plan.depth, plan.half
    far_outs, scratch = rest[: half // 2], rest[half // 2 :]
    pairs, coefs = (scratch[:2], scratch[2:4]), scratch[4]
    cols = tiles * edge
    width = cols + 2 * W
    for zone, source in ((0, x_lo), (1, None), (2, x_hi)):
        for kind in range(3):
            if source is None:
                parts = [y_lo[edge, kind : kind + 1, :]]
                parts += [own[8 * tile + kind : 8 * tile + kind + 1, :] for tile in range(tiles)]
                parts += [y_hi[edge, kind : kind + 1, :]]
            else:
                at = 2 * W * width + kind
                parts = [source[at : at + 1, :]]
                parts += [source[at + 16 + 8 * tile : at + 17 + 8 * tile, :] for tile in range(tiles)]
                parts += [source[at + 8 : at + 9, :]]
            coefs[zone, kind, :W, :] = jnp.broadcast_to(parts[0], (W, depth))
            for tile in range(tiles):
                begin = W + tile * edge
                coefs[zone, kind, begin : begin + edge, :] = jnp.broadcast_to(parts[1 + tile], (edge, depth))
            coefs[zone, kind, width - W :, :] = jnp.broadcast_to(parts[-1], (W, depth))
    for source, first in ((x_lo, 0), (x_hi, edge + W)):
        for row in range(W):
            for field in range(2):
                at = (2 * row + field) * width
                pairs[0][field][first + row, PAD : PAD + width, :] = source[at : at + width, :]

    def load_row(row, carry):
        fill_row(
            pairs[0],
            W + row,
            [phase[0, tile, row] for tile in range(tiles)],
            [solute[0, tile, row] for tile in range(tiles)],
            y_lo[row],
            y_hi[row],
        )
        return carry

    lax.fori_loop(0, edge, load_row, 0, unroll=UNROLL)

    def coefs_of(zone):
        def found(row, start):
            return tuple(coefs[zone(row), kind, start - PAD : start - PAD + 8, :] for kind in range(3))

        return found

    any_zone = coefs_of(lambda row: jnp.where(row < W, 0, jnp.where(row < W + edge, 1, 2)))

    for step in range(1, NSTEPS + 1):
        left = NSTEPS - step
        shift = W if step == NSTEPS else 0
        starts = range(PAD + shift, PAD + width - shift, 8)
        march(W - left, W + edge + left, starts, pairs[(step - 1) % 2], pairs[step % 2], any_zone)
    done = pairs[NSTEPS % 2]
    mine = lax.rem(lax.axis_index("gy"), half)
    for index, far_out in enumerate(far_outs):
        pack(plan, True, mine ^ (half // 2 + index), done, W, PAD + W, far_out)
    tail = 2 * tiles * plan.size
    for piece in range(half):
        pack(plan, False, piece, done, W, PAD + W, out.at[piece])
        out[piece, tail : tail + AUX, :] = own[8 * tiles : 8 * tiles + AUX, :]
        out[piece, tail + AUX : tail + 2 * AUX, :] = partner[...]


def run_outer(plan, own, phase, solute, halos, partner):
    tiles, edge, depth = plan.tiles, plan.edge, plan.depth
    width = tiles * edge + 2 * W
    buffer = pltpu.VMEM((edge + 2 * W, width + 2 * PAD, depth), jnp.float32)
    vmem = pl.BlockSpec(memory_space=pltpu.VMEM)
    near = jax.ShapeDtypeStruct((plan.half, 2 * tiles * plan.size + 2 * AUX, depth), jnp.float32)
    far = jax.ShapeDtypeStruct((2 * tiles * plan.size, depth), jnp.float32)
    return pl.pallas_call(
        functools.partial(outer_kernel, plan),
        in_specs=[vmem] * 8,
        out_specs=[vmem] * (1 + plan.half // 2),
        out_shape=[near] + [far] * (plan.half // 2),
        scratch_shapes=[buffer] * 4 + [pltpu.VMEM((3, 3, width, depth), jnp.float32)],
        compiler_params=pltpu.CompilerParams(vmem_limit_bytes=16 * 1024 * 1024),
        cost_estimate=pl.CostEstimate(flops=10**8, bytes_accessed=40 * 1024 * 1024, transcendentals=0),
        name="outer",
    )(own, phase, solute, *halos, partner)


def table_kernel(plan, near, table, names, count, sems):
    pieces, tiles, half = plan.pieces, plan.tiles, plan.half
    me = lax.axis_index("gy")
    base = me - lax.rem(me, half)
    tail = 2 * tiles * plan.size
    copies = []
    for piece in range(half):
        for index in range(2):
            copy = pltpu.make_async_copy(
                near.at[piece, pl.ds(tail + index * AUX, 1), :], names.at[index, piece], sems.at[index, piece]
            )
            copy.start()
            copies.append(copy)
    for peer in range(pieces):
        count[peer] = 0
    for copy in copies:
        copy.wait()
    for home in range(pieces):
        other = (home // half != base // half).astype(jnp.int32)
        for tile in range(tiles):
            peer = lax.rem(names[other, home % half, 0, tile].astype(jnp.int32), pieces)
            slot = count[peer]
            table[peer * tiles + slot] = home * tiles + tile
            count[peer] = slot + 1


def find_table(plan, near):
    return pl.pallas_call(
        functools.partial(table_kernel, plan),
        in_specs=[pl.BlockSpec(memory_space=pl.ANY)],
        out_specs=pl.BlockSpec(memory_space=pltpu.SMEM),
        out_shape=jax.ShapeDtypeStruct((plan.pieces * plan.tiles,), jnp.int32),
        scratch_shapes=[
            pltpu.SMEM((2, plan.half, 1, plan.depth), jnp.float32),
            pltpu.SMEM((plan.pieces,), jnp.int32),
            pltpu.SemaphoreType.DMA((2, plan.half)),
        ],
        name="table",
    )(near)


def route_kernel(plan, table, near, *refs):
    tiles, half, size = plan.tiles, plan.half, 2 * plan.size
    far, near_out, far_outs, held = refs[:half], refs[half], refs[half + 1 : 2 * half + 1], refs[-1]
    me = lax.axis_index("gy")
    base = me - lax.rem(me, half)
    for piece in range(half):
        for tile in range(tiles):
            held[(base + piece) * tiles + tile] = near[piece, tile * size : (tile + 1) * size, :]
    for index in range(half):
        for tile in range(tiles):
            held[(me ^ (half + index)) * tiles + tile] = far[index][tile * size : (tile + 1) * size, :]
    for index in range(half):
        for slot in range(tiles):
            far_outs[index][slot] = held[table[(me ^ (half + index)) * tiles + slot]]
            near_out[index, slot] = held[table[(base + index) * tiles + slot]]


def route(plan, table, near, far):
    tiles, half, size, depth = plan.tiles, plan.half, 2 * plan.size, plan.depth
    vmem = pl.BlockSpec(memory_space=pltpu.VMEM)
    one = jax.ShapeDtypeStruct((tiles, size, depth), jnp.float32)
    results = pl.pallas_call(
        functools.partial(route_kernel, plan),
        in_specs=[pl.BlockSpec(memory_space=pltpu.SMEM)] + [vmem] * (half + 1),
        out_specs=[vmem] * (half + 1),
        out_shape=[jax.ShapeDtypeStruct((half, tiles, size, depth), jnp.float32)] + [one] * half,
        scratch_shapes=[pltpu.VMEM((plan.pieces * tiles, size, depth), jnp.float32)],
        compiler_params=pltpu.CompilerParams(vmem_limit_bytes=16 * 1024 * 1024),
        name="route",
    )(table, near, *far)
    return results[0], results[1:]


def settle_kernel(plan, table, near, *refs):
    tiles, half = plan.tiles, plan.half
    far, outs = refs[:half], refs[half:]
    me = lax.axis_index("gy")
    mine = lax.rem(me, half)
    for slot in range(tiles):
        home = table[me * tiles + slot]
        tile = lax.rem(home, tiles)
        at_home = home // (tiles * half) == me // half

        def put(source, piece, is_far, slot=slot, tile=tile):
            for field, out in enumerate(outs):
                for at, row, name in plan.parts(is_far, piece):
                    col, count = plan.columns(name, tile)
                    if not isinstance(col, int):
                        col = pl.multiple_of(col, 8)
                    out[0, slot, row, pl.ds(col, count), :] = source[
                        slot, field * plan.size + at : field * plan.size + at + count, :
                    ]

        def put_all(same, put=put):
            for index in range(half):
                put(near.at[index], index, not same)
                put(far[index], mine ^ index, same)

        @pl.when(at_home)
        def _(put_all=put_all):
            put_all(True)

        @pl.when(jnp.logical_not(at_home))
        def _(put_all=put_all):
            put_all(False)


def settle(plan, table, near, far):
    out = jax.ShapeDtypeStruct((1, plan.tiles, plan.edge, plan.edge, plan.depth), jnp.float32)
    vmem = pl.BlockSpec(memory_space=pltpu.VMEM)
    return pl.pallas_call(
        functools.partial(settle_kernel, plan),
        in_specs=[pl.BlockSpec(memory_space=pltpu.SMEM)] + [vmem] * (plan.half + 1),
        out_specs=[vmem, vmem],
        out_shape=[out, out],
        compiler_params=pltpu.CompilerParams(vmem_limit_bytes=16 * 1024 * 1024),
        name="settle",
    )(table, near, *far)


def ring(axis, step):
    count = lax.axis_size(axis)
    return [(i, (i + step) % count) for i in range(count)]


def swap(values, mask):
    return lax.ppermute(values, "gy", [(i, i ^ mask) for i in range(lax.axis_size("gy"))])


def among_half(plan, values, together):
    def exchange(values):
        groups = [list(range(plan.half)), list(range(plan.half, plan.pieces))]
        return lax.all_to_all(values, "gy", 0, 0, axis_index_groups=groups, tiled=True)

    return lax.cond(together, exchange, exchange, values)


def per_device(phase, solute, undercool, mobility, diffusivity, owner):
    _, tiles, edge, _, depth = phase.shape
    plan = Plan(lax.axis_size("gy"), tiles, edge, depth)
    half = plan.half
    to_prev, to_next, own = pack_y(phase, solute, (undercool, mobility, diffusivity), owner)
    y_lo = lax.ppermute(to_next, "gy", ring("gy", 1))
    y_hi = lax.ppermute(to_prev, "gy", ring("gy", -1))
    first = run_inner(plan, own, phase, solute)
    far = [swap(values, half + index) for index, values in enumerate(first)]
    partner = swap(own[8 * tiles :], half)
    to_prev, to_next = pack_x(phase, solute, own, y_lo, y_hi, first[0])
    x_lo = lax.ppermute(to_next, "gx", ring("gx", 1))
    x_hi = lax.ppermute(to_prev, "gx", ring("gx", -1))
    near, *second = run_outer(plan, own, phase, solute, (y_lo, y_hi, x_lo, x_hi), partner)
    far += [swap(values, half + half // 2 + index) for index, values in enumerate(second)]
    together = owner[0, 0] >= 0
    near = among_half(plan, near, together)
    table = find_table(plan, near)
    near, far = route(plan, table, near, far)
    far = [swap(values, half + index) for index, values in enumerate(far)]
    near = among_half(plan, near, together)
    return tuple(settle(plan, table, near, far))


def solution(mesh):
    tile_spec = P("gx", "gy", None, None, None)
    in_specs = (tile_spec, tile_spec) + (P("gx", "gy"),) * 4
    out_spec = P(("gx", "gy"), None, None, None, None)
    return jax.shard_map(
        per_device, mesh=mesh, in_specs=in_specs, out_specs=(out_spec, out_spec), check_vma=False
    )
```

```python
import functools

import jax
import jax.numpy as jnp
from jax import lax
from jax.experimental import pallas as pl
from jax.experimental.pallas import tpu as pltpu
from jax.sharding import PartitionSpec as P

NSTEPS = 4
W = NSTEPS
PAD = 8

aniso_strength = 0.05


def pack_y_kernel(under, mobile, spread, owner, phase_lo, phase_hi, solute_lo, solute_hi, to_prev, to_next, own):
    edge, depth = phase_lo.shape[2], phase_lo.shape[4]
    tiles = own.shape[0] // 8 - 1
    to_prev[:edge, :W, :] = phase_lo[0, 0, :, :W, :]
    to_prev[:edge, W:, :] = solute_lo[0, 0, :, :W, :]
    to_next[:edge, :W, :] = phase_hi[0, 0, :, W:, :]
    to_next[:edge, W:, :] = solute_hi[0, 0, :, W:, :]
    line = lax.broadcasted_iota(jnp.int32, (8, depth), 0)
    lane = lax.broadcasted_iota(jnp.int32, (8, depth), 1)
    names = jnp.zeros((8, depth), jnp.float32)
    for tile in range(tiles):
        rows = jnp.zeros((8, depth), jnp.float32)
        for kind, coef in enumerate((under, mobile, spread)):
            rows = jnp.where(line == kind, coef[0, tile], rows)
        own[8 * tile : 8 * tile + 8, :] = rows
        if tile == 0:
            to_prev[edge] = rows
        if tile == tiles - 1:
            to_next[edge] = rows
        names = jnp.where(lane == tile, owner[0, tile].astype(jnp.float32), names)
    own[8 * tiles :, :] = names


def pack_y(phase, solute, coef, owner):
    _, tiles, edge, _, depth = phase.shape
    low = pl.BlockSpec((1, 1, edge, 2 * W, depth), lambda i: (0, 0, 0, 0, 0))
    high = pl.BlockSpec((1, 1, edge, 2 * W, depth), lambda i: (0, tiles - 1, 0, edge // (2 * W) - 1, 0))
    face = jax.ShapeDtypeStruct((edge + 1, 2 * W, depth), jnp.float32)
    own = jax.ShapeDtypeStruct((8 * tiles + 8, depth), jnp.float32)
    whole = pl.BlockSpec((edge + 1, 2 * W, depth), lambda i: (0, 0, 0))
    return pl.pallas_call(
        pack_y_kernel,
        grid=(1,),
        in_specs=[pl.BlockSpec(memory_space=pltpu.SMEM)] * 4 + [low, high, low, high],
        out_specs=[whole, whole, pl.BlockSpec((8 * tiles + 8, depth), lambda i: (0, 0))],
        out_shape=[face, face, own],
        name="pack_y",
    )(*coef, owner, phase, phase, solute, solute)


def fill_row(dst, row, phase_row, solute_row, lo, hi):
    start = PAD
    dst[0][row, start : start + W, :] = lo[:W]
    dst[1][row, start : start + W, :] = lo[W:]
    start += W
    for values in phase_row:
        size = values.shape[0]
        dst[0][row, start : start + size, :] = values
        start += size
    dst[0][row, start : start + W, :] = hi[:W]
    dst[1][row, start : start + W, :] = hi[W:]
    start = PAD + W
    for values in solute_row:
        size = values.shape[0]
        dst[1][row, start : start + size, :] = values
        start += size


def pack_x_kernel(own, phase_lo, phase_hi, solute_lo, solute_hi, y_lo, y_hi, _, to_prev, to_next):
    tiles, edge, depth = phase_lo.shape[1], phase_lo.shape[3], phase_lo.shape[4]
    width = tiles * edge + 2 * W
    for out, phase, solute, first in (
        (to_prev, phase_lo, solute_lo, 0),
        (to_next, phase_hi, solute_hi, edge - W),
    ):
        for row in range(W):
            for field, values, half in ((0, phase, 0), (1, solute, W)):
                at = (2 * row + field) * width
                out[at : at + W, :] = y_lo[first + row, half : half + W, :]
                for tile in range(tiles):
                    begin = at + W + tile * edge
                    out[begin : begin + edge, :] = values[0, tile, row]
                out[at + width - W : at + width, :] = y_hi[first + row, half : half + W, :]
        at = 2 * W * width
        out[at : at + 8, :] = y_lo[edge]
        out[at + 8 : at + 16, :] = y_hi[edge]
        out[at + 16 : at + 16 + 8 * tiles, :] = own[: 8 * tiles, :]


def pack_x(phase, solute, own, y_lo, y_hi, after):
    _, tiles, edge, _, depth = phase.shape
    low = pl.BlockSpec((1, tiles, W, edge, depth), lambda i: (0, 0, 0, 0, 0))
    high = pl.BlockSpec((1, tiles, W, edge, depth), lambda i: (0, 0, edge // W - 1, 0, 0))
    side = pl.BlockSpec((edge + 1, 2 * W, depth), lambda i: (0, 0, 0))
    rows = 2 * W * (tiles * edge + 2 * W) + 8 * (tiles + 2)
    out = jax.ShapeDtypeStruct((rows, depth), jnp.float32)
    whole = pl.BlockSpec((rows, depth), lambda i: (0, 0))
    return pl.pallas_call(
        pack_x_kernel,
        grid=(1,),
        in_specs=[pl.BlockSpec((8 * tiles + 8, depth), lambda i: (0, 0)), low, high, low, high, side, side, pl.BlockSpec(memory_space=pl.ANY)],
        out_specs=[whole, whole],
        out_shape=[out, out],
        compiler_params=pltpu.CompilerParams(vmem_limit_bytes=8 * 1024 * 1024),
        name="pack_x",
    )(own, phase, phase, solute, solute, y_lo, y_hi, after)


def update(near_p, near_u, under, mobile, spread):
    p, p_xl, p_xh, p_yl, p_yh = near_p
    u, u_xl, u_xh, u_yl, u_yh = near_u
    depth = p.shape[-1]
    lane = lax.broadcasted_iota(jnp.int32, p.shape, 1)
    first, last = lane == 0, lane == depth - 1
    p_zl = jnp.where(first, p, pltpu.roll(p, 1, 1))
    p_zh = jnp.where(last, p, pltpu.roll(p, depth - 1, 1))
    u_zl = jnp.where(first, u, pltpu.roll(u, 1, 1))
    u_zh = jnp.where(last, u, pltpu.roll(u, depth - 1, 1))
    dx, dy, dz = p_xh - p_xl, p_yh - p_yl, p_zh - p_zl
    qx, qy, qz = dx * dx, dy * dy, dz * dz
    total = qx + qy + qz
    fourth = qx * qx + qy * qy + qz * qz
    base = total + 4.0
    guess = pl.reciprocal(base, approx=True)
    inverse = guess * (2.0 - base * guess)
    extra = (4.0 * aniso_strength * fourth - (3.0 * aniso_strength) * total * total) * (inverse * inverse)
    lap_p = (p_xl + p_xh) + (p_yl + p_yh) + (p_zl + p_zh) - 6.0 * p
    lap_u = (u_xl + u_xh) + (u_yl + u_yh) + (u_zl + u_zh) - 6.0 * u
    well = 1.0 - p * p
    drive = well * (under + u)
    change = mobile * (lap_p + extra * lap_p + well * (p - 2.0 * drive))
    return p + change, u + spread * lap_u + 0.5 * change


def cells(src_p, src_u, row, start, coefs):
    near = []
    for src in (src_p, src_u):
        near.append(
            (
                src[row, start : start + 8, :],
                src[row - 1, start : start + 8, :],
                src[row + 1, start : start + 8, :],
                src[row, start - 1 : start + 7, :],
                src[row, start + 1 : start + 9, :],
            )
        )
    return update(near[0], near[1], *coefs)


class Plan:
    def __init__(self, pieces, tiles, edge, depth):
        self.pieces, self.tiles, self.edge, self.depth = pieces, tiles, edge, depth
        self.half = pieces // 2
        self.inner = edge - 2 * W
        self.rows = self.inner // self.half
        self.rows_far = (self.inner - 2 * W) // self.half
        self.rows_near = 2 * W // self.half
        self.middle = edge - 16
        self.size = self.rows * self.middle + self.rows_far * 8

        begins = [min(W + p * self.rows, 2 * W + p * self.rows_far) for p in range(self.half)]
        ends = [max(W + p * self.rows + self.rows, 2 * W + (p + 1) * self.rows_far) for p in range(self.half)]
        self.span = max(end - begin for begin, end in zip(begins, ends))

    def first_row(self, piece):
        begin = jnp.minimum(W + piece * self.rows, 2 * W + piece * self.rows_far)
        return jnp.minimum(begin, self.edge - W - self.span)

    def indices(self, early):
        return [0] if early else list(range(self.half // 2, self.half))

    def late(self):
        return list(range(1, self.half // 2))

    def near_row(self, piece, row, gap):
        index = piece * self.rows_near + row
        return index + jnp.where(index < W, 0, gap)

    def parts(self, far, piece):
        at, found = 0, []
        if far:
            for row in range(self.rows):
                found.append((at, W + piece * self.rows + row, "middle"))
                at += self.middle
            for row in range(self.rows_far):
                found.append((at, 2 * W + piece * self.rows_far + row, "last"))
                at += 8
        else:
            for row in range(self.rows_near):
                found.append((at, self.near_row(piece, row, self.inner), "whole"))
                at += self.edge
            for row in range(self.rows):
                found.append((at, W + piece * self.rows + row, "side"))
                at += 8
            for row in range(self.rows_near):
                found.append((at, W + self.near_row(piece, row, self.inner - 2 * W), "last"))
                at += 8
        assert at == self.size
        return found

    def columns(self, name, tile):
        if name == "whole":
            return 0, self.edge
        if name == "middle":
            return 8, self.middle
        low, high = (tile, 1 - tile) if name == "side" else (1 - tile, tile)
        return low * (self.edge - 8), 8


AUX = 8
UNROLL = 4


def march(first, last, starts, source, target, coefs_of, base=0):
    def one_row(index, carry):
        row = base + index
        for start in starts:
            new_p, new_u = cells(source[0], source[1], row, start, coefs_of(row, start))
            target[0][row, start : start + 8, :] = new_p
            target[1][row, start : start + 8, :] = new_u
        return carry

    lax.fori_loop(first, last, one_row, 0, unroll=UNROLL)


def inner_kernel(plan, early, own, phase, solute, _, *rest):
    tiles, edge = plan.tiles, plan.edge
    indices = plan.indices(early)
    outs, scratch = rest[: len(indices)], rest[len(indices) :]
    pairs = (scratch[:2], scratch[2:])
    mine = lax.rem(lax.axis_index("gy"), plan.half)
    if early:
        count = plan.span
        base = plan.first_row(mine) - W
    else:
        count = plan.inner // 2
        base = (1 - mine // (plan.half // 2)) * count

    def load_row(row, carry):
        for tile in range(tiles):
            start = PAD + tile * edge
            pairs[0][0][row, start : start + edge, :] = phase[0, tile, base + row]
            pairs[0][1][row, start : start + edge, :] = solute[0, tile, base + row]
        return carry

    lax.fori_loop(0, count + 2 * W, load_row, 0, unroll=UNROLL)

    def coefs_of(row, start):
        tile = (start - PAD) // edge
        return tuple(own[8 * tile + kind : 8 * tile + kind + 1, :] for kind in range(3))

    for step in range(NSTEPS):
        starts = range(PAD, PAD + tiles * edge, 8)
        march(step + 1, count + 2 * W - step - 1, starts, pairs[step % 2], pairs[(step + 1) % 2], coefs_of)
    for index, out in zip(indices, outs):
        pack(plan, True, mine ^ index, pairs[NSTEPS % 2], -base, PAD, out)
    if early:
        tail = 2 * tiles * plan.size
        outs[0][tail : tail + AUX, :] = own[8 * tiles : 8 * tiles + AUX, :]


def pack(plan, far, piece, done, row_shift, col_shift, out):
    for tile in range(plan.tiles):
        for field, values in enumerate(done):
            begin = (2 * tile + field) * plan.size
            for at, row, name in plan.parts(far, piece):
                col, count = plan.columns(name, tile)
                start = col_shift + tile * plan.edge + col
                out[begin + at : begin + at + count, :] = values[row + row_shift, start : start + count, :]


def run_inner(plan, early, own, phase, solute, after):
    rows = (plan.span if early else plan.inner // 2) + 2 * W
    buffer = pltpu.VMEM((rows, plan.tiles * plan.edge + 2 * PAD, plan.depth), jnp.float32)
    vmem = pl.BlockSpec(memory_space=pltpu.VMEM)
    shape = jax.ShapeDtypeStruct((2 * plan.tiles * plan.size + (AUX if early else 0), plan.depth), jnp.float32)
    count = len(plan.indices(early))
    return pl.pallas_call(
        functools.partial(inner_kernel, plan, early),
        in_specs=[vmem] * 3 + [pl.BlockSpec(memory_space=pl.ANY)],
        out_specs=[vmem] * count,
        out_shape=[shape] * count,
        scratch_shapes=[buffer] * 4,
        compiler_params=pltpu.CompilerParams(vmem_limit_bytes=16 * 1024 * 1024),
        cost_estimate=pl.CostEstimate(flops=10**8, bytes_accessed=16 * 1024 * 1024, transcendentals=0),
        name="first" if early else "inner",
    )(own, phase, solute, after)


def outer_kernel(plan, own, phase, solute, y_lo, y_hi, x_lo, x_hi, partner, out, *rest):
    tiles, edge, depth, half = plan.tiles, plan.edge, plan.depth, plan.half
    late = plan.late()
    far_outs, scratch = rest[: len(late)], rest[len(late) :]
    pairs, coefs = (scratch[:2], scratch[2:4]), scratch[4]
    cols = tiles * edge
    width = cols + 2 * W
    for zone, source in ((0, x_lo), (1, None), (2, x_hi)):
        for kind in range(3):
            if source is None:
                parts = [y_lo[edge, kind : kind + 1, :]]
                parts += [own[8 * tile + kind : 8 * tile + kind + 1, :] for tile in range(tiles)]
                parts += [y_hi[edge, kind : kind + 1, :]]
            else:
                at = 2 * W * width + kind
                parts = [source[at : at + 1, :]]
                parts += [source[at + 16 + 8 * tile : at + 17 + 8 * tile, :] for tile in range(tiles)]
                parts += [source[at + 8 : at + 9, :]]
            coefs[zone, kind, :W, :] = jnp.broadcast_to(parts[0], (W, depth))
            for tile in range(tiles):
                begin = W + tile * edge
                coefs[zone, kind, begin : begin + edge, :] = jnp.broadcast_to(parts[1 + tile], (edge, depth))
            coefs[zone, kind, width - W :, :] = jnp.broadcast_to(parts[-1], (W, depth))
    for source, first in ((x_lo, 0), (x_hi, edge + W)):
        for row in range(W):
            for field in range(2):
                at = (2 * row + field) * width
                pairs[0][field][first + row, PAD : PAD + width, :] = source[at : at + width, :]

    def load_row(row, carry):
        fill_row(
            pairs[0],
            W + row,
            [phase[0, tile, row] for tile in range(tiles)],
            [solute[0, tile, row] for tile in range(tiles)],
            y_lo[row],
            y_hi[row],
        )
        return carry

    lax.fori_loop(0, edge, load_row, 0, unroll=UNROLL)

    def coefs_of(zone):
        def found(row, start):
            return tuple(coefs[zone(row), kind, start - PAD : start - PAD + 8, :] for kind in range(3))

        return found

    any_zone = coefs_of(lambda row: jnp.where(row < W, 0, jnp.where(row < W + edge, 1, 2)))

    own_zone = coefs_of(lambda row: 1)

    def blocks(first, last):
        low, high = (first + W - shift) // 8 * 8, -(-(last + W - shift) // 8) * 8
        return list(range(PAD + shift + low, PAD + shift + high, 8))

    mine = lax.rem(lax.axis_index("gy"), half)
    for step in range(1, NSTEPS + 1):
        source, target = pairs[(step - 1) % 2], pairs[step % 2]
        left = NSTEPS - step
        shift = W if step == NSTEPS else 0
        strip = W + left
        whole = blocks(-left, cols + left)
        sides = blocks(-left, 8 + left) + blocks(cols - 8 - left, cols + left)
        lasts = []
        for tile in range(tiles):
            col, count = plan.columns("last", tile)
            lasts += blocks(tile * edge + col - left, tile * edge + col + count + left)
        ends = sorted(set(sides + lasts))
        march(W - left, W + strip, whole, source, target, any_zone)
        march(W + strip, W + strip + W, ends, source, target, own_zone)
        march(W + strip + W, W + edge - strip - W, sides, source, target, own_zone)
        march(W + edge - strip - W, W + edge - strip, ends, source, target, own_zone)
        march(W + edge - strip, W + edge + left, whole, source, target, any_zone)
        middle = [start for start in whole if start not in sides]
        for index in late:
            base = W + plan.first_row(mine ^ index)
            march(-left, plan.span + left, middle, source, target, own_zone, base)
    done = pairs[NSTEPS % 2]
    for index, far_out in zip(late, far_outs):
        pack(plan, True, mine ^ index, done, W, PAD + W, far_out)
    tail = 2 * tiles * plan.size
    for piece in range(half):
        pack(plan, False, piece, done, W, PAD + W, out.at[piece])
        out[piece, tail : tail + AUX, :] = own[8 * tiles : 8 * tiles + AUX, :]
        out[piece, tail + AUX : tail + 2 * AUX, :] = partner[tail : tail + AUX, :]


def run_outer(plan, own, phase, solute, halos, first):
    tiles, edge, depth = plan.tiles, plan.edge, plan.depth
    width = tiles * edge + 2 * W
    buffer = pltpu.VMEM((edge + 2 * W, width + 2 * PAD, depth), jnp.float32)
    vmem = pl.BlockSpec(memory_space=pltpu.VMEM)
    near = jax.ShapeDtypeStruct((plan.half, 2 * tiles * plan.size + 2 * AUX, depth), jnp.float32)
    far = jax.ShapeDtypeStruct((2 * tiles * plan.size, depth), jnp.float32)
    return pl.pallas_call(
        functools.partial(outer_kernel, plan),
        in_specs=[vmem] * 8,
        out_specs=[vmem] * (1 + len(plan.late())),
        out_shape=[near] + [far] * len(plan.late()),
        scratch_shapes=[buffer] * 4 + [pltpu.VMEM((3, 3, width, depth), jnp.float32)],
        compiler_params=pltpu.CompilerParams(vmem_limit_bytes=16 * 1024 * 1024),
        cost_estimate=pl.CostEstimate(flops=10**8, bytes_accessed=40 * 1024 * 1024, transcendentals=0),
        name="outer",
    )(own, phase, solute, *halos, first)


def route_kernel(plan, near, *refs):
    pieces, tiles, half, size = plan.pieces, plan.tiles, plan.half, 2 * plan.size
    far, near_out, far_outs, table = refs[:half], refs[half], refs[half + 1 : 2 * half + 1], refs[2 * half + 1]
    held, names, count, sem = refs[2 * half + 2 :]
    me = lax.axis_index("gy")
    base = me - lax.rem(me, half)
    copy = pltpu.make_async_copy(near.at[:, pl.ds(tiles * size, 2 * AUX), :], names, sem)
    copy.start()
    for peer in range(pieces):
        count[peer] = 0
    for piece in range(half):
        for tile in range(tiles):
            held[(base + piece) * tiles + tile] = near[piece, tile * size : (tile + 1) * size, :]
    for index in range(half):
        for tile in range(tiles):
            held[(me ^ (half + index)) * tiles + tile] = far[index][tile * size : (tile + 1) * size, :]
    copy.wait()
    for home in range(pieces):
        other = (home // half != base // half).astype(jnp.int32)
        for tile in range(tiles):
            peer = lax.rem(names[home % half, other * AUX, tile].astype(jnp.int32), pieces)
            slot = count[peer]
            table[peer * tiles + slot] = home * tiles + tile
            count[peer] = slot + 1
    for index in range(half):
        for slot in range(tiles):
            far_outs[index][slot] = held[table[(me ^ (half + index)) * tiles + slot]]
            near_out[index, slot] = held[table[(base + index) * tiles + slot]]


def route(plan, near, far):
    tiles, half, size, depth = plan.tiles, plan.half, 2 * plan.size, plan.depth
    vmem = pl.BlockSpec(memory_space=pltpu.VMEM)
    one = jax.ShapeDtypeStruct((tiles, size, depth), jnp.float32)
    count = plan.pieces * tiles
    results = pl.pallas_call(
        functools.partial(route_kernel, plan),
        in_specs=[vmem] * (half + 1),
        out_specs=[vmem] * (half + 1) + [pl.BlockSpec(memory_space=pltpu.SMEM)],
        out_shape=[jax.ShapeDtypeStruct((half, tiles, size, depth), jnp.float32)]
        + [one] * half
        + [jax.ShapeDtypeStruct((count,), jnp.int32)],
        scratch_shapes=[
            pltpu.VMEM((count, size, depth), jnp.float32),
            pltpu.SMEM((half, 2 * AUX, depth), jnp.float32),
            pltpu.SMEM((plan.pieces,), jnp.int32),
            pltpu.SemaphoreType.DMA,
        ],
        compiler_params=pltpu.CompilerParams(vmem_limit_bytes=16 * 1024 * 1024),
        name="route",
    )(near, *far)
    return results[0], results[1 : half + 1], results[-1]


def settle_kernel(plan, table, near, *refs):
    tiles, half = plan.tiles, plan.half
    far, outs = refs[:half], refs[half:]
    me = lax.axis_index("gy")
    mine = lax.rem(me, half)
    for slot in range(tiles):
        home = table[me * tiles + slot]
        tile = lax.rem(home, tiles)
        at_home = home // (tiles * half) == me // half

        def put(source, piece, is_far, slot=slot, tile=tile):
            for field, out in enumerate(outs):
                for at, row, name in plan.parts(is_far, piece):
                    col, count = plan.columns(name, tile)
                    if not isinstance(col, int):
                        col = pl.multiple_of(col, 8)
                    out[0, slot, row, pl.ds(col, count), :] = source[
                        slot, field * plan.size + at : field * plan.size + at + count, :
                    ]

        def put_all(same, put=put):
            for index in range(half):
                put(near.at[index], index, not same)
                put(far[index], mine ^ index, same)

        @pl.when(at_home)
        def _(put_all=put_all):
            put_all(True)

        @pl.when(jnp.logical_not(at_home))
        def _(put_all=put_all):
            put_all(False)


def settle(plan, table, near, far):
    out = jax.ShapeDtypeStruct((1, plan.tiles, plan.edge, plan.edge, plan.depth), jnp.float32)
    vmem = pl.BlockSpec(memory_space=pltpu.VMEM)
    return pl.pallas_call(
        functools.partial(settle_kernel, plan),
        in_specs=[pl.BlockSpec(memory_space=pltpu.SMEM)] + [vmem] * (plan.half + 1),
        out_specs=[vmem, vmem],
        out_shape=[out, out],
        compiler_params=pltpu.CompilerParams(vmem_limit_bytes=16 * 1024 * 1024),
        name="settle",
    )(table, near, *far)


def ring(axis, step):
    count = lax.axis_size(axis)
    return [(i, (i + step) % count) for i in range(count)]


def swap(values, mask):
    return lax.ppermute(values, "gy", [(i, i ^ mask) for i in range(lax.axis_size("gy"))])


def around(axis, low, high):
    return lax.ppermute(low, axis, ring(axis, 1)), lax.ppermute(high, axis, ring(axis, -1))


def at_once(exchange, together, *values):
    return lax.cond(together, exchange, exchange, *values)


def among_half(plan, values, together):
    groups = [list(range(plan.half)), list(range(plan.half, plan.pieces))]

    def exchange(values):
        return lax.all_to_all(values, "gy", 0, 0, axis_index_groups=groups, tiled=True)

    return at_once(exchange, together, values)


def per_device(phase, solute, undercool, mobility, diffusivity, owner):
    _, tiles, edge, _, depth = phase.shape
    plan = Plan(lax.axis_size("gy"), tiles, edge, depth)
    half = plan.half
    to_prev, to_next, own = pack_y(phase, solute, (undercool, mobility, diffusivity), owner)
    y_lo, y_hi = around("gy", to_next, to_prev)
    together = owner[0, 0] >= 0
    far = {}
    (first,) = run_inner(plan, True, own, phase, solute, own)
    far[0] = swap(first, half)
    inner = run_inner(plan, False, own, phase, solute, first)
    for index, values in zip(plan.indices(False), inner):
        far[index] = swap(values, half + index)
    to_prev, to_next = pack_x(phase, solute, own, y_lo, y_hi, inner[0])
    x_lo, x_hi = at_once(lambda low, high: around("gx", low, high), together, to_next, to_prev)
    near, *late = run_outer(plan, own, phase, solute, (y_lo, y_hi, x_lo, x_hi), far[0])
    for index, values in zip(plan.late(), late):
        far[index] = swap(values, half + index)
    near = among_half(plan, near, together)
    near, far, table = route(plan, near, [far[index] for index in range(half)])
    far = [swap(values, half + index) for index, values in enumerate(far)]
    near = among_half(plan, near, together)
    return tuple(settle(plan, table, near, far))


def solution(mesh):
    tile_spec = P("gx", "gy", None, None, None)
    in_specs = (tile_spec, tile_spec) + (P("gx", "gy"),) * 4
    out_spec = P(("gx", "gy"), None, None, None, None)
    return jax.shard_map(
        per_device, mesh=mesh, in_specs=in_specs, out_specs=(out_spec, out_spec), check_vma=False
    )
```

```python
import functools

import jax
import jax.numpy as jnp
from jax import lax
from jax.experimental import pallas as pl
from jax.experimental.pallas import tpu as pltpu
from jax.sharding import PartitionSpec as P

NSTEPS = 4
W = NSTEPS
PAD = 8

aniso_strength = 0.05


def pack_y_kernel(under, mobile, spread, owner, phase_lo, phase_hi, solute_lo, solute_hi, to_prev, to_next, own):
    edge, depth = phase_lo.shape[2], phase_lo.shape[4]
    tiles = own.shape[0] // 8 - 1
    to_prev[:edge, :W, :] = phase_lo[0, 0, :, :W, :]
    to_prev[:edge, W:, :] = solute_lo[0, 0, :, :W, :]
    to_next[:edge, :W, :] = phase_hi[0, 0, :, W:, :]
    to_next[:edge, W:, :] = solute_hi[0, 0, :, W:, :]
    line = lax.broadcasted_iota(jnp.int32, (8, depth), 0)
    lane = lax.broadcasted_iota(jnp.int32, (8, depth), 1)
    names = jnp.zeros((8, depth), jnp.float32)
    for tile in range(tiles):
        rows = jnp.zeros((8, depth), jnp.float32)
        for kind, coef in enumerate((under, mobile, spread)):
            rows = jnp.where(line == kind, coef[0, tile], rows)
        own[8 * tile : 8 * tile + 8, :] = rows
        if tile == 0:
            to_prev[edge] = rows
        if tile == tiles - 1:
            to_next[edge] = rows
        names = jnp.where(lane == tile, owner[0, tile].astype(jnp.float32), names)
    own[8 * tiles :, :] = names


def pack_y(phase, solute, coef, owner):
    _, tiles, edge, _, depth = phase.shape
    low = pl.BlockSpec((1, 1, edge, 2 * W, depth), lambda i: (0, 0, 0, 0, 0))
    high = pl.BlockSpec((1, 1, edge, 2 * W, depth), lambda i: (0, tiles - 1, 0, edge // (2 * W) - 1, 0))
    face = jax.ShapeDtypeStruct((edge + 1, 2 * W, depth), jnp.float32)
    own = jax.ShapeDtypeStruct((8 * tiles + 8, depth), jnp.float32)
    whole = pl.BlockSpec((edge + 1, 2 * W, depth), lambda i: (0, 0, 0))
    return pl.pallas_call(
        pack_y_kernel,
        grid=(1,),
        in_specs=[pl.BlockSpec(memory_space=pltpu.SMEM)] * 4 + [low, high, low, high],
        out_specs=[whole, whole, pl.BlockSpec((8 * tiles + 8, depth), lambda i: (0, 0))],
        out_shape=[face, face, own],
        name="pack_y",
    )(*coef, owner, phase, phase, solute, solute)


def fill_row(dst, row, phase_row, solute_row, lo, hi):
    start = PAD
    dst[0][row, start : start + W, :] = lo[:W]
    dst[1][row, start : start + W, :] = lo[W:]
    start += W
    for values in phase_row:
        size = values.shape[0]
        dst[0][row, start : start + size, :] = values
        start += size
    dst[0][row, start : start + W, :] = hi[:W]
    dst[1][row, start : start + W, :] = hi[W:]
    start = PAD + W
    for values in solute_row:
        size = values.shape[0]
        dst[1][row, start : start + size, :] = values
        start += size


def pack_x_kernel(own, phase_lo, phase_hi, solute_lo, solute_hi, y_lo, y_hi, *rest):
    to_prev, to_next = rest[-2:]
    tiles, edge, depth = phase_lo.shape[1], phase_lo.shape[3], phase_lo.shape[4]
    width = tiles * edge + 2 * W
    for out, phase, solute, first in (
        (to_prev, phase_lo, solute_lo, 0),
        (to_next, phase_hi, solute_hi, edge - W),
    ):
        for row in range(W):
            for field, values, half in ((0, phase, 0), (1, solute, W)):
                at = (2 * row + field) * width
                out[at : at + W, :] = y_lo[first + row, half : half + W, :]
                for tile in range(tiles):
                    begin = at + W + tile * edge
                    out[begin : begin + edge, :] = values[0, tile, row]
                out[at + width - W : at + width, :] = y_hi[first + row, half : half + W, :]
        at = 2 * W * width
        out[at : at + 8, :] = y_lo[edge]
        out[at + 8 : at + 16, :] = y_hi[edge]
        out[at + 16 : at + 16 + 8 * tiles, :] = own[: 8 * tiles, :]


def pack_x(phase, solute, own, y_lo, y_hi, *after):
    _, tiles, edge, _, depth = phase.shape
    low = pl.BlockSpec((1, tiles, W, edge, depth), lambda i: (0, 0, 0, 0, 0))
    high = pl.BlockSpec((1, tiles, W, edge, depth), lambda i: (0, 0, edge // W - 1, 0, 0))
    side = pl.BlockSpec((edge + 1, 2 * W, depth), lambda i: (0, 0, 0))
    rows = 2 * W * (tiles * edge + 2 * W) + 8 * (tiles + 2)
    out = jax.ShapeDtypeStruct((rows, depth), jnp.float32)
    whole = pl.BlockSpec((rows, depth), lambda i: (0, 0))
    return pl.pallas_call(
        pack_x_kernel,
        grid=(1,),
        in_specs=[pl.BlockSpec((8 * tiles + 8, depth), lambda i: (0, 0)), low, high, low, high, side, side] + [pl.BlockSpec(memory_space=pl.ANY)] * len(after),
        out_specs=[whole, whole],
        out_shape=[out, out],
        compiler_params=pltpu.CompilerParams(vmem_limit_bytes=8 * 1024 * 1024),
        name="pack_x",
    )(own, phase, phase, solute, solute, y_lo, y_hi, *after)


def update(near_p, near_u, under, mobile, spread):
    p, p_xl, p_xh, p_yl, p_yh = near_p
    u, u_xl, u_xh, u_yl, u_yh = near_u
    depth = p.shape[-1]
    lane = lax.broadcasted_iota(jnp.int32, p.shape, 1)
    first, last = lane == 0, lane == depth - 1
    p_zl = jnp.where(first, p, pltpu.roll(p, 1, 1))
    p_zh = jnp.where(last, p, pltpu.roll(p, depth - 1, 1))
    u_zl = jnp.where(first, u, pltpu.roll(u, 1, 1))
    u_zh = jnp.where(last, u, pltpu.roll(u, depth - 1, 1))
    dx, dy, dz = p_xh - p_xl, p_yh - p_yl, p_zh - p_zl
    qx, qy, qz = dx * dx, dy * dy, dz * dz
    total = qx + qy + qz
    fourth = qx * qx + qy * qy + qz * qz
    base = total + 4.0
    guess = pl.reciprocal(base, approx=True)
    inverse = guess * (2.0 - base * guess)
    extra = (4.0 * aniso_strength * fourth - (3.0 * aniso_strength) * total * total) * (inverse * inverse)
    lap_p = (p_xl + p_xh) + (p_yl + p_yh) + (p_zl + p_zh) - 6.0 * p
    lap_u = (u_xl + u_xh) + (u_yl + u_yh) + (u_zl + u_zh) - 6.0 * u
    well = 1.0 - p * p
    drive = well * (under + u)
    change = mobile * (lap_p + extra * lap_p + well * (p - 2.0 * drive))
    return p + change, u + spread * lap_u + 0.5 * change


def cells(src_p, src_u, row, start, coefs):
    near = []
    for src in (src_p, src_u):
        near.append(
            (
                src[row, start : start + 8, :],
                src[row - 1, start : start + 8, :],
                src[row + 1, start : start + 8, :],
                src[row, start - 1 : start + 7, :],
                src[row, start + 1 : start + 9, :],
            )
        )
    return update(near[0], near[1], *coefs)


class Plan:
    def __init__(self, pieces, tiles, edge, depth):
        self.pieces, self.tiles, self.edge, self.depth = pieces, tiles, edge, depth
        self.half = pieces // 2
        self.inner = edge - 2 * W
        self.rows = self.inner // self.half
        self.rows_far = (self.inner - 2 * W) // self.half
        self.rows_near = 2 * W // self.half
        self.middle = edge - 16
        self.size = self.rows * self.middle + self.rows_far * 8

    def near_row(self, piece, row, gap):
        index = piece * self.rows_near + row
        return index + jnp.where(index < W, 0, gap)

    def parts(self, far, piece):
        at, found = 0, []
        if far:
            for row in range(self.rows):
                found.append((at, W + piece * self.rows + row, "middle"))
                at += self.middle
            for row in range(self.rows_far):
                found.append((at, 2 * W + piece * self.rows_far + row, "last"))
                at += 8
        else:
            for row in range(self.rows_near):
                found.append((at, self.near_row(piece, row, self.inner), "whole"))
                at += self.edge
            for row in range(self.rows):
                found.append((at, W + piece * self.rows + row, "side"))
                at += 8
            for row in range(self.rows_near):
                found.append((at, W + self.near_row(piece, row, self.inner - 2 * W), "last"))
                at += 8
        assert at == self.size
        return found

    def columns(self, name, tile):
        if name == "whole":
            return 0, self.edge
        if name == "middle":
            return 8, self.middle
        low, high = (tile, 1 - tile) if name == "side" else (1 - tile, tile)
        return low * (self.edge - 8), 8


AUX = 8
UNROLL = 4


def march(first, last, starts, source, target, coefs_of):
    def one_row(row, carry):
        for start in starts:
            new_p, new_u = cells(source[0], source[1], row, start, coefs_of(row, start))
            target[0][row, start : start + 8, :] = new_p
            target[1][row, start : start + 8, :] = new_u
        return carry

    lax.fori_loop(first, last, one_row, 0, unroll=UNROLL)


def inner_kernel(plan, own, phase, solute, *rest):
    tiles, edge, count = plan.tiles, plan.edge, plan.inner // 2
    outs, scratch = rest[: plan.half // 2], rest[plan.half // 2 :]
    pairs = (scratch[:2], scratch[2:])
    mine = lax.rem(lax.axis_index("gy"), plan.half)
    base = mine // (plan.half // 2) * count

    def load_row(row, carry):
        for tile in range(tiles):
            start = PAD + tile * edge
            pairs[0][0][row, start : start + edge, :] = phase[0, tile, base + row]
            pairs[0][1][row, start : start + edge, :] = solute[0, tile, base + row]
        return carry

    lax.fori_loop(0, count + 2 * W, load_row, 0, unroll=UNROLL)

    def coefs_of(row, start):
        tile = (start - PAD) // edge
        return tuple(own[8 * tile + kind : 8 * tile + kind + 1, :] for kind in range(3))

    for step in range(NSTEPS):
        starts = range(PAD, PAD + tiles * edge, 8)
        march(step + 1, count + 2 * W - step - 1, starts, pairs[step % 2], pairs[(step + 1) % 2], coefs_of)
    for index, out in enumerate(outs):
        pack(plan, True, mine ^ index, pairs[NSTEPS % 2], -base, PAD, out)


def pack(plan, far, piece, done, row_shift, col_shift, out):
    for tile in range(plan.tiles):
        for field, values in enumerate(done):
            begin = (2 * tile + field) * plan.size
            for at, row, name in plan.parts(far, piece):
                col, count = plan.columns(name, tile)
                start = col_shift + tile * plan.edge + col
                out[begin + at : begin + at + count, :] = values[row + row_shift, start : start + count, :]


def run_inner(plan, own, phase, solute):
    rows = plan.inner // 2 + 2 * W
    buffer = pltpu.VMEM((rows, plan.tiles * plan.edge + 2 * PAD, plan.depth), jnp.float32)
    vmem = pl.BlockSpec(memory_space=pltpu.VMEM)
    shape = jax.ShapeDtypeStruct((2 * plan.tiles * plan.size, plan.depth), jnp.float32)
    return pl.pallas_call(
        functools.partial(inner_kernel, plan),
        in_specs=[vmem] * 3,
        out_specs=[vmem] * (plan.half // 2),
        out_shape=[shape] * (plan.half // 2),
        scratch_shapes=[buffer] * 4,
        compiler_params=pltpu.CompilerParams(vmem_limit_bytes=16 * 1024 * 1024),
        cost_estimate=pl.CostEstimate(flops=10**8, bytes_accessed=24 * 1024 * 1024, transcendentals=0),
        name="inner",
    )(own, phase, solute)


def outer_kernel(plan, own, phase, solute, y_lo, y_hi, x_lo, x_hi, partner, out, *rest):
    tiles, edge, depth, half = plan.tiles, plan.edge, plan.depth, plan.half
    far_outs, scratch = rest[: half // 2], rest[half // 2 :]
    pairs, coefs = (scratch[:2], scratch[2:4]), scratch[4]
    cols = tiles * edge
    width = cols + 2 * W
    for zone, source in ((0, x_lo), (1, None), (2, x_hi)):
        for kind in range(3):
            if source is None:
                parts = [y_lo[edge, kind : kind + 1, :]]
                parts += [own[8 * tile + kind : 8 * tile + kind + 1, :] for tile in range(tiles)]
                parts += [y_hi[edge, kind : kind + 1, :]]
            else:
                at = 2 * W * width + kind
                parts = [source[at : at + 1, :]]
                parts += [source[at + 16 + 8 * tile : at + 17 + 8 * tile, :] for tile in range(tiles)]
                parts += [source[at + 8 : at + 9, :]]
            coefs[zone, kind, :W, :] = jnp.broadcast_to(parts[0], (W, depth))
            for tile in range(tiles):
                begin = W + tile * edge
                coefs[zone, kind, begin : begin + edge, :] = jnp.broadcast_to(parts[1 + tile], (edge, depth))
            coefs[zone, kind, width - W :, :] = jnp.broadcast_to(parts[-1], (W, depth))
    for source, first in ((x_lo, 0), (x_hi, edge + W)):
        for row in range(W):
            for field in range(2):
                at = (2 * row + field) * width
                pairs[0][field][first + row, PAD : PAD + width, :] = source[at : at + width, :]

    def load_row(row, carry):
        fill_row(
            pairs[0],
            W + row,
            [phase[0, tile, row] for tile in range(tiles)],
            [solute[0, tile, row] for tile in range(tiles)],
            y_lo[row],
            y_hi[row],
        )
        return carry

    lax.fori_loop(0, edge, load_row, 0, unroll=UNROLL)

    def coefs_of(zone):
        def found(row, start):
            return tuple(coefs[zone(row), kind, start - PAD : start - PAD + 8, :] for kind in range(3))

        return found

    any_zone = coefs_of(lambda row: jnp.where(row < W, 0, jnp.where(row < W + edge, 1, 2)))

    for step in range(1, NSTEPS + 1):
        left = NSTEPS - step
        shift = W if step == NSTEPS else 0
        starts = range(PAD + shift, PAD + width - shift, 8)
        march(W - left, W + edge + left, starts, pairs[(step - 1) % 2], pairs[step % 2], any_zone)
    done = pairs[NSTEPS % 2]
    mine = lax.rem(lax.axis_index("gy"), half)
    for index, far_out in enumerate(far_outs):
        pack(plan, True, mine ^ (half // 2 + index), done, W, PAD + W, far_out)
    tail = 2 * tiles * plan.size
    for piece in range(half):
        pack(plan, False, piece, done, W, PAD + W, out.at[piece])
        out[piece, tail : tail + AUX, :] = own[8 * tiles : 8 * tiles + AUX, :]
        out[piece, tail + AUX : tail + 2 * AUX, :] = partner[...]


def run_outer(plan, own, phase, solute, halos, partner):
    tiles, edge, depth = plan.tiles, plan.edge, plan.depth
    width = tiles * edge + 2 * W
    buffer = pltpu.VMEM((edge + 2 * W, width + 2 * PAD, depth), jnp.float32)
    vmem = pl.BlockSpec(memory_space=pltpu.VMEM)
    near = jax.ShapeDtypeStruct((plan.half, 2 * tiles * plan.size + 2 * AUX, depth), jnp.float32)
    far = jax.ShapeDtypeStruct((2 * tiles * plan.size, depth), jnp.float32)
    return pl.pallas_call(
        functools.partial(outer_kernel, plan),
        in_specs=[vmem] * 8,
        out_specs=[vmem] * (1 + plan.half // 2),
        out_shape=[near] + [far] * (plan.half // 2),
        scratch_shapes=[buffer] * 4 + [pltpu.VMEM((3, 3, width, depth), jnp.float32)],
        compiler_params=pltpu.CompilerParams(vmem_limit_bytes=16 * 1024 * 1024),
        cost_estimate=pl.CostEstimate(flops=10**8, bytes_accessed=40 * 1024 * 1024, transcendentals=0),
        name="outer",
    )(own, phase, solute, *halos, partner)


def table_kernel(plan, near, table, names, count, sems):
    pieces, tiles, half = plan.pieces, plan.tiles, plan.half
    me = lax.axis_index("gy")
    base = me - lax.rem(me, half)
    tail = 2 * tiles * plan.size
    copies = []
    for piece in range(half):
        for index in range(2):
            copy = pltpu.make_async_copy(
                near.at[piece, pl.ds(tail + index * AUX, 1), :], names.at[index, piece], sems.at[index, piece]
            )
            copy.start()
            copies.append(copy)
    for peer in range(pieces):
        count[peer] = 0
    for copy in copies:
        copy.wait()
    for home in range(pieces):
        other = (home // half != base // half).astype(jnp.int32)
        for tile in range(tiles):
            peer = lax.rem(names[other, home % half, 0, tile].astype(jnp.int32), pieces)
            slot = count[peer]
            table[peer * tiles + slot] = home * tiles + tile
            count[peer] = slot + 1


def find_table(plan, near):
    return pl.pallas_call(
        functools.partial(table_kernel, plan),
        in_specs=[pl.BlockSpec(memory_space=pl.ANY)],
        out_specs=pl.BlockSpec(memory_space=pltpu.SMEM),
        out_shape=jax.ShapeDtypeStruct((plan.pieces * plan.tiles,), jnp.int32),
        scratch_shapes=[
            pltpu.SMEM((2, plan.half, 1, plan.depth), jnp.float32),
            pltpu.SMEM((plan.pieces,), jnp.int32),
            pltpu.SemaphoreType.DMA((2, plan.half)),
        ],
        name="table",
    )(near)


def route_kernel(plan, table, near, *refs):
    tiles, half, size = plan.tiles, plan.half, 2 * plan.size
    far, near_out, far_outs, held = refs[:half], refs[half], refs[half + 1 : 2 * half + 1], refs[-1]
    me = lax.axis_index("gy")
    base = me - lax.rem(me, half)
    for piece in range(half):
        for tile in range(tiles):
            held[(base + piece) * tiles + tile] = near[piece, tile * size : (tile + 1) * size, :]
    for index in range(half):
        for tile in range(tiles):
            held[(me ^ (half + index)) * tiles + tile] = far[index][tile * size : (tile + 1) * size, :]
    for index in range(half):
        for slot in range(tiles):
            far_outs[index][slot] = held[table[(me ^ (half + index)) * tiles + slot]]
            near_out[index, slot] = held[table[(base + index) * tiles + slot]]


def route(plan, table, near, far):
    tiles, half, size, depth = plan.tiles, plan.half, 2 * plan.size, plan.depth
    vmem = pl.BlockSpec(memory_space=pltpu.VMEM)
    one = jax.ShapeDtypeStruct((tiles, size, depth), jnp.float32)
    results = pl.pallas_call(
        functools.partial(route_kernel, plan),
        in_specs=[pl.BlockSpec(memory_space=pltpu.SMEM)] + [vmem] * (half + 1),
        out_specs=[vmem] * (half + 1),
        out_shape=[jax.ShapeDtypeStruct((half, tiles, size, depth), jnp.float32)] + [one] * half,
        scratch_shapes=[pltpu.VMEM((plan.pieces * tiles, size, depth), jnp.float32)],
        compiler_params=pltpu.CompilerParams(vmem_limit_bytes=16 * 1024 * 1024),
        name="route",
    )(table, near, *far)
    return results[0], results[1:]


def settle_kernel(plan, table, near, *refs):
    tiles, half = plan.tiles, plan.half
    far, outs = refs[:half], refs[half:]
    me = lax.axis_index("gy")
    mine = lax.rem(me, half)
    for slot in range(tiles):
        home = table[me * tiles + slot]
        tile = lax.rem(home, tiles)
        at_home = home // (tiles * half) == me // half

        def put(source, piece, is_far, slot=slot, tile=tile):
            for field, out in enumerate(outs):
                for at, row, name in plan.parts(is_far, piece):
                    col, count = plan.columns(name, tile)
                    if not isinstance(col, int):
                        col = pl.multiple_of(col, 8)
                    out[0, slot, row, pl.ds(col, count), :] = source[
                        slot, field * plan.size + at : field * plan.size + at + count, :
                    ]

        def put_all(same, put=put):
            for index in range(half):
                put(near.at[index], index, not same)
                put(far[index], mine ^ index, same)

        @pl.when(at_home)
        def _(put_all=put_all):
            put_all(True)

        @pl.when(jnp.logical_not(at_home))
        def _(put_all=put_all):
            put_all(False)


def settle(plan, table, near, far):
    out = jax.ShapeDtypeStruct((1, plan.tiles, plan.edge, plan.edge, plan.depth), jnp.float32)
    vmem = pl.BlockSpec(memory_space=pltpu.VMEM)
    return pl.pallas_call(
        functools.partial(settle_kernel, plan),
        in_specs=[pl.BlockSpec(memory_space=pltpu.SMEM)] + [vmem] * (plan.half + 1),
        out_specs=[vmem, vmem],
        out_shape=[out, out],
        compiler_params=pltpu.CompilerParams(vmem_limit_bytes=16 * 1024 * 1024),
        name="settle",
    )(table, near, *far)


def ring(axis, step):
    count = lax.axis_size(axis)
    return [(i, (i + step) % count) for i in range(count)]


def swap(values, mask):
    return lax.ppermute(values, "gy", [(i, i ^ mask) for i in range(lax.axis_size("gy"))])


def among_half(plan, values, together):
    def exchange(values):
        groups = [list(range(plan.half)), list(range(plan.half, plan.pieces))]
        return lax.all_to_all(values, "gy", 0, 0, axis_index_groups=groups, tiled=True)

    return lax.cond(together, exchange, exchange, values)


def per_device(phase, solute, undercool, mobility, diffusivity, owner):
    _, tiles, edge, _, depth = phase.shape
    plan = Plan(lax.axis_size("gy"), tiles, edge, depth)
    half = plan.half
    to_prev, to_next, own = pack_y(phase, solute, (undercool, mobility, diffusivity), owner)
    y_lo = lax.ppermute(to_next, "gy", ring("gy", 1))
    y_hi = lax.ppermute(to_prev, "gy", ring("gy", -1))
    partner = swap(own[8 * tiles :], half)
    first = run_inner(plan, own, phase, solute)
    far = [swap(values, half + index) for index, values in enumerate(first)]
    to_prev, to_next = pack_x(phase, solute, own, y_lo, y_hi, first[0], partner)
    x_lo = lax.ppermute(to_next, "gx", ring("gx", 1))
    x_hi = lax.ppermute(to_prev, "gx", ring("gx", -1))
    near, *second = run_outer(plan, own, phase, solute, (y_lo, y_hi, x_lo, x_hi), partner)
    far += [swap(values, half + half // 2 + index) for index, values in enumerate(second)]
    together = owner[0, 0] >= 0
    near = among_half(plan, near, together)
    table = find_table(plan, near)
    near, far = route(plan, table, near, far)
    far = [swap(values, half + index) for index, values in enumerate(far)]
    near = among_half(plan, near, together)
    return tuple(settle(plan, table, near, far))


def solution(mesh):
    tile_spec = P("gx", "gy", None, None, None)
    in_specs = (tile_spec, tile_spec) + (P("gx", "gy"),) * 4
    out_spec = P(("gx", "gy"), None, None, None, None)
    return jax.shard_map(
        per_device, mesh=mesh, in_specs=in_specs, out_specs=(out_spec, out_spec), check_vma=False
    )
```

```python
import functools

import jax
import jax.numpy as jnp
from jax import lax
from jax.experimental import pallas as pl
from jax.experimental.pallas import tpu as pltpu
from jax.sharding import PartitionSpec as P

NSTEPS = 4
W = NSTEPS
PAD = 8

aniso_strength = 0.05


def pack_y_kernel(under, mobile, spread, owner, phase_lo, phase_hi, solute_lo, solute_hi, to_prev, to_next, own):
    edge, depth = phase_lo.shape[2], phase_lo.shape[4]
    tiles = own.shape[0] // 8 - 1
    to_prev[:edge, :W, :] = phase_lo[0, 0, :, :W, :]
    to_prev[:edge, W:, :] = solute_lo[0, 0, :, :W, :]
    to_next[:edge, :W, :] = phase_hi[0, 0, :, W:, :]
    to_next[:edge, W:, :] = solute_hi[0, 0, :, W:, :]
    line = lax.broadcasted_iota(jnp.int32, (8, depth), 0)
    lane = lax.broadcasted_iota(jnp.int32, (8, depth), 1)
    names = jnp.zeros((8, depth), jnp.float32)
    for tile in range(tiles):
        rows = jnp.zeros((8, depth), jnp.float32)
        ready = (2.0 * under[0, tile], mobile[0, tile], spread[0, tile], 1.0 - 6.0 * spread[0, tile])
        for kind, coef in enumerate(ready):
            rows = jnp.where(line == kind, coef, rows)
        own[8 * tile : 8 * tile + 8, :] = rows
        if tile == 0:
            to_prev[edge] = rows
        if tile == tiles - 1:
            to_next[edge] = rows
        names = jnp.where(lane == tile, owner[0, tile].astype(jnp.float32), names)
    own[8 * tiles :, :] = names


def pack_y(phase, solute, coef, owner):
    _, tiles, edge, _, depth = phase.shape
    low = pl.BlockSpec((1, 1, edge, 2 * W, depth), lambda i: (0, 0, 0, 0, 0))
    high = pl.BlockSpec((1, 1, edge, 2 * W, depth), lambda i: (0, tiles - 1, 0, edge // (2 * W) - 1, 0))
    face = jax.ShapeDtypeStruct((edge + 1, 2 * W, depth), jnp.float32)
    own = jax.ShapeDtypeStruct((8 * tiles + 8, depth), jnp.float32)
    whole = pl.BlockSpec((edge + 1, 2 * W, depth), lambda i: (0, 0, 0))
    return pl.pallas_call(
        pack_y_kernel,
        grid=(1,),
        in_specs=[pl.BlockSpec(memory_space=pltpu.SMEM)] * 4 + [low, high, low, high],
        out_specs=[whole, whole, pl.BlockSpec((8 * tiles + 8, depth), lambda i: (0, 0))],
        out_shape=[face, face, own],
        name="pack_y",
    )(*coef, owner, phase, phase, solute, solute)


def fill_row(dst, row, phase_row, solute_row, lo, hi):
    start = PAD
    dst[0][row, start : start + W, :] = lo[:W]
    dst[1][row, start : start + W, :] = 2.0 * lo[W:]
    start += W
    for values in phase_row:
        size = values.shape[0]
        dst[0][row, start : start + size, :] = values
        start += size
    dst[0][row, start : start + W, :] = hi[:W]
    dst[1][row, start : start + W, :] = 2.0 * hi[W:]
    start = PAD + W
    for values in solute_row:
        size = values.shape[0]
        dst[1][row, start : start + size, :] = 2.0 * values
        start += size


def pack_x_kernel(own, phase_lo, phase_hi, solute_lo, solute_hi, y_lo, y_hi, _, to_prev, to_next):
    tiles, edge, depth = phase_lo.shape[1], phase_lo.shape[3], phase_lo.shape[4]
    width = tiles * edge + 2 * W
    for out, phase, solute, first in (
        (to_prev, phase_lo, solute_lo, 0),
        (to_next, phase_hi, solute_hi, edge - W),
    ):
        for row in range(W):
            for field, values, half in ((0, phase, 0), (1, solute, W)):
                at = (2 * row + field) * width
                out[at : at + W, :] = y_lo[first + row, half : half + W, :]
                for tile in range(tiles):
                    begin = at + W + tile * edge
                    out[begin : begin + edge, :] = values[0, tile, row]
                out[at + width - W : at + width, :] = y_hi[first + row, half : half + W, :]
        at = 2 * W * width
        out[at : at + 8, :] = y_lo[edge]
        out[at + 8 : at + 16, :] = y_hi[edge]
        out[at + 16 : at + 16 + 8 * tiles, :] = own[: 8 * tiles, :]


def pack_x(phase, solute, own, y_lo, y_hi, after):
    _, tiles, edge, _, depth = phase.shape
    low = pl.BlockSpec((1, tiles, W, edge, depth), lambda i: (0, 0, 0, 0, 0))
    high = pl.BlockSpec((1, tiles, W, edge, depth), lambda i: (0, 0, edge // W - 1, 0, 0))
    side = pl.BlockSpec((edge + 1, 2 * W, depth), lambda i: (0, 0, 0))
    rows = 2 * W * (tiles * edge + 2 * W) + 8 * (tiles + 2)
    out = jax.ShapeDtypeStruct((rows, depth), jnp.float32)
    whole = pl.BlockSpec((rows, depth), lambda i: (0, 0))
    return pl.pallas_call(
        pack_x_kernel,
        grid=(1,),
        in_specs=[pl.BlockSpec((8 * tiles + 8, depth), lambda i: (0, 0)), low, high, low, high, side, side, pl.BlockSpec(memory_space=pl.ANY)],
        out_specs=[whole, whole],
        out_shape=[out, out],
        compiler_params=pltpu.CompilerParams(vmem_limit_bytes=8 * 1024 * 1024),
        name="pack_x",
    )(own, phase, phase, solute, solute, y_lo, y_hi, after)


def update(near_p, near_v, under, mobile, spread, keep):
    p, p_xl, p_xh, p_yl, p_yh = near_p
    v, v_xl, v_xh, v_yl, v_yh = near_v
    depth = p.shape[-1]
    lane = lax.broadcasted_iota(jnp.int32, p.shape, 1)
    first, last = lane == 0, lane == depth - 1
    p_zl = jnp.where(first, p, pltpu.roll(p, 1, 1))
    p_zh = jnp.where(last, p, pltpu.roll(p, depth - 1, 1))
    v_zl = jnp.where(first, v, pltpu.roll(v, 1, 1))
    v_zh = jnp.where(last, v, pltpu.roll(v, depth - 1, 1))
    dx, dy, dz = p_xh - p_xl, p_yh - p_yl, p_zh - p_zl
    qx, qy, qz = dx * dx, dy * dy, dz * dz
    flat = qx + qy
    total = flat + qz
    pairs = qx * qy + flat * qz
    base = total + 4.0
    guess = pl.reciprocal(base, approx=True)
    inverse = guess * (2.0 - base * guess)
    extra = (aniso_strength * total * total - (8.0 * aniso_strength) * pairs) * (inverse * inverse)
    lap_p = (p_xl + p_xh) + (p_yl + p_yh) + (p_zl + p_zh) - 6.0 * p
    sum_v = (v_xl + v_xh) + (v_yl + v_yh) + (v_zl + v_zh)
    well = 1.0 - p * p
    change = mobile * (lap_p + extra * lap_p + well * (p - well * (under + v)))
    return p + change, keep * v + spread * sum_v + change


KINDS = 4


def cells(src_p, src_u, row, start, coefs):
    near = []
    for src in (src_p, src_u):
        near.append(
            (
                src[row, start : start + 8, :],
                src[row - 1, start : start + 8, :],
                src[row + 1, start : start + 8, :],
                src[row, start - 1 : start + 7, :],
                src[row, start + 1 : start + 9, :],
            )
        )
    return update(near[0], near[1], *coefs)


class Plan:
    def __init__(self, pieces, tiles, edge, depth):
        self.pieces, self.tiles, self.edge, self.depth = pieces, tiles, edge, depth
        self.half = pieces // 2
        self.inner = edge - 2 * W
        self.rows = self.inner // self.half
        self.rows_far = (self.inner - 2 * W) // self.half
        self.rows_near = 2 * W // self.half
        self.middle = edge - 16
        self.size = self.rows * self.middle + self.rows_far * 8

    def near_row(self, piece, row, gap):
        index = piece * self.rows_near + row
        return index + jnp.where(index < W, 0, gap)

    def parts(self, far, piece):
        at, found = 0, []
        if far:
            for row in range(self.rows):
                found.append((at, W + piece * self.rows + row, "middle"))
                at += self.middle
            for row in range(self.rows_far):
                found.append((at, 2 * W + piece * self.rows_far + row, "last"))
                at += 8
        else:
            for row in range(self.rows_near):
                found.append((at, self.near_row(piece, row, self.inner), "whole"))
                at += self.edge
            for row in range(self.rows):
                found.append((at, W + piece * self.rows + row, "side"))
                at += 8
            for row in range(self.rows_near):
                found.append((at, W + self.near_row(piece, row, self.inner - 2 * W), "last"))
                at += 8
        assert at == self.size
        return found

    def columns(self, name, tile):
        if name == "whole":
            return 0, self.edge
        if name == "middle":
            return 8, self.middle
        low, high = (tile, 1 - tile) if name == "side" else (1 - tile, tile)
        return low * (self.edge - 8), 8


AUX = 8
UNROLL = 4


def march(first, last, starts, source, target, coefs_of):
    def one_row(row, carry):
        for start in starts:
            new_p, new_u = cells(source[0], source[1], row, start, coefs_of(row, start))
            target[0][row, start : start + 8, :] = new_p
            target[1][row, start : start + 8, :] = new_u
        return carry

    lax.fori_loop(first, last, one_row, 0, unroll=UNROLL)


def inner_kernel(plan, own, phase, solute, *rest):
    tiles, edge, count = plan.tiles, plan.edge, plan.inner // 2
    outs, scratch = rest[: plan.half // 2], rest[plan.half // 2 :]
    pairs = (scratch[:2], scratch[2:])
    mine = lax.rem(lax.axis_index("gy"), plan.half)
    base = mine // (plan.half // 2) * count

    def load_row(row, carry):
        for tile in range(tiles):
            start = PAD + tile * edge
            pairs[0][0][row, start : start + edge, :] = phase[0, tile, base + row]
            pairs[0][1][row, start : start + edge, :] = 2.0 * solute[0, tile, base + row]
        return carry

    lax.fori_loop(0, count + 2 * W, load_row, 0, unroll=UNROLL)

    def coefs_of(row, start):
        tile = (start - PAD) // edge
        return tuple(own[8 * tile + kind : 8 * tile + kind + 1, :] for kind in range(KINDS))

    for step in range(NSTEPS):
        starts = range(PAD, PAD + tiles * edge, 8)
        march(step + 1, count + 2 * W - step - 1, starts, pairs[step % 2], pairs[(step + 1) % 2], coefs_of)
    for index, out in enumerate(outs):
        pack(plan, True, mine ^ index, pairs[NSTEPS % 2], -base, PAD, own, out)


def pack(plan, far, piece, done, row_shift, col_shift, own, out):
    for tile in range(plan.tiles):
        for field, values in enumerate(done):
            begin = (2 * tile + field) * plan.size
            for at, row, name in plan.parts(far, piece):
                col, count = plan.columns(name, tile)
                start = col_shift + tile * plan.edge + col
                cells = values[row + row_shift, start : start + count, :]
                out[begin + at : begin + at + count, :] = 0.5 * cells if field else cells
    tail = 2 * plan.tiles * plan.size
    out[tail : tail + AUX, :] = own[8 * plan.tiles : 8 * plan.tiles + AUX, :]


def run_inner(plan, own, phase, solute):
    rows = plan.inner // 2 + 2 * W
    buffer = pltpu.VMEM((rows, plan.tiles * plan.edge + 2 * PAD, plan.depth), jnp.float32)
    vmem = pl.BlockSpec(memory_space=pltpu.VMEM)
    shape = jax.ShapeDtypeStruct((2 * plan.tiles * plan.size + AUX, plan.depth), jnp.float32)
    return pl.pallas_call(
        functools.partial(inner_kernel, plan),
        in_specs=[vmem] * 3,
        out_specs=[vmem] * (plan.half // 2),
        out_shape=[shape] * (plan.half // 2),
        scratch_shapes=[buffer] * 4,
        compiler_params=pltpu.CompilerParams(vmem_limit_bytes=16 * 1024 * 1024),
        cost_estimate=pl.CostEstimate(flops=10**8, bytes_accessed=24 * 1024 * 1024, transcendentals=0),
        name="inner",
    )(own, phase, solute)


def outer_kernel(plan, own, phase, solute, y_lo, y_hi, x_lo, x_hi, out, *rest):
    tiles, edge, depth, half = plan.tiles, plan.edge, plan.depth, plan.half
    far_outs, scratch = rest[: half // 2], rest[half // 2 :]
    pairs, coefs = (scratch[:2], scratch[2:4]), scratch[4]
    cols = tiles * edge
    width = cols + 2 * W
    for zone, source in ((0, x_lo), (1, None), (2, x_hi)):
        for kind in range(KINDS):
            if source is None:
                parts = [y_lo[edge, kind : kind + 1, :]]
                parts += [own[8 * tile + kind : 8 * tile + kind + 1, :] for tile in range(tiles)]
                parts += [y_hi[edge, kind : kind + 1, :]]
            else:
                at = 2 * W * width + kind
                parts = [source[at : at + 1, :]]
                parts += [source[at + 16 + 8 * tile : at + 17 + 8 * tile, :] for tile in range(tiles)]
                parts += [source[at + 8 : at + 9, :]]
            coefs[zone, kind, :W, :] = jnp.broadcast_to(parts[0], (W, depth))
            for tile in range(tiles):
                begin = W + tile * edge
                coefs[zone, kind, begin : begin + edge, :] = jnp.broadcast_to(parts[1 + tile], (edge, depth))
            coefs[zone, kind, width - W :, :] = jnp.broadcast_to(parts[-1], (W, depth))
    for source, first in ((x_lo, 0), (x_hi, edge + W)):
        for row in range(W):
            for field in range(2):
                at = (2 * row + field) * width
                values = source[at : at + width, :]
                pairs[0][field][first + row, PAD : PAD + width, :] = 2.0 * values if field else values

    def load_row(row, carry):
        fill_row(
            pairs[0],
            W + row,
            [phase[0, tile, row] for tile in range(tiles)],
            [solute[0, tile, row] for tile in range(tiles)],
            y_lo[row],
            y_hi[row],
        )
        return carry

    lax.fori_loop(0, edge, load_row, 0, unroll=UNROLL)

    def coefs_of(zone):
        def found(row, start):
            return tuple(coefs[zone(row), kind, start - PAD : start - PAD + 8, :] for kind in range(KINDS))

        return found

    any_zone = coefs_of(lambda row: jnp.where(row < W, 0, jnp.where(row < W + edge, 1, 2)))

    for step in range(1, NSTEPS + 1):
        left = NSTEPS - step
        shift = W if step == NSTEPS else 0
        starts = range(PAD + shift, PAD + width - shift, 8)
        march(W - left, W + edge + left, starts, pairs[(step - 1) % 2], pairs[step % 2], any_zone)
    done = pairs[NSTEPS % 2]
    mine = lax.rem(lax.axis_index("gy"), half)
    for index, far_out in enumerate(far_outs):
        pack(plan, True, mine ^ (half // 2 + index), done, W, PAD + W, own, far_out)
    for piece in range(half):
        pack(plan, False, piece, done, W, PAD + W, own, out.at[piece])


def run_outer(plan, own, phase, solute, halos):
    tiles, edge, depth = plan.tiles, plan.edge, plan.depth
    width = tiles * edge + 2 * W
    buffer = pltpu.VMEM((edge + 2 * W, width + 2 * PAD, depth), jnp.float32)
    vmem = pl.BlockSpec(memory_space=pltpu.VMEM)
    near = jax.ShapeDtypeStruct((plan.half, 2 * tiles * plan.size + AUX, depth), jnp.float32)
    far = jax.ShapeDtypeStruct((2 * tiles * plan.size + AUX, depth), jnp.float32)
    return pl.pallas_call(
        functools.partial(outer_kernel, plan),
        in_specs=[vmem] * 7,
        out_specs=[vmem] * (1 + plan.half // 2),
        out_shape=[near] + [far] * (plan.half // 2),
        scratch_shapes=[buffer] * 4 + [pltpu.VMEM((3, KINDS, width, depth), jnp.float32)],
        compiler_params=pltpu.CompilerParams(vmem_limit_bytes=16 * 1024 * 1024),
        cost_estimate=pl.CostEstimate(flops=10**8, bytes_accessed=40 * 1024 * 1024, transcendentals=0),
        name="outer",
    )(own, phase, solute, *halos)


def route_kernel(plan, near, *refs):
    pieces, tiles, half, size = plan.pieces, plan.tiles, plan.half, 2 * plan.size
    far, near_out, far_outs, table = refs[:half], refs[half], refs[half + 1 : 2 * half + 1], refs[2 * half + 1]
    held, peers, count = refs[2 * half + 2 :]
    me = lax.axis_index("gy")
    base = me - lax.rem(me, half)
    tail = tiles * size
    for tile in range(tiles):
        for piece in range(half):
            peer = lax.rem(near[piece, tail, tile].astype(jnp.int32), pieces)
            peers[(base + piece) * tiles + tile] = peer
        for index in range(half):
            peer = lax.rem(far[index][tail, tile].astype(jnp.int32), pieces)
            peers[(me ^ (half + index)) * tiles + tile] = peer
    for piece in range(half):
        for tile in range(tiles):
            held[(base + piece) * tiles + tile] = near[piece, tile * size : (tile + 1) * size, :]
    for index in range(half):
        for tile in range(tiles):
            held[(me ^ (half + index)) * tiles + tile] = far[index][tile * size : (tile + 1) * size, :]
    for peer in range(pieces):
        count[peer] = 0
    for home in range(pieces * tiles):
        peer = peers[home]
        slot = count[peer]
        table[peer * tiles + slot] = home
        count[peer] = slot + 1
    for index in range(half):
        for slot in range(tiles):
            far_outs[index][slot] = held[table[(me ^ (half + index)) * tiles + slot]]
            near_out[index, slot] = held[table[(base + index) * tiles + slot]]


def route(plan, near, far):
    tiles, half, size, depth = plan.tiles, plan.half, 2 * plan.size, plan.depth
    vmem = pl.BlockSpec(memory_space=pltpu.VMEM)
    one = jax.ShapeDtypeStruct((tiles, size, depth), jnp.float32)
    count = plan.pieces * tiles
    results = pl.pallas_call(
        functools.partial(route_kernel, plan),
        in_specs=[vmem] * (half + 1),
        out_specs=[vmem] * (half + 1) + [pl.BlockSpec(memory_space=pltpu.SMEM)],
        out_shape=[jax.ShapeDtypeStruct((half, tiles, size, depth), jnp.float32)]
        + [one] * half
        + [jax.ShapeDtypeStruct((count,), jnp.int32)],
        scratch_shapes=[
            pltpu.VMEM((count, size, depth), jnp.float32),
            pltpu.SMEM((count,), jnp.int32),
            pltpu.SMEM((plan.pieces,), jnp.int32),
        ],
        compiler_params=pltpu.CompilerParams(vmem_limit_bytes=16 * 1024 * 1024),
        name="route",
    )(near, *far)
    return results[0], results[1 : half + 1], results[-1]


def settle_kernel(plan, table, near, *refs):
    tiles, half = plan.tiles, plan.half
    far, outs = refs[:half], refs[half:]
    me = lax.axis_index("gy")
    mine = lax.rem(me, half)
    for slot in range(tiles):
        home = table[me * tiles + slot]
        tile = lax.rem(home, tiles)
        at_home = home // (tiles * half) == me // half

        def put(source, piece, is_far, slot=slot, tile=tile):
            for field, out in enumerate(outs):
                for at, row, name in plan.parts(is_far, piece):
                    col, count = plan.columns(name, tile)
                    if not isinstance(col, int):
                        col = pl.multiple_of(col, 8)
                    out[0, slot, row, pl.ds(col, count), :] = source[
                        slot, field * plan.size + at : field * plan.size + at + count, :
                    ]

        def put_all(same, put=put):
            for index in range(half):
                put(near.at[index], index, not same)
                put(far[index], mine ^ index, same)

        @pl.when(at_home)
        def _(put_all=put_all):
            put_all(True)

        @pl.when(jnp.logical_not(at_home))
        def _(put_all=put_all):
            put_all(False)


def settle(plan, table, near, far):
    out = jax.ShapeDtypeStruct((1, plan.tiles, plan.edge, plan.edge, plan.depth), jnp.float32)
    vmem = pl.BlockSpec(memory_space=pltpu.VMEM)
    return pl.pallas_call(
        functools.partial(settle_kernel, plan),
        in_specs=[pl.BlockSpec(memory_space=pltpu.SMEM)] + [vmem] * (plan.half + 1),
        out_specs=[vmem, vmem],
        out_shape=[out, out],
        compiler_params=pltpu.CompilerParams(vmem_limit_bytes=16 * 1024 * 1024),
        name="settle",
    )(table, near, *far)


def ring(axis, step):
    count = lax.axis_size(axis)
    return [(i, (i + step) % count) for i in range(count)]


def swap(values, mask):
    return lax.ppermute(values, "gy", [(i, i ^ mask) for i in range(lax.axis_size("gy"))])


def among_half(plan, values, together):
    def exchange(values):
        groups = [list(range(plan.half)), list(range(plan.half, plan.pieces))]
        return lax.all_to_all(values, "gy", 0, 0, axis_index_groups=groups, tiled=True)

    return lax.cond(together, exchange, exchange, values)


def per_device(phase, solute, undercool, mobility, diffusivity, owner):
    _, tiles, edge, _, depth = phase.shape
    plan = Plan(lax.axis_size("gy"), tiles, edge, depth)
    half = plan.half
    to_prev, to_next, own = pack_y(phase, solute, (undercool, mobility, diffusivity), owner)
    y_lo = lax.ppermute(to_next, "gy", ring("gy", 1))
    y_hi = lax.ppermute(to_prev, "gy", ring("gy", -1))
    first = run_inner(plan, own, phase, solute)
    far = [swap(values, half + index) for index, values in enumerate(first)]
    to_prev, to_next = pack_x(phase, solute, own, y_lo, y_hi, first[0])
    x_lo = lax.ppermute(to_next, "gx", ring("gx", 1))
    x_hi = lax.ppermute(to_prev, "gx", ring("gx", -1))
    near, *second = run_outer(plan, own, phase, solute, (y_lo, y_hi, x_lo, x_hi))
    far += [swap(values, half + half // 2 + index) for index, values in enumerate(second)]
    together = owner[0, 0] >= 0
    near = among_half(plan, near, together)
    near, far, table = route(plan, near, far)
    far = [swap(values, half + index) for index, values in enumerate(far)]
    near = among_half(plan, near, together)
    return tuple(settle(plan, table, near, far))


def solution(mesh):
    tile_spec = P("gx", "gy", None, None, None)
    in_specs = (tile_spec, tile_spec) + (P("gx", "gy"),) * 4
    out_spec = P(("gx", "gy"), None, None, None, None)
    return jax.shard_map(
        per_device, mesh=mesh, in_specs=in_specs, out_specs=(out_spec, out_spec), check_vma=False
    )
```

```python
import functools

import jax
import jax.numpy as jnp
from jax import lax
from jax.experimental import pallas as pl
from jax.experimental.pallas import tpu as pltpu
from jax.sharding import PartitionSpec as P

NSTEPS = 4
W = NSTEPS
PAD = 8

aniso_strength = 0.05


def pack_y_kernel(under, mobile, spread, owner, phase_lo, phase_hi, solute_lo, solute_hi, to_prev, to_next, own):
    edge, depth = phase_lo.shape[2], phase_lo.shape[4]
    tiles = own.shape[0] // 8 - 1
    to_prev[:edge, :W, :] = phase_lo[0, 0, :, :W, :]
    to_prev[:edge, W:, :] = solute_lo[0, 0, :, :W, :]
    to_next[:edge, :W, :] = phase_hi[0, 0, :, W:, :]
    to_next[:edge, W:, :] = solute_hi[0, 0, :, W:, :]
    line = lax.broadcasted_iota(jnp.int32, (8, depth), 0)
    lane = lax.broadcasted_iota(jnp.int32, (8, depth), 1)
    names = jnp.zeros((8, depth), jnp.float32)
    for tile in range(tiles):
        rows = jnp.zeros((8, depth), jnp.float32)
        ready = (2.0 * under[0, tile], mobile[0, tile], spread[0, tile], 1.0 - 6.0 * spread[0, tile])
        for kind, coef in enumerate(ready):
            rows = jnp.where(line == kind, coef, rows)
        own[8 * tile : 8 * tile + 8, :] = rows
        if tile == 0:
            to_prev[edge] = rows
        if tile == tiles - 1:
            to_next[edge] = rows
        names = jnp.where(lane == tile, owner[0, tile].astype(jnp.float32), names)
    own[8 * tiles :, :] = names


def pack_y(phase, solute, coef, owner):
    _, tiles, edge, _, depth = phase.shape
    low = pl.BlockSpec((1, 1, edge, 2 * W, depth), lambda i: (0, 0, 0, 0, 0))
    high = pl.BlockSpec((1, 1, edge, 2 * W, depth), lambda i: (0, tiles - 1, 0, edge // (2 * W) - 1, 0))
    face = jax.ShapeDtypeStruct((edge + 1, 2 * W, depth), jnp.float32)
    own = jax.ShapeDtypeStruct((8 * tiles + 8, depth), jnp.float32)
    whole = pl.BlockSpec((edge + 1, 2 * W, depth), lambda i: (0, 0, 0))
    return pl.pallas_call(
        pack_y_kernel,
        grid=(1,),
        in_specs=[pl.BlockSpec(memory_space=pltpu.SMEM)] * 4 + [low, high, low, high],
        out_specs=[whole, whole, pl.BlockSpec((8 * tiles + 8, depth), lambda i: (0, 0))],
        out_shape=[face, face, own],
        name="pack_y",
    )(*coef, owner, phase, phase, solute, solute)


def fill_row(dst, row, phase_row, solute_row, lo, hi):
    start = PAD
    dst[0][row, start : start + W, :] = lo[:W]
    dst[1][row, start : start + W, :] = 2.0 * lo[W:]
    start += W
    for values in phase_row:
        size = values.shape[0]
        dst[0][row, start : start + size, :] = values
        start += size
    dst[0][row, start : start + W, :] = hi[:W]
    dst[1][row, start : start + W, :] = 2.0 * hi[W:]
    start = PAD + W
    for values in solute_row:
        size = values.shape[0]
        dst[1][row, start : start + size, :] = 2.0 * values
        start += size


def pack_x_kernel(own, phase_lo, phase_hi, solute_lo, solute_hi, y_lo, y_hi, _, to_prev, to_next):
    tiles, edge, depth = phase_lo.shape[1], phase_lo.shape[3], phase_lo.shape[4]
    width = tiles * edge + 2 * W
    for out, phase, solute, first in (
        (to_prev, phase_lo, solute_lo, 0),
        (to_next, phase_hi, solute_hi, edge - W),
    ):
        for row in range(W):
            for field, values, half in ((0, phase, 0), (1, solute, W)):
                at = (2 * row + field) * width
                out[at : at + W, :] = y_lo[first + row, half : half + W, :]
                for tile in range(tiles):
                    begin = at + W + tile * edge
                    out[begin : begin + edge, :] = values[0, tile, row]
                out[at + width - W : at + width, :] = y_hi[first + row, half : half + W, :]
        at = 2 * W * width
        out[at : at + 8, :] = y_lo[edge]
        out[at + 8 : at + 16, :] = y_hi[edge]
        out[at + 16 : at + 16 + 8 * tiles, :] = own[: 8 * tiles, :]


def pack_x(phase, solute, own, y_lo, y_hi, after):
    _, tiles, edge, _, depth = phase.shape
    low = pl.BlockSpec((1, tiles, W, edge, depth), lambda i: (0, 0, 0, 0, 0))
    high = pl.BlockSpec((1, tiles, W, edge, depth), lambda i: (0, 0, edge // W - 1, 0, 0))
    side = pl.BlockSpec((edge + 1, 2 * W, depth), lambda i: (0, 0, 0))
    rows = 2 * W * (tiles * edge + 2 * W) + 8 * (tiles + 2)
    out = jax.ShapeDtypeStruct((rows, depth), jnp.float32)
    whole = pl.BlockSpec((rows, depth), lambda i: (0, 0))
    return pl.pallas_call(
        pack_x_kernel,
        grid=(1,),
        in_specs=[pl.BlockSpec((8 * tiles + 8, depth), lambda i: (0, 0)), low, high, low, high, side, side, pl.BlockSpec(memory_space=pl.ANY)],
        out_specs=[whole, whole],
        out_shape=[out, out],
        compiler_params=pltpu.CompilerParams(vmem_limit_bytes=8 * 1024 * 1024),
        name="pack_x",
    )(own, phase, phase, solute, solute, y_lo, y_hi, after)


def update(near_p, near_v, under, mobile, spread, keep):
    p, p_xl, p_xh, p_yl, p_yh = near_p
    v, v_xl, v_xh, v_yl, v_yh = near_v
    depth = p.shape[-1]
    lane = lax.broadcasted_iota(jnp.int32, p.shape, 1)
    first, last = lane == 0, lane == depth - 1
    p_zl = jnp.where(first, p, pltpu.roll(p, 1, 1))
    p_zh = jnp.where(last, p, pltpu.roll(p, depth - 1, 1))
    v_zl = jnp.where(first, v, pltpu.roll(v, 1, 1))
    v_zh = jnp.where(last, v, pltpu.roll(v, depth - 1, 1))
    dx, dy, dz = p_xh - p_xl, p_yh - p_yl, p_zh - p_zl
    qx, qy, qz = dx * dx, dy * dy, dz * dz
    flat = qx + qy
    total = flat + qz
    pairs = qx * qy + flat * qz
    base = total + 4.0
    guess = pl.reciprocal(base, approx=True)
    inverse = guess * (2.0 - base * guess)
    extra = (aniso_strength * total * total - (8.0 * aniso_strength) * pairs) * (inverse * inverse)
    lap_p = (p_xl + p_xh) + (p_yl + p_yh) + (p_zl + p_zh) - 6.0 * p
    sum_v = (v_xl + v_xh) + (v_yl + v_yh) + (v_zl + v_zh)
    well = 1.0 - p * p
    change = mobile * (lap_p + extra * lap_p + well * (p - well * (under + v)))
    return p + change, keep * v + spread * sum_v + change


KINDS = 4


def cells(src_p, src_u, row, start, coefs):
    near = []
    for src in (src_p, src_u):
        near.append(
            (
                src[row, start : start + 8, :],
                src[row - 1, start : start + 8, :],
                src[row + 1, start : start + 8, :],
                src[row, start - 1 : start + 7, :],
                src[row, start + 1 : start + 9, :],
            )
        )
    return update(near[0], near[1], *coefs)


class Plan:
    def __init__(self, pieces, tiles, edge, depth):
        self.pieces, self.tiles, self.edge, self.depth = pieces, tiles, edge, depth
        self.half = pieces // 2
        self.inner = edge - 2 * W
        self.rows = self.inner // self.half
        self.rows_far = (self.inner - 2 * W) // self.half
        self.rows_near = 2 * W // self.half
        self.middle = edge - 16
        self.size = self.rows * self.middle + self.rows_far * 8

    def near_row(self, piece, row, gap):
        index = piece * self.rows_near + row
        return index + jnp.where(index < W, 0, gap)

    def parts(self, far, piece):
        at, found = 0, []
        if far:
            for row in range(self.rows):
                found.append((at, W + piece * self.rows + row, "middle"))
                at += self.middle
            for row in range(self.rows_far):
                found.append((at, 2 * W + piece * self.rows_far + row, "last"))
                at += 8
        else:
            for row in range(self.rows_near):
                found.append((at, self.near_row(piece, row, self.inner), "whole"))
                at += self.edge
            for row in range(self.rows):
                found.append((at, W + piece * self.rows + row, "side"))
                at += 8
            for row in range(self.rows_near):
                found.append((at, W + self.near_row(piece, row, self.inner - 2 * W), "last"))
                at += 8
        assert at == self.size
        return found

    def columns(self, name, tile):
        if name == "whole":
            return 0, self.edge
        if name == "middle":
            return 8, self.middle
        low, high = (tile, 1 - tile) if name == "side" else (1 - tile, tile)
        return low * (self.edge - 8), 8


AUX = 8
UNROLL = 4


def march(first, last, starts, source, target, coefs_of):
    def one_row(row, carry):
        for start in starts:
            new_p, new_u = cells(source[0], source[1], row, start, coefs_of(row, start))
            target[0][row, start : start + 8, :] = new_p
            target[1][row, start : start + 8, :] = new_u
        return carry

    lax.fori_loop(first, last, one_row, 0, unroll=UNROLL)


def inner_kernel(plan, own, phase, solute, *rest):
    tiles, edge, count = plan.tiles, plan.edge, plan.inner // 2
    outs, scratch = rest[: plan.half // 2], rest[plan.half // 2 :]
    pairs = (scratch[:2], scratch[2:])
    mine = lax.rem(lax.axis_index("gy"), plan.half)
    base = mine // (plan.half // 2) * count

    def load_row(row, carry):
        for tile in range(tiles):
            start = PAD + tile * edge
            pairs[0][0][row, start : start + edge, :] = phase[0, tile, base + row]
            pairs[0][1][row, start : start + edge, :] = 2.0 * solute[0, tile, base + row]
        return carry

    lax.fori_loop(0, count + 2 * W, load_row, 0, unroll=UNROLL)

    def coefs_of(row, start):
        tile = (start - PAD) // edge
        return tuple(own[8 * tile + kind : 8 * tile + kind + 1, :] for kind in range(KINDS))

    for step in range(NSTEPS):
        starts = range(PAD, PAD + tiles * edge, 8)
        march(step + 1, count + 2 * W - step - 1, starts, pairs[step % 2], pairs[(step + 1) % 2], coefs_of)
    for index, out in enumerate(outs):
        pack(plan, True, mine ^ index, pairs[NSTEPS % 2], -base, PAD, own, out)


def pack(plan, far, piece, done, row_shift, col_shift, own, out):
    for tile in range(plan.tiles):
        for field, values in enumerate(done):
            begin = (2 * tile + field) * plan.size
            for at, row, name in plan.parts(far, piece):
                col, count = plan.columns(name, tile)
                start = col_shift + tile * plan.edge + col
                cells = values[row + row_shift, start : start + count, :]
                out[begin + at : begin + at + count, :] = 0.5 * cells if field else cells
    tail = 2 * plan.tiles * plan.size
    out[tail : tail + AUX, :] = own[8 * plan.tiles : 8 * plan.tiles + AUX, :]


def run_inner(plan, own, phase, solute):
    rows = plan.inner // 2 + 2 * W
    buffer = pltpu.VMEM((rows, plan.tiles * plan.edge + 2 * PAD, plan.depth), jnp.float32)
    vmem = pl.BlockSpec(memory_space=pltpu.VMEM)
    shape = jax.ShapeDtypeStruct((2 * plan.tiles * plan.size + AUX, plan.depth), jnp.float32)
    return pl.pallas_call(
        functools.partial(inner_kernel, plan),
        in_specs=[vmem] * 3,
        out_specs=[vmem] * (plan.half // 2),
        out_shape=[shape] * (plan.half // 2),
        scratch_shapes=[buffer] * 4,
        compiler_params=pltpu.CompilerParams(vmem_limit_bytes=16 * 1024 * 1024),
        cost_estimate=pl.CostEstimate(flops=10**8, bytes_accessed=24 * 1024 * 1024, transcendentals=0),
        name="inner",
    )(own, phase, solute)


def outer_kernel(plan, own, phase, solute, y_lo, y_hi, x_lo, x_hi, out, *rest):
    tiles, edge, depth, half = plan.tiles, plan.edge, plan.depth, plan.half
    far_outs, scratch = rest[: half // 2], rest[half // 2 :]
    pairs, coefs = (scratch[:2], scratch[2:4]), scratch[4]
    cols = tiles * edge
    width = cols + 2 * W
    for zone, source in ((0, x_lo), (1, None), (2, x_hi)):
        for kind in range(KINDS):
            if source is None:
                parts = [y_lo[edge, kind : kind + 1, :]]
                parts += [own[8 * tile + kind : 8 * tile + kind + 1, :] for tile in range(tiles)]
                parts += [y_hi[edge, kind : kind + 1, :]]
            else:
                at = 2 * W * width + kind
                parts = [source[at : at + 1, :]]
                parts += [source[at + 16 + 8 * tile : at + 17 + 8 * tile, :] for tile in range(tiles)]
                parts += [source[at + 8 : at + 9, :]]
            coefs[zone, kind, :W, :] = jnp.broadcast_to(parts[0], (W, depth))
            for tile in range(tiles):
                begin = W + tile * edge
                coefs[zone, kind, begin : begin + edge, :] = jnp.broadcast_to(parts[1 + tile], (edge, depth))
            coefs[zone, kind, width - W :, :] = jnp.broadcast_to(parts[-1], (W, depth))
    for source, first in ((x_lo, 0), (x_hi, edge + W)):
        for row in range(W):
            for field in range(2):
                at = (2 * row + field) * width
                values = source[at : at + width, :]
                pairs[0][field][first + row, PAD : PAD + width, :] = 2.0 * values if field else values

    def load_row(row, carry):
        fill_row(
            pairs[0],
            W + row,
            [phase[0, tile, row] for tile in range(tiles)],
            [solute[0, tile, row] for tile in range(tiles)],
            y_lo[row],
            y_hi[row],
        )
        return carry

    lax.fori_loop(0, edge, load_row, 0, unroll=UNROLL)

    def coefs_of(zone):
        def found(row, start):
            return tuple(coefs[zone(row), kind, start - PAD : start - PAD + 8, :] for kind in range(KINDS))

        return found

    any_zone = coefs_of(lambda row: jnp.where(row < W, 0, jnp.where(row < W + edge, 1, 2)))

    for step in range(1, NSTEPS + 1):
        left = NSTEPS - step
        shift = W if step == NSTEPS else 0
        starts = range(PAD + shift, PAD + width - shift, 8)
        march(W - left, W + edge + left, starts, pairs[(step - 1) % 2], pairs[step % 2], any_zone)
    done = pairs[NSTEPS % 2]
    mine = lax.rem(lax.axis_index("gy"), half)
    for index, far_out in enumerate(far_outs):
        pack(plan, True, mine ^ (half // 2 + index), done, W, PAD + W, own, far_out)
    for piece in range(half):
        pack(plan, False, piece, done, W, PAD + W, own, out.at[piece])


def run_outer(plan, own, phase, solute, halos):
    tiles, edge, depth = plan.tiles, plan.edge, plan.depth
    width = tiles * edge + 2 * W
    buffer = pltpu.VMEM((edge + 2 * W, width + 2 * PAD, depth), jnp.float32)
    vmem = pl.BlockSpec(memory_space=pltpu.VMEM)
    near = jax.ShapeDtypeStruct((plan.half, 2 * tiles * plan.size + AUX, depth), jnp.float32)
    far = jax.ShapeDtypeStruct((2 * tiles * plan.size + AUX, depth), jnp.float32)
    return pl.pallas_call(
        functools.partial(outer_kernel, plan),
        in_specs=[vmem] * 7,
        out_specs=[vmem] * (1 + plan.half // 2),
        out_shape=[near] + [far] * (plan.half // 2),
        scratch_shapes=[buffer] * 4 + [pltpu.VMEM((3, KINDS, width, depth), jnp.float32)],
        compiler_params=pltpu.CompilerParams(vmem_limit_bytes=16 * 1024 * 1024),
        cost_estimate=pl.CostEstimate(flops=10**8, bytes_accessed=40 * 1024 * 1024, transcendentals=0),
        name="outer",
    )(own, phase, solute, *halos)


def route_kernel(plan, near, *refs):
    pieces, tiles, half, size = plan.pieces, plan.tiles, plan.half, 2 * plan.size
    far, near_out, far_outs, table = refs[:half], refs[half], refs[half + 1 : 2 * half + 1], refs[2 * half + 1]
    held, peers, count = refs[2 * half + 2 :]
    me = lax.axis_index("gy")
    base = me - lax.rem(me, half)
    tail = tiles * size
    for tile in range(tiles):
        for piece in range(half):
            peer = lax.rem(near[piece, tail, tile].astype(jnp.int32), pieces)
            peers[(base + piece) * tiles + tile] = peer
        for index in range(half):
            peer = lax.rem(far[index][tail, tile].astype(jnp.int32), pieces)
            peers[(me ^ (half + index)) * tiles + tile] = peer
    for piece in range(half):
        for tile in range(tiles):
            held[(base + piece) * tiles + tile] = near[piece, tile * size : (tile + 1) * size, :]
    for index in range(half):
        for tile in range(tiles):
            held[(me ^ (half + index)) * tiles + tile] = far[index][tile * size : (tile + 1) * size, :]
    for peer in range(pieces):
        count[peer] = 0
    for home in range(pieces * tiles):
        peer = peers[home]
        slot = count[peer]
        table[peer * tiles + slot] = home
        count[peer] = slot + 1
    for index in range(half):
        for slot in range(tiles):
            far_outs[index][slot] = held[table[(me ^ (half + index)) * tiles + slot]]
            near_out[index, slot] = held[table[(base + index) * tiles + slot]]


def route(plan, near, far):
    tiles, half, size, depth = plan.tiles, plan.half, 2 * plan.size, plan.depth
    vmem = pl.BlockSpec(memory_space=pltpu.VMEM)
    one = jax.ShapeDtypeStruct((tiles, size, depth), jnp.float32)
    count = plan.pieces * tiles
    results = pl.pallas_call(
        functools.partial(route_kernel, plan),
        in_specs=[vmem] * (half + 1),
        out_specs=[vmem] * (half + 1) + [pl.BlockSpec(memory_space=pltpu.SMEM)],
        out_shape=[jax.ShapeDtypeStruct((half, tiles, size, depth), jnp.float32)]
        + [one] * half
        + [jax.ShapeDtypeStruct((count,), jnp.int32)],
        scratch_shapes=[
            pltpu.VMEM((count, size, depth), jnp.float32),
            pltpu.SMEM((count,), jnp.int32),
            pltpu.SMEM((plan.pieces,), jnp.int32),
        ],
        compiler_params=pltpu.CompilerParams(vmem_limit_bytes=16 * 1024 * 1024),
        name="route",
    )(near, *far)
    return results[0], results[1 : half + 1], results[-1]


def settle_kernel(plan, table, near, *refs):
    tiles, half = plan.tiles, plan.half
    far, outs = refs[:half], refs[half:]
    me = lax.axis_index("gy")
    mine = lax.rem(me, half)
    for slot in range(tiles):
        home = table[me * tiles + slot]
        tile = lax.rem(home, tiles)
        at_home = home // (tiles * half) == me // half

        def put(source, piece, is_far, slot=slot, tile=tile):
            for field, out in enumerate(outs):
                for at, row, name in plan.parts(is_far, piece):
                    col, count = plan.columns(name, tile)
                    if not isinstance(col, int):
                        col = pl.multiple_of(col, 8)
                    out[0, slot, row, pl.ds(col, count), :] = source[
                        slot, field * plan.size + at : field * plan.size + at + count, :
                    ]

        def put_all(same, put=put):
            for index in range(half):
                put(near.at[index], index, not same)
                put(far[index], mine ^ index, same)

        @pl.when(at_home)
        def _(put_all=put_all):
            put_all(True)

        @pl.when(jnp.logical_not(at_home))
        def _(put_all=put_all):
            put_all(False)


def settle(plan, table, near, far):
    out = jax.ShapeDtypeStruct((1, plan.tiles, plan.edge, plan.edge, plan.depth), jnp.float32)
    vmem = pl.BlockSpec(memory_space=pltpu.VMEM)
    return pl.pallas_call(
        functools.partial(settle_kernel, plan),
        in_specs=[pl.BlockSpec(memory_space=pltpu.SMEM)] + [vmem] * (plan.half + 1),
        out_specs=[vmem, vmem],
        out_shape=[out, out],
        compiler_params=pltpu.CompilerParams(vmem_limit_bytes=16 * 1024 * 1024),
        name="settle",
    )(table, near, *far)


def ring(axis, step):
    count = lax.axis_size(axis)
    return [(i, (i + step) % count) for i in range(count)]


def swap(values, mask):
    return lax.ppermute(values, "gy", [(i, i ^ mask) for i in range(lax.axis_size("gy"))])


def exchange_near(plan, values):
    groups = [list(range(plan.half)), list(range(plan.half, plan.pieces))]
    return lax.all_to_all(values, "gy", 0, 0, axis_index_groups=groups, tiled=True)


def exchange_far(plan, index, values):
    return swap(values, plan.half + index)


def at_once(together, exchange, *values):
    return lax.cond(together, exchange, exchange, *values)


def per_device(phase, solute, undercool, mobility, diffusivity, owner):
    _, tiles, edge, _, depth = phase.shape
    plan = Plan(lax.axis_size("gy"), tiles, edge, depth)
    half = plan.half
    to_prev, to_next, own = pack_y(phase, solute, (undercool, mobility, diffusivity), owner)
    y_lo = lax.ppermute(to_next, "gy", ring("gy", 1))
    y_hi = lax.ppermute(to_prev, "gy", ring("gy", -1))
    first = run_inner(plan, own, phase, solute)
    far = [exchange_far(plan, index, values) for index, values in enumerate(first)]
    to_prev, to_next = pack_x(phase, solute, own, y_lo, y_hi, first[0])
    x_lo = lax.ppermute(to_next, "gx", ring("gx", 1))
    x_hi = lax.ppermute(to_prev, "gx", ring("gx", -1))
    near, *second = run_outer(plan, own, phase, solute, (y_lo, y_hi, x_lo, x_hi))
    together = owner[0, 0] >= 0

    def exchange_late(near, *second):
        late = [exchange_far(plan, half // 2 + index, values) for index, values in enumerate(second)]
        return exchange_near(plan, near), late

    near, late = at_once(together, exchange_late, near, *second)
    near, far, table = route(plan, near, far + late)
    far = [exchange_far(plan, index, values) for index, values in enumerate(far)]
    near = at_once(together, functools.partial(exchange_near, plan), near)
    return tuple(settle(plan, table, near, far))


def solution(mesh):
    tile_spec = P("gx", "gy", None, None, None)
    in_specs = (tile_spec, tile_spec) + (P("gx", "gy"),) * 4
    out_spec = P(("gx", "gy"), None, None, None, None)
    return jax.shard_map(
        per_device, mesh=mesh, in_specs=in_specs, out_specs=(out_spec, out_spec), check_vma=False
    )
```

```python
import functools

import jax
import jax.numpy as jnp
from jax import lax
from jax.experimental import pallas as pl
from jax.experimental.pallas import tpu as pltpu
from jax.sharding import PartitionSpec as P

NSTEPS = 4
W = NSTEPS
PAD = 8

aniso_strength = 0.05


def pack_y_kernel(under, mobile, spread, owner, phase_lo, phase_hi, solute_lo, solute_hi, to_prev, to_next, own):
    edge, depth = phase_lo.shape[2], phase_lo.shape[4]
    tiles = own.shape[0] // 8 - 1
    to_prev[:edge, :W, :] = phase_lo[0, 0, :, :W, :]
    to_prev[:edge, W:, :] = solute_lo[0, 0, :, :W, :]
    to_next[:edge, :W, :] = phase_hi[0, 0, :, W:, :]
    to_next[:edge, W:, :] = solute_hi[0, 0, :, W:, :]
    line = lax.broadcasted_iota(jnp.int32, (8, depth), 0)
    lane = lax.broadcasted_iota(jnp.int32, (8, depth), 1)
    names = jnp.zeros((8, depth), jnp.float32)
    for tile in range(tiles):
        rows = jnp.zeros((8, depth), jnp.float32)
        ready = (2.0 * under[0, tile], mobile[0, tile], spread[0, tile], 1.0 - 6.0 * spread[0, tile])
        for kind, coef in enumerate(ready):
            rows = jnp.where(line == kind, coef, rows)
        own[8 * tile : 8 * tile + 8, :] = rows
        if tile == 0:
            to_prev[edge] = rows
        if tile == tiles - 1:
            to_next[edge] = rows
        names = jnp.where(lane == tile, owner[0, tile].astype(jnp.float32), names)
    own[8 * tiles :, :] = names


def pack_y(phase, solute, coef, owner):
    _, tiles, edge, _, depth = phase.shape
    low = pl.BlockSpec((1, 1, edge, 2 * W, depth), lambda i: (0, 0, 0, 0, 0))
    high = pl.BlockSpec((1, 1, edge, 2 * W, depth), lambda i: (0, tiles - 1, 0, edge // (2 * W) - 1, 0))
    face = jax.ShapeDtypeStruct((edge + 1, 2 * W, depth), jnp.float32)
    own = jax.ShapeDtypeStruct((8 * tiles + 8, depth), jnp.float32)
    whole = pl.BlockSpec((edge + 1, 2 * W, depth), lambda i: (0, 0, 0))
    return pl.pallas_call(
        pack_y_kernel,
        grid=(1,),
        in_specs=[pl.BlockSpec(memory_space=pltpu.SMEM)] * 4 + [low, high, low, high],
        out_specs=[whole, whole, pl.BlockSpec((8 * tiles + 8, depth), lambda i: (0, 0))],
        out_shape=[face, face, own],
        name="pack_y",
    )(*coef, owner, phase, phase, solute, solute)


def fill_row(dst, row, phase_row, solute_row, lo, hi):
    start = PAD
    dst[0][row, start : start + W, :] = lo[:W]
    dst[1][row, start : start + W, :] = 2.0 * lo[W:]
    start += W
    for values in phase_row:
        size = values.shape[0]
        dst[0][row, start : start + size, :] = values
        start += size
    dst[0][row, start : start + W, :] = hi[:W]
    dst[1][row, start : start + W, :] = 2.0 * hi[W:]
    start = PAD + W
    for values in solute_row:
        size = values.shape[0]
        dst[1][row, start : start + size, :] = 2.0 * values
        start += size


def pack_x_kernel(own, phase_lo, phase_hi, solute_lo, solute_hi, y_lo, y_hi, _, to_prev, to_next):
    tiles, edge, depth = phase_lo.shape[1], phase_lo.shape[3], phase_lo.shape[4]
    width = tiles * edge + 2 * W
    for out, phase, solute, first in (
        (to_prev, phase_lo, solute_lo, 0),
        (to_next, phase_hi, solute_hi, edge - W),
    ):
        for row in range(W):
            for field, values, half in ((0, phase, 0), (1, solute, W)):
                at = (2 * row + field) * width
                out[at : at + W, :] = y_lo[first + row, half : half + W, :]
                for tile in range(tiles):
                    begin = at + W + tile * edge
                    out[begin : begin + edge, :] = values[0, tile, row]
                out[at + width - W : at + width, :] = y_hi[first + row, half : half + W, :]
        at = 2 * W * width
        out[at : at + 8, :] = y_lo[edge]
        out[at + 8 : at + 16, :] = y_hi[edge]
        out[at + 16 : at + 16 + 8 * tiles, :] = own[: 8 * tiles, :]


def pack_x(phase, solute, own, y_lo, y_hi, after):
    _, tiles, edge, _, depth = phase.shape
    low = pl.BlockSpec((1, tiles, W, edge, depth), lambda i: (0, 0, 0, 0, 0))
    high = pl.BlockSpec((1, tiles, W, edge, depth), lambda i: (0, 0, edge // W - 1, 0, 0))
    side = pl.BlockSpec((edge + 1, 2 * W, depth), lambda i: (0, 0, 0))
    rows = 2 * W * (tiles * edge + 2 * W) + 8 * (tiles + 2)
    out = jax.ShapeDtypeStruct((rows, depth), jnp.float32)
    whole = pl.BlockSpec((rows, depth), lambda i: (0, 0))
    return pl.pallas_call(
        pack_x_kernel,
        grid=(1,),
        in_specs=[pl.BlockSpec((8 * tiles + 8, depth), lambda i: (0, 0)), low, high, low, high, side, side, pl.BlockSpec(memory_space=pl.ANY)],
        out_specs=[whole, whole],
        out_shape=[out, out],
        compiler_params=pltpu.CompilerParams(vmem_limit_bytes=8 * 1024 * 1024),
        name="pack_x",
    )(own, phase, phase, solute, solute, y_lo, y_hi, after)


def update(near_p, near_v, under, mobile, spread, keep):
    p, p_xl, p_xh, p_yl, p_yh = near_p
    v, v_xl, v_xh, v_yl, v_yh = near_v
    depth = p.shape[-1]
    lane = lax.broadcasted_iota(jnp.int32, p.shape, 1)
    first, last = lane == 0, lane == depth - 1
    p_zl = jnp.where(first, p, pltpu.roll(p, 1, 1))
    p_zh = jnp.where(last, p, pltpu.roll(p, depth - 1, 1))
    v_zl = jnp.where(first, v, pltpu.roll(v, 1, 1))
    v_zh = jnp.where(last, v, pltpu.roll(v, depth - 1, 1))
    dx, dy, dz = p_xh - p_xl, p_yh - p_yl, p_zh - p_zl
    qx, qy, qz = dx * dx, dy * dy, dz * dz
    flat = qx + qy
    total = flat + qz
    pairs = qx * qy + flat * qz
    base = total + 4.0
    guess = pl.reciprocal(base, approx=True)
    inverse = guess * (2.0 - base * guess)
    extra = (aniso_strength * total * total - (8.0 * aniso_strength) * pairs) * (inverse * inverse)
    lap_p = (p_xl + p_xh) + (p_yl + p_yh) + (p_zl + p_zh) - 6.0 * p
    sum_v = (v_xl + v_xh) + (v_yl + v_yh) + (v_zl + v_zh)
    well = 1.0 - p * p
    change = mobile * (lap_p + extra * lap_p + well * (p - well * (under + v)))
    return p + change, keep * v + spread * sum_v + change


KINDS = 4


def cells(src_p, src_u, row, start, coefs):
    near = []
    for src in (src_p, src_u):
        near.append(
            (
                src[row, start : start + 8, :],
                src[row - 1, start : start + 8, :],
                src[row + 1, start : start + 8, :],
                src[row, start - 1 : start + 7, :],
                src[row, start + 1 : start + 9, :],
            )
        )
    return update(near[0], near[1], *coefs)


class Plan:
    def __init__(self, pieces, tiles, edge, depth):
        self.pieces, self.tiles, self.edge, self.depth = pieces, tiles, edge, depth
        self.half = pieces // 2
        self.inner = edge - 2 * W
        self.rows = self.inner // self.half
        self.rows_far = (self.inner - 2 * W) // self.half
        self.rows_near = 2 * W // self.half
        self.middle = edge - 16
        self.size = self.rows * self.middle + self.rows_far * 8

    def near_row(self, piece, row, gap):
        index = piece * self.rows_near + row
        return index + jnp.where(index < W, 0, gap)

    def parts(self, far, piece):
        at, found = 0, []
        if far:
            for row in range(self.rows):
                found.append((at, W + piece * self.rows + row, "middle"))
                at += self.middle
            for row in range(self.rows_far):
                found.append((at, 2 * W + piece * self.rows_far + row, "last"))
                at += 8
        else:
            for row in range(self.rows_near):
                found.append((at, self.near_row(piece, row, self.inner), "whole"))
                at += self.edge
            for row in range(self.rows):
                found.append((at, W + piece * self.rows + row, "side"))
                at += 8
            for row in range(self.rows_near):
                found.append((at, W + self.near_row(piece, row, self.inner - 2 * W), "last"))
                at += 8
        assert at == self.size
        return found

    def columns(self, name, tile):
        if name == "whole":
            return 0, self.edge
        if name == "middle":
            return 8, self.middle
        low, high = (tile, 1 - tile) if name == "side" else (1 - tile, tile)
        return low * (self.edge - 8), 8


AUX = 8
UNROLL = 8


def march(count, row_of, starts, source, target, coefs_of):
    def one_row(index, carry):
        row = row_of(index)
        for start in starts:
            new_p, new_u = cells(source[0], source[1], row, start, coefs_of(row, start))
            target[0][row, start : start + 8, :] = new_p
            target[1][row, start : start + 8, :] = new_u
        return carry

    lax.fori_loop(0, count, one_row, 0, unroll=UNROLL)


def inner_kernel(plan, own, phase, solute, *rest):
    tiles, edge, count = plan.tiles, plan.edge, plan.inner // 2
    outs, scratch = rest[: plan.half // 2], rest[plan.half // 2 :]
    pairs = (scratch[:2], scratch[2:])
    mine = lax.rem(lax.axis_index("gy"), plan.half)
    base = mine // (plan.half // 2) * count

    def load_row(row, carry):
        for tile in range(tiles):
            start = PAD + tile * edge
            pairs[0][0][row, start : start + edge, :] = phase[0, tile, base + row]
            pairs[0][1][row, start : start + edge, :] = 2.0 * solute[0, tile, base + row]
        return carry

    lax.fori_loop(0, count + 2 * W, load_row, 0, unroll=UNROLL)

    line = lax.broadcasted_iota(jnp.int32, (8, plan.depth), 0)

    def coefs_of(row, start):
        low, high = (start - PAD) // edge, (start + 7 - PAD) // edge
        rows = [[own[8 * tile + kind : 8 * tile + kind + 1, :] for tile in (low, high)] for kind in range(KINDS)]
        if low == high:
            return tuple(pair[0] for pair in rows)
        return tuple(jnp.where(line < W, *pair) for pair in rows)

    for step in range(NSTEPS):
        margin = 8 if step == NSTEPS - 1 else W
        starts = range(PAD + margin, PAD + tiles * edge - margin, 8)
        rows = count + 2 * W - 2 * (step + 1)
        march(rows, lambda i, step=step: step + 1 + i, starts, pairs[step % 2], pairs[(step + 1) % 2], coefs_of)
    for index, out in enumerate(outs):
        pack(plan, True, mine ^ index, pairs[NSTEPS % 2], -base, PAD, own, out)


def pack(plan, far, piece, done, row_shift, col_shift, own, out):
    for tile in range(plan.tiles):
        for field, values in enumerate(done):
            begin = (2 * tile + field) * plan.size
            for at, row, name in plan.parts(far, piece):
                col, count = plan.columns(name, tile)
                start = col_shift + tile * plan.edge + col
                cells = values[row + row_shift, start : start + count, :]
                out[begin + at : begin + at + count, :] = 0.5 * cells if field else cells
    tail = 2 * plan.tiles * plan.size
    out[tail : tail + AUX, :] = own[8 * plan.tiles : 8 * plan.tiles + AUX, :]


def run_inner(plan, own, phase, solute):
    rows = plan.inner // 2 + 2 * W
    buffer = pltpu.VMEM((rows, plan.tiles * plan.edge + 2 * PAD, plan.depth), jnp.float32)
    vmem = pl.BlockSpec(memory_space=pltpu.VMEM)
    shape = jax.ShapeDtypeStruct((2 * plan.tiles * plan.size + AUX, plan.depth), jnp.float32)
    return pl.pallas_call(
        functools.partial(inner_kernel, plan),
        in_specs=[vmem] * 3,
        out_specs=[vmem] * (plan.half // 2),
        out_shape=[shape] * (plan.half // 2),
        scratch_shapes=[buffer] * 4,
        compiler_params=pltpu.CompilerParams(vmem_limit_bytes=16 * 1024 * 1024),
        cost_estimate=pl.CostEstimate(flops=10**8, bytes_accessed=24 * 1024 * 1024, transcendentals=0),
        name="inner",
    )(own, phase, solute)


def outer_kernel(plan, own, phase, solute, y_lo, y_hi, x_lo, x_hi, out, *rest):
    tiles, edge, depth, half = plan.tiles, plan.edge, plan.depth, plan.half
    far_outs, scratch = rest[: half // 2], rest[half // 2 :]
    pairs, coefs = (scratch[:2], scratch[2:4]), scratch[4]
    cols = tiles * edge
    width = cols + 2 * W
    for zone, source in ((0, x_lo), (1, None), (2, x_hi)):
        for kind in range(KINDS):
            if source is None:
                parts = [y_lo[edge, kind : kind + 1, :]]
                parts += [own[8 * tile + kind : 8 * tile + kind + 1, :] for tile in range(tiles)]
                parts += [y_hi[edge, kind : kind + 1, :]]
            else:
                at = 2 * W * width + kind
                parts = [source[at : at + 1, :]]
                parts += [source[at + 16 + 8 * tile : at + 17 + 8 * tile, :] for tile in range(tiles)]
                parts += [source[at + 8 : at + 9, :]]
            coefs[zone, kind, :W, :] = jnp.broadcast_to(parts[0], (W, depth))
            for tile in range(tiles):
                begin = W + tile * edge
                coefs[zone, kind, begin : begin + edge, :] = jnp.broadcast_to(parts[1 + tile], (edge, depth))
            coefs[zone, kind, width - W :, :] = jnp.broadcast_to(parts[-1], (W, depth))
    for source, first in ((x_lo, 0), (x_hi, edge + W)):
        for row in range(W):
            for field in range(2):
                at = (2 * row + field) * width
                values = source[at : at + width, :]
                pairs[0][field][first + row, PAD : PAD + width, :] = 2.0 * values if field else values

    def load_row(row, carry):
        fill_row(
            pairs[0],
            W + row,
            [phase[0, tile, row] for tile in range(tiles)],
            [solute[0, tile, row] for tile in range(tiles)],
            y_lo[row],
            y_hi[row],
        )
        return carry

    lax.fori_loop(0, edge, load_row, 0, unroll=UNROLL)

    def coefs_of(zone):
        def found(row, start):
            return tuple(coefs[zone(row), kind, start - PAD : start - PAD + 8, :] for kind in range(KINDS))

        return found

    any_zone = coefs_of(lambda row: jnp.where(row < W, 0, jnp.where(row < W + edge, 1, 2)))

    own_zone = coefs_of(lambda row: 1)
    mine = lax.rem(lax.axis_index("gy"), half)
    made = plan.inner // 2
    first_made = 2 * W + mine // (half // 2) * made

    def blocks(first, last):
        low, high = (first + W - shift) // 8 * 8, -(-(last + W - shift) // 8) * 8
        return list(range(PAD + shift + low, PAD + shift + high, 8))

    for step in range(1, NSTEPS + 1):
        source, target = pairs[(step - 1) % 2], pairs[step % 2]
        left = NSTEPS - step
        shift = W if step == NSTEPS else 0
        whole = blocks(-left, cols + left)
        ends = blocks(-left, 8 + left) + blocks(cols - 8 - left, cols + left)
        for tile in range(tiles):
            col, count = plan.columns("last", tile)
            ends += blocks(tile * edge + col - left, tile * edge + col + count + left)
        gap, gap_rows = first_made + left, made - 2 * left

        def outside(index, left=left, gap=gap, gap_rows=gap_rows):
            row = W - left + index
            return row + jnp.where(row < gap, 0, gap_rows)

        march(edge + 2 * left - gap_rows, outside, whole, source, target, any_zone)
        march(gap_rows, lambda i, gap=gap: gap + i, sorted(set(ends)), source, target, own_zone)
    done = pairs[NSTEPS % 2]
    for index, far_out in enumerate(far_outs):
        pack(plan, True, mine ^ (half // 2 + index), done, W, PAD + W, own, far_out)
    for piece in range(half):
        pack(plan, False, piece, done, W, PAD + W, own, out.at[piece])


def run_outer(plan, own, phase, solute, halos):
    tiles, edge, depth = plan.tiles, plan.edge, plan.depth
    width = tiles * edge + 2 * W
    buffer = pltpu.VMEM((edge + 2 * W, width + 2 * PAD, depth), jnp.float32)
    vmem = pl.BlockSpec(memory_space=pltpu.VMEM)
    near = jax.ShapeDtypeStruct((plan.half, 2 * tiles * plan.size + AUX, depth), jnp.float32)
    far = jax.ShapeDtypeStruct((2 * tiles * plan.size + AUX, depth), jnp.float32)
    return pl.pallas_call(
        functools.partial(outer_kernel, plan),
        in_specs=[vmem] * 7,
        out_specs=[vmem] * (1 + plan.half // 2),
        out_shape=[near] + [far] * (plan.half // 2),
        scratch_shapes=[buffer] * 4 + [pltpu.VMEM((3, KINDS, width, depth), jnp.float32)],
        compiler_params=pltpu.CompilerParams(vmem_limit_bytes=16 * 1024 * 1024),
        cost_estimate=pl.CostEstimate(flops=10**8, bytes_accessed=40 * 1024 * 1024, transcendentals=0),
        name="outer",
    )(own, phase, solute, *halos)


def route_kernel(plan, near, *refs):
    pieces, tiles, half, size = plan.pieces, plan.tiles, plan.half, 2 * plan.size
    far, near_out, far_outs, table = refs[:half], refs[half], refs[half + 1 : 2 * half + 1], refs[2 * half + 1]
    held, peers, count = refs[2 * half + 2 :]
    me = lax.axis_index("gy")
    base = me - lax.rem(me, half)
    tail = tiles * size
    for tile in range(tiles):
        for piece in range(half):
            peer = lax.rem(near[piece, tail, tile].astype(jnp.int32), pieces)
            peers[(base + piece) * tiles + tile] = peer
        for index in range(half):
            peer = lax.rem(far[index][tail, tile].astype(jnp.int32), pieces)
            peers[(me ^ (half + index)) * tiles + tile] = peer
    for piece in range(half):
        for tile in range(tiles):
            held[(base + piece) * tiles + tile] = near[piece, tile * size : (tile + 1) * size, :]
    for index in range(half):
        for tile in range(tiles):
            held[(me ^ (half + index)) * tiles + tile] = far[index][tile * size : (tile + 1) * size, :]
    for peer in range(pieces):
        count[peer] = 0
    for home in range(pieces * tiles):
        peer = peers[home]
        slot = count[peer]
        table[peer * tiles + slot] = home
        count[peer] = slot + 1
    for index in range(half):
        for slot in range(tiles):
            far_outs[index][slot] = held[table[(me ^ (half + index)) * tiles + slot]]
            near_out[index, slot] = held[table[(base + index) * tiles + slot]]


def route(plan, near, far):
    tiles, half, size, depth = plan.tiles, plan.half, 2 * plan.size, plan.depth
    vmem = pl.BlockSpec(memory_space=pltpu.VMEM)
    one = jax.ShapeDtypeStruct((tiles, size, depth), jnp.float32)
    count = plan.pieces * tiles
    results = pl.pallas_call(
        functools.partial(route_kernel, plan),
        in_specs=[vmem] * (half + 1),
        out_specs=[vmem] * (half + 1) + [pl.BlockSpec(memory_space=pltpu.SMEM)],
        out_shape=[jax.ShapeDtypeStruct((half, tiles, size, depth), jnp.float32)]
        + [one] * half
        + [jax.ShapeDtypeStruct((count,), jnp.int32)],
        scratch_shapes=[
            pltpu.VMEM((count, size, depth), jnp.float32),
            pltpu.SMEM((count,), jnp.int32),
            pltpu.SMEM((plan.pieces,), jnp.int32),
        ],
        compiler_params=pltpu.CompilerParams(vmem_limit_bytes=16 * 1024 * 1024),
        name="route",
    )(near, *far)
    return results[0], results[1 : half + 1], results[-1]


def settle_kernel(plan, table, near, *refs):
    tiles, half = plan.tiles, plan.half
    far, outs, (ready, sems) = refs[:half], refs[half : half + 2], refs[half + 2 :]
    me = lax.axis_index("gy")
    mine = lax.rem(me, half)
    copies = []
    for slot in range(tiles):
        home = table[me * tiles + slot]
        tile = lax.rem(home, tiles)
        at_home = home // (tiles * half) == me // half

        def put(source, piece, is_far, slot=slot, tile=tile):
            for field in range(2):
                for at, row, name in plan.parts(is_far, piece):
                    col, count = plan.columns(name, tile)
                    if not isinstance(col, int):
                        col = pl.multiple_of(col, 8)
                    ready[field, slot, row, pl.ds(col, count), :] = source[
                        slot, field * plan.size + at : field * plan.size + at + count, :
                    ]

        def put_all(same, put=put):
            for index in range(half):
                put(near.at[index], index, not same)
                put(far[index], mine ^ index, same)

        @pl.when(at_home)
        def _(put_all=put_all):
            put_all(True)

        @pl.when(jnp.logical_not(at_home))
        def _(put_all=put_all):
            put_all(False)

        for field, out in enumerate(outs):
            copy = pltpu.make_async_copy(ready.at[field, slot], out.at[0, slot], sems.at[field, slot])
            copy.start()
            copies.append(copy)
    for copy in copies:
        copy.wait()


def settle(plan, table, near, far):
    tiles, edge, depth = plan.tiles, plan.edge, plan.depth
    out = jax.ShapeDtypeStruct((1, tiles, edge, edge, depth), jnp.float32)
    vmem = pl.BlockSpec(memory_space=pltpu.VMEM)
    return pl.pallas_call(
        functools.partial(settle_kernel, plan),
        in_specs=[pl.BlockSpec(memory_space=pltpu.SMEM)] + [vmem] * (plan.half + 1),
        out_specs=[pl.BlockSpec(memory_space=pl.ANY)] * 2,
        out_shape=[out, out],
        scratch_shapes=[
            pltpu.VMEM((2, tiles, edge, edge, depth), jnp.float32),
            pltpu.SemaphoreType.DMA((2, tiles)),
        ],
        compiler_params=pltpu.CompilerParams(vmem_limit_bytes=16 * 1024 * 1024),
        name="settle",
    )(table, near, *far)


def ring(axis, step):
    count = lax.axis_size(axis)
    return [(i, (i + step) % count) for i in range(count)]


def swap(values, mask):
    return lax.ppermute(values, "gy", [(i, i ^ mask) for i in range(lax.axis_size("gy"))])


def among_half(plan, values, together):
    def exchange(values):
        groups = [list(range(plan.half)), list(range(plan.half, plan.pieces))]
        return lax.all_to_all(values, "gy", 0, 0, axis_index_groups=groups, tiled=True)

    return lax.cond(together, exchange, exchange, values)


def per_device(phase, solute, undercool, mobility, diffusivity, owner):
    _, tiles, edge, _, depth = phase.shape
    plan = Plan(lax.axis_size("gy"), tiles, edge, depth)
    half = plan.half
    to_prev, to_next, own = pack_y(phase, solute, (undercool, mobility, diffusivity), owner)
    y_lo = lax.ppermute(to_next, "gy", ring("gy", 1))
    y_hi = lax.ppermute(to_prev, "gy", ring("gy", -1))
    first = run_inner(plan, own, phase, solute)
    far = [swap(values, half + index) for index, values in enumerate(first)]
    to_prev, to_next = pack_x(phase, solute, own, y_lo, y_hi, first[0])
    x_lo = lax.ppermute(to_next, "gx", ring("gx", 1))
    x_hi = lax.ppermute(to_prev, "gx", ring("gx", -1))
    near, *second = run_outer(plan, own, phase, solute, (y_lo, y_hi, x_lo, x_hi))
    far += [swap(values, half + half // 2 + index) for index, values in enumerate(second)]
    together = owner[0, 0] >= 0
    near = among_half(plan, near, together)
    near, far, table = route(plan, near, far)
    far = [swap(values, half + index) for index, values in enumerate(far)]
    near = among_half(plan, near, together)
    return tuple(settle(plan, table, near, far))


def solution(mesh):
    tile_spec = P("gx", "gy", None, None, None)
    in_specs = (tile_spec, tile_spec) + (P("gx", "gy"),) * 4
    out_spec = P(("gx", "gy"), None, None, None, None)
    return jax.shard_map(
        per_device, mesh=mesh, in_specs=in_specs, out_specs=(out_spec, out_spec), check_vma=False
    )
```

```python
import functools

import jax
import jax.numpy as jnp
from jax import lax
from jax.experimental import pallas as pl
from jax.experimental.pallas import tpu as pltpu
from jax.sharding import PartitionSpec as P

NSTEPS = 4
W = NSTEPS
PAD = 8

aniso_strength = 0.05


def pack_y_kernel(under, mobile, spread, owner, phase_lo, phase_hi, solute_lo, solute_hi, to_prev, to_next, own):
    edge, depth = phase_lo.shape[2], phase_lo.shape[4]
    tiles = own.shape[0] // 8 - 1
    to_prev[:edge, :W, :] = phase_lo[0, 0, :, :W, :]
    to_prev[:edge, W:, :] = solute_lo[0, 0, :, :W, :]
    to_next[:edge, :W, :] = phase_hi[0, 0, :, W:, :]
    to_next[:edge, W:, :] = solute_hi[0, 0, :, W:, :]
    line = lax.broadcasted_iota(jnp.int32, (8, depth), 0)
    lane = lax.broadcasted_iota(jnp.int32, (8, depth), 1)
    names = jnp.zeros((8, depth), jnp.float32)
    for tile in range(tiles):
        rows = jnp.zeros((8, depth), jnp.float32)
        ready = (2.0 * under[0, tile], mobile[0, tile], spread[0, tile], 1.0 - 6.0 * spread[0, tile])
        for kind, coef in enumerate(ready):
            rows = jnp.where(line == kind, coef, rows)
        own[8 * tile : 8 * tile + 8, :] = rows
        if tile == 0:
            to_prev[edge] = rows
        if tile == tiles - 1:
            to_next[edge] = rows
        names = jnp.where(lane == tile, owner[0, tile].astype(jnp.float32), names)
    own[8 * tiles :, :] = names


def pack_y(phase, solute, coef, owner):
    _, tiles, edge, _, depth = phase.shape
    low = pl.BlockSpec((1, 1, edge, 2 * W, depth), lambda i: (0, 0, 0, 0, 0))
    high = pl.BlockSpec((1, 1, edge, 2 * W, depth), lambda i: (0, tiles - 1, 0, edge // (2 * W) - 1, 0))
    face = jax.ShapeDtypeStruct((edge + 1, 2 * W, depth), jnp.float32)
    own = jax.ShapeDtypeStruct((8 * tiles + 8, depth), jnp.float32)
    whole = pl.BlockSpec((edge + 1, 2 * W, depth), lambda i: (0, 0, 0))
    return pl.pallas_call(
        pack_y_kernel,
        grid=(1,),
        in_specs=[pl.BlockSpec(memory_space=pltpu.SMEM)] * 4 + [low, high, low, high],
        out_specs=[whole, whole, pl.BlockSpec((8 * tiles + 8, depth), lambda i: (0, 0))],
        out_shape=[face, face, own],
        name="pack_y",
    )(*coef, owner, phase, phase, solute, solute)


def fill_row(dst, row, phase_row, solute_row, lo, hi):
    start = PAD
    dst[0][row, start : start + W, :] = lo[:W]
    dst[1][row, start : start + W, :] = 2.0 * lo[W:]
    start += W
    for values in phase_row:
        size = values.shape[0]
        dst[0][row, start : start + size, :] = values
        start += size
    dst[0][row, start : start + W, :] = hi[:W]
    dst[1][row, start : start + W, :] = 2.0 * hi[W:]
    start = PAD + W
    for values in solute_row:
        size = values.shape[0]
        dst[1][row, start : start + size, :] = 2.0 * values
        start += size


def pack_x_kernel(own, phase_lo, phase_hi, solute_lo, solute_hi, y_lo, y_hi, _, to_prev, to_next):
    tiles, edge, depth = phase_lo.shape[1], phase_lo.shape[3], phase_lo.shape[4]
    width = tiles * edge + 2 * W
    for out, phase, solute, first in (
        (to_prev, phase_lo, solute_lo, 0),
        (to_next, phase_hi, solute_hi, edge - W),
    ):
        for row in range(W):
            for field, values, half in ((0, phase, 0), (1, solute, W)):
                at = (2 * row + field) * width
                out[at : at + W, :] = y_lo[first + row, half : half + W, :]
                for tile in range(tiles):
                    begin = at + W + tile * edge
                    out[begin : begin + edge, :] = values[0, tile, row]
                out[at + width - W : at + width, :] = y_hi[first + row, half : half + W, :]
        at = 2 * W * width
        out[at : at + 8, :] = y_lo[edge]
        out[at + 8 : at + 16, :] = y_hi[edge]
        out[at + 16 : at + 16 + 8 * tiles, :] = own[: 8 * tiles, :]


def pack_x(phase, solute, own, y_lo, y_hi, after):
    _, tiles, edge, _, depth = phase.shape
    low = pl.BlockSpec((1, tiles, W, edge, depth), lambda i: (0, 0, 0, 0, 0))
    high = pl.BlockSpec((1, tiles, W, edge, depth), lambda i: (0, 0, edge // W - 1, 0, 0))
    side = pl.BlockSpec((edge + 1, 2 * W, depth), lambda i: (0, 0, 0))
    rows = 2 * W * (tiles * edge + 2 * W) + 8 * (tiles + 2)
    out = jax.ShapeDtypeStruct((rows, depth), jnp.float32)
    whole = pl.BlockSpec((rows, depth), lambda i: (0, 0))
    return pl.pallas_call(
        pack_x_kernel,
        grid=(1,),
        in_specs=[pl.BlockSpec((8 * tiles + 8, depth), lambda i: (0, 0)), low, high, low, high, side, side, pl.BlockSpec(memory_space=pl.ANY)],
        out_specs=[whole, whole],
        out_shape=[out, out],
        compiler_params=pltpu.CompilerParams(vmem_limit_bytes=8 * 1024 * 1024),
        name="pack_x",
    )(own, phase, phase, solute, solute, y_lo, y_hi, after)


def update(near_p, near_v, under, mobile, spread, keep):
    p, p_xl, p_xh, p_yl, p_yh = near_p
    v, v_xl, v_xh, v_yl, v_yh = near_v
    depth = p.shape[-1]
    lane = lax.broadcasted_iota(jnp.int32, p.shape, 1)
    first, last = lane == 0, lane == depth - 1
    p_zl = jnp.where(first, p, pltpu.roll(p, 1, 1))
    p_zh = jnp.where(last, p, pltpu.roll(p, depth - 1, 1))
    v_zl = jnp.where(first, v, pltpu.roll(v, 1, 1))
    v_zh = jnp.where(last, v, pltpu.roll(v, depth - 1, 1))
    dx, dy, dz = p_xh - p_xl, p_yh - p_yl, p_zh - p_zl
    qx, qy, qz = dx * dx, dy * dy, dz * dz
    flat = qx + qy
    total = flat + qz
    pairs = qx * qy + flat * qz
    base = total + 4.0
    guess = pl.reciprocal(base, approx=True)
    inverse = guess * (2.0 - base * guess)
    extra = (aniso_strength * total * total - (8.0 * aniso_strength) * pairs) * (inverse * inverse)
    lap_p = (p_xl + p_xh) + (p_yl + p_yh) + (p_zl + p_zh) - 6.0 * p
    sum_v = (v_xl + v_xh) + (v_yl + v_yh) + (v_zl + v_zh)
    well = 1.0 - p * p
    change = mobile * (lap_p + extra * lap_p + well * (p - well * (under + v)))
    return p + change, keep * v + spread * sum_v + change


KINDS = 4


def cells(src_p, src_u, row, start, coefs):
    near = []
    for src in (src_p, src_u):
        near.append(
            (
                src[row, start : start + 8, :],
                src[row - 1, start : start + 8, :],
                src[row + 1, start : start + 8, :],
                src[row, start - 1 : start + 7, :],
                src[row, start + 1 : start + 9, :],
            )
        )
    return update(near[0], near[1], *coefs)


class Plan:
    def __init__(self, pieces, tiles, edge, depth):
        self.pieces, self.tiles, self.edge, self.depth = pieces, tiles, edge, depth
        self.half = pieces // 2
        self.inner = edge - 2 * W
        self.rows = self.inner // self.half
        self.rows_far = (self.inner - 2 * W) // self.half
        self.rows_near = 2 * W // self.half
        self.middle = edge - 16
        self.size = self.rows * self.middle + self.rows_far * 8

    def near_row(self, piece, row, gap):
        index = piece * self.rows_near + row
        return index + jnp.where(index < W, 0, gap)

    def parts(self, far, piece):
        at, found = 0, []
        if far:
            for row in range(self.rows):
                found.append((at, W + piece * self.rows + row, "middle"))
                at += self.middle
            for row in range(self.rows_far):
                found.append((at, 2 * W + piece * self.rows_far + row, "last"))
                at += 8
        else:
            for row in range(self.rows_near):
                found.append((at, self.near_row(piece, row, self.inner), "whole"))
                at += self.edge
            for row in range(self.rows):
                found.append((at, W + piece * self.rows + row, "side"))
                at += 8
            for row in range(self.rows_near):
                found.append((at, W + self.near_row(piece, row, self.inner - 2 * W), "last"))
                at += 8
        assert at == self.size
        return found

    def columns(self, name, tile):
        if name == "whole":
            return 0, self.edge
        if name == "middle":
            return 8, self.middle
        low, high = (tile, 1 - tile) if name == "side" else (1 - tile, tile)
        return low * (self.edge - 8), 8


AUX = 8
UNROLL = 8


def march(count, row_of, starts, source, target, coefs_of):
    def one_row(index, carry):
        row = row_of(index)
        for start in starts:
            new_p, new_u = cells(source[0], source[1], row, start, coefs_of(row, start))
            target[0][row, start : start + 8, :] = new_p
            target[1][row, start : start + 8, :] = new_u
        return carry

    lax.fori_loop(0, count, one_row, 0, unroll=UNROLL)


def inner_kernel(plan, own, phase, solute, *rest):
    tiles, edge, count = plan.tiles, plan.edge, plan.inner // 2
    outs, scratch = rest[: plan.half // 2], rest[plan.half // 2 :]
    pairs = (scratch[:2], scratch[2:])
    mine = lax.rem(lax.axis_index("gy"), plan.half)
    base = mine // (plan.half // 2) * count

    def load_row(row, carry):
        for tile in range(tiles):
            start = PAD + tile * edge
            pairs[0][0][row, start : start + edge, :] = phase[0, tile, base + row]
            pairs[0][1][row, start : start + edge, :] = 2.0 * solute[0, tile, base + row]
        return carry

    lax.fori_loop(0, count + 2 * W, load_row, 0, unroll=UNROLL)

    line = lax.broadcasted_iota(jnp.int32, (8, plan.depth), 0)

    def coefs_of(row, start):
        low, high = (start - PAD) // edge, (start + 7 - PAD) // edge
        rows = [[own[8 * tile + kind : 8 * tile + kind + 1, :] for tile in (low, high)] for kind in range(KINDS)]
        if low == high:
            return tuple(pair[0] for pair in rows)
        return tuple(jnp.where(line < W, *pair) for pair in rows)

    for step in range(NSTEPS):
        margin = 8 if step == NSTEPS - 1 else W
        starts = range(PAD + margin, PAD + tiles * edge - margin, 8)
        rows = count + 2 * W - 2 * (step + 1)
        march(rows, lambda i, step=step: step + 1 + i, starts, pairs[step % 2], pairs[(step + 1) % 2], coefs_of)
    for index, out in enumerate(outs):
        pack(plan, True, mine ^ index, pairs[NSTEPS % 2], -base, PAD, own, out)


def pack(plan, far, piece, done, row_shift, col_shift, own, out):
    for tile in range(plan.tiles):
        for field, values in enumerate(done):
            begin = (2 * tile + field) * plan.size
            for at, row, name in plan.parts(far, piece):
                col, count = plan.columns(name, tile)
                start = col_shift + tile * plan.edge + col
                cells = values[row + row_shift, start : start + count, :]
                out[begin + at : begin + at + count, :] = 0.5 * cells if field else cells
    tail = 2 * plan.tiles * plan.size
    out[tail : tail + AUX, :] = own[8 * plan.tiles : 8 * plan.tiles + AUX, :]


def run_inner(plan, own, phase, solute):
    rows = plan.inner // 2 + 2 * W
    buffer = pltpu.VMEM((rows, plan.tiles * plan.edge + 2 * PAD, plan.depth), jnp.float32)
    vmem = pl.BlockSpec(memory_space=pltpu.VMEM)
    shape = jax.ShapeDtypeStruct((2 * plan.tiles * plan.size + AUX, plan.depth), jnp.float32)
    return pl.pallas_call(
        functools.partial(inner_kernel, plan),
        in_specs=[vmem] * 3,
        out_specs=[vmem] * (plan.half // 2),
        out_shape=[shape] * (plan.half // 2),
        scratch_shapes=[buffer] * 4,
        compiler_params=pltpu.CompilerParams(vmem_limit_bytes=16 * 1024 * 1024),
        cost_estimate=pl.CostEstimate(flops=10**8, bytes_accessed=24 * 1024 * 1024, transcendentals=0),
        name="inner",
    )(own, phase, solute)


def outer_kernel(plan, own, phase, solute, y_lo, y_hi, x_lo, x_hi, out, *rest):
    tiles, edge, depth, half = plan.tiles, plan.edge, plan.depth, plan.half
    far_outs, scratch = rest[: half // 2], rest[half // 2 :]
    pairs, coefs = (scratch[:2], scratch[2:4]), scratch[4]
    cols = tiles * edge
    width = cols + 2 * W
    for zone, source in ((0, x_lo), (1, None), (2, x_hi)):
        for kind in range(KINDS):
            if source is None:
                parts = [y_lo[edge, kind : kind + 1, :]]
                parts += [own[8 * tile + kind : 8 * tile + kind + 1, :] for tile in range(tiles)]
                parts += [y_hi[edge, kind : kind + 1, :]]
            else:
                at = 2 * W * width + kind
                parts = [source[at : at + 1, :]]
                parts += [source[at + 16 + 8 * tile : at + 17 + 8 * tile, :] for tile in range(tiles)]
                parts += [source[at + 8 : at + 9, :]]
            coefs[zone, kind, :W, :] = jnp.broadcast_to(parts[0], (W, depth))
            for tile in range(tiles):
                begin = W + tile * edge
                coefs[zone, kind, begin : begin + edge, :] = jnp.broadcast_to(parts[1 + tile], (edge, depth))
            coefs[zone, kind, width - W :, :] = jnp.broadcast_to(parts[-1], (W, depth))
    for source, first in ((x_lo, 0), (x_hi, edge + W)):
        for row in range(W):
            for field in range(2):
                at = (2 * row + field) * width
                values = source[at : at + width, :]
                pairs[0][field][first + row, PAD : PAD + width, :] = 2.0 * values if field else values

    def load_row(row, carry):
        fill_row(
            pairs[0],
            W + row,
            [phase[0, tile, row] for tile in range(tiles)],
            [solute[0, tile, row] for tile in range(tiles)],
            y_lo[row],
            y_hi[row],
        )
        return carry

    lax.fori_loop(0, edge, load_row, 0, unroll=UNROLL)

    def coefs_of(zone):
        def found(row, start):
            return tuple(coefs[zone(row), kind, start - PAD : start - PAD + 8, :] for kind in range(KINDS))

        return found

    any_zone = coefs_of(lambda row: jnp.where(row < W, 0, jnp.where(row < W + edge, 1, 2)))

    own_zone = coefs_of(lambda row: 1)
    mine = lax.rem(lax.axis_index("gy"), half)
    made = plan.inner // 2
    first_made = 2 * W + mine // (half // 2) * made

    def blocks(first, last):
        low, high = (first + W - shift) // 8 * 8, -(-(last + W - shift) // 8) * 8
        return list(range(PAD + shift + low, PAD + shift + high, 8))

    for step in range(1, NSTEPS + 1):
        source, target = pairs[(step - 1) % 2], pairs[step % 2]
        left = NSTEPS - step
        shift = W if step == NSTEPS else 0
        whole = blocks(-left, cols + left)
        ends = blocks(-left, 8 + left) + blocks(cols - 8 - left, cols + left)
        for tile in range(tiles):
            col, count = plan.columns("last", tile)
            ends += blocks(tile * edge + col - left, tile * edge + col + count + left)
        gap, gap_rows = first_made + left, made - 2 * left

        def outside(index, left=left, gap=gap, gap_rows=gap_rows):
            row = W - left + index
            return row + jnp.where(row < gap, 0, gap_rows)

        march(edge + 2 * left - gap_rows, outside, whole, source, target, any_zone)
        march(gap_rows, lambda i, gap=gap: gap + i, sorted(set(ends)), source, target, own_zone)
    done = pairs[NSTEPS % 2]
    for index, far_out in enumerate(far_outs):
        pack(plan, True, mine ^ (half // 2 + index), done, W, PAD + W, own, far_out)
    for piece in range(half):
        pack(plan, False, piece, done, W, PAD + W, own, out.at[piece])


def run_outer(plan, own, phase, solute, halos):
    tiles, edge, depth = plan.tiles, plan.edge, plan.depth
    width = tiles * edge + 2 * W
    buffer = pltpu.VMEM((edge + 2 * W, width + 2 * PAD, depth), jnp.float32)
    vmem = pl.BlockSpec(memory_space=pltpu.VMEM)
    near = jax.ShapeDtypeStruct((plan.half, 2 * tiles * plan.size + AUX, depth), jnp.float32)
    far = jax.ShapeDtypeStruct((2 * tiles * plan.size + AUX, depth), jnp.float32)
    return pl.pallas_call(
        functools.partial(outer_kernel, plan),
        in_specs=[vmem] * 7,
        out_specs=[vmem] * (1 + plan.half // 2),
        out_shape=[near] + [far] * (plan.half // 2),
        scratch_shapes=[buffer] * 4 + [pltpu.VMEM((3, KINDS, width, depth), jnp.float32)],
        compiler_params=pltpu.CompilerParams(vmem_limit_bytes=16 * 1024 * 1024),
        cost_estimate=pl.CostEstimate(flops=10**8, bytes_accessed=40 * 1024 * 1024, transcendentals=0),
        name="outer",
    )(own, phase, solute, *halos)


def route_kernel(plan, near, *refs):
    pieces, tiles, half, size = plan.pieces, plan.tiles, plan.half, 2 * plan.size
    far, near_out, far_outs, table = refs[:half], refs[half], refs[half + 1 : 2 * half + 1], refs[2 * half + 1]
    held, peers, count = refs[2 * half + 2 :]
    me = lax.axis_index("gy")
    base = me - lax.rem(me, half)
    tail = tiles * size
    for tile in range(tiles):
        for piece in range(half):
            peer = lax.rem(near[piece, tail, tile].astype(jnp.int32), pieces)
            peers[(base + piece) * tiles + tile] = peer
        for index in range(half):
            peer = lax.rem(far[index][tail, tile].astype(jnp.int32), pieces)
            peers[(me ^ (half + index)) * tiles + tile] = peer
    for piece in range(half):
        for tile in range(tiles):
            held[(base + piece) * tiles + tile] = near[piece, tile * size : (tile + 1) * size, :]
    for index in range(half):
        for tile in range(tiles):
            held[(me ^ (half + index)) * tiles + tile] = far[index][tile * size : (tile + 1) * size, :]
    for peer in range(pieces):
        count[peer] = 0
    for home in range(pieces * tiles):
        peer = peers[home]
        slot = count[peer]
        table[peer * tiles + slot] = home
        count[peer] = slot + 1
    for index in range(half):
        for slot in range(tiles):
            far_outs[index][slot] = held[table[(me ^ (half + index)) * tiles + slot]]
            near_out[index, slot] = held[table[(base + index) * tiles + slot]]


def route(plan, near, far):
    tiles, half, size, depth = plan.tiles, plan.half, 2 * plan.size, plan.depth
    vmem = pl.BlockSpec(memory_space=pltpu.VMEM)
    one = jax.ShapeDtypeStruct((tiles, size, depth), jnp.float32)
    count = plan.pieces * tiles
    results = pl.pallas_call(
        functools.partial(route_kernel, plan),
        in_specs=[vmem] * (half + 1),
        out_specs=[vmem] * (half + 1) + [pl.BlockSpec(memory_space=pltpu.SMEM)],
        out_shape=[jax.ShapeDtypeStruct((half, tiles, size, depth), jnp.float32)]
        + [one] * half
        + [jax.ShapeDtypeStruct((count,), jnp.int32)],
        scratch_shapes=[
            pltpu.VMEM((count, size, depth), jnp.float32),
            pltpu.SMEM((count,), jnp.int32),
            pltpu.SMEM((plan.pieces,), jnp.int32),
        ],
        compiler_params=pltpu.CompilerParams(vmem_limit_bytes=16 * 1024 * 1024),
        name="route",
    )(near, *far)
    return results[0], results[1 : half + 1], results[-1]


def settle_kernel(plan, table, near, *refs):
    tiles, half = plan.tiles, plan.half
    far, outs, (ready, sems) = refs[:half], refs[half : half + 2], refs[half + 2 :]
    me = lax.axis_index("gy")
    mine = lax.rem(me, half)
    copies = []
    for slot in range(tiles):
        home = table[me * tiles + slot]
        tile = lax.rem(home, tiles)
        at_home = home // (tiles * half) == me // half

        def put(source, piece, is_far, slot=slot, tile=tile):
            for field in range(2):
                for at, row, name in plan.parts(is_far, piece):
                    col, count = plan.columns(name, tile)
                    if not isinstance(col, int):
                        col = pl.multiple_of(col, 8)
                    ready[field, slot, row, pl.ds(col, count), :] = source[
                        slot, field * plan.size + at : field * plan.size + at + count, :
                    ]

        def put_all(same, put=put):
            for index in range(half):
                put(near.at[index], index, not same)
                put(far[index], mine ^ index, same)

        @pl.when(at_home)
        def _(put_all=put_all):
            put_all(True)

        @pl.when(jnp.logical_not(at_home))
        def _(put_all=put_all):
            put_all(False)

        for field, out in enumerate(outs):
            copy = pltpu.make_async_copy(ready.at[field, slot], out.at[0, slot], sems.at[field, slot])
            copy.start()
            copies.append(copy)
    for copy in copies:
        copy.wait()


def settle(plan, table, near, far):
    tiles, edge, depth = plan.tiles, plan.edge, plan.depth
    out = jax.ShapeDtypeStruct((1, tiles, edge, edge, depth), jnp.float32)
    vmem = pl.BlockSpec(memory_space=pltpu.VMEM)
    return pl.pallas_call(
        functools.partial(settle_kernel, plan),
        in_specs=[pl.BlockSpec(memory_space=pltpu.SMEM)] + [vmem] * (plan.half + 1),
        out_specs=[pl.BlockSpec(memory_space=pl.ANY)] * 2,
        out_shape=[out, out],
        scratch_shapes=[
            pltpu.VMEM((2, tiles, edge, edge, depth), jnp.float32),
            pltpu.SemaphoreType.DMA((2, tiles)),
        ],
        compiler_params=pltpu.CompilerParams(vmem_limit_bytes=16 * 1024 * 1024),
        name="settle",
    )(table, near, *far)


def ring(axis, step):
    count = lax.axis_size(axis)
    return [(i, (i + step) % count) for i in range(count)]


def swap(values, mask):
    return lax.ppermute(values, "gy", [(i, i ^ mask) for i in range(lax.axis_size("gy"))])


def among_half(plan, values, together):
    def exchange(values):
        groups = [list(range(plan.half)), list(range(plan.half, plan.pieces))]
        return lax.all_to_all(values, "gy", 0, 0, axis_index_groups=groups, tiled=True)

    return lax.cond(together, exchange, exchange, values)


def per_device(phase, solute, undercool, mobility, diffusivity, owner):
    _, tiles, edge, _, depth = phase.shape
    plan = Plan(lax.axis_size("gy"), tiles, edge, depth)
    half = plan.half
    to_prev, to_next, own = pack_y(phase, solute, (undercool, mobility, diffusivity), owner)
    y_lo = lax.ppermute(to_next, "gy", ring("gy", 1))
    y_hi = lax.ppermute(to_prev, "gy", ring("gy", -1))
    first = run_inner(plan, own, phase, solute)
    far = [swap(values, half + index) for index, values in enumerate(first)]
    to_prev, to_next = pack_x(phase, solute, own, y_lo, y_hi, first[0])
    together = owner[0, 0] >= 0

    def around(low, high):
        return lax.ppermute(low, "gx", ring("gx", 1)), lax.ppermute(high, "gx", ring("gx", -1))

    x_lo, x_hi = lax.cond(together, around, around, to_next, to_prev)
    near, *second = run_outer(plan, own, phase, solute, (y_lo, y_hi, x_lo, x_hi))
    far += [swap(values, half + half // 2 + index) for index, values in enumerate(second)]
    near = among_half(plan, near, together)
    near, far, table = route(plan, near, far)
    far = [swap(values, half + index) for index, values in enumerate(far)]
    near = among_half(plan, near, together)
    return tuple(settle(plan, table, near, far))


def solution(mesh):
    tile_spec = P("gx", "gy", None, None, None)
    in_specs = (tile_spec, tile_spec) + (P("gx", "gy"),) * 4
    out_spec = P(("gx", "gy"), None, None, None, None)
    return jax.shard_map(
        per_device, mesh=mesh, in_specs=in_specs, out_specs=(out_spec, out_spec), check_vma=False
    )
```

```python
import functools

import jax
import jax.numpy as jnp
from jax import lax
from jax.experimental import pallas as pl
from jax.experimental.pallas import tpu as pltpu
from jax.sharding import PartitionSpec as P

NSTEPS = 4
W = NSTEPS
PAD = 8

aniso_strength = 0.05


def pack_y_kernel(under, mobile, spread, owner, phase_lo, phase_hi, solute_lo, solute_hi, to_prev, to_next, own):
    edge, depth = phase_lo.shape[2], phase_lo.shape[4]
    tiles = own.shape[0] // 8 - 1
    to_prev[:edge, :W, :] = phase_lo[0, 0, :, :W, :]
    to_prev[:edge, W:, :] = solute_lo[0, 0, :, :W, :]
    to_next[:edge, :W, :] = phase_hi[0, 0, :, W:, :]
    to_next[:edge, W:, :] = solute_hi[0, 0, :, W:, :]
    line = lax.broadcasted_iota(jnp.int32, (8, depth), 0)
    lane = lax.broadcasted_iota(jnp.int32, (8, depth), 1)
    names = jnp.zeros((8, depth), jnp.float32)
    for tile in range(tiles):
        rows = jnp.zeros((8, depth), jnp.float32)
        ready = (2.0 * under[0, tile], mobile[0, tile], spread[0, tile], 1.0 - 6.0 * spread[0, tile])
        for kind, coef in enumerate(ready):
            rows = jnp.where(line == kind, coef, rows)
        own[8 * tile : 8 * tile + 8, :] = rows
        if tile == 0:
            to_prev[edge] = rows
        if tile == tiles - 1:
            to_next[edge] = rows
        names = jnp.where(lane == tile, owner[0, tile].astype(jnp.float32), names)
    own[8 * tiles :, :] = names


def pack_y(phase, solute, coef, owner):
    _, tiles, edge, _, depth = phase.shape
    low = pl.BlockSpec((1, 1, edge, 2 * W, depth), lambda i: (0, 0, 0, 0, 0))
    high = pl.BlockSpec((1, 1, edge, 2 * W, depth), lambda i: (0, tiles - 1, 0, edge // (2 * W) - 1, 0))
    face = jax.ShapeDtypeStruct((edge + 1, 2 * W, depth), jnp.float32)
    own = jax.ShapeDtypeStruct((8 * tiles + 8, depth), jnp.float32)
    whole = pl.BlockSpec((edge + 1, 2 * W, depth), lambda i: (0, 0, 0))
    return pl.pallas_call(
        pack_y_kernel,
        grid=(1,),
        in_specs=[pl.BlockSpec(memory_space=pltpu.SMEM)] * 4 + [low, high, low, high],
        out_specs=[whole, whole, pl.BlockSpec((8 * tiles + 8, depth), lambda i: (0, 0))],
        out_shape=[face, face, own],
        name="pack_y",
    )(*coef, owner, phase, phase, solute, solute)


def fill_row(dst, row, phase_row, solute_row, lo, hi):
    start = PAD
    dst[0][row, start : start + W, :] = lo[:W]
    dst[1][row, start : start + W, :] = 2.0 * lo[W:]
    start += W
    for values in phase_row:
        size = values.shape[0]
        dst[0][row, start : start + size, :] = values
        start += size
    dst[0][row, start : start + W, :] = hi[:W]
    dst[1][row, start : start + W, :] = 2.0 * hi[W:]
    start = PAD + W
    for values in solute_row:
        size = values.shape[0]
        dst[1][row, start : start + size, :] = 2.0 * values
        start += size


def pack_x_kernel(own, phase_lo, phase_hi, solute_lo, solute_hi, y_lo, y_hi, _, to_prev, to_next):
    tiles, edge, depth = phase_lo.shape[1], phase_lo.shape[3], phase_lo.shape[4]
    width = tiles * edge + 2 * W
    for out, phase, solute, first in (
        (to_prev, phase_lo, solute_lo, 0),
        (to_next, phase_hi, solute_hi, edge - W),
    ):
        for row in range(W):
            for field, values, half in ((0, phase, 0), (1, solute, W)):
                at = (2 * row + field) * width
                out[at : at + W, :] = y_lo[first + row, half : half + W, :]
                for tile in range(tiles):
                    begin = at + W + tile * edge
                    out[begin : begin + edge, :] = values[0, tile, row]
                out[at + width - W : at + width, :] = y_hi[first + row, half : half + W, :]
        at = 2 * W * width
        out[at : at + 8, :] = y_lo[edge]
        out[at + 8 : at + 16, :] = y_hi[edge]
        out[at + 16 : at + 16 + 8 * tiles, :] = own[: 8 * tiles, :]


def pack_x(phase, solute, own, y_lo, y_hi, after):
    _, tiles, edge, _, depth = phase.shape
    low = pl.BlockSpec((1, tiles, W, edge, depth), lambda i: (0, 0, 0, 0, 0))
    high = pl.BlockSpec((1, tiles, W, edge, depth), lambda i: (0, 0, edge // W - 1, 0, 0))
    side = pl.BlockSpec((edge + 1, 2 * W, depth), lambda i: (0, 0, 0))
    rows = 2 * W * (tiles * edge + 2 * W) + 8 * (tiles + 2)
    out = jax.ShapeDtypeStruct((rows, depth), jnp.float32)
    whole = pl.BlockSpec((rows, depth), lambda i: (0, 0))
    return pl.pallas_call(
        pack_x_kernel,
        grid=(1,),
        in_specs=[pl.BlockSpec((8 * tiles + 8, depth), lambda i: (0, 0)), low, high, low, high, side, side, pl.BlockSpec(memory_space=pl.ANY)],
        out_specs=[whole, whole],
        out_shape=[out, out],
        compiler_params=pltpu.CompilerParams(vmem_limit_bytes=8 * 1024 * 1024),
        name="pack_x",
    )(own, phase, phase, solute, solute, y_lo, y_hi, after)


def update(near_p, near_v, under, mobile, spread, keep):
    p, p_xl, p_xh, p_yl, p_yh = near_p
    v, v_xl, v_xh, v_yl, v_yh = near_v
    depth = p.shape[-1]
    lane = lax.broadcasted_iota(jnp.int32, p.shape, 1)
    first, last = lane == 0, lane == depth - 1
    p_zl = jnp.where(first, p, pltpu.roll(p, 1, 1))
    p_zh = jnp.where(last, p, pltpu.roll(p, depth - 1, 1))
    v_zl = jnp.where(first, v, pltpu.roll(v, 1, 1))
    v_zh = jnp.where(last, v, pltpu.roll(v, depth - 1, 1))
    dx, dy, dz = p_xh - p_xl, p_yh - p_yl, p_zh - p_zl
    qx, qy, qz = dx * dx, dy * dy, dz * dz
    flat = qx + qy
    total = flat + qz
    pairs = qx * qy + flat * qz
    base = total + 4.0
    guess = pl.reciprocal(base, approx=True)
    inverse = guess * (2.0 - base * guess)
    extra = (aniso_strength * total * total - (8.0 * aniso_strength) * pairs) * (inverse * inverse)
    lap_p = (p_xl + p_xh) + (p_yl + p_yh) + (p_zl + p_zh) - 6.0 * p
    sum_v = (v_xl + v_xh) + (v_yl + v_yh) + (v_zl + v_zh)
    well = 1.0 - p * p
    change = mobile * (lap_p + extra * lap_p + well * (p - well * (under + v)))
    return p + change, keep * v + spread * sum_v + change


KINDS = 4


def cells(src_p, src_u, row, start, coefs):
    near = []
    for src in (src_p, src_u):
        near.append(
            (
                src[row, start : start + 8, :],
                src[row - 1, start : start + 8, :],
                src[row + 1, start : start + 8, :],
                src[row, start - 1 : start + 7, :],
                src[row, start + 1 : start + 9, :],
            )
        )
    return update(near[0], near[1], *coefs)


class Plan:
    def __init__(self, pieces, tiles, edge, depth):
        self.pieces, self.tiles, self.edge, self.depth = pieces, tiles, edge, depth
        self.half = pieces // 2
        self.inner = edge - 2 * W
        self.rows = self.inner // self.half
        self.rows_far = (self.inner - 2 * W) // self.half
        self.rows_near = 2 * W // self.half
        self.middle = edge - 16
        self.size = self.rows * self.middle + self.rows_far * 8

        begins = [min(W + p * self.rows, 2 * W + p * self.rows_far) for p in range(self.half)]
        ends = [max(W + p * self.rows + self.rows, 2 * W + (p + 1) * self.rows_far) for p in range(self.half)]
        self.span = max(end - begin for begin, end in zip(begins, ends))
        side = self.half // 2
        self.batches = (list(range(side)), [side], list(range(side + 1, self.half)))

    def batch_rows(self, batch, mine):
        if batch == 0:
            count = self.inner // 2
            return W + mine // (self.half // 2) * count, count
        piece = mine ^ self.batches[1][0]
        begin = jnp.minimum(W + piece * self.rows, 2 * W + piece * self.rows_far)
        return jnp.minimum(begin, self.edge - W - self.span), self.span

    def near_row(self, piece, row, gap):
        index = piece * self.rows_near + row
        return index + jnp.where(index < W, 0, gap)

    def parts(self, far, piece):
        at, found = 0, []
        if far:
            for row in range(self.rows):
                found.append((at, W + piece * self.rows + row, "middle"))
                at += self.middle
            for row in range(self.rows_far):
                found.append((at, 2 * W + piece * self.rows_far + row, "last"))
                at += 8
        else:
            for row in range(self.rows_near):
                found.append((at, self.near_row(piece, row, self.inner), "whole"))
                at += self.edge
            for row in range(self.rows):
                found.append((at, W + piece * self.rows + row, "side"))
                at += 8
            for row in range(self.rows_near):
                found.append((at, W + self.near_row(piece, row, self.inner - 2 * W), "last"))
                at += 8
        assert at == self.size
        return found

    def columns(self, name, tile):
        if name == "whole":
            return 0, self.edge
        if name == "middle":
            return 8, self.middle
        low, high = (tile, 1 - tile) if name == "side" else (1 - tile, tile)
        return low * (self.edge - 8), 8


AUX = 8
UNROLL = 8


def march(count, row_of, starts, source, target, coefs_of):
    def one_row(index, carry):
        row = row_of(index)
        for start in starts:
            new_p, new_u = cells(source[0], source[1], row, start, coefs_of(row, start))
            target[0][row, start : start + 8, :] = new_p
            target[1][row, start : start + 8, :] = new_u
        return carry

    lax.fori_loop(0, count, one_row, 0, unroll=UNROLL)


def inner_kernel(plan, batch, own, phase, solute, *rest):
    tiles, edge, indices = plan.tiles, plan.edge, plan.batches[batch]
    outs, scratch = rest[: len(indices)], rest[len(indices) :]
    pairs = (scratch[:2], scratch[2:])
    mine = lax.rem(lax.axis_index("gy"), plan.half)
    begin, count = plan.batch_rows(batch, mine)
    base = begin - W

    def load_row(row, carry):
        for tile in range(tiles):
            start = PAD + tile * edge
            pairs[0][0][row, start : start + edge, :] = phase[0, tile, base + row]
            pairs[0][1][row, start : start + edge, :] = 2.0 * solute[0, tile, base + row]
        return carry

    lax.fori_loop(0, count + 2 * W, load_row, 0, unroll=UNROLL)

    line = lax.broadcasted_iota(jnp.int32, (8, plan.depth), 0)

    def coefs_of(row, start):
        low, high = (start - PAD) // edge, (start + 7 - PAD) // edge
        rows = [[own[8 * tile + kind : 8 * tile + kind + 1, :] for tile in (low, high)] for kind in range(KINDS)]
        if low == high:
            return tuple(pair[0] for pair in rows)
        return tuple(jnp.where(line < W, *pair) for pair in rows)

    for step in range(NSTEPS):
        margin = 8 if step == NSTEPS - 1 else W
        starts = range(PAD + margin, PAD + tiles * edge - margin, 8)
        rows = count + 2 * W - 2 * (step + 1)
        march(rows, lambda i, step=step: step + 1 + i, starts, pairs[step % 2], pairs[(step + 1) % 2], coefs_of)
    for index, out in zip(indices, outs):
        pack(plan, True, mine ^ index, pairs[NSTEPS % 2], -base, PAD, own, out)


def pack(plan, far, piece, done, row_shift, col_shift, own, out):
    for tile in range(plan.tiles):
        for field, values in enumerate(done):
            begin = (2 * tile + field) * plan.size
            for at, row, name in plan.parts(far, piece):
                col, count = plan.columns(name, tile)
                start = col_shift + tile * plan.edge + col
                cells = values[row + row_shift, start : start + count, :]
                out[begin + at : begin + at + count, :] = 0.5 * cells if field else cells
    tail = 2 * plan.tiles * plan.size
    out[tail : tail + AUX, :] = own[8 * plan.tiles : 8 * plan.tiles + AUX, :]


def run_inner(plan, batch, own, phase, solute):
    rows = plan.batch_rows(batch, 0)[1] + 2 * W
    count = len(plan.batches[batch])
    buffer = pltpu.VMEM((rows, plan.tiles * plan.edge + 2 * PAD, plan.depth), jnp.float32)
    vmem = pl.BlockSpec(memory_space=pltpu.VMEM)
    shape = jax.ShapeDtypeStruct((2 * plan.tiles * plan.size + AUX, plan.depth), jnp.float32)
    return pl.pallas_call(
        functools.partial(inner_kernel, plan, batch),
        in_specs=[vmem] * 3,
        out_specs=[vmem] * count,
        out_shape=[shape] * count,
        scratch_shapes=[buffer] * 4,
        compiler_params=pltpu.CompilerParams(vmem_limit_bytes=16 * 1024 * 1024),
        cost_estimate=pl.CostEstimate(flops=10**8, bytes_accessed=24 * 1024 * 1024, transcendentals=0),
        name="inner",
    )(own, phase, solute)


def outer_kernel(plan, own, phase, solute, y_lo, y_hi, x_lo, x_hi, out, *rest):
    tiles, edge, depth, half = plan.tiles, plan.edge, plan.depth, plan.half
    late = plan.batches[2]
    far_outs, scratch = rest[: len(late)], rest[len(late) :]
    pairs, coefs = (scratch[:2], scratch[2:4]), scratch[4]
    cols = tiles * edge
    width = cols + 2 * W
    for zone, source in ((0, x_lo), (1, None), (2, x_hi)):
        for kind in range(KINDS):
            if source is None:
                parts = [y_lo[edge, kind : kind + 1, :]]
                parts += [own[8 * tile + kind : 8 * tile + kind + 1, :] for tile in range(tiles)]
                parts += [y_hi[edge, kind : kind + 1, :]]
            else:
                at = 2 * W * width + kind
                parts = [source[at : at + 1, :]]
                parts += [source[at + 16 + 8 * tile : at + 17 + 8 * tile, :] for tile in range(tiles)]
                parts += [source[at + 8 : at + 9, :]]
            coefs[zone, kind, :W, :] = jnp.broadcast_to(parts[0], (W, depth))
            for tile in range(tiles):
                begin = W + tile * edge
                coefs[zone, kind, begin : begin + edge, :] = jnp.broadcast_to(parts[1 + tile], (edge, depth))
            coefs[zone, kind, width - W :, :] = jnp.broadcast_to(parts[-1], (W, depth))
    for source, first in ((x_lo, 0), (x_hi, edge + W)):
        for row in range(W):
            for field in range(2):
                at = (2 * row + field) * width
                values = source[at : at + width, :]
                pairs[0][field][first + row, PAD : PAD + width, :] = 2.0 * values if field else values

    def load_row(row, carry):
        fill_row(
            pairs[0],
            W + row,
            [phase[0, tile, row] for tile in range(tiles)],
            [solute[0, tile, row] for tile in range(tiles)],
            y_lo[row],
            y_hi[row],
        )
        return carry

    lax.fori_loop(0, edge, load_row, 0, unroll=UNROLL)

    def coefs_of(zone):
        def found(row, start):
            return tuple(coefs[zone(row), kind, start - PAD : start - PAD + 8, :] for kind in range(KINDS))

        return found

    any_zone = coefs_of(lambda row: jnp.where(row < W, 0, jnp.where(row < W + edge, 1, 2)))

    own_zone = coefs_of(lambda row: 1)
    mine = lax.rem(lax.axis_index("gy"), half)
    made = plan.inner // 2
    first_made = 2 * W + mine // (half // 2) * made

    def blocks(first, last):
        low, high = (first + W - shift) // 8 * 8, -(-(last + W - shift) // 8) * 8
        return list(range(PAD + shift + low, PAD + shift + high, 8))

    for step in range(1, NSTEPS + 1):
        source, target = pairs[(step - 1) % 2], pairs[step % 2]
        left = NSTEPS - step
        shift = W if step == NSTEPS else 0
        whole = blocks(-left, cols + left)
        ends = blocks(-left, 8 + left) + blocks(cols - 8 - left, cols + left)
        for tile in range(tiles):
            col, count = plan.columns("last", tile)
            ends += blocks(tile * edge + col - left, tile * edge + col + count + left)
        gap, gap_rows = first_made + left, made - 2 * left

        def outside(index, left=left, gap=gap, gap_rows=gap_rows):
            row = W - left + index
            return row + jnp.where(row < gap, 0, gap_rows)

        march(edge + 2 * left - gap_rows, outside, whole, source, target, any_zone)
        march(gap_rows, lambda i, gap=gap: gap + i, sorted(set(ends)), source, target, own_zone)
    done = pairs[NSTEPS % 2]
    for index, far_out in zip(late, far_outs):
        pack(plan, True, mine ^ index, done, W, PAD + W, own, far_out)
    for piece in range(half):
        pack(plan, False, piece, done, W, PAD + W, own, out.at[piece])


def run_outer(plan, own, phase, solute, halos):
    tiles, edge, depth = plan.tiles, plan.edge, plan.depth
    width = tiles * edge + 2 * W
    buffer = pltpu.VMEM((edge + 2 * W, width + 2 * PAD, depth), jnp.float32)
    vmem = pl.BlockSpec(memory_space=pltpu.VMEM)
    near = jax.ShapeDtypeStruct((plan.half, 2 * tiles * plan.size + AUX, depth), jnp.float32)
    far = jax.ShapeDtypeStruct((2 * tiles * plan.size + AUX, depth), jnp.float32)
    return pl.pallas_call(
        functools.partial(outer_kernel, plan),
        in_specs=[vmem] * 7,
        out_specs=[vmem] * (1 + len(plan.batches[2])),
        out_shape=[near] + [far] * len(plan.batches[2]),
        scratch_shapes=[buffer] * 4 + [pltpu.VMEM((3, KINDS, width, depth), jnp.float32)],
        compiler_params=pltpu.CompilerParams(vmem_limit_bytes=16 * 1024 * 1024),
        cost_estimate=pl.CostEstimate(flops=10**8, bytes_accessed=40 * 1024 * 1024, transcendentals=0),
        name="outer",
    )(own, phase, solute, *halos)


def route_kernel(plan, near, *refs):
    pieces, tiles, half, size = plan.pieces, plan.tiles, plan.half, 2 * plan.size
    far, near_out, far_outs, table = refs[:half], refs[half], refs[half + 1 : 2 * half + 1], refs[2 * half + 1]
    held, peers, count = refs[2 * half + 2 :]
    me = lax.axis_index("gy")
    base = me - lax.rem(me, half)
    tail = tiles * size
    for tile in range(tiles):
        for piece in range(half):
            peer = lax.rem(near[piece, tail, tile].astype(jnp.int32), pieces)
            peers[(base + piece) * tiles + tile] = peer
        for index in range(half):
            peer = lax.rem(far[index][tail, tile].astype(jnp.int32), pieces)
            peers[(me ^ (half + index)) * tiles + tile] = peer
    for piece in range(half):
        for tile in range(tiles):
            held[(base + piece) * tiles + tile] = near[piece, tile * size : (tile + 1) * size, :]
    for index in range(half):
        for tile in range(tiles):
            held[(me ^ (half + index)) * tiles + tile] = far[index][tile * size : (tile + 1) * size, :]
    for peer in range(pieces):
        count[peer] = 0
    for home in range(pieces * tiles):
        peer = peers[home]
        slot = count[peer]
        table[peer * tiles + slot] = home
        count[peer] = slot + 1
    for index in range(half):
        for slot in range(tiles):
            far_outs[index][slot] = held[table[(me ^ (half + index)) * tiles + slot]]
            near_out[index, slot] = held[table[(base + index) * tiles + slot]]


def route(plan, near, far):
    tiles, half, size, depth = plan.tiles, plan.half, 2 * plan.size, plan.depth
    vmem = pl.BlockSpec(memory_space=pltpu.VMEM)
    one = jax.ShapeDtypeStruct((tiles, size, depth), jnp.float32)
    count = plan.pieces * tiles
    results = pl.pallas_call(
        functools.partial(route_kernel, plan),
        in_specs=[vmem] * (half + 1),
        out_specs=[vmem] * (half + 1) + [pl.BlockSpec(memory_space=pltpu.SMEM)],
        out_shape=[jax.ShapeDtypeStruct((half, tiles, size, depth), jnp.float32)]
        + [one] * half
        + [jax.ShapeDtypeStruct((count,), jnp.int32)],
        scratch_shapes=[
            pltpu.VMEM((count, size, depth), jnp.float32),
            pltpu.SMEM((count,), jnp.int32),
            pltpu.SMEM((plan.pieces,), jnp.int32),
        ],
        compiler_params=pltpu.CompilerParams(vmem_limit_bytes=16 * 1024 * 1024),
        name="route",
    )(near, *far)
    return results[0], results[1 : half + 1], results[-1]


def settle_kernel(plan, table, near, *refs):
    tiles, half = plan.tiles, plan.half
    far, outs, (ready, sems) = refs[:half], refs[half : half + 2], refs[half + 2 :]
    me = lax.axis_index("gy")
    mine = lax.rem(me, half)
    copies = []
    for slot in range(tiles):
        home = table[me * tiles + slot]
        tile = lax.rem(home, tiles)
        at_home = home // (tiles * half) == me // half

        def put(source, piece, is_far, slot=slot, tile=tile):
            for field in range(2):
                for at, row, name in plan.parts(is_far, piece):
                    col, count = plan.columns(name, tile)
                    if not isinstance(col, int):
                        col = pl.multiple_of(col, 8)
                    ready[field, slot, row, pl.ds(col, count), :] = source[
                        slot, field * plan.size + at : field * plan.size + at + count, :
                    ]

        def put_all(same, put=put):
            for index in range(half):
                put(near.at[index], index, not same)
                put(far[index], mine ^ index, same)

        @pl.when(at_home)
        def _(put_all=put_all):
            put_all(True)

        @pl.when(jnp.logical_not(at_home))
        def _(put_all=put_all):
            put_all(False)

        for field, out in enumerate(outs):
            copy = pltpu.make_async_copy(ready.at[field, slot], out.at[0, slot], sems.at[field, slot])
            copy.start()
            copies.append(copy)
    for copy in copies:
        copy.wait()


def settle(plan, table, near, far):
    tiles, edge, depth = plan.tiles, plan.edge, plan.depth
    out = jax.ShapeDtypeStruct((1, tiles, edge, edge, depth), jnp.float32)
    vmem = pl.BlockSpec(memory_space=pltpu.VMEM)
    return pl.pallas_call(
        functools.partial(settle_kernel, plan),
        in_specs=[pl.BlockSpec(memory_space=pltpu.SMEM)] + [vmem] * (plan.half + 1),
        out_specs=[pl.BlockSpec(memory_space=pl.ANY)] * 2,
        out_shape=[out, out],
        scratch_shapes=[
            pltpu.VMEM((2, tiles, edge, edge, depth), jnp.float32),
            pltpu.SemaphoreType.DMA((2, tiles)),
        ],
        compiler_params=pltpu.CompilerParams(vmem_limit_bytes=16 * 1024 * 1024),
        name="settle",
    )(table, near, *far)


def ring(axis, step):
    count = lax.axis_size(axis)
    return [(i, (i + step) % count) for i in range(count)]


def swap(values, mask):
    return lax.ppermute(values, "gy", [(i, i ^ mask) for i in range(lax.axis_size("gy"))])


def among_half(plan, values, together):
    def exchange(values):
        groups = [list(range(plan.half)), list(range(plan.half, plan.pieces))]
        return lax.all_to_all(values, "gy", 0, 0, axis_index_groups=groups, tiled=True)

    return lax.cond(together, exchange, exchange, values)


def per_device(phase, solute, undercool, mobility, diffusivity, owner):
    _, tiles, edge, _, depth = phase.shape
    plan = Plan(lax.axis_size("gy"), tiles, edge, depth)
    half = plan.half
    to_prev, to_next, own = pack_y(phase, solute, (undercool, mobility, diffusivity), owner)
    y_lo = lax.ppermute(to_next, "gy", ring("gy", 1))
    y_hi = lax.ppermute(to_prev, "gy", ring("gy", -1))
    far = {}

    def send_far(batch, values):
        for index, value in zip(plan.batches[batch], values):
            far[index] = swap(value, half + index)

    first = run_inner(plan, 0, own, phase, solute)
    send_far(0, first)
    to_prev, to_next = pack_x(phase, solute, own, y_lo, y_hi, first[0])
    together = owner[0, 0] >= 0

    def around(low, high, *values):
        return ring_swap(low, high), run_inner(plan, 1, *values)

    def ring_swap(low, high):
        return lax.ppermute(low, "gx", ring("gx", 1)), lax.ppermute(high, "gx", ring("gx", -1))

    (x_lo, x_hi), second = lax.cond(together, around, around, to_next, to_prev, own, phase, solute)
    send_far(1, second)
    near, *third = run_outer(plan, own, phase, solute, (y_lo, y_hi, x_lo, x_hi))
    send_far(2, third)
    far = [far[index] for index in range(half)]
    near = among_half(plan, near, together)
    near, far, table = route(plan, near, far)
    far = [swap(values, half + index) for index, values in enumerate(far)]
    near = among_half(plan, near, together)
    return tuple(settle(plan, table, near, far))


def solution(mesh):
    tile_spec = P("gx", "gy", None, None, None)
    in_specs = (tile_spec, tile_spec) + (P("gx", "gy"),) * 4
    out_spec = P(("gx", "gy"), None, None, None, None)
    return jax.shard_map(
        per_device, mesh=mesh, in_specs=in_specs, out_specs=(out_spec, out_spec), check_vma=False
    )
```

```python
import functools

import jax
import jax.numpy as jnp
from jax import lax
from jax.experimental import pallas as pl
from jax.experimental.pallas import tpu as pltpu
from jax.sharding import PartitionSpec as P

NSTEPS = 4
W = NSTEPS
PAD = 8

aniso_strength = 0.05


def pack_y_kernel(under, mobile, spread, owner, phase_lo, phase_hi, solute_lo, solute_hi, to_prev, to_next, own):
    edge, depth = phase_lo.shape[2], phase_lo.shape[4]
    tiles = own.shape[0] // 8 - 1
    to_prev[:edge, :W, :] = phase_lo[0, 0, :, :W, :]
    to_prev[:edge, W:, :] = solute_lo[0, 0, :, :W, :]
    to_next[:edge, :W, :] = phase_hi[0, 0, :, W:, :]
    to_next[:edge, W:, :] = solute_hi[0, 0, :, W:, :]
    line = lax.broadcasted_iota(jnp.int32, (8, depth), 0)
    lane = lax.broadcasted_iota(jnp.int32, (8, depth), 1)
    names = jnp.zeros((8, depth), jnp.float32)
    for tile in range(tiles):
        rows = jnp.zeros((8, depth), jnp.float32)
        ready = (2.0 * under[0, tile], mobile[0, tile], spread[0, tile], 1.0 - 6.0 * spread[0, tile])
        for kind, coef in enumerate(ready):
            rows = jnp.where(line == kind, coef, rows)
        own[8 * tile : 8 * tile + 8, :] = rows
        if tile == 0:
            to_prev[edge] = rows
        if tile == tiles - 1:
            to_next[edge] = rows
        names = jnp.where(lane == tile, owner[0, tile].astype(jnp.float32), names)
    own[8 * tiles :, :] = names


def pack_y(phase, solute, coef, owner):
    _, tiles, edge, _, depth = phase.shape
    low = pl.BlockSpec((1, 1, edge, 2 * W, depth), lambda i: (0, 0, 0, 0, 0))
    high = pl.BlockSpec((1, 1, edge, 2 * W, depth), lambda i: (0, tiles - 1, 0, edge // (2 * W) - 1, 0))
    face = jax.ShapeDtypeStruct((edge + 1, 2 * W, depth), jnp.float32)
    own = jax.ShapeDtypeStruct((8 * tiles + 8, depth), jnp.float32)
    whole = pl.BlockSpec((edge + 1, 2 * W, depth), lambda i: (0, 0, 0))
    return pl.pallas_call(
        pack_y_kernel,
        grid=(1,),
        in_specs=[pl.BlockSpec(memory_space=pltpu.SMEM)] * 4 + [low, high, low, high],
        out_specs=[whole, whole, pl.BlockSpec((8 * tiles + 8, depth), lambda i: (0, 0))],
        out_shape=[face, face, own],
        name="pack_y",
    )(*coef, owner, phase, phase, solute, solute)


def fill_row(dst, row, phase_row, solute_row, lo, hi):
    start = PAD
    dst[0][row, start : start + W, :] = lo[:W]
    dst[1][row, start : start + W, :] = 2.0 * lo[W:]
    start += W
    for values in phase_row:
        size = values.shape[0]
        dst[0][row, start : start + size, :] = values
        start += size
    dst[0][row, start : start + W, :] = hi[:W]
    dst[1][row, start : start + W, :] = 2.0 * hi[W:]
    start = PAD + W
    for values in solute_row:
        size = values.shape[0]
        dst[1][row, start : start + size, :] = 2.0 * values
        start += size


def pack_x_kernel(own, phase_lo, phase_hi, solute_lo, solute_hi, y_lo, y_hi, _, to_prev, to_next):
    tiles, edge, depth = phase_lo.shape[1], phase_lo.shape[3], phase_lo.shape[4]
    width = tiles * edge + 2 * W
    for out, phase, solute, first in (
        (to_prev, phase_lo, solute_lo, 0),
        (to_next, phase_hi, solute_hi, edge - W),
    ):
        for row in range(W):
            for field, values, half in ((0, phase, 0), (1, solute, W)):
                at = (2 * row + field) * width
                out[at : at + W, :] = y_lo[first + row, half : half + W, :]
                for tile in range(tiles):
                    begin = at + W + tile * edge
                    out[begin : begin + edge, :] = values[0, tile, row]
                out[at + width - W : at + width, :] = y_hi[first + row, half : half + W, :]
        at = 2 * W * width
        out[at : at + 8, :] = y_lo[edge]
        out[at + 8 : at + 16, :] = y_hi[edge]
        out[at + 16 : at + 16 + 8 * tiles, :] = own[: 8 * tiles, :]


def pack_x(phase, solute, own, y_lo, y_hi, after):
    _, tiles, edge, _, depth = phase.shape
    low = pl.BlockSpec((1, tiles, W, edge, depth), lambda i: (0, 0, 0, 0, 0))
    high = pl.BlockSpec((1, tiles, W, edge, depth), lambda i: (0, 0, edge // W - 1, 0, 0))
    side = pl.BlockSpec((edge + 1, 2 * W, depth), lambda i: (0, 0, 0))
    rows = 2 * W * (tiles * edge + 2 * W) + 8 * (tiles + 2)
    out = jax.ShapeDtypeStruct((rows, depth), jnp.float32)
    whole = pl.BlockSpec((rows, depth), lambda i: (0, 0))
    return pl.pallas_call(
        pack_x_kernel,
        grid=(1,),
        in_specs=[pl.BlockSpec((8 * tiles + 8, depth), lambda i: (0, 0)), low, high, low, high, side, side, pl.BlockSpec(memory_space=pl.ANY)],
        out_specs=[whole, whole],
        out_shape=[out, out],
        compiler_params=pltpu.CompilerParams(vmem_limit_bytes=8 * 1024 * 1024),
        name="pack_x",
    )(own, phase, phase, solute, solute, y_lo, y_hi, after)


def update(near_p, near_v, under, mobile, spread, keep):
    p, p_xl, p_xh, p_yl, p_yh = near_p
    v, v_xl, v_xh, v_yl, v_yh = near_v
    depth = p.shape[-1]
    lane = lax.broadcasted_iota(jnp.int32, p.shape, 1)
    first, last = lane == 0, lane == depth - 1
    p_zl = jnp.where(first, p, pltpu.roll(p, 1, 1))
    p_zh = jnp.where(last, p, pltpu.roll(p, depth - 1, 1))
    v_zl = jnp.where(first, v, pltpu.roll(v, 1, 1))
    v_zh = jnp.where(last, v, pltpu.roll(v, depth - 1, 1))
    dx, dy, dz = p_xh - p_xl, p_yh - p_yl, p_zh - p_zl
    qx, qy, qz = dx * dx, dy * dy, dz * dz
    flat = qx + qy
    total = flat + qz
    pairs = qx * qy + flat * qz
    base = total + 4.0
    guess = pl.reciprocal(base, approx=True)
    inverse = guess * (2.0 - base * guess)
    extra = (aniso_strength * total * total - (8.0 * aniso_strength) * pairs) * (inverse * inverse)
    lap_p = (p_xl + p_xh) + (p_yl + p_yh) + (p_zl + p_zh) - 6.0 * p
    sum_v = (v_xl + v_xh) + (v_yl + v_yh) + (v_zl + v_zh)
    well = 1.0 - p * p
    change = mobile * (lap_p + extra * lap_p + well * (p - well * (under + v)))
    return p + change, keep * v + spread * sum_v + change


KINDS = 4


def cells(src_p, src_u, row, start, coefs):
    near = []
    for src in (src_p, src_u):
        near.append(
            (
                src[row, start : start + 8, :],
                src[row - 1, start : start + 8, :],
                src[row + 1, start : start + 8, :],
                src[row, start - 1 : start + 7, :],
                src[row, start + 1 : start + 9, :],
            )
        )
    return update(near[0], near[1], *coefs)


class Plan:
    def __init__(self, pieces, tiles, edge, depth):
        self.pieces, self.tiles, self.edge, self.depth = pieces, tiles, edge, depth
        self.half = pieces // 2
        self.inner = edge - 2 * W
        self.rows = self.inner // self.half
        self.rows_far = (self.inner - 2 * W) // self.half
        self.rows_near = 2 * W // self.half
        self.middle = edge - 16
        self.size = self.rows * self.middle + self.rows_far * 8

        begins = [min(W + p * self.rows, 2 * W + p * self.rows_far) for p in range(self.half)]
        ends = [max(W + p * self.rows + self.rows, 2 * W + (p + 1) * self.rows_far) for p in range(self.half)]
        self.span = max(end - begin for begin, end in zip(begins, ends))
        side = self.half // 2
        self.batches = (list(range(side)), [side], list(range(side + 1, self.half)))

    def batch_rows(self, batch, mine):
        if batch == 0:
            count = self.inner // 2
            return W + mine // (self.half // 2) * count, count
        piece = mine ^ self.batches[1][0]
        begin = jnp.minimum(W + piece * self.rows, 2 * W + piece * self.rows_far)
        return jnp.minimum(begin, self.edge - W - self.span), self.span

    def near_row(self, piece, row, gap):
        index = piece * self.rows_near + row
        return index + jnp.where(index < W, 0, gap)

    def parts(self, far, piece):
        at, found = 0, []
        if far:
            for row in range(self.rows):
                found.append((at, W + piece * self.rows + row, "middle"))
                at += self.middle
            for row in range(self.rows_far):
                found.append((at, 2 * W + piece * self.rows_far + row, "last"))
                at += 8
        else:
            for row in range(self.rows_near):
                found.append((at, self.near_row(piece, row, self.inner), "whole"))
                at += self.edge
            for row in range(self.rows):
                found.append((at, W + piece * self.rows + row, "side"))
                at += 8
            for row in range(self.rows_near):
                found.append((at, W + self.near_row(piece, row, self.inner - 2 * W), "last"))
                at += 8
        assert at == self.size
        return found

    def columns(self, name, tile):
        if name == "whole":
            return 0, self.edge
        if name == "middle":
            return 8, self.middle
        low, high = (tile, 1 - tile) if name == "side" else (1 - tile, tile)
        return low * (self.edge - 8), 8


AUX = 8
UNROLL = 8


def march(count, row_of, starts, source, target, coefs_of):
    def one_row(index, carry):
        row = row_of(index)
        for start in starts:
            new_p, new_u = cells(source[0], source[1], row, start, coefs_of(row, start))
            target[0][row, start : start + 8, :] = new_p
            target[1][row, start : start + 8, :] = new_u
        return carry

    lax.fori_loop(0, count, one_row, 0, unroll=UNROLL)


def inner_kernel(plan, batch, own, phase, solute, *rest):
    tiles, edge, indices = plan.tiles, plan.edge, plan.batches[batch]
    outs, scratch = rest[: len(indices)], rest[len(indices) :]
    pairs = (scratch[:2], scratch[2:])
    mine = lax.rem(lax.axis_index("gy"), plan.half)
    begin, count = plan.batch_rows(batch, mine)
    base = begin - W

    def load_row(row, carry):
        for tile in range(tiles):
            start = PAD + tile * edge
            pairs[0][0][row, start : start + edge, :] = phase[0, tile, base + row]
            pairs[0][1][row, start : start + edge, :] = 2.0 * solute[0, tile, base + row]
        return carry

    lax.fori_loop(0, count + 2 * W, load_row, 0, unroll=UNROLL)

    line = lax.broadcasted_iota(jnp.int32, (8, plan.depth), 0)

    def coefs_of(row, start):
        low, high = (start - PAD) // edge, (start + 7 - PAD) // edge
        rows = [[own[8 * tile + kind : 8 * tile + kind + 1, :] for tile in (low, high)] for kind in range(KINDS)]
        if low == high:
            return tuple(pair[0] for pair in rows)
        return tuple(jnp.where(line < W, *pair) for pair in rows)

    for step in range(NSTEPS):
        margin = 8 if step == NSTEPS - 1 else W
        starts = range(PAD + margin, PAD + tiles * edge - margin, 8)
        rows = count + 2 * W - 2 * (step + 1)
        march(rows, lambda i, step=step: step + 1 + i, starts, pairs[step % 2], pairs[(step + 1) % 2], coefs_of)
    for index, out in zip(indices, outs):
        pack(plan, True, mine ^ index, pairs[NSTEPS % 2], -base, PAD, own, out)


def pack(plan, far, piece, done, row_shift, col_shift, own, out):
    for tile in range(plan.tiles):
        for field, values in enumerate(done):
            begin = (2 * tile + field) * plan.size
            for at, row, name in plan.parts(far, piece):
                col, count = plan.columns(name, tile)
                start = col_shift + tile * plan.edge + col
                cells = values[row + row_shift, start : start + count, :]
                out[begin + at : begin + at + count, :] = 0.5 * cells if field else cells
    tail = 2 * plan.tiles * plan.size
    out[tail : tail + AUX, :] = own[8 * plan.tiles : 8 * plan.tiles + AUX, :]


def run_inner(plan, batch, own, phase, solute):
    rows = plan.batch_rows(batch, 0)[1] + 2 * W
    count = len(plan.batches[batch])
    buffer = pltpu.VMEM((rows, plan.tiles * plan.edge + 2 * PAD, plan.depth), jnp.float32)
    vmem = pl.BlockSpec(memory_space=pltpu.VMEM)
    shape = jax.ShapeDtypeStruct((2 * plan.tiles * plan.size + AUX, plan.depth), jnp.float32)
    return pl.pallas_call(
        functools.partial(inner_kernel, plan, batch),
        in_specs=[vmem] * 3,
        out_specs=[vmem] * count,
        out_shape=[shape] * count,
        scratch_shapes=[buffer] * 4,
        compiler_params=pltpu.CompilerParams(vmem_limit_bytes=16 * 1024 * 1024),
        cost_estimate=pl.CostEstimate(flops=10**8, bytes_accessed=24 * 1024 * 1024, transcendentals=0),
        name="inner",
    )(own, phase, solute)


def outer_kernel(plan, own, phase, solute, y_lo, y_hi, x_lo, x_hi, out, *rest):
    tiles, edge, depth, half = plan.tiles, plan.edge, plan.depth, plan.half
    late = plan.batches[2]
    far_outs, scratch = rest[: len(late)], rest[len(late) :]
    pairs, coefs = (scratch[:2], scratch[2:4]), scratch[4]
    cols = tiles * edge
    width = cols + 2 * W
    for zone, source in ((0, x_lo), (1, None), (2, x_hi)):
        for kind in range(KINDS):
            if source is None:
                parts = [y_lo[edge, kind : kind + 1, :]]
                parts += [own[8 * tile + kind : 8 * tile + kind + 1, :] for tile in range(tiles)]
                parts += [y_hi[edge, kind : kind + 1, :]]
            else:
                at = 2 * W * width + kind
                parts = [source[at : at + 1, :]]
                parts += [source[at + 16 + 8 * tile : at + 17 + 8 * tile, :] for tile in range(tiles)]
                parts += [source[at + 8 : at + 9, :]]
            coefs[zone, kind, :W, :] = jnp.broadcast_to(parts[0], (W, depth))
            for tile in range(tiles):
                begin = W + tile * edge
                coefs[zone, kind, begin : begin + edge, :] = jnp.broadcast_to(parts[1 + tile], (edge, depth))
            coefs[zone, kind, width - W :, :] = jnp.broadcast_to(parts[-1], (W, depth))
    for source, first in ((x_lo, 0), (x_hi, edge + W)):
        for row in range(W):
            for field in range(2):
                at = (2 * row + field) * width
                values = source[at : at + width, :]
                pairs[0][field][first + row, PAD : PAD + width, :] = 2.0 * values if field else values

    def load_row(row, carry):
        fill_row(
            pairs[0],
            W + row,
            [phase[0, tile, row] for tile in range(tiles)],
            [solute[0, tile, row] for tile in range(tiles)],
            y_lo[row],
            y_hi[row],
        )
        return carry

    lax.fori_loop(0, edge, load_row, 0, unroll=UNROLL)

    def coefs_of(zone):
        def found(row, start):
            return tuple(coefs[zone(row), kind, start - PAD : start - PAD + 8, :] for kind in range(KINDS))

        return found

    any_zone = coefs_of(lambda row: jnp.where(row < W, 0, jnp.where(row < W + edge, 1, 2)))

    own_zone = coefs_of(lambda row: 1)
    mine = lax.rem(lax.axis_index("gy"), half)
    made = plan.inner // 2
    first_made = 2 * W + mine // (half // 2) * made

    def blocks(first, last):
        low, high = (first + W - shift) // 8 * 8, -(-(last + W - shift) // 8) * 8
        return list(range(PAD + shift + low, PAD + shift + high, 8))

    for step in range(1, NSTEPS + 1):
        source, target = pairs[(step - 1) % 2], pairs[step % 2]
        left = NSTEPS - step
        shift = W if step == NSTEPS else 0
        whole = blocks(-left, cols + left)
        ends = blocks(-left, 8 + left) + blocks(cols - 8 - left, cols + left)
        for tile in range(tiles):
            col, count = plan.columns("last", tile)
            ends += blocks(tile * edge + col - left, tile * edge + col + count + left)
        gap, gap_rows = first_made + left, made - 2 * left

        def outside(index, left=left, gap=gap, gap_rows=gap_rows):
            row = W - left + index
            return row + jnp.where(row < gap, 0, gap_rows)

        march(edge + 2 * left - gap_rows, outside, whole, source, target, any_zone)
        march(gap_rows, lambda i, gap=gap: gap + i, sorted(set(ends)), source, target, own_zone)
    done = pairs[NSTEPS % 2]
    for index, far_out in zip(late, far_outs):
        pack(plan, True, mine ^ index, done, W, PAD + W, own, far_out)
    for piece in range(half):
        pack(plan, False, piece, done, W, PAD + W, own, out.at[piece])


def run_outer(plan, own, phase, solute, halos):
    tiles, edge, depth = plan.tiles, plan.edge, plan.depth
    width = tiles * edge + 2 * W
    buffer = pltpu.VMEM((edge + 2 * W, width + 2 * PAD, depth), jnp.float32)
    vmem = pl.BlockSpec(memory_space=pltpu.VMEM)
    near = jax.ShapeDtypeStruct((plan.half, 2 * tiles * plan.size + AUX, depth), jnp.float32)
    far = jax.ShapeDtypeStruct((2 * tiles * plan.size + AUX, depth), jnp.float32)
    return pl.pallas_call(
        functools.partial(outer_kernel, plan),
        in_specs=[vmem] * 7,
        out_specs=[vmem] * (1 + len(plan.batches[2])),
        out_shape=[near] + [far] * len(plan.batches[2]),
        scratch_shapes=[buffer] * 4 + [pltpu.VMEM((3, KINDS, width, depth), jnp.float32)],
        compiler_params=pltpu.CompilerParams(vmem_limit_bytes=16 * 1024 * 1024),
        cost_estimate=pl.CostEstimate(flops=10**8, bytes_accessed=40 * 1024 * 1024, transcendentals=0),
        name="outer",
    )(own, phase, solute, *halos)


def route_kernel(plan, near, *refs):
    pieces, tiles, half, size = plan.pieces, plan.tiles, plan.half, 2 * plan.size
    far, near_out, far_outs, table = refs[:half], refs[half], refs[half + 1 : 2 * half + 1], refs[2 * half + 1]
    held, peers, count = refs[2 * half + 2 :]
    me = lax.axis_index("gy")
    base = me - lax.rem(me, half)
    tail = tiles * size
    for tile in range(tiles):
        for piece in range(half):
            peer = lax.rem(near[piece, tail, tile].astype(jnp.int32), pieces)
            peers[(base + piece) * tiles + tile] = peer
        for index in range(half):
            peer = lax.rem(far[index][tail, tile].astype(jnp.int32), pieces)
            peers[(me ^ (half + index)) * tiles + tile] = peer
    for piece in range(half):
        for tile in range(tiles):
            held[(base + piece) * tiles + tile] = near[piece, tile * size : (tile + 1) * size, :]
    for index in range(half):
        for tile in range(tiles):
            held[(me ^ (half + index)) * tiles + tile] = far[index][tile * size : (tile + 1) * size, :]
    for peer in range(pieces):
        count[peer] = 0
    for home in range(pieces * tiles):
        peer = peers[home]
        slot = count[peer]
        table[peer * tiles + slot] = home
        count[peer] = slot + 1
    for index in range(half):
        for slot in range(tiles):
            far_outs[index][slot] = held[table[(me ^ (half + index)) * tiles + slot]]
            near_out[index, slot] = held[table[(base + index) * tiles + slot]]


def route(plan, near, far):
    tiles, half, size, depth = plan.tiles, plan.half, 2 * plan.size, plan.depth
    vmem = pl.BlockSpec(memory_space=pltpu.VMEM)
    one = jax.ShapeDtypeStruct((tiles, size, depth), jnp.float32)
    count = plan.pieces * tiles
    results = pl.pallas_call(
        functools.partial(route_kernel, plan),
        in_specs=[vmem] * (half + 1),
        out_specs=[vmem] * (half + 1) + [pl.BlockSpec(memory_space=pltpu.SMEM)],
        out_shape=[jax.ShapeDtypeStruct((half, tiles, size, depth), jnp.float32)]
        + [one] * half
        + [jax.ShapeDtypeStruct((count,), jnp.int32)],
        scratch_shapes=[
            pltpu.VMEM((count, size, depth), jnp.float32),
            pltpu.SMEM((count,), jnp.int32),
            pltpu.SMEM((plan.pieces,), jnp.int32),
        ],
        compiler_params=pltpu.CompilerParams(vmem_limit_bytes=16 * 1024 * 1024),
        name="route",
    )(near, *far)
    return results[0], results[1 : half + 1], results[-1]


def settle_kernel(plan, table, near, *refs):
    tiles, half = plan.tiles, plan.half
    far, outs, (ready, sems) = refs[:half], refs[half : half + 2], refs[half + 2 :]
    me = lax.axis_index("gy")
    mine = lax.rem(me, half)
    copies = []
    for slot in range(tiles):
        home = table[me * tiles + slot]
        tile = lax.rem(home, tiles)
        at_home = home // (tiles * half) == me // half

        def put(source, piece, is_far, slot=slot, tile=tile):
            for field in range(2):
                for at, row, name in plan.parts(is_far, piece):
                    col, count = plan.columns(name, tile)
                    if not isinstance(col, int):
                        col = pl.multiple_of(col, 8)
                    ready[field, slot, row, pl.ds(col, count), :] = source[
                        slot, field * plan.size + at : field * plan.size + at + count, :
                    ]

        def put_all(same, put=put):
            for index in range(half):
                put(near.at[index], index, not same)
                put(far[index], mine ^ index, same)

        @pl.when(at_home)
        def _(put_all=put_all):
            put_all(True)

        @pl.when(jnp.logical_not(at_home))
        def _(put_all=put_all):
            put_all(False)

        for field, out in enumerate(outs):
            copy = pltpu.make_async_copy(ready.at[field, slot], out.at[0, slot], sems.at[field, slot])
            copy.start()
            copies.append(copy)
    for copy in copies:
        copy.wait()


def settle(plan, table, near, far):
    tiles, edge, depth = plan.tiles, plan.edge, plan.depth
    out = jax.ShapeDtypeStruct((1, tiles, edge, edge, depth), jnp.float32)
    vmem = pl.BlockSpec(memory_space=pltpu.VMEM)
    return pl.pallas_call(
        functools.partial(settle_kernel, plan),
        in_specs=[pl.BlockSpec(memory_space=pltpu.SMEM)] + [vmem] * (plan.half + 1),
        out_specs=[pl.BlockSpec(memory_space=pl.ANY)] * 2,
        out_shape=[out, out],
        scratch_shapes=[
            pltpu.VMEM((2, tiles, edge, edge, depth), jnp.float32),
            pltpu.SemaphoreType.DMA((2, tiles)),
        ],
        compiler_params=pltpu.CompilerParams(vmem_limit_bytes=16 * 1024 * 1024),
        name="settle",
    )(table, near, *far)


def ring(axis, step):
    count = lax.axis_size(axis)
    return [(i, (i + step) % count) for i in range(count)]


def swap(values, mask):
    return lax.ppermute(values, "gy", [(i, i ^ mask) for i in range(lax.axis_size("gy"))])


def among_half(plan, values, together):
    def exchange(values):
        groups = [list(range(plan.half)), list(range(plan.half, plan.pieces))]
        return lax.all_to_all(values, "gy", 0, 0, axis_index_groups=groups, tiled=True)

    return lax.cond(together, exchange, exchange, values)


def in_vmem(values):
    return pltpu.with_memory_space_constraint(values, pltpu.VMEM)


def per_device(phase, solute, undercool, mobility, diffusivity, owner):
    _, tiles, edge, _, depth = phase.shape
    plan = Plan(lax.axis_size("gy"), tiles, edge, depth)
    half = plan.half
    to_prev, to_next, own = pack_y(phase, solute, (undercool, mobility, diffusivity), owner)
    y_lo = lax.ppermute(to_next, "gy", ring("gy", 1))
    y_hi = lax.ppermute(to_prev, "gy", ring("gy", -1))
    far = {}

    def send_far(batch, values):
        for index, value in zip(plan.batches[batch], values):
            far[index] = swap(value, half + index)

    own_here, phase_here, solute_here = in_vmem(own), in_vmem(phase), in_vmem(solute)
    first = run_inner(plan, 0, own_here, phase_here, solute_here)
    send_far(0, first)
    to_prev, to_next = pack_x(phase_here, solute_here, own_here, y_lo, y_hi, first[0])
    together = owner[0, 0] >= 0

    def around(low, high, *values):
        return ring_swap(low, high), run_inner(plan, 1, *values)

    def ring_swap(low, high):
        return lax.ppermute(low, "gx", ring("gx", 1)), lax.ppermute(high, "gx", ring("gx", -1))

    (x_lo, x_hi), second = lax.cond(together, around, around, to_next, to_prev, own, phase, solute)
    send_far(1, second)
    near, *third = run_outer(plan, own_here, phase_here, solute_here, (y_lo, y_hi, in_vmem(x_lo), in_vmem(x_hi)))
    send_far(2, third)
    far = [far[index] for index in range(half)]
    near = among_half(plan, near, together)
    near, far, table = route(plan, in_vmem(near), far)
    far = [swap(values, half + index) for index, values in enumerate(far)]
    near = among_half(plan, near, together)
    return tuple(settle(plan, table, near, far))


def solution(mesh):
    tile_spec = P("gx", "gy", None, None, None)
    in_specs = (tile_spec, tile_spec) + (P("gx", "gy"),) * 4
    out_spec = P(("gx", "gy"), None, None, None, None)
    return jax.shard_map(
        per_device, mesh=mesh, in_specs=in_specs, out_specs=(out_spec, out_spec), check_vma=False
    )
```

```python
import functools

import jax
import jax.numpy as jnp
from jax import lax
from jax.experimental import pallas as pl
from jax.experimental.pallas import tpu as pltpu
from jax.sharding import PartitionSpec as P

NSTEPS = 4
W = NSTEPS
PAD = 8

aniso_strength = 0.05


def pack_y_kernel(under, mobile, spread, owner, phase_lo, phase_hi, solute_lo, solute_hi, to_prev, to_next, own):
    edge, depth = phase_lo.shape[2], phase_lo.shape[4]
    tiles = own.shape[0] // 8 - 1
    to_prev[:edge, :W, :] = phase_lo[0, 0, :, :W, :]
    to_prev[:edge, W:, :] = solute_lo[0, 0, :, :W, :]
    to_next[:edge, :W, :] = phase_hi[0, 0, :, W:, :]
    to_next[:edge, W:, :] = solute_hi[0, 0, :, W:, :]
    line = lax.broadcasted_iota(jnp.int32, (8, depth), 0)
    lane = lax.broadcasted_iota(jnp.int32, (8, depth), 1)
    names = jnp.zeros((8, depth), jnp.float32)
    for tile in range(tiles):
        rows = jnp.zeros((8, depth), jnp.float32)
        ready = (2.0 * under[0, tile], mobile[0, tile], spread[0, tile], 1.0 - 6.0 * spread[0, tile])
        for kind, coef in enumerate(ready):
            rows = jnp.where(line == kind, coef, rows)
        own[8 * tile : 8 * tile + 8, :] = rows
        if tile == 0:
            to_prev[edge] = rows
        if tile == tiles - 1:
            to_next[edge] = rows
        names = jnp.where(lane == tile, owner[0, tile].astype(jnp.float32), names)
    own[8 * tiles :, :] = names


def pack_y(phase, solute, coef, owner):
    _, tiles, edge, _, depth = phase.shape
    low = pl.BlockSpec((1, 1, edge, 2 * W, depth), lambda i: (0, 0, 0, 0, 0))
    high = pl.BlockSpec((1, 1, edge, 2 * W, depth), lambda i: (0, tiles - 1, 0, edge // (2 * W) - 1, 0))
    face = jax.ShapeDtypeStruct((edge + 1, 2 * W, depth), jnp.float32)
    own = jax.ShapeDtypeStruct((8 * tiles + 8, depth), jnp.float32)
    whole = pl.BlockSpec((edge + 1, 2 * W, depth), lambda i: (0, 0, 0))
    return pl.pallas_call(
        pack_y_kernel,
        grid=(1,),
        in_specs=[pl.BlockSpec(memory_space=pltpu.SMEM)] * 4 + [low, high, low, high],
        out_specs=[whole, whole, pl.BlockSpec((8 * tiles + 8, depth), lambda i: (0, 0))],
        out_shape=[face, face, own],
        name="pack_y",
    )(*coef, owner, phase, phase, solute, solute)


def fill_row(dst, row, phase_row, solute_row, lo, hi):
    start = PAD
    dst[0][row, start : start + W, :] = lo[:W]
    dst[1][row, start : start + W, :] = 2.0 * lo[W:]
    start += W
    for values in phase_row:
        size = values.shape[0]
        dst[0][row, start : start + size, :] = values
        start += size
    dst[0][row, start : start + W, :] = hi[:W]
    dst[1][row, start : start + W, :] = 2.0 * hi[W:]
    start = PAD + W
    for values in solute_row:
        size = values.shape[0]
        dst[1][row, start : start + size, :] = 2.0 * values
        start += size


def pack_x_kernel(own, phase_lo, phase_hi, solute_lo, solute_hi, y_lo, y_hi, _, to_prev, to_next):
    tiles, edge, depth = phase_lo.shape[1], phase_lo.shape[3], phase_lo.shape[4]
    width = tiles * edge + 2 * W
    for out, phase, solute, first in (
        (to_prev, phase_lo, solute_lo, 0),
        (to_next, phase_hi, solute_hi, edge - W),
    ):
        for row in range(W):
            for field, values, half in ((0, phase, 0), (1, solute, W)):
                at = (2 * row + field) * width
                out[at : at + W, :] = y_lo[first + row, half : half + W, :]
                for tile in range(tiles):
                    begin = at + W + tile * edge
                    out[begin : begin + edge, :] = values[0, tile, row]
                out[at + width - W : at + width, :] = y_hi[first + row, half : half + W, :]
        at = 2 * W * width
        out[at : at + 8, :] = y_lo[edge]
        out[at + 8 : at + 16, :] = y_hi[edge]
        out[at + 16 : at + 16 + 8 * tiles, :] = own[: 8 * tiles, :]


def pack_x(phase, solute, own, y_lo, y_hi, after):
    _, tiles, edge, _, depth = phase.shape
    low = pl.BlockSpec((1, tiles, W, edge, depth), lambda i: (0, 0, 0, 0, 0))
    high = pl.BlockSpec((1, tiles, W, edge, depth), lambda i: (0, 0, edge // W - 1, 0, 0))
    side = pl.BlockSpec((edge + 1, 2 * W, depth), lambda i: (0, 0, 0))
    rows = 2 * W * (tiles * edge + 2 * W) + 8 * (tiles + 2)
    out = jax.ShapeDtypeStruct((rows, depth), jnp.float32)
    whole = pl.BlockSpec((rows, depth), lambda i: (0, 0))
    return pl.pallas_call(
        pack_x_kernel,
        grid=(1,),
        in_specs=[pl.BlockSpec((8 * tiles + 8, depth), lambda i: (0, 0)), low, high, low, high, side, side, pl.BlockSpec(memory_space=pl.ANY)],
        out_specs=[whole, whole],
        out_shape=[out, out],
        compiler_params=pltpu.CompilerParams(vmem_limit_bytes=8 * 1024 * 1024),
        name="pack_x",
    )(own, phase, phase, solute, solute, y_lo, y_hi, after)


def update(near_p, near_v, under, mobile, spread, keep):
    p, p_xl, p_xh, p_yl, p_yh = near_p
    v, v_xl, v_xh, v_yl, v_yh = near_v
    depth = p.shape[-1]
    lane = lax.broadcasted_iota(jnp.int32, p.shape, 1)
    first, last = lane == 0, lane == depth - 1
    p_zl = jnp.where(first, p, pltpu.roll(p, 1, 1))
    p_zh = jnp.where(last, p, pltpu.roll(p, depth - 1, 1))
    v_zl = jnp.where(first, v, pltpu.roll(v, 1, 1))
    v_zh = jnp.where(last, v, pltpu.roll(v, depth - 1, 1))
    dx, dy, dz = p_xh - p_xl, p_yh - p_yl, p_zh - p_zl
    qx, qy, qz = dx * dx, dy * dy, dz * dz
    flat = qx + qy
    total = flat + qz
    pairs = qx * qy + flat * qz
    base = total + 4.0
    guess = pl.reciprocal(base, approx=True)
    inverse = guess * (2.0 - base * guess)
    extra = (aniso_strength * total * total - (8.0 * aniso_strength) * pairs) * (inverse * inverse)
    lap_p = (p_xl + p_xh) + (p_yl + p_yh) + (p_zl + p_zh) - 6.0 * p
    sum_v = (v_xl + v_xh) + (v_yl + v_yh) + (v_zl + v_zh)
    well = 1.0 - p * p
    change = mobile * (lap_p + extra * lap_p + well * (p - well * (under + v)))
    return p + change, keep * v + spread * sum_v + change


KINDS = 4


def cells(src_p, src_u, row, start, coefs):
    near = []
    for src in (src_p, src_u):
        near.append(
            (
                src[row, start : start + 8, :],
                src[row - 1, start : start + 8, :],
                src[row + 1, start : start + 8, :],
                src[row, start - 1 : start + 7, :],
                src[row, start + 1 : start + 9, :],
            )
        )
    return update(near[0], near[1], *coefs)


class Plan:
    def __init__(self, pieces, tiles, edge, depth):
        self.pieces, self.tiles, self.edge, self.depth = pieces, tiles, edge, depth
        self.half = pieces // 2
        self.inner = edge - 2 * W
        self.rows = self.inner // self.half
        self.rows_far = (self.inner - 2 * W) // self.half
        self.rows_near = 2 * W // self.half
        self.middle = edge - 16
        self.size = self.rows * self.middle + self.rows_far * 8

        begins = [min(W + p * self.rows, 2 * W + p * self.rows_far) for p in range(self.half)]
        ends = [max(W + p * self.rows + self.rows, 2 * W + (p + 1) * self.rows_far) for p in range(self.half)]
        self.span = max(end - begin for begin, end in zip(begins, ends))
        side = self.half // 2
        self.batches = (list(range(side)), [side], list(range(side + 1, self.half)))

    def batch_rows(self, batch, mine):
        if batch == 0:
            count = self.inner // 2
            return W + mine // (self.half // 2) * count, count
        piece = mine ^ self.batches[1][0]
        begin = jnp.minimum(W + piece * self.rows, 2 * W + piece * self.rows_far)
        return jnp.minimum(begin, self.edge - W - self.span), self.span

    def near_row(self, piece, row, gap):
        index = piece * self.rows_near + row
        return index + jnp.where(index < W, 0, gap)

    def parts(self, far, piece):
        at, found = 0, []
        if far:
            for row in range(self.rows):
                found.append((at, W + piece * self.rows + row, "middle"))
                at += self.middle
            for row in range(self.rows_far):
                found.append((at, 2 * W + piece * self.rows_far + row, "last"))
                at += 8
        else:
            for row in range(self.rows_near):
                found.append((at, self.near_row(piece, row, self.inner), "whole"))
                at += self.edge
            for row in range(self.rows):
                found.append((at, W + piece * self.rows + row, "side"))
                at += 8
            for row in range(self.rows_near):
                found.append((at, W + self.near_row(piece, row, self.inner - 2 * W), "last"))
                at += 8
        assert at == self.size
        return found

    def columns(self, name, tile):
        if name == "whole":
            return 0, self.edge
        if name == "middle":
            return 8, self.middle
        low, high = (tile, 1 - tile) if name == "side" else (1 - tile, tile)
        return low * (self.edge - 8), 8


AUX = 8
UNROLL = 8


def march(count, row_of, starts, source, target, coefs_of):
    def one_row(index, carry):
        row = row_of(index)
        for start in starts:
            new_p, new_u = cells(source[0], source[1], row, start, coefs_of(row, start))
            target[0][row, start : start + 8, :] = new_p
            target[1][row, start : start + 8, :] = new_u
        return carry

    lax.fori_loop(0, count, one_row, 0, unroll=UNROLL)


def inner_kernel(plan, batch, own, phase, solute, *rest):
    tiles, edge, indices = plan.tiles, plan.edge, plan.batches[batch]
    outs, scratch = rest[: len(indices)], rest[len(indices) :]
    pairs = (scratch[:2], scratch[2:])
    mine = lax.rem(lax.axis_index("gy"), plan.half)
    begin, count = plan.batch_rows(batch, mine)
    base = begin - W

    def load_row(row, carry):
        for tile in range(tiles):
            start = PAD + tile * edge
            pairs[0][0][row, start : start + edge, :] = phase[0, tile, base + row]
            pairs[0][1][row, start : start + edge, :] = 2.0 * solute[0, tile, base + row]
        return carry

    lax.fori_loop(0, count + 2 * W, load_row, 0, unroll=UNROLL)

    line = lax.broadcasted_iota(jnp.int32, (8, plan.depth), 0)

    def coefs_of(row, start):
        low, high = (start - PAD) // edge, (start + 7 - PAD) // edge
        rows = [[own[8 * tile + kind : 8 * tile + kind + 1, :] for tile in (low, high)] for kind in range(KINDS)]
        if low == high:
            return tuple(pair[0] for pair in rows)
        return tuple(jnp.where(line < W, *pair) for pair in rows)

    for step in range(NSTEPS):
        margin = 8 if step == NSTEPS - 1 else W
        starts = range(PAD + margin, PAD + tiles * edge - margin, 8)
        rows = count + 2 * W - 2 * (step + 1)
        march(rows, lambda i, step=step: step + 1 + i, starts, pairs[step % 2], pairs[(step + 1) % 2], coefs_of)
    for index, out in zip(indices, outs):
        pack(plan, True, mine ^ index, pairs[NSTEPS % 2], -base, PAD, own, out)


def pack(plan, far, piece, done, row_shift, col_shift, own, out):
    for tile in range(plan.tiles):
        for field, values in enumerate(done):
            begin = (2 * tile + field) * plan.size
            for at, row, name in plan.parts(far, piece):
                col, count = plan.columns(name, tile)
                start = col_shift + tile * plan.edge + col
                cells = values[row + row_shift, start : start + count, :]
                out[begin + at : begin + at + count, :] = 0.5 * cells if field else cells
    tail = 2 * plan.tiles * plan.size
    out[tail : tail + AUX, :] = own[8 * plan.tiles : 8 * plan.tiles + AUX, :]


def run_inner(plan, batch, own, phase, solute):
    rows = plan.batch_rows(batch, 0)[1] + 2 * W
    count = len(plan.batches[batch])
    buffer = pltpu.VMEM((rows, plan.tiles * plan.edge + 2 * PAD, plan.depth), jnp.float32)
    vmem = pl.BlockSpec(memory_space=pltpu.VMEM)
    shape = jax.ShapeDtypeStruct((2 * plan.tiles * plan.size + AUX, plan.depth), jnp.float32)
    return pl.pallas_call(
        functools.partial(inner_kernel, plan, batch),
        in_specs=[vmem] * 3,
        out_specs=[vmem] * count,
        out_shape=[shape] * count,
        scratch_shapes=[buffer] * 4,
        compiler_params=pltpu.CompilerParams(vmem_limit_bytes=16 * 1024 * 1024),
        cost_estimate=pl.CostEstimate(flops=10**8, bytes_accessed=24 * 1024 * 1024, transcendentals=0),
        name="inner",
    )(own, phase, solute)


def outer_kernel(plan, own, phase, solute, y_lo, y_hi, x_lo, x_hi, out, *rest):
    tiles, edge, depth, half = plan.tiles, plan.edge, plan.depth, plan.half
    late = plan.batches[2]
    far_outs, scratch = rest[: len(late)], rest[len(late) :]
    pairs, coefs = (scratch[:2], scratch[2:4]), scratch[4]
    cols = tiles * edge
    width = cols + 2 * W
    for zone, source in ((0, x_lo), (1, None), (2, x_hi)):
        for kind in range(KINDS):
            if source is None:
                parts = [y_lo[edge, kind : kind + 1, :]]
                parts += [own[8 * tile + kind : 8 * tile + kind + 1, :] for tile in range(tiles)]
                parts += [y_hi[edge, kind : kind + 1, :]]
            else:
                at = 2 * W * width + kind
                parts = [source[at : at + 1, :]]
                parts += [source[at + 16 + 8 * tile : at + 17 + 8 * tile, :] for tile in range(tiles)]
                parts += [source[at + 8 : at + 9, :]]
            coefs[zone, kind, :W, :] = jnp.broadcast_to(parts[0], (W, depth))
            for tile in range(tiles):
                begin = W + tile * edge
                coefs[zone, kind, begin : begin + edge, :] = jnp.broadcast_to(parts[1 + tile], (edge, depth))
            coefs[zone, kind, width - W :, :] = jnp.broadcast_to(parts[-1], (W, depth))
    for source, first in ((x_lo, 0), (x_hi, edge + W)):
        for row in range(W):
            for field in range(2):
                at = (2 * row + field) * width
                values = source[at : at + width, :]
                pairs[0][field][first + row, PAD : PAD + width, :] = 2.0 * values if field else values

    def load_row(row, carry):
        fill_row(
            pairs[0],
            W + row,
            [phase[0, tile, row] for tile in range(tiles)],
            [solute[0, tile, row] for tile in range(tiles)],
            y_lo[row],
            y_hi[row],
        )
        return carry

    lax.fori_loop(0, edge, load_row, 0, unroll=UNROLL)

    def coefs_of(zone):
        def found(row, start):
            return tuple(coefs[zone(row), kind, start - PAD : start - PAD + 8, :] for kind in range(KINDS))

        return found

    any_zone = coefs_of(lambda row: jnp.where(row < W, 0, jnp.where(row < W + edge, 1, 2)))

    own_zone = coefs_of(lambda row: 1)
    mine = lax.rem(lax.axis_index("gy"), half)
    made = plan.inner // 2
    first_made = 2 * W + mine // (half // 2) * made

    def blocks(first, last):
        low, high = (first + W - shift) // 8 * 8, -(-(last + W - shift) // 8) * 8
        return list(range(PAD + shift + low, PAD + shift + high, 8))

    for step in range(1, NSTEPS + 1):
        source, target = pairs[(step - 1) % 2], pairs[step % 2]
        left = NSTEPS - step
        shift = W if step == NSTEPS else 0
        whole = blocks(-left, cols + left)
        ends = blocks(-left, 8 + left) + blocks(cols - 8 - left, cols + left)
        for tile in range(tiles):
            col, count = plan.columns("last", tile)
            ends += blocks(tile * edge + col - left, tile * edge + col + count + left)
        gap, gap_rows = first_made + left, made - 2 * left

        def outside(index, left=left, gap=gap, gap_rows=gap_rows):
            row = W - left + index
            return row + jnp.where(row < gap, 0, gap_rows)

        march(edge + 2 * left - gap_rows, outside, whole, source, target, any_zone)
        march(gap_rows, lambda i, gap=gap: gap + i, sorted(set(ends)), source, target, own_zone)
    done = pairs[NSTEPS % 2]
    for index, far_out in zip(late, far_outs):
        pack(plan, True, mine ^ index, done, W, PAD + W, own, far_out)
    for piece in range(half):
        pack(plan, False, piece, done, W, PAD + W, own, out.at[piece])


def run_outer(plan, own, phase, solute, halos):
    tiles, edge, depth = plan.tiles, plan.edge, plan.depth
    width = tiles * edge + 2 * W
    buffer = pltpu.VMEM((edge + 2 * W, width + 2 * PAD, depth), jnp.float32)
    vmem = pl.BlockSpec(memory_space=pltpu.VMEM)
    near = jax.ShapeDtypeStruct((plan.half, 2 * tiles * plan.size + AUX, depth), jnp.float32)
    far = jax.ShapeDtypeStruct((2 * tiles * plan.size + AUX, depth), jnp.float32)
    return pl.pallas_call(
        functools.partial(outer_kernel, plan),
        in_specs=[vmem] * 7,
        out_specs=[vmem] * (1 + len(plan.batches[2])),
        out_shape=[near] + [far] * len(plan.batches[2]),
        scratch_shapes=[buffer] * 4 + [pltpu.VMEM((3, KINDS, width, depth), jnp.float32)],
        compiler_params=pltpu.CompilerParams(vmem_limit_bytes=16 * 1024 * 1024),
        cost_estimate=pl.CostEstimate(flops=10**8, bytes_accessed=40 * 1024 * 1024, transcendentals=0),
        name="outer",
    )(own, phase, solute, *halos)


def route_kernel(plan, near, *refs):
    pieces, tiles, half, size = plan.pieces, plan.tiles, plan.half, 2 * plan.size
    far, near_out, far_outs, table = refs[:half], refs[half], refs[half + 1 : 2 * half + 1], refs[2 * half + 1]
    held, peers, count = refs[2 * half + 2 :]
    me = lax.axis_index("gy")
    base = me - lax.rem(me, half)
    tail = tiles * size
    for tile in range(tiles):
        for piece in range(half):
            peer = lax.rem(near[piece, tail, tile].astype(jnp.int32), pieces)
            peers[(base + piece) * tiles + tile] = peer
        for index in range(half):
            peer = lax.rem(far[index][tail, tile].astype(jnp.int32), pieces)
            peers[(me ^ (half + index)) * tiles + tile] = peer
    for piece in range(half):
        for tile in range(tiles):
            held[(base + piece) * tiles + tile] = near[piece, tile * size : (tile + 1) * size, :]
    for index in range(half):
        for tile in range(tiles):
            held[(me ^ (half + index)) * tiles + tile] = far[index][tile * size : (tile + 1) * size, :]
    for peer in range(pieces):
        count[peer] = 0
    for home in range(pieces * tiles):
        peer = peers[home]
        slot = count[peer]
        table[peer * tiles + slot] = home
        count[peer] = slot + 1
    for index in range(half):
        for slot in range(tiles):
            far_outs[index][slot] = held[table[(me ^ (half + index)) * tiles + slot]]
            near_out[index, slot] = held[table[(base + index) * tiles + slot]]


def route(plan, near, far):
    tiles, half, size, depth = plan.tiles, plan.half, 2 * plan.size, plan.depth
    vmem = pl.BlockSpec(memory_space=pltpu.VMEM)
    one = jax.ShapeDtypeStruct((tiles, size, depth), jnp.float32)
    count = plan.pieces * tiles
    results = pl.pallas_call(
        functools.partial(route_kernel, plan),
        in_specs=[vmem] * (half + 1),
        out_specs=[vmem] * (half + 1) + [pl.BlockSpec(memory_space=pltpu.SMEM)],
        out_shape=[jax.ShapeDtypeStruct((half, tiles, size, depth), jnp.float32)]
        + [one] * half
        + [jax.ShapeDtypeStruct((count,), jnp.int32)],
        scratch_shapes=[
            pltpu.VMEM((count, size, depth), jnp.float32),
            pltpu.SMEM((count,), jnp.int32),
            pltpu.SMEM((plan.pieces,), jnp.int32),
        ],
        compiler_params=pltpu.CompilerParams(vmem_limit_bytes=16 * 1024 * 1024),
        name="route",
    )(near, *far)
    return results[0], results[1 : half + 1], results[-1]


def settle_kernel(plan, table, near, *refs):
    tiles, half = plan.tiles, plan.half
    far, outs, (ready, sems) = refs[:half], refs[half : half + 2], refs[half + 2 :]
    me = lax.axis_index("gy")
    mine = lax.rem(me, half)
    copies = []
    for slot in range(tiles):
        home = table[me * tiles + slot]
        tile = lax.rem(home, tiles)
        at_home = home // (tiles * half) == me // half

        def put(source, piece, is_far, slot=slot, tile=tile):
            for field in range(2):
                for at, row, name in plan.parts(is_far, piece):
                    col, count = plan.columns(name, tile)
                    if not isinstance(col, int):
                        col = pl.multiple_of(col, 8)
                    ready[field, slot, row, pl.ds(col, count), :] = source[
                        slot, field * plan.size + at : field * plan.size + at + count, :
                    ]

        def put_all(same, put=put):
            for index in range(half):
                put(near.at[index], index, not same)
                put(far[index], mine ^ index, same)

        @pl.when(at_home)
        def _(put_all=put_all):
            put_all(True)

        @pl.when(jnp.logical_not(at_home))
        def _(put_all=put_all):
            put_all(False)

        for field, out in enumerate(outs):
            copy = pltpu.make_async_copy(ready.at[field, slot], out.at[0, slot], sems.at[field, slot])
            copy.start()
            copies.append(copy)
    for copy in copies:
        copy.wait()


def settle(plan, table, near, far):
    tiles, edge, depth = plan.tiles, plan.edge, plan.depth
    out = jax.ShapeDtypeStruct((1, tiles, edge, edge, depth), jnp.float32)
    vmem = pl.BlockSpec(memory_space=pltpu.VMEM)
    return pl.pallas_call(
        functools.partial(settle_kernel, plan),
        in_specs=[pl.BlockSpec(memory_space=pltpu.SMEM)] + [vmem] * (plan.half + 1),
        out_specs=[pl.BlockSpec(memory_space=pl.ANY)] * 2,
        out_shape=[out, out],
        scratch_shapes=[
            pltpu.VMEM((2, tiles, edge, edge, depth), jnp.float32),
            pltpu.SemaphoreType.DMA((2, tiles)),
        ],
        compiler_params=pltpu.CompilerParams(vmem_limit_bytes=16 * 1024 * 1024),
        name="settle",
    )(table, near, *far)


def ring(axis, step):
    count = lax.axis_size(axis)
    return [(i, (i + step) % count) for i in range(count)]


def swap(values, mask):
    return lax.ppermute(values, "gy", [(i, i ^ mask) for i in range(lax.axis_size("gy"))])


def among_half(plan, values, together):
    def exchange(values):
        groups = [list(range(plan.half)), list(range(plan.half, plan.pieces))]
        return lax.all_to_all(values, "gy", 0, 0, axis_index_groups=groups, tiled=True)

    return lax.cond(together, exchange, exchange, values)


def in_vmem(values):
    return pltpu.with_memory_space_constraint(values, pltpu.VMEM)


def per_device(phase, solute, undercool, mobility, diffusivity, owner):
    _, tiles, edge, _, depth = phase.shape
    plan = Plan(lax.axis_size("gy"), tiles, edge, depth)
    half = plan.half
    to_prev, to_next, own = pack_y(phase, solute, (undercool, mobility, diffusivity), owner)
    y_lo = lax.ppermute(to_next, "gy", ring("gy", 1))
    y_hi = lax.ppermute(to_prev, "gy", ring("gy", -1))
    far = {}

    def send_far(batch, values):
        for index, value in zip(plan.batches[batch], values):
            far[index] = swap(value, half + index)

    first = run_inner(plan, 0, own, phase, solute)
    send_far(0, first)
    to_prev, to_next = pack_x(phase, solute, own, y_lo, y_hi, first[0])
    together = owner[0, 0] >= 0

    def around(low, high, *values):
        return ring_swap(low, high), run_inner(plan, 1, *values)

    def ring_swap(low, high):
        return lax.ppermute(low, "gx", ring("gx", 1)), lax.ppermute(high, "gx", ring("gx", -1))

    (x_lo, x_hi), second = lax.cond(together, around, around, to_next, to_prev, own, phase, solute)
    send_far(1, second)
    near, *third = run_outer(plan, own, phase, solute, (y_lo, y_hi, in_vmem(x_lo), in_vmem(x_hi)))
    send_far(2, third)
    far = [far[index] for index in range(half)]
    near = among_half(plan, near, together)
    near, far, table = route(plan, in_vmem(near), far)
    far = [swap(values, half + index) for index, values in enumerate(far)]
    near = among_half(plan, near, together)
    return tuple(settle(plan, table, near, far))


def solution(mesh):
    tile_spec = P("gx", "gy", None, None, None)
    in_specs = (tile_spec, tile_spec) + (P("gx", "gy"),) * 4
    out_spec = P(("gx", "gy"), None, None, None, None)
    return jax.shard_map(
        per_device, mesh=mesh, in_specs=in_specs, out_specs=(out_spec, out_spec), check_vma=False
    )
```

```python
import functools

import jax
import jax.numpy as jnp
from jax import lax
from jax.experimental import pallas as pl
from jax.experimental.pallas import tpu as pltpu
from jax.sharding import PartitionSpec as P

NSTEPS = 4
W = NSTEPS
PAD = 8

aniso_strength = 0.05


def pack_y_kernel(under, mobile, spread, owner, phase_lo, phase_hi, solute_lo, solute_hi, to_prev, to_next, own):
    edge, depth = phase_lo.shape[2], phase_lo.shape[4]
    tiles = own.shape[0] // 8 - 1
    to_prev[:edge, :W, :] = phase_lo[0, 0, :, :W, :]
    to_prev[:edge, W:, :] = solute_lo[0, 0, :, :W, :]
    to_next[:edge, :W, :] = phase_hi[0, 0, :, W:, :]
    to_next[:edge, W:, :] = solute_hi[0, 0, :, W:, :]
    line = lax.broadcasted_iota(jnp.int32, (8, depth), 0)
    lane = lax.broadcasted_iota(jnp.int32, (8, depth), 1)
    names = jnp.zeros((8, depth), jnp.float32)
    for tile in range(tiles):
        rows = jnp.zeros((8, depth), jnp.float32)
        ready = (2.0 * under[0, tile], mobile[0, tile], spread[0, tile], 1.0 - 6.0 * spread[0, tile])
        for kind, coef in enumerate(ready):
            rows = jnp.where(line == kind, coef, rows)
        own[8 * tile : 8 * tile + 8, :] = rows
        if tile == 0:
            to_prev[edge] = rows
        if tile == tiles - 1:
            to_next[edge] = rows
        names = jnp.where(lane == tile, owner[0, tile].astype(jnp.float32), names)
    own[8 * tiles :, :] = names


def pack_y(phase, solute, coef, owner):
    _, tiles, edge, _, depth = phase.shape
    low = pl.BlockSpec((1, 1, edge, 2 * W, depth), lambda i: (0, 0, 0, 0, 0))
    high = pl.BlockSpec((1, 1, edge, 2 * W, depth), lambda i: (0, tiles - 1, 0, edge // (2 * W) - 1, 0))
    face = jax.ShapeDtypeStruct((edge + 1, 2 * W, depth), jnp.float32)
    own = jax.ShapeDtypeStruct((8 * tiles + 8, depth), jnp.float32)
    whole = pl.BlockSpec((edge + 1, 2 * W, depth), lambda i: (0, 0, 0))
    return pl.pallas_call(
        pack_y_kernel,
        grid=(1,),
        in_specs=[pl.BlockSpec(memory_space=pltpu.SMEM)] * 4 + [low, high, low, high],
        out_specs=[whole, whole, pl.BlockSpec((8 * tiles + 8, depth), lambda i: (0, 0))],
        out_shape=[face, face, own],
        name="pack_y",
    )(*coef, owner, phase, phase, solute, solute)


def fill_row(dst, row, phase_row, solute_row, lo, hi):
    start = PAD
    dst[0][row, start : start + W, :] = lo[:W]
    dst[1][row, start : start + W, :] = 2.0 * lo[W:]
    start += W
    for values in phase_row:
        size = values.shape[0]
        dst[0][row, start : start + size, :] = values
        start += size
    dst[0][row, start : start + W, :] = hi[:W]
    dst[1][row, start : start + W, :] = 2.0 * hi[W:]
    start = PAD + W
    for values in solute_row:
        size = values.shape[0]
        dst[1][row, start : start + size, :] = 2.0 * values
        start += size


def pack_x_kernel(own, phase_lo, phase_hi, solute_lo, solute_hi, y_lo, y_hi, _, to_prev, to_next):
    tiles, edge, depth = phase_lo.shape[1], phase_lo.shape[3], phase_lo.shape[4]
    width = tiles * edge + 2 * W
    for out, phase, solute, first in (
        (to_prev, phase_lo, solute_lo, 0),
        (to_next, phase_hi, solute_hi, edge - W),
    ):
        for row in range(W):
            for field, values, half in ((0, phase, 0), (1, solute, W)):
                at = (2 * row + field) * width
                out[at : at + W, :] = y_lo[first + row, half : half + W, :]
                for tile in range(tiles):
                    begin = at + W + tile * edge
                    out[begin : begin + edge, :] = values[0, tile, row]
                out[at + width - W : at + width, :] = y_hi[first + row, half : half + W, :]
        at = 2 * W * width
        out[at : at + 8, :] = y_lo[edge]
        out[at + 8 : at + 16, :] = y_hi[edge]
        out[at + 16 : at + 16 + 8 * tiles, :] = own[: 8 * tiles, :]


def pack_x(phase, solute, own, y_lo, y_hi, after):
    _, tiles, edge, _, depth = phase.shape
    low = pl.BlockSpec((1, tiles, W, edge, depth), lambda i: (0, 0, 0, 0, 0))
    high = pl.BlockSpec((1, tiles, W, edge, depth), lambda i: (0, 0, edge // W - 1, 0, 0))
    side = pl.BlockSpec((edge + 1, 2 * W, depth), lambda i: (0, 0, 0))
    rows = 2 * W * (tiles * edge + 2 * W) + 8 * (tiles + 2)
    out = jax.ShapeDtypeStruct((rows, depth), jnp.float32)
    whole = pl.BlockSpec((rows, depth), lambda i: (0, 0))
    return pl.pallas_call(
        pack_x_kernel,
        grid=(1,),
        in_specs=[pl.BlockSpec((8 * tiles + 8, depth), lambda i: (0, 0)), low, high, low, high, side, side, pl.BlockSpec(memory_space=pl.ANY)],
        out_specs=[whole, whole],
        out_shape=[out, out],
        compiler_params=pltpu.CompilerParams(vmem_limit_bytes=8 * 1024 * 1024),
        name="pack_x",
    )(own, phase, phase, solute, solute, y_lo, y_hi, after)


def update(near_p, near_v, under, mobile, spread, keep):
    p, p_xl, p_xh, p_yl, p_yh = near_p
    v, v_xl, v_xh, v_yl, v_yh = near_v
    depth = p.shape[-1]
    lane = lax.broadcasted_iota(jnp.int32, p.shape, 1)
    first, last = lane == 0, lane == depth - 1
    p_zl = jnp.where(first, p, pltpu.roll(p, 1, 1))
    p_zh = jnp.where(last, p, pltpu.roll(p, depth - 1, 1))
    v_zl = jnp.where(first, v, pltpu.roll(v, 1, 1))
    v_zh = jnp.where(last, v, pltpu.roll(v, depth - 1, 1))
    dx, dy, dz = p_xh - p_xl, p_yh - p_yl, p_zh - p_zl
    qx, qy, qz = dx * dx, dy * dy, dz * dz
    flat = qx + qy
    total = flat + qz
    pairs = qx * qy + flat * qz
    base = total + 4.0
    guess = pl.reciprocal(base, approx=True)
    inverse = guess * (2.0 - base * guess)
    extra = (aniso_strength * total * total - (8.0 * aniso_strength) * pairs) * (inverse * inverse)
    lap_p = (p_xl + p_xh) + (p_yl + p_yh) + (p_zl + p_zh) - 6.0 * p
    sum_v = (v_xl + v_xh) + (v_yl + v_yh) + (v_zl + v_zh)
    well = 1.0 - p * p
    change = mobile * (lap_p + extra * lap_p + well * (p - well * (under + v)))
    return p + change, keep * v + spread * sum_v + change


KINDS = 4


def cells(src_p, src_u, row, start, coefs):
    near = []
    for src in (src_p, src_u):
        near.append(
            (
                src[row, start : start + 8, :],
                src[row - 1, start : start + 8, :],
                src[row + 1, start : start + 8, :],
                src[row, start - 1 : start + 7, :],
                src[row, start + 1 : start + 9, :],
            )
        )
    return update(near[0], near[1], *coefs)


class Plan:
    def __init__(self, pieces, tiles, edge, depth):
        self.pieces, self.tiles, self.edge, self.depth = pieces, tiles, edge, depth
        self.half = pieces // 2
        self.inner = edge - 2 * W
        self.rows = self.inner // self.half
        self.rows_far = (self.inner - 2 * W) // self.half
        self.rows_near = 2 * W // self.half
        self.middle = edge - 16
        self.size = self.rows * self.middle + self.rows_far * 8

        begins = [min(W + p * self.rows, 2 * W + p * self.rows_far) for p in range(self.half)]
        ends = [max(W + p * self.rows + self.rows, 2 * W + (p + 1) * self.rows_far) for p in range(self.half)]
        self.span = max(end - begin for begin, end in zip(begins, ends))
        side = self.half // 2
        self.batches = (list(range(side)), [side], list(range(side + 1, self.half)))

    def batch_rows(self, batch, mine):
        if batch == 0:
            count = self.inner // 2
            return W + mine // (self.half // 2) * count, count
        piece = mine ^ self.batches[1][0]
        begin = jnp.minimum(W + piece * self.rows, 2 * W + piece * self.rows_far)
        return jnp.minimum(begin, self.edge - W - self.span), self.span

    def near_row(self, piece, row, gap):
        index = piece * self.rows_near + row
        return index + jnp.where(index < W, 0, gap)

    def parts(self, far, piece):
        at, found = 0, []
        if far:
            for row in range(self.rows):
                found.append((at, W + piece * self.rows + row, "middle"))
                at += self.middle
            for row in range(self.rows_far):
                found.append((at, 2 * W + piece * self.rows_far + row, "last"))
                at += 8
        else:
            for row in range(self.rows_near):
                found.append((at, self.near_row(piece, row, self.inner), "whole"))
                at += self.edge
            for row in range(self.rows):
                found.append((at, W + piece * self.rows + row, "side"))
                at += 8
            for row in range(self.rows_near):
                found.append((at, W + self.near_row(piece, row, self.inner - 2 * W), "last"))
                at += 8
        assert at == self.size
        return found

    def columns(self, name, tile):
        if name == "whole":
            return 0, self.edge
        if name == "middle":
            return 8, self.middle
        low, high = (tile, 1 - tile) if name == "side" else (1 - tile, tile)
        return low * (self.edge - 8), 8


AUX = 8
UNROLL = 8


def march(count, row_of, starts, source, target, coefs_of):
    def one_row(index, carry):
        row = row_of(index)
        for start in starts:
            new_p, new_u = cells(source[0], source[1], row, start, coefs_of(row, start))
            target[0][row, start : start + 8, :] = new_p
            target[1][row, start : start + 8, :] = new_u
        return carry

    lax.fori_loop(0, count, one_row, 0, unroll=UNROLL)


def inner_kernel(plan, batch, own, phase, solute, *rest):
    tiles, edge, indices = plan.tiles, plan.edge, plan.batches[batch]
    outs, scratch = rest[: len(indices)], rest[len(indices) :]
    pairs = (scratch[:2], scratch[2:])
    mine = lax.rem(lax.axis_index("gy"), plan.half)
    begin, count = plan.batch_rows(batch, mine)
    base = begin - W

    def load_row(row, carry):
        for tile in range(tiles):
            start = PAD + tile * edge
            pairs[0][0][row, start : start + edge, :] = phase[0, tile, base + row]
            pairs[0][1][row, start : start + edge, :] = 2.0 * solute[0, tile, base + row]
        return carry

    lax.fori_loop(0, count + 2 * W, load_row, 0, unroll=UNROLL)

    line = lax.broadcasted_iota(jnp.int32, (8, plan.depth), 0)

    def coefs_of(row, start):
        low, high = (start - PAD) // edge, (start + 7 - PAD) // edge
        rows = [[own[8 * tile + kind : 8 * tile + kind + 1, :] for tile in (low, high)] for kind in range(KINDS)]
        if low == high:
            return tuple(pair[0] for pair in rows)
        return tuple(jnp.where(line < W, *pair) for pair in rows)

    for step in range(NSTEPS):
        margin = 8 if step == NSTEPS - 1 else W
        starts = range(PAD + margin, PAD + tiles * edge - margin, 8)
        rows = count + 2 * W - 2 * (step + 1)
        march(rows, lambda i, step=step: step + 1 + i, starts, pairs[step % 2], pairs[(step + 1) % 2], coefs_of)
    for index, out in zip(indices, outs):
        pack(plan, True, mine ^ index, pairs[NSTEPS % 2], -base, PAD, own, out)


def pack(plan, far, piece, done, row_shift, col_shift, own, out):
    for tile in range(plan.tiles):
        for field, values in enumerate(done):
            begin = (2 * tile + field) * plan.size
            for at, row, name in plan.parts(far, piece):
                col, count = plan.columns(name, tile)
                start = col_shift + tile * plan.edge + col
                cells = values[row + row_shift, start : start + count, :]
                out[begin + at : begin + at + count, :] = 0.5 * cells if field else cells
    tail = 2 * plan.tiles * plan.size
    out[tail : tail + AUX, :] = own[8 * plan.tiles : 8 * plan.tiles + AUX, :]


def run_inner(plan, batch, own, phase, solute):
    rows = plan.batch_rows(batch, 0)[1] + 2 * W
    count = len(plan.batches[batch])
    buffer = pltpu.VMEM((rows, plan.tiles * plan.edge + 2 * PAD, plan.depth), jnp.float32)
    vmem = pl.BlockSpec(memory_space=pltpu.VMEM)
    shape = jax.ShapeDtypeStruct((2 * plan.tiles * plan.size + AUX, plan.depth), jnp.float32)
    return pl.pallas_call(
        functools.partial(inner_kernel, plan, batch),
        in_specs=[vmem] * 3,
        out_specs=[vmem] * count,
        out_shape=[shape] * count,
        scratch_shapes=[buffer] * 4,
        compiler_params=pltpu.CompilerParams(vmem_limit_bytes=16 * 1024 * 1024),
        cost_estimate=pl.CostEstimate(flops=10**8, bytes_accessed=24 * 1024 * 1024, transcendentals=0),
        name="inner",
    )(own, phase, solute)


def outer_kernel(plan, own, phase_in, solute_in, y_lo, y_hi, x_lo, x_hi, out, *rest):
    tiles, edge, depth, half = plan.tiles, plan.edge, plan.depth, plan.half
    late = plan.batches[2]
    far_outs, scratch = rest[: len(late)], rest[len(late) :]
    pairs, coefs, phase, solute, sems = (scratch[:2], scratch[2:4]), *scratch[4:]
    copies = []
    for field, (source, target) in enumerate(((phase_in, phase), (solute_in, solute))):
        copies.append(pltpu.make_async_copy(source, target, sems.at[field]))
        copies[-1].start()
    cols = tiles * edge
    width = cols + 2 * W
    for zone, source in ((0, x_lo), (1, None), (2, x_hi)):
        for kind in range(KINDS):
            if source is None:
                parts = [y_lo[edge, kind : kind + 1, :]]
                parts += [own[8 * tile + kind : 8 * tile + kind + 1, :] for tile in range(tiles)]
                parts += [y_hi[edge, kind : kind + 1, :]]
            else:
                at = 2 * W * width + kind
                parts = [source[at : at + 1, :]]
                parts += [source[at + 16 + 8 * tile : at + 17 + 8 * tile, :] for tile in range(tiles)]
                parts += [source[at + 8 : at + 9, :]]
            coefs[zone, kind, :W, :] = jnp.broadcast_to(parts[0], (W, depth))
            for tile in range(tiles):
                begin = W + tile * edge
                coefs[zone, kind, begin : begin + edge, :] = jnp.broadcast_to(parts[1 + tile], (edge, depth))
            coefs[zone, kind, width - W :, :] = jnp.broadcast_to(parts[-1], (W, depth))
    for source, first in ((x_lo, 0), (x_hi, edge + W)):
        for row in range(W):
            for field in range(2):
                at = (2 * row + field) * width
                values = source[at : at + width, :]
                pairs[0][field][first + row, PAD : PAD + width, :] = 2.0 * values if field else values

    def load_row(row, carry):
        fill_row(
            pairs[0],
            W + row,
            [phase[0, tile, row] for tile in range(tiles)],
            [solute[0, tile, row] for tile in range(tiles)],
            y_lo[row],
            y_hi[row],
        )
        return carry

    for copy in copies:
        copy.wait()
    lax.fori_loop(0, edge, load_row, 0, unroll=UNROLL)

    def coefs_of(zone):
        def found(row, start):
            return tuple(coefs[zone(row), kind, start - PAD : start - PAD + 8, :] for kind in range(KINDS))

        return found

    any_zone = coefs_of(lambda row: jnp.where(row < W, 0, jnp.where(row < W + edge, 1, 2)))

    own_zone = coefs_of(lambda row: 1)
    mine = lax.rem(lax.axis_index("gy"), half)
    made = plan.inner // 2
    first_made = 2 * W + mine // (half // 2) * made

    def blocks(first, last):
        low, high = (first + W - shift) // 8 * 8, -(-(last + W - shift) // 8) * 8
        return list(range(PAD + shift + low, PAD + shift + high, 8))

    for step in range(1, NSTEPS + 1):
        source, target = pairs[(step - 1) % 2], pairs[step % 2]
        left = NSTEPS - step
        shift = W if step == NSTEPS else 0
        whole = blocks(-left, cols + left)
        ends = blocks(-left, 8 + left) + blocks(cols - 8 - left, cols + left)
        for tile in range(tiles):
            col, count = plan.columns("last", tile)
            ends += blocks(tile * edge + col - left, tile * edge + col + count + left)
        gap, gap_rows = first_made + left, made - 2 * left

        def outside(index, left=left, gap=gap, gap_rows=gap_rows):
            row = W - left + index
            return row + jnp.where(row < gap, 0, gap_rows)

        march(edge + 2 * left - gap_rows, outside, whole, source, target, any_zone)
        march(gap_rows, lambda i, gap=gap: gap + i, sorted(set(ends)), source, target, own_zone)
    done = pairs[NSTEPS % 2]
    for index, far_out in zip(late, far_outs):
        pack(plan, True, mine ^ index, done, W, PAD + W, own, far_out)
    for piece in range(half):
        pack(plan, False, piece, done, W, PAD + W, own, out.at[piece])


def run_outer(plan, own, phase, solute, halos):
    tiles, edge, depth = plan.tiles, plan.edge, plan.depth
    width = tiles * edge + 2 * W
    buffer = pltpu.VMEM((edge + 2 * W, width + 2 * PAD, depth), jnp.float32)
    vmem = pl.BlockSpec(memory_space=pltpu.VMEM)
    near = jax.ShapeDtypeStruct((plan.half, 2 * tiles * plan.size + AUX, depth), jnp.float32)
    far = jax.ShapeDtypeStruct((2 * tiles * plan.size + AUX, depth), jnp.float32)
    return pl.pallas_call(
        functools.partial(outer_kernel, plan),
        in_specs=[vmem] + [pl.BlockSpec(memory_space=pl.ANY)] * 2 + [vmem] * 4,
        out_specs=[vmem] * (1 + len(plan.batches[2])),
        out_shape=[near] + [far] * len(plan.batches[2]),
        scratch_shapes=[buffer] * 4 + [pltpu.VMEM((3, KINDS, width, depth), jnp.float32)]
        + [pltpu.VMEM(phase.shape, jnp.float32)] * 2
        + [pltpu.SemaphoreType.DMA((2,))],
        compiler_params=pltpu.CompilerParams(vmem_limit_bytes=16 * 1024 * 1024),
        cost_estimate=pl.CostEstimate(flops=10**8, bytes_accessed=40 * 1024 * 1024, transcendentals=0),
        name="outer",
    )(own, phase, solute, *halos)


def route_kernel(plan, near, *refs):
    pieces, tiles, half, size = plan.pieces, plan.tiles, plan.half, 2 * plan.size
    far, near_out, far_outs, table = refs[:half], refs[half], refs[half + 1 : 2 * half + 1], refs[2 * half + 1]
    held, peers, count, names, sems = refs[2 * half + 2 :]
    me = lax.axis_index("gy")
    base = me - lax.rem(me, half)
    tail = tiles * size
    names_copy = pltpu.make_async_copy(near.at[:, pl.ds(tail, AUX), :], names, sems.at[half * tiles])
    names_copy.start()
    copies = []
    for piece in range(half):
        for tile in range(tiles):
            source = near.at[piece, pl.ds(tile * size, size), :]
            copy = pltpu.make_async_copy(source, held.at[(base + piece) * tiles + tile], sems.at[len(copies)])
            copy.start()
            copies.append(copy)
    for tile in range(tiles):
        for index in range(half):
            peer = lax.rem(far[index][tail, tile].astype(jnp.int32), pieces)
            peers[(me ^ (half + index)) * tiles + tile] = peer
    for index in range(half):
        for tile in range(tiles):
            held[(me ^ (half + index)) * tiles + tile] = far[index][tile * size : (tile + 1) * size, :]
    for peer in range(pieces):
        count[peer] = 0
    names_copy.wait()
    for tile in range(tiles):
        for piece in range(half):
            peer = lax.rem(names[piece, 0, tile].astype(jnp.int32), pieces)
            peers[(base + piece) * tiles + tile] = peer
    for home in range(pieces * tiles):
        peer = peers[home]
        slot = count[peer]
        table[peer * tiles + slot] = home
        count[peer] = slot + 1
    for copy in copies:
        copy.wait()
    for index in range(half):
        for slot in range(tiles):
            far_outs[index][slot] = held[table[(me ^ (half + index)) * tiles + slot]]
            near_out[index, slot] = held[table[(base + index) * tiles + slot]]


def route(plan, near, far):
    tiles, half, size, depth = plan.tiles, plan.half, 2 * plan.size, plan.depth
    vmem = pl.BlockSpec(memory_space=pltpu.VMEM)
    one = jax.ShapeDtypeStruct((tiles, size, depth), jnp.float32)
    count = plan.pieces * tiles
    results = pl.pallas_call(
        functools.partial(route_kernel, plan),
        in_specs=[pl.BlockSpec(memory_space=pl.ANY)] + [vmem] * half,
        out_specs=[vmem] * (half + 1) + [pl.BlockSpec(memory_space=pltpu.SMEM)],
        out_shape=[jax.ShapeDtypeStruct((half, tiles, size, depth), jnp.float32)]
        + [one] * half
        + [jax.ShapeDtypeStruct((count,), jnp.int32)],
        scratch_shapes=[
            pltpu.VMEM((count, size, depth), jnp.float32),
            pltpu.SMEM((count,), jnp.int32),
            pltpu.SMEM((plan.pieces,), jnp.int32),
            pltpu.SMEM((half, AUX, depth), jnp.float32),
            pltpu.SemaphoreType.DMA((half * tiles + 1,)),
        ],
        compiler_params=pltpu.CompilerParams(vmem_limit_bytes=16 * 1024 * 1024),
        name="route",
    )(near, *far)
    return results[0], results[1 : half + 1], results[-1]


def settle_kernel(plan, table, near, *refs):
    tiles, half = plan.tiles, plan.half
    far, outs, (ready, sems) = refs[:half], refs[half : half + 2], refs[half + 2 :]
    me = lax.axis_index("gy")
    mine = lax.rem(me, half)
    copies = []
    for slot in range(tiles):
        home = table[me * tiles + slot]
        tile = lax.rem(home, tiles)
        at_home = home // (tiles * half) == me // half

        def put(source, piece, is_far, slot=slot, tile=tile):
            for field in range(2):
                for at, row, name in plan.parts(is_far, piece):
                    col, count = plan.columns(name, tile)
                    if not isinstance(col, int):
                        col = pl.multiple_of(col, 8)
                    ready[field, slot, row, pl.ds(col, count), :] = source[
                        slot, field * plan.size + at : field * plan.size + at + count, :
                    ]

        def put_all(same, put=put):
            for index in range(half):
                put(near.at[index], index, not same)
                put(far[index], mine ^ index, same)

        @pl.when(at_home)
        def _(put_all=put_all):
            put_all(True)

        @pl.when(jnp.logical_not(at_home))
        def _(put_all=put_all):
            put_all(False)

        for field, out in enumerate(outs):
            copy = pltpu.make_async_copy(ready.at[field, slot], out.at[0, slot], sems.at[field, slot])
            copy.start()
            copies.append(copy)
    for copy in copies:
        copy.wait()


def settle(plan, table, near, far):
    tiles, edge, depth = plan.tiles, plan.edge, plan.depth
    out = jax.ShapeDtypeStruct((1, tiles, edge, edge, depth), jnp.float32)
    vmem = pl.BlockSpec(memory_space=pltpu.VMEM)
    return pl.pallas_call(
        functools.partial(settle_kernel, plan),
        in_specs=[pl.BlockSpec(memory_space=pltpu.SMEM)] + [vmem] * (plan.half + 1),
        out_specs=[pl.BlockSpec(memory_space=pl.ANY)] * 2,
        out_shape=[out, out],
        scratch_shapes=[
            pltpu.VMEM((2, tiles, edge, edge, depth), jnp.float32),
            pltpu.SemaphoreType.DMA((2, tiles)),
        ],
        compiler_params=pltpu.CompilerParams(vmem_limit_bytes=16 * 1024 * 1024),
        name="settle",
    )(table, near, *far)


def ring(axis, step):
    count = lax.axis_size(axis)
    return [(i, (i + step) % count) for i in range(count)]


def swap(values, mask):
    return lax.ppermute(values, "gy", [(i, i ^ mask) for i in range(lax.axis_size("gy"))])


def among_half(plan, values, together):
    def exchange(values):
        groups = [list(range(plan.half)), list(range(plan.half, plan.pieces))]
        return lax.all_to_all(values, "gy", 0, 0, axis_index_groups=groups, tiled=True)

    return lax.cond(together, exchange, exchange, values)


def per_device(phase, solute, undercool, mobility, diffusivity, owner):
    _, tiles, edge, _, depth = phase.shape
    plan = Plan(lax.axis_size("gy"), tiles, edge, depth)
    half = plan.half
    to_prev, to_next, own = pack_y(phase, solute, (undercool, mobility, diffusivity), owner)
    y_lo = lax.ppermute(to_next, "gy", ring("gy", 1))
    y_hi = lax.ppermute(to_prev, "gy", ring("gy", -1))
    far = {}

    def send_far(batch, values):
        for index, value in zip(plan.batches[batch], values):
            far[index] = swap(value, half + index)

    first = run_inner(plan, 0, own, phase, solute)
    send_far(0, first)
    to_prev, to_next = pack_x(phase, solute, own, y_lo, y_hi, first[0])
    together = owner[0, 0] >= 0

    def around(low, high, *values):
        return ring_swap(low, high), run_inner(plan, 1, *values)

    def ring_swap(low, high):
        return lax.ppermute(low, "gx", ring("gx", 1)), lax.ppermute(high, "gx", ring("gx", -1))

    (x_lo, x_hi), second = lax.cond(together, around, around, to_next, to_prev, own, phase, solute)
    send_far(1, second)
    near, *third = run_outer(plan, own, phase, solute, (y_lo, y_hi, x_lo, x_hi))
    send_far(2, third)
    far = [far[index] for index in range(half)]
    near = among_half(plan, near, together)
    near, far, table = route(plan, near, far)
    far = [swap(values, half + index) for index, values in enumerate(far)]
    near = among_half(plan, near, together)
    return tuple(settle(plan, table, near, far))


def solution(mesh):
    tile_spec = P("gx", "gy", None, None, None)
    in_specs = (tile_spec, tile_spec) + (P("gx", "gy"),) * 4
    out_spec = P(("gx", "gy"), None, None, None, None)
    return jax.shard_map(
        per_device, mesh=mesh, in_specs=in_specs, out_specs=(out_spec, out_spec), check_vma=False
    )
```

```python
import functools

import jax
import jax.numpy as jnp
from jax import lax
from jax.experimental import pallas as pl
from jax.experimental.pallas import tpu as pltpu
from jax.sharding import PartitionSpec as P

NSTEPS = 4
W = NSTEPS
PAD = 8

aniso_strength = 0.05


def pack_y_kernel(under, mobile, spread, owner, phase_lo, phase_hi, solute_lo, solute_hi, to_prev, to_next, own):
    edge, depth = phase_lo.shape[2], phase_lo.shape[4]
    tiles = own.shape[0] // 8 - 1
    to_prev[:edge, :W, :] = phase_lo[0, 0, :, :W, :]
    to_prev[:edge, W:, :] = solute_lo[0, 0, :, :W, :]
    to_next[:edge, :W, :] = phase_hi[0, 0, :, W:, :]
    to_next[:edge, W:, :] = solute_hi[0, 0, :, W:, :]
    line = lax.broadcasted_iota(jnp.int32, (8, depth), 0)
    lane = lax.broadcasted_iota(jnp.int32, (8, depth), 1)
    names = jnp.zeros((8, depth), jnp.float32)
    for tile in range(tiles):
        rows = jnp.zeros((8, depth), jnp.float32)
        ready = (2.0 * under[0, tile], mobile[0, tile], spread[0, tile], 1.0 - 6.0 * spread[0, tile])
        for kind, coef in enumerate(ready):
            rows = jnp.where(line == kind, coef, rows)
        own[8 * tile : 8 * tile + 8, :] = rows
        if tile == 0:
            to_prev[edge] = rows
        if tile == tiles - 1:
            to_next[edge] = rows
        names = jnp.where(lane == tile, owner[0, tile].astype(jnp.float32), names)
    own[8 * tiles :, :] = names


def pack_y(phase, solute, coef, owner):
    _, tiles, edge, _, depth = phase.shape
    low = pl.BlockSpec((1, 1, edge, 2 * W, depth), lambda i: (0, 0, 0, 0, 0))
    high = pl.BlockSpec((1, 1, edge, 2 * W, depth), lambda i: (0, tiles - 1, 0, edge // (2 * W) - 1, 0))
    face = jax.ShapeDtypeStruct((edge + 1, 2 * W, depth), jnp.float32)
    own = jax.ShapeDtypeStruct((8 * tiles + 8, depth), jnp.float32)
    whole = pl.BlockSpec((edge + 1, 2 * W, depth), lambda i: (0, 0, 0))
    return pl.pallas_call(
        pack_y_kernel,
        grid=(1,),
        in_specs=[pl.BlockSpec(memory_space=pltpu.SMEM)] * 4 + [low, high, low, high],
        out_specs=[whole, whole, pl.BlockSpec((8 * tiles + 8, depth), lambda i: (0, 0))],
        out_shape=[face, face, own],
        name="pack_y",
    )(*coef, owner, phase, phase, solute, solute)


def fill_row(dst, row, phase_row, solute_row, lo, hi):
    start = PAD
    dst[0][row, start : start + W, :] = lo[:W]
    dst[1][row, start : start + W, :] = 2.0 * lo[W:]
    start += W
    for values in phase_row:
        size = values.shape[0]
        dst[0][row, start : start + size, :] = values
        start += size
    dst[0][row, start : start + W, :] = hi[:W]
    dst[1][row, start : start + W, :] = 2.0 * hi[W:]
    start = PAD + W
    for values in solute_row:
        size = values.shape[0]
        dst[1][row, start : start + size, :] = 2.0 * values
        start += size


def pack_x_kernel(own, phase_lo, phase_hi, solute_lo, solute_hi, y_lo, y_hi, _, to_prev, to_next):
    tiles, edge, depth = phase_lo.shape[1], phase_lo.shape[3], phase_lo.shape[4]
    width = tiles * edge + 2 * W
    for out, phase, solute, first in (
        (to_prev, phase_lo, solute_lo, 0),
        (to_next, phase_hi, solute_hi, edge - W),
    ):
        for row in range(W):
            for field, values, half in ((0, phase, 0), (1, solute, W)):
                at = (2 * row + field) * width
                out[at : at + W, :] = y_lo[first + row, half : half + W, :]
                for tile in range(tiles):
                    begin = at + W + tile * edge
                    out[begin : begin + edge, :] = values[0, tile, row]
                out[at + width - W : at + width, :] = y_hi[first + row, half : half + W, :]
        at = 2 * W * width
        out[at : at + 8, :] = y_lo[edge]
        out[at + 8 : at + 16, :] = y_hi[edge]
        out[at + 16 : at + 16 + 8 * tiles, :] = own[: 8 * tiles, :]


def pack_x(phase, solute, own, y_lo, y_hi, after):
    _, tiles, edge, _, depth = phase.shape
    low = pl.BlockSpec((1, tiles, W, edge, depth), lambda i: (0, 0, 0, 0, 0))
    high = pl.BlockSpec((1, tiles, W, edge, depth), lambda i: (0, 0, edge // W - 1, 0, 0))
    side = pl.BlockSpec((edge + 1, 2 * W, depth), lambda i: (0, 0, 0))
    rows = 2 * W * (tiles * edge + 2 * W) + 8 * (tiles + 2)
    out = jax.ShapeDtypeStruct((rows, depth), jnp.float32)
    whole = pl.BlockSpec((rows, depth), lambda i: (0, 0))
    return pl.pallas_call(
        pack_x_kernel,
        grid=(1,),
        in_specs=[pl.BlockSpec((8 * tiles + 8, depth), lambda i: (0, 0)), low, high, low, high, side, side, pl.BlockSpec(memory_space=pl.ANY)],
        out_specs=[whole, whole],
        out_shape=[out, out],
        compiler_params=pltpu.CompilerParams(vmem_limit_bytes=8 * 1024 * 1024),
        name="pack_x",
    )(own, phase, phase, solute, solute, y_lo, y_hi, after)


def update(near_p, near_v, under, mobile, spread, keep):
    p, p_xl, p_xh, p_yl, p_yh = near_p
    v, v_xl, v_xh, v_yl, v_yh = near_v
    depth = p.shape[-1]
    lane = lax.broadcasted_iota(jnp.int32, p.shape, 1)
    first, last = lane == 0, lane == depth - 1
    p_zl = jnp.where(first, p, pltpu.roll(p, 1, 1))
    p_zh = jnp.where(last, p, pltpu.roll(p, depth - 1, 1))
    v_zl = jnp.where(first, v, pltpu.roll(v, 1, 1))
    v_zh = jnp.where(last, v, pltpu.roll(v, depth - 1, 1))
    dx, dy, dz = p_xh - p_xl, p_yh - p_yl, p_zh - p_zl
    qx, qy, qz = dx * dx, dy * dy, dz * dz
    flat = qx + qy
    total = flat + qz
    pairs = qx * qy + flat * qz
    base = total + 4.0
    guess = pl.reciprocal(base, approx=True)
    inverse = guess * (2.0 - base * guess)
    extra = (aniso_strength * total * total - (8.0 * aniso_strength) * pairs) * (inverse * inverse)
    lap_p = (p_xl + p_xh) + (p_yl + p_yh) + (p_zl + p_zh) - 6.0 * p
    sum_v = (v_xl + v_xh) + (v_yl + v_yh) + (v_zl + v_zh)
    well = 1.0 - p * p
    change = mobile * (lap_p + extra * lap_p + well * (p - well * (under + v)))
    return p + change, keep * v + spread * sum_v + change


KINDS = 4


def cells(src_p, src_u, row, start, coefs):
    near = []
    for src in (src_p, src_u):
        near.append(
            (
                src[row, start : start + 8, :],
                src[row - 1, start : start + 8, :],
                src[row + 1, start : start + 8, :],
                src[row, start - 1 : start + 7, :],
                src[row, start + 1 : start + 9, :],
            )
        )
    return update(near[0], near[1], *coefs)


class Plan:
    def __init__(self, pieces, tiles, edge, depth):
        self.pieces, self.tiles, self.edge, self.depth = pieces, tiles, edge, depth
        self.half = pieces // 2
        self.inner = edge - 2 * W
        self.rows = self.inner // self.half
        self.rows_far = (self.inner - 2 * W) // self.half
        self.rows_near = 2 * W // self.half
        self.middle = edge - 16
        self.size = self.rows * self.middle + self.rows_far * 8

        begins = [min(W + p * self.rows, 2 * W + p * self.rows_far) for p in range(self.half)]
        ends = [max(W + p * self.rows + self.rows, 2 * W + (p + 1) * self.rows_far) for p in range(self.half)]
        self.span = max(end - begin for begin, end in zip(begins, ends))
        side = self.half // 2
        self.batches = (list(range(side)), [side], list(range(side + 1, self.half)))

    def batch_rows(self, batch, mine):
        if batch == 0:
            count = self.inner // 2
            return W + mine // (self.half // 2) * count, count
        piece = mine ^ self.batches[1][0]
        begin = jnp.minimum(W + piece * self.rows, 2 * W + piece * self.rows_far)
        return jnp.minimum(begin, self.edge - W - self.span), self.span

    def near_row(self, piece, row, gap):
        index = piece * self.rows_near + row
        return index + jnp.where(index < W, 0, gap)

    def parts(self, far, piece):
        at, found = 0, []
        if far:
            for row in range(self.rows):
                found.append((at, W + piece * self.rows + row, "middle"))
                at += self.middle
            for row in range(self.rows_far):
                found.append((at, 2 * W + piece * self.rows_far + row, "last"))
                at += 8
        else:
            for row in range(self.rows_near):
                found.append((at, self.near_row(piece, row, self.inner), "whole"))
                at += self.edge
            for row in range(self.rows):
                found.append((at, W + piece * self.rows + row, "side"))
                at += 8
            for row in range(self.rows_near):
                found.append((at, W + self.near_row(piece, row, self.inner - 2 * W), "last"))
                at += 8
        assert at == self.size
        return found

    def columns(self, name, tile):
        if name == "whole":
            return 0, self.edge
        if name == "middle":
            return 8, self.middle
        low, high = (tile, 1 - tile) if name == "side" else (1 - tile, tile)
        return low * (self.edge - 8), 8


AUX = 8
UNROLL = 4


def march(count, row_of, starts, source, target, coefs_of):
    def one_row(index, carry):
        row = row_of(index)
        for start in starts:
            new_p, new_u = cells(source[0], source[1], row, start, coefs_of(row, start))
            target[0][row, start : start + 8, :] = new_p
            target[1][row, start : start + 8, :] = new_u
        return carry

    lax.fori_loop(0, count, one_row, 0, unroll=UNROLL)


def inner_kernel(plan, batch, own, phase, solute, *rest):
    tiles, edge, indices = plan.tiles, plan.edge, plan.batches[batch]
    outs, scratch = rest[: len(indices)], rest[len(indices) :]
    pairs = (scratch[:2], scratch[2:])
    mine = lax.rem(lax.axis_index("gy"), plan.half)
    begin, count = plan.batch_rows(batch, mine)
    base = begin - W

    def load_row(row, carry):
        for tile in range(tiles):
            start = PAD + tile * edge
            pairs[0][0][row, start : start + edge, :] = phase[0, tile, base + row]
            pairs[0][1][row, start : start + edge, :] = 2.0 * solute[0, tile, base + row]
        return carry

    lax.fori_loop(0, count + 2 * W, load_row, 0, unroll=UNROLL)

    line = lax.broadcasted_iota(jnp.int32, (8, plan.depth), 0)

    def coefs_of(row, start):
        low, high = (start - PAD) // edge, (start + 7 - PAD) // edge
        rows = [[own[8 * tile + kind : 8 * tile + kind + 1, :] for tile in (low, high)] for kind in range(KINDS)]
        if low == high:
            return tuple(pair[0] for pair in rows)
        return tuple(jnp.where(line < W, *pair) for pair in rows)

    for step in range(NSTEPS):
        margin = 8 if step == NSTEPS - 1 else W
        starts = range(PAD + margin, PAD + tiles * edge - margin, 8)
        rows = count + 2 * W - 2 * (step + 1)
        march(rows, lambda i, step=step: step + 1 + i, starts, pairs[step % 2], pairs[(step + 1) % 2], coefs_of)
    for index, out in zip(indices, outs):
        pack(plan, True, mine ^ index, pairs[NSTEPS % 2], -base, PAD, own, out)


def pack(plan, far, piece, done, row_shift, col_shift, own, out):
    for tile in range(plan.tiles):
        for field, values in enumerate(done):
            begin = (2 * tile + field) * plan.size
            for at, row, name in plan.parts(far, piece):
                col, count = plan.columns(name, tile)
                start = col_shift + tile * plan.edge + col
                cells = values[row + row_shift, start : start + count, :]
                out[begin + at : begin + at + count, :] = 0.5 * cells if field else cells
    tail = 2 * plan.tiles * plan.size
    out[tail : tail + AUX, :] = own[8 * plan.tiles : 8 * plan.tiles + AUX, :]


def run_inner(plan, batch, own, phase, solute):
    rows = plan.batch_rows(batch, 0)[1] + 2 * W
    count = len(plan.batches[batch])
    buffer = pltpu.VMEM((rows, plan.tiles * plan.edge + 2 * PAD, plan.depth), jnp.float32)
    vmem = pl.BlockSpec(memory_space=pltpu.VMEM)
    shape = jax.ShapeDtypeStruct((2 * plan.tiles * plan.size + AUX, plan.depth), jnp.float32)
    return pl.pallas_call(
        functools.partial(inner_kernel, plan, batch),
        in_specs=[vmem] * 3,
        out_specs=[vmem] * count,
        out_shape=[shape] * count,
        scratch_shapes=[buffer] * 4,
        compiler_params=pltpu.CompilerParams(vmem_limit_bytes=16 * 1024 * 1024),
        cost_estimate=pl.CostEstimate(flops=10**8, bytes_accessed=24 * 1024 * 1024, transcendentals=0),
        name="inner",
    )(own, phase, solute)


def outer_kernel(plan, own, phase, solute, y_lo, y_hi, x_lo, x_hi, out, *rest):
    tiles, edge, depth, half = plan.tiles, plan.edge, plan.depth, plan.half
    late = plan.batches[2]
    far_outs, scratch = rest[: len(late)], rest[len(late) :]
    pairs, coefs = (scratch[:2], scratch[2:4]), scratch[4]
    cols = tiles * edge
    width = cols + 2 * W
    for zone, source in ((0, x_lo), (1, None), (2, x_hi)):
        for kind in range(KINDS):
            if source is None:
                parts = [y_lo[edge, kind : kind + 1, :]]
                parts += [own[8 * tile + kind : 8 * tile + kind + 1, :] for tile in range(tiles)]
                parts += [y_hi[edge, kind : kind + 1, :]]
            else:
                at = 2 * W * width + kind
                parts = [source[at : at + 1, :]]
                parts += [source[at + 16 + 8 * tile : at + 17 + 8 * tile, :] for tile in range(tiles)]
                parts += [source[at + 8 : at + 9, :]]
            coefs[zone, kind, :W, :] = jnp.broadcast_to(parts[0], (W, depth))
            for tile in range(tiles):
                begin = W + tile * edge
                coefs[zone, kind, begin : begin + edge, :] = jnp.broadcast_to(parts[1 + tile], (edge, depth))
            coefs[zone, kind, width - W :, :] = jnp.broadcast_to(parts[-1], (W, depth))
    for source, first in ((x_lo, 0), (x_hi, edge + W)):
        for row in range(W):
            for field in range(2):
                at = (2 * row + field) * width
                values = source[at : at + width, :]
                pairs[0][field][first + row, PAD : PAD + width, :] = 2.0 * values if field else values

    def load_row(row, carry):
        fill_row(
            pairs[0],
            W + row,
            [phase[0, tile, row] for tile in range(tiles)],
            [solute[0, tile, row] for tile in range(tiles)],
            y_lo[row],
            y_hi[row],
        )
        return carry

    lax.fori_loop(0, edge, load_row, 0, unroll=UNROLL)

    def coefs_of(zone):
        def found(row, start):
            return tuple(coefs[zone(row), kind, start - PAD : start - PAD + 8, :] for kind in range(KINDS))

        return found

    any_zone = coefs_of(lambda row: jnp.where(row < W, 0, jnp.where(row < W + edge, 1, 2)))

    own_zone = coefs_of(lambda row: 1)
    mine = lax.rem(lax.axis_index("gy"), half)
    made = plan.inner // 2
    first_made = 2 * W + mine // (half // 2) * made

    def blocks(first, last):
        low, high = (first + W - shift) // 8 * 8, -(-(last + W - shift) // 8) * 8
        return list(range(PAD + shift + low, PAD + shift + high, 8))

    for step in range(1, NSTEPS + 1):
        source, target = pairs[(step - 1) % 2], pairs[step % 2]
        left = NSTEPS - step
        shift = W if step == NSTEPS else 0
        whole = blocks(-left, cols + left)
        ends = blocks(-left, 8 + left) + blocks(cols - 8 - left, cols + left)
        for tile in range(tiles):
            col, count = plan.columns("last", tile)
            ends += blocks(tile * edge + col - left, tile * edge + col + count + left)
        gap, gap_rows = first_made + left, made - 2 * left

        def outside(index, left=left, gap=gap, gap_rows=gap_rows):
            row = W - left + index
            return row + jnp.where(row < gap, 0, gap_rows)

        march(edge + 2 * left - gap_rows, outside, whole, source, target, any_zone)
        march(gap_rows, lambda i, gap=gap: gap + i, sorted(set(ends)), source, target, own_zone)
    done = pairs[NSTEPS % 2]
    for index, far_out in zip(late, far_outs):
        pack(plan, True, mine ^ index, done, W, PAD + W, own, far_out)
    for piece in range(half):
        pack(plan, False, piece, done, W, PAD + W, own, out.at[piece])


def run_outer(plan, own, phase, solute, halos):
    tiles, edge, depth = plan.tiles, plan.edge, plan.depth
    width = tiles * edge + 2 * W
    buffer = pltpu.VMEM((edge + 2 * W, width + 2 * PAD, depth), jnp.float32)
    vmem = pl.BlockSpec(memory_space=pltpu.VMEM)
    near = jax.ShapeDtypeStruct((plan.half, 2 * tiles * plan.size + AUX, depth), jnp.float32)
    far = jax.ShapeDtypeStruct((2 * tiles * plan.size + AUX, depth), jnp.float32)
    return pl.pallas_call(
        functools.partial(outer_kernel, plan),
        in_specs=[vmem] * 7,
        out_specs=[vmem] * (1 + len(plan.batches[2])),
        out_shape=[near] + [far] * len(plan.batches[2]),
        scratch_shapes=[buffer] * 4 + [pltpu.VMEM((3, KINDS, width, depth), jnp.float32)],
        compiler_params=pltpu.CompilerParams(vmem_limit_bytes=16 * 1024 * 1024),
        cost_estimate=pl.CostEstimate(flops=10**8, bytes_accessed=40 * 1024 * 1024, transcendentals=0),
        name="outer",
    )(own, phase, solute, *halos)


def route_kernel(plan, near, *refs):
    pieces, tiles, half, size = plan.pieces, plan.tiles, plan.half, 2 * plan.size
    far, near_out, far_outs, table = refs[:half], refs[half], refs[half + 1 : 2 * half + 1], refs[2 * half + 1]
    held, peers, count = refs[2 * half + 2 :]
    me = lax.axis_index("gy")
    base = me - lax.rem(me, half)
    tail = tiles * size
    for tile in range(tiles):
        for piece in range(half):
            peer = lax.rem(near[piece, tail, tile].astype(jnp.int32), pieces)
            peers[(base + piece) * tiles + tile] = peer
        for index in range(half):
            peer = lax.rem(far[index][tail, tile].astype(jnp.int32), pieces)
            peers[(me ^ (half + index)) * tiles + tile] = peer
    for piece in range(half):
        for tile in range(tiles):
            held[(base + piece) * tiles + tile] = near[piece, tile * size : (tile + 1) * size, :]
    for index in range(half):
        for tile in range(tiles):
            held[(me ^ (half + index)) * tiles + tile] = far[index][tile * size : (tile + 1) * size, :]
    for peer in range(pieces):
        count[peer] = 0
    for home in range(pieces * tiles):
        peer = peers[home]
        slot = count[peer]
        table[peer * tiles + slot] = home
        count[peer] = slot + 1
    for index in range(half):
        for slot in range(tiles):
            far_outs[index][slot] = held[table[(me ^ (half + index)) * tiles + slot]]
            near_out[index, slot] = held[table[(base + index) * tiles + slot]]


def route(plan, near, far):
    tiles, half, size, depth = plan.tiles, plan.half, 2 * plan.size, plan.depth
    vmem = pl.BlockSpec(memory_space=pltpu.VMEM)
    one = jax.ShapeDtypeStruct((tiles, size, depth), jnp.float32)
    count = plan.pieces * tiles
    results = pl.pallas_call(
        functools.partial(route_kernel, plan),
        in_specs=[vmem] * (half + 1),
        out_specs=[vmem] * (half + 1) + [pl.BlockSpec(memory_space=pltpu.SMEM)],
        out_shape=[jax.ShapeDtypeStruct((half, tiles, size, depth), jnp.float32)]
        + [one] * half
        + [jax.ShapeDtypeStruct((count,), jnp.int32)],
        scratch_shapes=[
            pltpu.VMEM((count, size, depth), jnp.float32),
            pltpu.SMEM((count,), jnp.int32),
            pltpu.SMEM((plan.pieces,), jnp.int32),
        ],
        compiler_params=pltpu.CompilerParams(vmem_limit_bytes=16 * 1024 * 1024),
        name="route",
    )(near, *far)
    return results[0], results[1 : half + 1], results[-1]


def settle_kernel(plan, table, near, *refs):
    tiles, half = plan.tiles, plan.half
    far, outs, (ready, sems) = refs[:half], refs[half : half + 2], refs[half + 2 :]
    me = lax.axis_index("gy")
    mine = lax.rem(me, half)
    copies = []
    for slot in range(tiles):
        home = table[me * tiles + slot]
        tile = lax.rem(home, tiles)
        at_home = home // (tiles * half) == me // half

        def put(source, piece, is_far, slot=slot, tile=tile):
            for field in range(2):
                for at, row, name in plan.parts(is_far, piece):
                    col, count = plan.columns(name, tile)
                    if not isinstance(col, int):
                        col = pl.multiple_of(col, 8)
                    ready[field, slot, row, pl.ds(col, count), :] = source[
                        slot, field * plan.size + at : field * plan.size + at + count, :
                    ]

        def put_all(same, put=put):
            for index in range(half):
                put(near.at[index], index, not same)
                put(far[index], mine ^ index, same)

        @pl.when(at_home)
        def _(put_all=put_all):
            put_all(True)

        @pl.when(jnp.logical_not(at_home))
        def _(put_all=put_all):
            put_all(False)

        for field, out in enumerate(outs):
            copy = pltpu.make_async_copy(ready.at[field, slot], out.at[0, slot], sems.at[field, slot])
            copy.start()
            copies.append(copy)
    for copy in copies:
        copy.wait()


def settle(plan, table, near, far):
    tiles, edge, depth = plan.tiles, plan.edge, plan.depth
    out = jax.ShapeDtypeStruct((1, tiles, edge, edge, depth), jnp.float32)
    vmem = pl.BlockSpec(memory_space=pltpu.VMEM)
    return pl.pallas_call(
        functools.partial(settle_kernel, plan),
        in_specs=[pl.BlockSpec(memory_space=pltpu.SMEM)] + [vmem] * (plan.half + 1),
        out_specs=[pl.BlockSpec(memory_space=pl.ANY)] * 2,
        out_shape=[out, out],
        scratch_shapes=[
            pltpu.VMEM((2, tiles, edge, edge, depth), jnp.float32),
            pltpu.SemaphoreType.DMA((2, tiles)),
        ],
        compiler_params=pltpu.CompilerParams(vmem_limit_bytes=16 * 1024 * 1024),
        name="settle",
    )(table, near, *far)


def ring(axis, step):
    count = lax.axis_size(axis)
    return [(i, (i + step) % count) for i in range(count)]


def swap(values, mask):
    return lax.ppermute(values, "gy", [(i, i ^ mask) for i in range(lax.axis_size("gy"))])


def among_half(plan, values, together):
    def exchange(values):
        groups = [list(range(plan.half)), list(range(plan.half, plan.pieces))]
        return lax.all_to_all(values, "gy", 0, 0, axis_index_groups=groups, tiled=True)

    return lax.cond(together, exchange, exchange, values)


def in_vmem(values):
    return pltpu.with_memory_space_constraint(values, pltpu.VMEM)


def per_device(phase, solute, undercool, mobility, diffusivity, owner):
    _, tiles, edge, _, depth = phase.shape
    plan = Plan(lax.axis_size("gy"), tiles, edge, depth)
    half = plan.half
    to_prev, to_next, own = pack_y(phase, solute, (undercool, mobility, diffusivity), owner)
    y_lo = lax.ppermute(to_next, "gy", ring("gy", 1))
    y_hi = lax.ppermute(to_prev, "gy", ring("gy", -1))
    far = {}

    def send_far(batch, values):
        for index, value in zip(plan.batches[batch], values):
            far[index] = swap(value, half + index)

    own_here, phase_here, solute_here = in_vmem(own), in_vmem(phase), in_vmem(solute)
    first = run_inner(plan, 0, own_here, phase_here, solute_here)
    send_far(0, first)
    to_prev, to_next = pack_x(phase_here, solute_here, own_here, y_lo, y_hi, first[0])
    together = owner[0, 0] >= 0

    def around(low, high, *values):
        return ring_swap(low, high), run_inner(plan, 1, *values)

    def ring_swap(low, high):
        return lax.ppermute(low, "gx", ring("gx", 1)), lax.ppermute(high, "gx", ring("gx", -1))

    (x_lo, x_hi), second = lax.cond(together, around, around, to_next, to_prev, own, phase, solute)
    send_far(1, second)
    near, *third = run_outer(plan, own_here, phase_here, solute_here, (y_lo, y_hi, in_vmem(x_lo), in_vmem(x_hi)))
    send_far(2, third)
    far = [far[index] for index in range(half)]
    near = among_half(plan, near, together)
    near, far, table = route(plan, in_vmem(near), far)
    far = [swap(values, half + index) for index, values in enumerate(far)]
    near = among_half(plan, near, together)
    return tuple(settle(plan, table, near, far))


def solution(mesh):
    tile_spec = P("gx", "gy", None, None, None)
    in_specs = (tile_spec, tile_spec) + (P("gx", "gy"),) * 4
    out_spec = P(("gx", "gy"), None, None, None, None)
    return jax.shard_map(
        per_device, mesh=mesh, in_specs=in_specs, out_specs=(out_spec, out_spec), check_vma=False
    )
```

```python
import functools

import jax
import jax.numpy as jnp
from jax import lax
from jax.experimental import pallas as pl
from jax.experimental.pallas import tpu as pltpu
from jax.sharding import PartitionSpec as P

NSTEPS = 4
W = NSTEPS
PAD = 8

aniso_strength = 0.05


def pack_y_kernel(under, mobile, spread, owner, phase_lo, phase_hi, solute_lo, solute_hi, to_prev, to_next, own):
    edge, depth = phase_lo.shape[2], phase_lo.shape[4]
    tiles = own.shape[0] // 8 - 1
    to_prev[:edge, :W, :] = phase_lo[0, 0, :, :W, :]
    to_prev[:edge, W:, :] = solute_lo[0, 0, :, :W, :]
    to_next[:edge, :W, :] = phase_hi[0, 0, :, W:, :]
    to_next[:edge, W:, :] = solute_hi[0, 0, :, W:, :]
    line = lax.broadcasted_iota(jnp.int32, (8, depth), 0)
    lane = lax.broadcasted_iota(jnp.int32, (8, depth), 1)
    names = jnp.zeros((8, depth), jnp.float32)
    for tile in range(tiles):
        rows = jnp.zeros((8, depth), jnp.float32)
        ready = (2.0 * under[0, tile], mobile[0, tile], spread[0, tile], 1.0 - 6.0 * spread[0, tile])
        for kind, coef in enumerate(ready):
            rows = jnp.where(line == kind, coef, rows)
        own[8 * tile : 8 * tile + 8, :] = rows
        if tile == 0:
            to_prev[edge] = rows
        if tile == tiles - 1:
            to_next[edge] = rows
        names = jnp.where(lane == tile, owner[0, tile].astype(jnp.float32), names)
    own[8 * tiles :, :] = names


def pack_y(phase, solute, coef, owner):
    _, tiles, edge, _, depth = phase.shape
    low = pl.BlockSpec((1, 1, edge, 2 * W, depth), lambda i: (0, 0, 0, 0, 0))
    high = pl.BlockSpec((1, 1, edge, 2 * W, depth), lambda i: (0, tiles - 1, 0, edge // (2 * W) - 1, 0))
    face = jax.ShapeDtypeStruct((edge + 1, 2 * W, depth), jnp.float32)
    own = jax.ShapeDtypeStruct((8 * tiles + 8, depth), jnp.float32)
    whole = pl.BlockSpec((edge + 1, 2 * W, depth), lambda i: (0, 0, 0))
    return pl.pallas_call(
        pack_y_kernel,
        grid=(1,),
        in_specs=[pl.BlockSpec(memory_space=pltpu.SMEM)] * 4 + [low, high, low, high],
        out_specs=[whole, whole, pl.BlockSpec((8 * tiles + 8, depth), lambda i: (0, 0))],
        out_shape=[face, face, own],
        name="pack_y",
    )(*coef, owner, phase, phase, solute, solute)


def fill_row(dst, row, phase_row, solute_row, lo, hi):
    start = PAD
    dst[0][row, start : start + W, :] = lo[:W]
    dst[1][row, start : start + W, :] = 2.0 * lo[W:]
    start += W
    for values in phase_row:
        size = values.shape[0]
        dst[0][row, start : start + size, :] = values
        start += size
    dst[0][row, start : start + W, :] = hi[:W]
    dst[1][row, start : start + W, :] = 2.0 * hi[W:]
    start = PAD + W
    for values in solute_row:
        size = values.shape[0]
        dst[1][row, start : start + size, :] = 2.0 * values
        start += size


def pack_x_kernel(own, phase_lo, phase_hi, solute_lo, solute_hi, y_lo, y_hi, _, to_prev, to_next):
    tiles, edge, depth = phase_lo.shape[1], phase_lo.shape[3], phase_lo.shape[4]
    width = tiles * edge + 2 * W
    for out, phase, solute, first in (
        (to_prev, phase_lo, solute_lo, 0),
        (to_next, phase_hi, solute_hi, edge - W),
    ):
        for row in range(W):
            for field, values, half in ((0, phase, 0), (1, solute, W)):
                at = (2 * row + field) * width
                out[at : at + W, :] = y_lo[first + row, half : half + W, :]
                for tile in range(tiles):
                    begin = at + W + tile * edge
                    out[begin : begin + edge, :] = values[0, tile, row]
                out[at + width - W : at + width, :] = y_hi[first + row, half : half + W, :]
        at = 2 * W * width
        out[at : at + 8, :] = y_lo[edge]
        out[at + 8 : at + 16, :] = y_hi[edge]
        out[at + 16 : at + 16 + 8 * tiles, :] = own[: 8 * tiles, :]


def pack_x(phase, solute, own, y_lo, y_hi, after):
    _, tiles, edge, _, depth = phase.shape
    low = pl.BlockSpec((1, tiles, W, edge, depth), lambda i: (0, 0, 0, 0, 0))
    high = pl.BlockSpec((1, tiles, W, edge, depth), lambda i: (0, 0, edge // W - 1, 0, 0))
    side = pl.BlockSpec((edge + 1, 2 * W, depth), lambda i: (0, 0, 0))
    rows = 2 * W * (tiles * edge + 2 * W) + 8 * (tiles + 2)
    out = jax.ShapeDtypeStruct((rows, depth), jnp.float32)
    whole = pl.BlockSpec((rows, depth), lambda i: (0, 0))
    return pl.pallas_call(
        pack_x_kernel,
        grid=(1,),
        in_specs=[pl.BlockSpec((8 * tiles + 8, depth), lambda i: (0, 0)), low, high, low, high, side, side, pl.BlockSpec(memory_space=pl.ANY)],
        out_specs=[whole, whole],
        out_shape=[out, out],
        compiler_params=pltpu.CompilerParams(vmem_limit_bytes=8 * 1024 * 1024),
        name="pack_x",
    )(own, phase, phase, solute, solute, y_lo, y_hi, after)


def update(near_p, near_v, under, mobile, spread, keep):
    p, p_xl, p_xh, p_yl, p_yh = near_p
    v, v_xl, v_xh, v_yl, v_yh = near_v
    depth = p.shape[-1]
    lane = lax.broadcasted_iota(jnp.int32, p.shape, 1)
    first, last = lane == 0, lane == depth - 1
    p_zl = jnp.where(first, p, pltpu.roll(p, 1, 1))
    p_zh = jnp.where(last, p, pltpu.roll(p, depth - 1, 1))
    v_zl = jnp.where(first, v, pltpu.roll(v, 1, 1))
    v_zh = jnp.where(last, v, pltpu.roll(v, depth - 1, 1))
    dx, dy, dz = p_xh - p_xl, p_yh - p_yl, p_zh - p_zl
    qx, qy, qz = dx * dx, dy * dy, dz * dz
    flat = qx + qy
    total = flat + qz
    pairs = qx * qy + flat * qz
    base = total + 4.0
    guess = pl.reciprocal(base, approx=True)
    inverse = guess * (2.0 - base * guess)
    extra = (aniso_strength * total * total - (8.0 * aniso_strength) * pairs) * (inverse * inverse)
    lap_p = (p_xl + p_xh) + (p_yl + p_yh) + (p_zl + p_zh) - 6.0 * p
    sum_v = (v_xl + v_xh) + (v_yl + v_yh) + (v_zl + v_zh)
    well = 1.0 - p * p
    change = mobile * (lap_p + extra * lap_p + well * (p - well * (under + v)))
    return p + change, keep * v + spread * sum_v + change


KINDS = 4


def cells(src_p, src_u, row, start, coefs):
    near = []
    for src in (src_p, src_u):
        near.append(
            (
                src[row, start : start + 8, :],
                src[row - 1, start : start + 8, :],
                src[row + 1, start : start + 8, :],
                src[row, start - 1 : start + 7, :],
                src[row, start + 1 : start + 9, :],
            )
        )
    return update(near[0], near[1], *coefs)


class Plan:
    def __init__(self, pieces, tiles, edge, depth):
        self.pieces, self.tiles, self.edge, self.depth = pieces, tiles, edge, depth
        self.half = pieces // 2
        self.inner = edge - 2 * W
        self.rows = self.inner // self.half
        self.rows_far = (self.inner - 2 * W) // self.half
        self.rows_near = 2 * W // self.half
        self.middle = edge - 16
        self.size = self.rows * self.middle + self.rows_far * 8

        side = self.half // 2
        self.batches = (list(range(side)), list(range(side, self.half)))

    def batch_rows(self, batch, mine):
        count = self.inner // 2
        side = mine // (self.half // 2)
        return W + (side if batch == 0 else 1 - side) * count, count

    def near_row(self, piece, row, gap):
        index = piece * self.rows_near + row
        return index + jnp.where(index < W, 0, gap)

    def parts(self, far, piece):
        at, found = 0, []
        if far:
            for row in range(self.rows):
                found.append((at, W + piece * self.rows + row, "middle"))
                at += self.middle
            for row in range(self.rows_far):
                found.append((at, 2 * W + piece * self.rows_far + row, "last"))
                at += 8
        else:
            for row in range(self.rows_near):
                found.append((at, self.near_row(piece, row, self.inner), "whole"))
                at += self.edge
            for row in range(self.rows):
                found.append((at, W + piece * self.rows + row, "side"))
                at += 8
            for row in range(self.rows_near):
                found.append((at, W + self.near_row(piece, row, self.inner - 2 * W), "last"))
                at += 8
        assert at == self.size
        return found

    def columns(self, name, tile):
        if name == "whole":
            return 0, self.edge
        if name == "middle":
            return 8, self.middle
        low, high = (tile, 1 - tile) if name == "side" else (1 - tile, tile)
        return low * (self.edge - 8), 8


AUX = 8
UNROLL = 4


def march(count, row_of, starts, source, target, coefs_of):
    def one_row(index, carry):
        row = row_of(index)
        for start in starts:
            new_p, new_u = cells(source[0], source[1], row, start, coefs_of(row, start))
            target[0][row, start : start + 8, :] = new_p
            target[1][row, start : start + 8, :] = new_u
        return carry

    lax.fori_loop(0, count, one_row, 0, unroll=UNROLL)


def inner_kernel(plan, batch, own, phase, solute, *rest):
    tiles, edge, indices = plan.tiles, plan.edge, plan.batches[batch]
    outs, scratch = rest[: len(indices)], rest[len(indices) :]
    pairs = (scratch[:2], scratch[2:])
    mine = lax.rem(lax.axis_index("gy"), plan.half)
    begin, count = plan.batch_rows(batch, mine)
    base = begin - W

    def load_row(row, carry):
        for tile in range(tiles):
            start = PAD + tile * edge
            pairs[0][0][row, start : start + edge, :] = phase[0, tile, base + row]
            pairs[0][1][row, start : start + edge, :] = 2.0 * solute[0, tile, base + row]
        return carry

    lax.fori_loop(0, count + 2 * W, load_row, 0, unroll=UNROLL)

    line = lax.broadcasted_iota(jnp.int32, (8, plan.depth), 0)

    def coefs_of(row, start):
        low, high = (start - PAD) // edge, (start + 7 - PAD) // edge
        rows = [[own[8 * tile + kind : 8 * tile + kind + 1, :] for tile in (low, high)] for kind in range(KINDS)]
        if low == high:
            return tuple(pair[0] for pair in rows)
        return tuple(jnp.where(line < W, *pair) for pair in rows)

    for step in range(NSTEPS):
        margin = 8 if step == NSTEPS - 1 else W
        starts = range(PAD + margin, PAD + tiles * edge - margin, 8)
        rows = count + 2 * W - 2 * (step + 1)
        march(rows, lambda i, step=step: step + 1 + i, starts, pairs[step % 2], pairs[(step + 1) % 2], coefs_of)
    for index, out in zip(indices, outs):
        pack(plan, True, mine ^ index, pairs[NSTEPS % 2], -base, PAD, own, out)


def pack(plan, far, piece, done, row_shift, col_shift, own, out):
    for tile in range(plan.tiles):
        for field, values in enumerate(done):
            begin = (2 * tile + field) * plan.size
            for at, row, name in plan.parts(far, piece):
                col, count = plan.columns(name, tile)
                start = col_shift + tile * plan.edge + col
                cells = values[row + row_shift, start : start + count, :]
                out[begin + at : begin + at + count, :] = 0.5 * cells if field else cells
    tail = 2 * plan.tiles * plan.size
    out[tail : tail + AUX, :] = own[8 * plan.tiles : 8 * plan.tiles + AUX, :]


def run_inner(plan, batch, own, phase, solute):
    rows = plan.batch_rows(batch, 0)[1] + 2 * W
    count = len(plan.batches[batch])
    buffer = pltpu.VMEM((rows, plan.tiles * plan.edge + 2 * PAD, plan.depth), jnp.float32)
    vmem = pl.BlockSpec(memory_space=pltpu.VMEM)
    shape = jax.ShapeDtypeStruct((2 * plan.tiles * plan.size + AUX, plan.depth), jnp.float32)
    return pl.pallas_call(
        functools.partial(inner_kernel, plan, batch),
        in_specs=[vmem] * 3,
        out_specs=[vmem] * count,
        out_shape=[shape] * count,
        scratch_shapes=[buffer] * 4,
        compiler_params=pltpu.CompilerParams(vmem_limit_bytes=16 * 1024 * 1024),
        cost_estimate=pl.CostEstimate(flops=10**8, bytes_accessed=24 * 1024 * 1024, transcendentals=0),
        name="inner",
    )(own, phase, solute)


def outer_kernel(plan, own, phase, solute, y_lo, y_hi, x_lo, x_hi, out, *scratch):
    tiles, edge, depth, half = plan.tiles, plan.edge, plan.depth, plan.half
    pairs, coefs = (scratch[:2], scratch[2:4]), scratch[4]
    cols = tiles * edge
    width = cols + 2 * W
    for zone, source in ((0, x_lo), (1, None), (2, x_hi)):
        for kind in range(KINDS):
            if source is None:
                parts = [y_lo[edge, kind : kind + 1, :]]
                parts += [own[8 * tile + kind : 8 * tile + kind + 1, :] for tile in range(tiles)]
                parts += [y_hi[edge, kind : kind + 1, :]]
            else:
                at = 2 * W * width + kind
                parts = [source[at : at + 1, :]]
                parts += [source[at + 16 + 8 * tile : at + 17 + 8 * tile, :] for tile in range(tiles)]
                parts += [source[at + 8 : at + 9, :]]
            coefs[zone, kind, :W, :] = jnp.broadcast_to(parts[0], (W, depth))
            for tile in range(tiles):
                begin = W + tile * edge
                coefs[zone, kind, begin : begin + edge, :] = jnp.broadcast_to(parts[1 + tile], (edge, depth))
            coefs[zone, kind, width - W :, :] = jnp.broadcast_to(parts[-1], (W, depth))
    for source, first in ((x_lo, 0), (x_hi, edge + W)):
        for row in range(W):
            for field in range(2):
                at = (2 * row + field) * width
                values = source[at : at + width, :]
                pairs[0][field][first + row, PAD : PAD + width, :] = 2.0 * values if field else values

    def load_row(row, carry):
        fill_row(
            pairs[0],
            W + row,
            [phase[0, tile, row] for tile in range(tiles)],
            [solute[0, tile, row] for tile in range(tiles)],
            y_lo[row],
            y_hi[row],
        )
        return carry

    lax.fori_loop(0, edge, load_row, 0, unroll=UNROLL)

    def coefs_of(zone):
        def found(row, start):
            return tuple(coefs[zone(row), kind, start - PAD : start - PAD + 8, :] for kind in range(KINDS))

        return found

    any_zone = coefs_of(lambda row: jnp.where(row < W, 0, jnp.where(row < W + edge, 1, 2)))

    own_zone = coefs_of(lambda row: 1)
    def blocks(first, last):
        low, high = (first + W - shift) // 8 * 8, -(-(last + W - shift) // 8) * 8
        return list(range(PAD + shift + low, PAD + shift + high, 8))

    for step in range(1, NSTEPS + 1):
        source, target = pairs[(step - 1) % 2], pairs[step % 2]
        left = NSTEPS - step
        shift = W if step == NSTEPS else 0
        whole = blocks(-left, cols + left)
        sides = blocks(-left, 8 + left) + blocks(cols - 8 - left, cols + left)
        ends = list(sides)
        for tile in range(tiles):
            col, count = plan.columns("last", tile)
            ends += blocks(tile * edge + col - left, tile * edge + col + count + left)
        strip = W + left

        def two(size, begin):
            mirror = 2 * W + edge - begin - size
            return lambda i: i + jnp.where(i < size, begin, mirror - size)

        march(2 * (strip + left), two(strip + left, W - left), whole, source, target, any_zone)
        march(2 * W, two(W, W + strip), sorted(set(ends)), source, target, own_zone)
        march(edge - 2 * strip - 2 * W, lambda i, strip=strip: i + 2 * W + strip, sides, source, target, own_zone)
    done = pairs[NSTEPS % 2]
    for piece in range(half):
        pack(plan, False, piece, done, W, PAD + W, own, out.at[piece])


def run_outer(plan, own, phase, solute, halos):
    tiles, edge, depth = plan.tiles, plan.edge, plan.depth
    width = tiles * edge + 2 * W
    buffer = pltpu.VMEM((edge + 2 * W, width + 2 * PAD, depth), jnp.float32)
    vmem = pl.BlockSpec(memory_space=pltpu.VMEM)
    near = jax.ShapeDtypeStruct((plan.half, 2 * tiles * plan.size + AUX, depth), jnp.float32)
    return pl.pallas_call(
        functools.partial(outer_kernel, plan),
        in_specs=[vmem] * 7,
        out_specs=vmem,
        out_shape=near,
        scratch_shapes=[buffer] * 4 + [pltpu.VMEM((3, KINDS, width, depth), jnp.float32)],
        compiler_params=pltpu.CompilerParams(vmem_limit_bytes=16 * 1024 * 1024),
        cost_estimate=pl.CostEstimate(flops=10**8, bytes_accessed=40 * 1024 * 1024, transcendentals=0),
        name="outer",
    )(own, phase, solute, *halos)


def route_kernel(plan, near, *refs):
    pieces, tiles, half, size = plan.pieces, plan.tiles, plan.half, 2 * plan.size
    far, near_out, far_outs, table = refs[:half], refs[half], refs[half + 1 : 2 * half + 1], refs[2 * half + 1]
    held, peers, count = refs[2 * half + 2 :]
    me = lax.axis_index("gy")
    base = me - lax.rem(me, half)
    tail = tiles * size
    for tile in range(tiles):
        for piece in range(half):
            peer = lax.rem(near[piece, tail, tile].astype(jnp.int32), pieces)
            peers[(base + piece) * tiles + tile] = peer
        for index in range(half):
            peer = lax.rem(far[index][tail, tile].astype(jnp.int32), pieces)
            peers[(me ^ (half + index)) * tiles + tile] = peer
    for piece in range(half):
        for tile in range(tiles):
            held[(base + piece) * tiles + tile] = near[piece, tile * size : (tile + 1) * size, :]
    for index in range(half):
        for tile in range(tiles):
            held[(me ^ (half + index)) * tiles + tile] = far[index][tile * size : (tile + 1) * size, :]
    for peer in range(pieces):
        count[peer] = 0
    for home in range(pieces * tiles):
        peer = peers[home]
        slot = count[peer]
        table[peer * tiles + slot] = home
        count[peer] = slot + 1
    for index in range(half):
        for slot in range(tiles):
            far_outs[index][slot] = held[table[(me ^ (half + index)) * tiles + slot]]
            near_out[index, slot] = held[table[(base + index) * tiles + slot]]


def route(plan, near, far):
    tiles, half, size, depth = plan.tiles, plan.half, 2 * plan.size, plan.depth
    vmem = pl.BlockSpec(memory_space=pltpu.VMEM)
    one = jax.ShapeDtypeStruct((tiles, size, depth), jnp.float32)
    count = plan.pieces * tiles
    results = pl.pallas_call(
        functools.partial(route_kernel, plan),
        in_specs=[vmem] * (half + 1),
        out_specs=[vmem] * (half + 1) + [pl.BlockSpec(memory_space=pltpu.SMEM)],
        out_shape=[jax.ShapeDtypeStruct((half, tiles, size, depth), jnp.float32)]
        + [one] * half
        + [jax.ShapeDtypeStruct((count,), jnp.int32)],
        scratch_shapes=[
            pltpu.VMEM((count, size, depth), jnp.float32),
            pltpu.SMEM((count,), jnp.int32),
            pltpu.SMEM((plan.pieces,), jnp.int32),
        ],
        compiler_params=pltpu.CompilerParams(vmem_limit_bytes=16 * 1024 * 1024),
        name="route",
    )(near, *far)
    return results[0], results[1 : half + 1], results[-1]


def settle_kernel(plan, table, near, *refs):
    tiles, half = plan.tiles, plan.half
    far, outs, (ready, sems) = refs[:half], refs[half : half + 2], refs[half + 2 :]
    me = lax.axis_index("gy")
    mine = lax.rem(me, half)
    copies = []
    for slot in range(tiles):
        home = table[me * tiles + slot]
        tile = lax.rem(home, tiles)
        at_home = home // (tiles * half) == me // half

        def put(source, piece, is_far, slot=slot, tile=tile):
            for field in range(2):
                for at, row, name in plan.parts(is_far, piece):
                    col, count = plan.columns(name, tile)
                    if not isinstance(col, int):
                        col = pl.multiple_of(col, 8)
                    ready[field, slot, row, pl.ds(col, count), :] = source[
                        slot, field * plan.size + at : field * plan.size + at + count, :
                    ]

        def put_all(same, put=put):
            for index in range(half):
                put(near.at[index], index, not same)
                put(far[index], mine ^ index, same)

        @pl.when(at_home)
        def _(put_all=put_all):
            put_all(True)

        @pl.when(jnp.logical_not(at_home))
        def _(put_all=put_all):
            put_all(False)

        for field, out in enumerate(outs):
            copy = pltpu.make_async_copy(ready.at[field, slot], out.at[0, slot], sems.at[field, slot])
            copy.start()
            copies.append(copy)
    for copy in copies:
        copy.wait()


def settle(plan, table, near, far):
    tiles, edge, depth = plan.tiles, plan.edge, plan.depth
    out = jax.ShapeDtypeStruct((1, tiles, edge, edge, depth), jnp.float32)
    vmem = pl.BlockSpec(memory_space=pltpu.VMEM)
    return pl.pallas_call(
        functools.partial(settle_kernel, plan),
        in_specs=[pl.BlockSpec(memory_space=pltpu.SMEM)] + [vmem] * (plan.half + 1),
        out_specs=[pl.BlockSpec(memory_space=pl.ANY)] * 2,
        out_shape=[out, out],
        scratch_shapes=[
            pltpu.VMEM((2, tiles, edge, edge, depth), jnp.float32),
            pltpu.SemaphoreType.DMA((2, tiles)),
        ],
        compiler_params=pltpu.CompilerParams(vmem_limit_bytes=16 * 1024 * 1024),
        name="settle",
    )(table, near, *far)


def ring(axis, step):
    count = lax.axis_size(axis)
    return [(i, (i + step) % count) for i in range(count)]


def swap(values, mask):
    return lax.ppermute(values, "gy", [(i, i ^ mask) for i in range(lax.axis_size("gy"))])


def among_half(plan, values, together):
    def exchange(values):
        groups = [list(range(plan.half)), list(range(plan.half, plan.pieces))]
        return lax.all_to_all(values, "gy", 0, 0, axis_index_groups=groups, tiled=True)

    return lax.cond(together, exchange, exchange, values)


def in_vmem(values):
    return pltpu.with_memory_space_constraint(values, pltpu.VMEM)


def per_device(phase, solute, undercool, mobility, diffusivity, owner):
    _, tiles, edge, _, depth = phase.shape
    plan = Plan(lax.axis_size("gy"), tiles, edge, depth)
    half = plan.half
    to_prev, to_next, own = pack_y(phase, solute, (undercool, mobility, diffusivity), owner)
    y_lo = lax.ppermute(to_next, "gy", ring("gy", 1))
    y_hi = lax.ppermute(to_prev, "gy", ring("gy", -1))
    far = {}

    def send_far(batch, values):
        for index, value in zip(plan.batches[batch], values):
            far[index] = swap(value, half + index)

    own_here, phase_here, solute_here = in_vmem(own), in_vmem(phase), in_vmem(solute)
    first = run_inner(plan, 0, own_here, phase_here, solute_here)
    send_far(0, first)
    to_prev, to_next = pack_x(phase_here, solute_here, own_here, y_lo, y_hi, first[0])
    together = owner[0, 0] >= 0

    def around(low, high, *values):
        return ring_swap(low, high), run_inner(plan, 1, *values)

    def ring_swap(low, high):
        return lax.ppermute(low, "gx", ring("gx", 1)), lax.ppermute(high, "gx", ring("gx", -1))

    (x_lo, x_hi), second = lax.cond(together, around, around, to_next, to_prev, own, phase, solute)
    send_far(1, second)
    near = run_outer(plan, own_here, phase_here, solute_here, (y_lo, y_hi, in_vmem(x_lo), in_vmem(x_hi)))
    far = [far[index] for index in range(half)]
    near = among_half(plan, near, together)
    near, far, table = route(plan, in_vmem(near), far)
    far = [swap(values, half + index) for index, values in enumerate(far)]
    near = among_half(plan, near, together)
    return tuple(settle(plan, table, near, far))


def solution(mesh):
    tile_spec = P("gx", "gy", None, None, None)
    in_specs = (tile_spec, tile_spec) + (P("gx", "gy"),) * 4
    out_spec = P(("gx", "gy"), None, None, None, None)
    return jax.shard_map(
        per_device, mesh=mesh, in_specs=in_specs, out_specs=(out_spec, out_spec), check_vma=False
    )
```

```python
import functools

import jax
import jax.numpy as jnp
from jax import lax
from jax.experimental import pallas as pl
from jax.experimental.pallas import tpu as pltpu
from jax.sharding import PartitionSpec as P

NSTEPS = 4
W = NSTEPS
PAD = 8

aniso_strength = 0.05


def pack_y_kernel(under, mobile, spread, owner, phase_lo, phase_hi, solute_lo, solute_hi, to_prev, to_next, own):
    edge, depth = phase_lo.shape[2], phase_lo.shape[4]
    tiles = own.shape[0] // 8 - 1
    to_prev[:edge, :W, :] = phase_lo[0, 0, :, :W, :]
    to_prev[:edge, W:, :] = solute_lo[0, 0, :, :W, :]
    to_next[:edge, :W, :] = phase_hi[0, 0, :, W:, :]
    to_next[:edge, W:, :] = solute_hi[0, 0, :, W:, :]
    line = lax.broadcasted_iota(jnp.int32, (8, depth), 0)
    lane = lax.broadcasted_iota(jnp.int32, (8, depth), 1)
    names = jnp.zeros((8, depth), jnp.float32)
    for tile in range(tiles):
        rows = jnp.zeros((8, depth), jnp.float32)
        ready = (2.0 * under[0, tile], mobile[0, tile], spread[0, tile], 1.0 - 6.0 * spread[0, tile])
        for kind, coef in enumerate(ready):
            rows = jnp.where(line == kind, coef, rows)
        own[8 * tile : 8 * tile + 8, :] = rows
        if tile == 0:
            to_prev[edge] = rows
        if tile == tiles - 1:
            to_next[edge] = rows
        names = jnp.where(lane == tile, owner[0, tile].astype(jnp.float32), names)
    own[8 * tiles :, :] = names


def pack_y(phase, solute, coef, owner):
    _, tiles, edge, _, depth = phase.shape
    low = pl.BlockSpec((1, 1, edge, 2 * W, depth), lambda i: (0, 0, 0, 0, 0))
    high = pl.BlockSpec((1, 1, edge, 2 * W, depth), lambda i: (0, tiles - 1, 0, edge // (2 * W) - 1, 0))
    face = jax.ShapeDtypeStruct((edge + 1, 2 * W, depth), jnp.float32)
    own = jax.ShapeDtypeStruct((8 * tiles + 8, depth), jnp.float32)
    whole = pl.BlockSpec((edge + 1, 2 * W, depth), lambda i: (0, 0, 0))
    return pl.pallas_call(
        pack_y_kernel,
        grid=(1,),
        in_specs=[pl.BlockSpec(memory_space=pltpu.SMEM)] * 4 + [low, high, low, high],
        out_specs=[whole, whole, pl.BlockSpec((8 * tiles + 8, depth), lambda i: (0, 0))],
        out_shape=[face, face, own],
        name="pack_y",
    )(*coef, owner, phase, phase, solute, solute)


def fill_row(dst, row, phase_row, solute_row, lo, hi):
    start = PAD
    dst[0][row, start : start + W, :] = lo[:W]
    dst[1][row, start : start + W, :] = 2.0 * lo[W:]
    start += W
    for values in phase_row:
        size = values.shape[0]
        dst[0][row, start : start + size, :] = values
        start += size
    dst[0][row, start : start + W, :] = hi[:W]
    dst[1][row, start : start + W, :] = 2.0 * hi[W:]
    start = PAD + W
    for values in solute_row:
        size = values.shape[0]
        dst[1][row, start : start + size, :] = 2.0 * values
        start += size


def pack_x_kernel(own, phase_lo, phase_hi, solute_lo, solute_hi, y_lo, y_hi, _, to_prev, to_next):
    tiles, edge, depth = phase_lo.shape[1], phase_lo.shape[3], phase_lo.shape[4]
    width = tiles * edge + 2 * W
    for out, phase, solute, first in (
        (to_prev, phase_lo, solute_lo, 0),
        (to_next, phase_hi, solute_hi, edge - W),
    ):
        for row in range(W):
            for field, values, half in ((0, phase, 0), (1, solute, W)):
                at = (2 * row + field) * width
                out[at : at + W, :] = y_lo[first + row, half : half + W, :]
                for tile in range(tiles):
                    begin = at + W + tile * edge
                    out[begin : begin + edge, :] = values[0, tile, row]
                out[at + width - W : at + width, :] = y_hi[first + row, half : half + W, :]
        at = 2 * W * width
        out[at : at + 8, :] = y_lo[edge]
        out[at + 8 : at + 16, :] = y_hi[edge]
        out[at + 16 : at + 16 + 8 * tiles, :] = own[: 8 * tiles, :]


def pack_x(phase, solute, own, y_lo, y_hi, after):
    _, tiles, edge, _, depth = phase.shape
    low = pl.BlockSpec((1, tiles, W, edge, depth), lambda i: (0, 0, 0, 0, 0))
    high = pl.BlockSpec((1, tiles, W, edge, depth), lambda i: (0, 0, edge // W - 1, 0, 0))
    side = pl.BlockSpec((edge + 1, 2 * W, depth), lambda i: (0, 0, 0))
    rows = 2 * W * (tiles * edge + 2 * W) + 8 * (tiles + 2)
    out = jax.ShapeDtypeStruct((rows, depth), jnp.float32)
    whole = pl.BlockSpec((rows, depth), lambda i: (0, 0))
    return pl.pallas_call(
        pack_x_kernel,
        grid=(1,),
        in_specs=[pl.BlockSpec((8 * tiles + 8, depth), lambda i: (0, 0)), low, high, low, high, side, side, pl.BlockSpec(memory_space=pl.ANY)],
        out_specs=[whole, whole],
        out_shape=[out, out],
        compiler_params=pltpu.CompilerParams(vmem_limit_bytes=8 * 1024 * 1024),
        name="pack_x",
    )(own, phase, phase, solute, solute, y_lo, y_hi, after)


def update(near_p, near_v, under, mobile, spread, keep):
    p, p_xl, p_xh, p_yl, p_yh = near_p
    v, v_xl, v_xh, v_yl, v_yh = near_v
    depth = p.shape[-1]
    lane = lax.broadcasted_iota(jnp.int32, p.shape, 1)
    first, last = lane == 0, lane == depth - 1
    p_zl = jnp.where(first, p, pltpu.roll(p, 1, 1))
    p_zh = jnp.where(last, p, pltpu.roll(p, depth - 1, 1))
    v_zl = jnp.where(first, v, pltpu.roll(v, 1, 1))
    v_zh = jnp.where(last, v, pltpu.roll(v, depth - 1, 1))
    dx, dy, dz = p_xh - p_xl, p_yh - p_yl, p_zh - p_zl
    qx, qy, qz = dx * dx, dy * dy, dz * dz
    flat = qx + qy
    total = flat + qz
    pairs = qx * qy + flat * qz
    base = total + 4.0
    guess = pl.reciprocal(base, approx=True)
    inverse = guess * (2.0 - base * guess)
    extra = (aniso_strength * total * total - (8.0 * aniso_strength) * pairs) * (inverse * inverse)
    lap_p = (p_xl + p_xh) + (p_yl + p_yh) + (p_zl + p_zh) - 6.0 * p
    sum_v = (v_xl + v_xh) + (v_yl + v_yh) + (v_zl + v_zh)
    well = 1.0 - p * p
    change = mobile * (lap_p + extra * lap_p + well * (p - well * (under + v)))
    return p + change, keep * v + spread * sum_v + change


KINDS = 4


def cells(src_p, src_u, row, start, coefs):
    near = []
    for src in (src_p, src_u):
        near.append(
            (
                src[row, start : start + 8, :],
                src[row - 1, start : start + 8, :],
                src[row + 1, start : start + 8, :],
                src[row, start - 1 : start + 7, :],
                src[row, start + 1 : start + 9, :],
            )
        )
    return update(near[0], near[1], *coefs)


class Plan:
    def __init__(self, pieces, tiles, edge, depth):
        self.pieces, self.tiles, self.edge, self.depth = pieces, tiles, edge, depth
        self.half = pieces // 2
        self.inner = edge - 2 * W
        self.rows = self.inner // self.half
        self.rows_far = (self.inner - 2 * W) // self.half
        self.rows_near = 2 * W // self.half
        self.middle = edge - 16
        self.size = self.rows * self.middle + self.rows_far * 8

        side = self.half // 2
        self.batches = (list(range(side)), list(range(side, self.half)))

    def batch_rows(self, batch, mine):
        count = self.inner // 2
        side = mine // (self.half // 2)
        return W + (side if batch == 0 else 1 - side) * count, count

    def near_row(self, piece, row, gap):
        index = piece * self.rows_near + row
        return index + jnp.where(index < W, 0, gap)

    def parts(self, far, piece):
        at, found = 0, []
        if far:
            for row in range(self.rows):
                found.append((at, W + piece * self.rows + row, "middle"))
                at += self.middle
            for row in range(self.rows_far):
                found.append((at, 2 * W + piece * self.rows_far + row, "last"))
                at += 8
        else:
            for row in range(self.rows_near):
                found.append((at, self.near_row(piece, row, self.inner), "whole"))
                at += self.edge
            for row in range(self.rows):
                found.append((at, W + piece * self.rows + row, "side"))
                at += 8
            for row in range(self.rows_near):
                found.append((at, W + self.near_row(piece, row, self.inner - 2 * W), "last"))
                at += 8
        assert at == self.size
        return found

    def columns(self, name, tile):
        if name == "whole":
            return 0, self.edge
        if name == "middle":
            return 8, self.middle
        low, high = (tile, 1 - tile) if name == "side" else (1 - tile, tile)
        return low * (self.edge - 8), 8


AUX = 8
UNROLL = 4


def march(count, row_of, starts, source, target, coefs_of):
    def one_row(index, carry):
        row = row_of(index)
        for start in starts:
            new_p, new_u = cells(source[0], source[1], row, start, coefs_of(row, start))
            target[0][row, start : start + 8, :] = new_p
            target[1][row, start : start + 8, :] = new_u
        return carry

    lax.fori_loop(0, count, one_row, 0, unroll=UNROLL)


def inner_kernel(plan, batch, own, phase, solute, *rest):
    tiles, edge, indices = plan.tiles, plan.edge, plan.batches[batch]
    outs, scratch = rest[: len(indices)], rest[len(indices) :]
    pairs = (scratch[:2], scratch[2:])
    mine = lax.rem(lax.axis_index("gy"), plan.half)
    begin, count = plan.batch_rows(batch, mine)
    base = begin - W

    def load_row(row, carry):
        for tile in range(tiles):
            start = PAD + tile * edge
            pairs[0][0][row, start : start + edge, :] = phase[0, tile, base + row]
            pairs[0][1][row, start : start + edge, :] = 2.0 * solute[0, tile, base + row]
        return carry

    lax.fori_loop(0, count + 2 * W, load_row, 0, unroll=UNROLL)

    line = lax.broadcasted_iota(jnp.int32, (8, plan.depth), 0)

    def coefs_of(row, start):
        low, high = (start - PAD) // edge, (start + 7 - PAD) // edge
        rows = [[own[8 * tile + kind : 8 * tile + kind + 1, :] for tile in (low, high)] for kind in range(KINDS)]
        if low == high:
            return tuple(pair[0] for pair in rows)
        return tuple(jnp.where(line < W, *pair) for pair in rows)

    for step in range(NSTEPS):
        margin = 8 if step == NSTEPS - 1 else W
        starts = range(PAD + margin, PAD + tiles * edge - margin, 8)
        rows = count + 2 * W - 2 * (step + 1)
        march(rows, lambda i, step=step: step + 1 + i, starts, pairs[step % 2], pairs[(step + 1) % 2], coefs_of)
    for index, out in zip(indices, outs):
        pack(plan, True, mine ^ index, pairs[NSTEPS % 2], -base, PAD, own, out)


def pack(plan, far, piece, done, row_shift, col_shift, own, out):
    for tile in range(plan.tiles):
        for field, values in enumerate(done):
            begin = (2 * tile + field) * plan.size
            for at, row, name in plan.parts(far, piece):
                col, count = plan.columns(name, tile)
                start = col_shift + tile * plan.edge + col
                cells = values[row + row_shift, start : start + count, :]
                out[begin + at : begin + at + count, :] = 0.5 * cells if field else cells
    tail = 2 * plan.tiles * plan.size
    out[tail : tail + AUX, :] = own[8 * plan.tiles : 8 * plan.tiles + AUX, :]


def run_inner(plan, batch, own, phase, solute):
    rows = plan.batch_rows(batch, 0)[1] + 2 * W
    count = len(plan.batches[batch])
    buffer = pltpu.VMEM((rows, plan.tiles * plan.edge + 2 * PAD, plan.depth), jnp.float32)
    vmem = pl.BlockSpec(memory_space=pltpu.VMEM)
    shape = jax.ShapeDtypeStruct((2 * plan.tiles * plan.size + AUX, plan.depth), jnp.float32)
    return pl.pallas_call(
        functools.partial(inner_kernel, plan, batch),
        in_specs=[vmem] * 3,
        out_specs=[vmem] * count,
        out_shape=[shape] * count,
        scratch_shapes=[buffer] * 4,
        compiler_params=pltpu.CompilerParams(vmem_limit_bytes=16 * 1024 * 1024),
        cost_estimate=pl.CostEstimate(flops=10**8, bytes_accessed=24 * 1024 * 1024, transcendentals=0),
        name="inner",
    )(own, phase, solute)


def outer_kernel(plan, own, phase, solute, y_lo, y_hi, x_lo, x_hi, out, *scratch):
    tiles, edge, depth, half = plan.tiles, plan.edge, plan.depth, plan.half
    pairs, coefs = (scratch[:2], scratch[2:4]), scratch[4]
    cols = tiles * edge
    width = cols + 2 * W
    for zone, source in ((0, x_lo), (1, None), (2, x_hi)):
        for kind in range(KINDS):
            if source is None:
                parts = [y_lo[edge, kind : kind + 1, :]]
                parts += [own[8 * tile + kind : 8 * tile + kind + 1, :] for tile in range(tiles)]
                parts += [y_hi[edge, kind : kind + 1, :]]
            else:
                at = 2 * W * width + kind
                parts = [source[at : at + 1, :]]
                parts += [source[at + 16 + 8 * tile : at + 17 + 8 * tile, :] for tile in range(tiles)]
                parts += [source[at + 8 : at + 9, :]]
            coefs[zone, kind, :W, :] = jnp.broadcast_to(parts[0], (W, depth))
            for tile in range(tiles):
                begin = W + tile * edge
                coefs[zone, kind, begin : begin + edge, :] = jnp.broadcast_to(parts[1 + tile], (edge, depth))
            coefs[zone, kind, width - W :, :] = jnp.broadcast_to(parts[-1], (W, depth))
    for source, first in ((x_lo, 0), (x_hi, edge + W)):
        for row in range(W):
            for field in range(2):
                at = (2 * row + field) * width
                values = source[at : at + width, :]
                pairs[0][field][first + row, PAD : PAD + width, :] = 2.0 * values if field else values

    def load_row(row, carry):
        fill_row(
            pairs[0],
            W + row,
            [phase[0, tile, row] for tile in range(tiles)],
            [solute[0, tile, row] for tile in range(tiles)],
            y_lo[row],
            y_hi[row],
        )
        return carry

    lax.fori_loop(0, edge, load_row, 0, unroll=UNROLL)

    def coefs_of(zone):
        def found(row, start):
            return tuple(coefs[zone(row), kind, start - PAD : start - PAD + 8, :] for kind in range(KINDS))

        return found

    any_zone = coefs_of(lambda row: jnp.where(row < W, 0, jnp.where(row < W + edge, 1, 2)))

    own_zone = coefs_of(lambda row: 1)
    def blocks(first, last):
        low, high = (first + W - shift) // 8 * 8, -(-(last + W - shift) // 8) * 8
        return list(range(PAD + shift + low, PAD + shift + high, 8))

    for step in range(1, NSTEPS + 1):
        source, target = pairs[(step - 1) % 2], pairs[step % 2]
        left = NSTEPS - step
        shift = W if step == NSTEPS else 0
        whole = blocks(-left, cols + left)
        sides = blocks(-left, 8 + left) + blocks(cols - 8 - left, cols + left)
        ends = list(sides)
        for tile in range(tiles):
            col, count = plan.columns("last", tile)
            ends += blocks(tile * edge + col - left, tile * edge + col + count + left)
        strip = W + left

        def two(size, begin):
            mirror = 2 * W + edge - begin - size
            return lambda i: i + jnp.where(i < size, begin, mirror - size)

        march(2 * (strip + left), two(strip + left, W - left), whole, source, target, any_zone)
        march(2 * W, two(W, W + strip), sorted(set(ends)), source, target, own_zone)
        march(edge - 2 * strip - 2 * W, lambda i, strip=strip: i + 2 * W + strip, sides, source, target, own_zone)
    done = pairs[NSTEPS % 2]
    for piece in range(half):
        pack(plan, False, piece, done, W, PAD + W, own, out.at[piece])


def run_outer(plan, own, phase, solute, halos):
    tiles, edge, depth = plan.tiles, plan.edge, plan.depth
    width = tiles * edge + 2 * W
    buffer = pltpu.VMEM((edge + 2 * W, width + 2 * PAD, depth), jnp.float32)
    vmem = pl.BlockSpec(memory_space=pltpu.VMEM)
    near = jax.ShapeDtypeStruct((plan.half, 2 * tiles * plan.size + AUX, depth), jnp.float32)
    return pl.pallas_call(
        functools.partial(outer_kernel, plan),
        in_specs=[vmem] * 7,
        out_specs=vmem,
        out_shape=near,
        scratch_shapes=[buffer] * 4 + [pltpu.VMEM((3, KINDS, width, depth), jnp.float32)],
        compiler_params=pltpu.CompilerParams(vmem_limit_bytes=16 * 1024 * 1024),
        cost_estimate=pl.CostEstimate(flops=10**8, bytes_accessed=40 * 1024 * 1024, transcendentals=0),
        name="outer",
    )(own, phase, solute, *halos)


def route_kernel(plan, near, *refs):
    pieces, tiles, half, size = plan.pieces, plan.tiles, plan.half, 2 * plan.size
    far, near_out, far_outs, table = refs[:half], refs[half], refs[half + 1 : 2 * half + 1], refs[2 * half + 1]
    held, peers, count = refs[2 * half + 2 :]
    me = lax.axis_index("gy")
    base = me - lax.rem(me, half)
    tail = tiles * size
    for tile in range(tiles):
        for piece in range(half):
            peer = lax.rem(near[piece, tail, tile].astype(jnp.int32), pieces)
            peers[(base + piece) * tiles + tile] = peer
        for index in range(half):
            peer = lax.rem(far[index][tail, tile].astype(jnp.int32), pieces)
            peers[(me ^ (half + index)) * tiles + tile] = peer
    for piece in range(half):
        for tile in range(tiles):
            held[(base + piece) * tiles + tile] = near[piece, tile * size : (tile + 1) * size, :]
    for index in range(half):
        for tile in range(tiles):
            held[(me ^ (half + index)) * tiles + tile] = far[index][tile * size : (tile + 1) * size, :]
    for peer in range(pieces):
        count[peer] = 0
    for home in range(pieces * tiles):
        peer = peers[home]
        slot = count[peer]
        table[peer * tiles + slot] = home
        count[peer] = slot + 1
    for index in range(half):
        for slot in range(tiles):
            far_outs[index][slot] = held[table[(me ^ (half + index)) * tiles + slot]]
            near_out[index, slot] = held[table[(base + index) * tiles + slot]]


def route(plan, near, far):
    tiles, half, size, depth = plan.tiles, plan.half, 2 * plan.size, plan.depth
    vmem = pl.BlockSpec(memory_space=pltpu.VMEM)
    one = jax.ShapeDtypeStruct((tiles, size, depth), jnp.float32)
    count = plan.pieces * tiles
    results = pl.pallas_call(
        functools.partial(route_kernel, plan),
        in_specs=[vmem] * (half + 1),
        out_specs=[vmem] * (half + 1) + [pl.BlockSpec(memory_space=pltpu.SMEM)],
        out_shape=[jax.ShapeDtypeStruct((half, tiles, size, depth), jnp.float32)]
        + [one] * half
        + [jax.ShapeDtypeStruct((count,), jnp.int32)],
        scratch_shapes=[
            pltpu.VMEM((count, size, depth), jnp.float32),
            pltpu.SMEM((count,), jnp.int32),
            pltpu.SMEM((plan.pieces,), jnp.int32),
        ],
        compiler_params=pltpu.CompilerParams(vmem_limit_bytes=16 * 1024 * 1024),
        name="route",
    )(near, *far)
    return results[0], results[1 : half + 1], results[-1]


def settle_kernel(plan, table, near, *refs):
    tiles, half = plan.tiles, plan.half
    far, outs, (ready, sems) = refs[:half], refs[half : half + 2], refs[half + 2 :]
    me = lax.axis_index("gy")
    mine = lax.rem(me, half)
    copies = []
    for slot in range(tiles):
        home = table[me * tiles + slot]
        tile = lax.rem(home, tiles)
        at_home = home // (tiles * half) == me // half

        def put(source, piece, is_far, slot=slot, tile=tile):
            for field in range(2):
                for at, row, name in plan.parts(is_far, piece):
                    col, count = plan.columns(name, tile)
                    if not isinstance(col, int):
                        col = pl.multiple_of(col, 8)
                    ready[field, slot, row, pl.ds(col, count), :] = source[
                        slot, field * plan.size + at : field * plan.size + at + count, :
                    ]

        def put_all(same, put=put):
            for index in range(half):
                put(near.at[index], index, not same)
                put(far[index], mine ^ index, same)

        @pl.when(at_home)
        def _(put_all=put_all):
            put_all(True)

        @pl.when(jnp.logical_not(at_home))
        def _(put_all=put_all):
            put_all(False)

        for field, out in enumerate(outs):
            copy = pltpu.make_async_copy(ready.at[field, slot], out.at[0, slot], sems.at[field, slot])
            copy.start()
            copies.append(copy)
    for copy in copies:
        copy.wait()


def settle(plan, table, near, far):
    tiles, edge, depth = plan.tiles, plan.edge, plan.depth
    out = jax.ShapeDtypeStruct((1, tiles, edge, edge, depth), jnp.float32)
    vmem = pl.BlockSpec(memory_space=pltpu.VMEM)
    return pl.pallas_call(
        functools.partial(settle_kernel, plan),
        in_specs=[pl.BlockSpec(memory_space=pltpu.SMEM)] + [vmem] * (plan.half + 1),
        out_specs=[pl.BlockSpec(memory_space=pl.ANY)] * 2,
        out_shape=[out, out],
        scratch_shapes=[
            pltpu.VMEM((2, tiles, edge, edge, depth), jnp.float32),
            pltpu.SemaphoreType.DMA((2, tiles)),
        ],
        compiler_params=pltpu.CompilerParams(vmem_limit_bytes=16 * 1024 * 1024),
        name="settle",
    )(table, near, *far)


def ring(axis, step):
    count = lax.axis_size(axis)
    return [(i, (i + step) % count) for i in range(count)]


def swap(values, mask):
    return lax.ppermute(values, "gy", [(i, i ^ mask) for i in range(lax.axis_size("gy"))])


def among_half(plan, values, together):
    def exchange(values):
        groups = [list(range(plan.half)), list(range(plan.half, plan.pieces))]
        return lax.all_to_all(values, "gy", 0, 0, axis_index_groups=groups, tiled=True)

    return lax.cond(together, exchange, exchange, values)


def in_vmem(values):
    return pltpu.with_memory_space_constraint(values, pltpu.VMEM)


def per_device(phase, solute, undercool, mobility, diffusivity, owner):
    _, tiles, edge, _, depth = phase.shape
    plan = Plan(lax.axis_size("gy"), tiles, edge, depth)
    half = plan.half
    to_prev, to_next, own = pack_y(phase, solute, (undercool, mobility, diffusivity), owner)
    y_lo = lax.ppermute(to_next, "gy", ring("gy", 1))
    y_hi = lax.ppermute(to_prev, "gy", ring("gy", -1))
    far = {}

    def send_far(batch, values):
        for index, value in zip(plan.batches[batch], values):
            far[index] = swap(value, half + index)

    own_here, phase_here, solute_here = own, phase, solute
    first = run_inner(plan, 0, own_here, phase_here, solute_here)
    send_far(0, first)
    to_prev, to_next = pack_x(phase_here, solute_here, own_here, y_lo, y_hi, first[0])
    together = owner[0, 0] >= 0

    def around(low, high, *values):
        return ring_swap(low, high), run_inner(plan, 1, *values)

    def ring_swap(low, high):
        return lax.ppermute(low, "gx", ring("gx", 1)), lax.ppermute(high, "gx", ring("gx", -1))

    (x_lo, x_hi), second = lax.cond(together, around, around, to_next, to_prev, own, phase, solute)
    send_far(1, second)
    near = run_outer(plan, own_here, phase_here, solute_here, (y_lo, y_hi, in_vmem(x_lo), in_vmem(x_hi)))
    far = [in_vmem(far[index]) for index in range(half)]
    near = among_half(plan, near, together)
    near, far, table = route(plan, in_vmem(near), far)
    far = [swap(values, half + index) for index, values in enumerate(far)]
    near = among_half(plan, near, together)
    return tuple(settle(plan, table, near, far))


def solution(mesh):
    tile_spec = P("gx", "gy", None, None, None)
    in_specs = (tile_spec, tile_spec) + (P("gx", "gy"),) * 4
    out_spec = P(("gx", "gy"), None, None, None, None)
    return jax.shard_map(
        per_device, mesh=mesh, in_specs=in_specs, out_specs=(out_spec, out_spec), check_vma=False
    )
```

```python
import functools

import jax
import jax.numpy as jnp
from jax import lax
from jax.experimental import pallas as pl
from jax.experimental.pallas import tpu as pltpu
from jax.sharding import PartitionSpec as P

NSTEPS = 4
W = NSTEPS
PAD = 8

aniso_strength = 0.05


def pack_y_kernel(under, mobile, spread, owner, phase_lo, phase_hi, solute_lo, solute_hi, to_prev, to_next, own):
    edge, depth = phase_lo.shape[2], phase_lo.shape[4]
    tiles = own.shape[0] // 8 - 1
    to_prev[:edge, :W, :] = phase_lo[0, 0, :, :W, :]
    to_prev[:edge, W:, :] = solute_lo[0, 0, :, :W, :]
    to_next[:edge, :W, :] = phase_hi[0, 0, :, W:, :]
    to_next[:edge, W:, :] = solute_hi[0, 0, :, W:, :]
    line = lax.broadcasted_iota(jnp.int32, (8, depth), 0)
    lane = lax.broadcasted_iota(jnp.int32, (8, depth), 1)
    names = jnp.zeros((8, depth), jnp.float32)
    for tile in range(tiles):
        rows = jnp.zeros((8, depth), jnp.float32)
        ready = (2.0 * under[0, tile], mobile[0, tile], spread[0, tile], 1.0 - 6.0 * spread[0, tile])
        for kind, coef in enumerate(ready):
            rows = jnp.where(line == kind, coef, rows)
        own[8 * tile : 8 * tile + 8, :] = rows
        if tile == 0:
            to_prev[edge] = rows
        if tile == tiles - 1:
            to_next[edge] = rows
        names = jnp.where(lane == tile, owner[0, tile].astype(jnp.float32), names)
    own[8 * tiles :, :] = names


def pack_y(phase, solute, coef, owner):
    _, tiles, edge, _, depth = phase.shape
    low = pl.BlockSpec((1, 1, edge, 2 * W, depth), lambda i: (0, 0, 0, 0, 0))
    high = pl.BlockSpec((1, 1, edge, 2 * W, depth), lambda i: (0, tiles - 1, 0, edge // (2 * W) - 1, 0))
    face = jax.ShapeDtypeStruct((edge + 1, 2 * W, depth), jnp.float32)
    own = jax.ShapeDtypeStruct((8 * tiles + 8, depth), jnp.float32)
    whole = pl.BlockSpec((edge + 1, 2 * W, depth), lambda i: (0, 0, 0))
    return pl.pallas_call(
        pack_y_kernel,
        grid=(1,),
        in_specs=[pl.BlockSpec(memory_space=pltpu.SMEM)] * 4 + [low, high, low, high],
        out_specs=[whole, whole, pl.BlockSpec((8 * tiles + 8, depth), lambda i: (0, 0))],
        out_shape=[face, face, own],
        name="pack_y",
    )(*coef, owner, phase, phase, solute, solute)


def fill_row(dst, row, phase_row, solute_row, lo, hi):
    start = PAD
    dst[0][row, start : start + W, :] = lo[:W]
    dst[1][row, start : start + W, :] = 2.0 * lo[W:]
    start += W
    for values in phase_row:
        size = values.shape[0]
        dst[0][row, start : start + size, :] = values
        start += size
    dst[0][row, start : start + W, :] = hi[:W]
    dst[1][row, start : start + W, :] = 2.0 * hi[W:]
    start = PAD + W
    for values in solute_row:
        size = values.shape[0]
        dst[1][row, start : start + size, :] = 2.0 * values
        start += size


def pack_x_kernel(own, phase_lo, phase_hi, solute_lo, solute_hi, y_lo, y_hi, _, to_prev, to_next):
    tiles, edge, depth = phase_lo.shape[1], phase_lo.shape[3], phase_lo.shape[4]
    width = tiles * edge + 2 * W
    for out, phase, solute, first in (
        (to_prev, phase_lo, solute_lo, 0),
        (to_next, phase_hi, solute_hi, edge - W),
    ):
        for row in range(W):
            for field, values, half in ((0, phase, 0), (1, solute, W)):
                at = (2 * row + field) * width
                out[at : at + W, :] = y_lo[first + row, half : half + W, :]
                for tile in range(tiles):
                    begin = at + W + tile * edge
                    out[begin : begin + edge, :] = values[0, tile, row]
                out[at + width - W : at + width, :] = y_hi[first + row, half : half + W, :]
        at = 2 * W * width
        out[at : at + 8, :] = y_lo[edge]
        out[at + 8 : at + 16, :] = y_hi[edge]
        out[at + 16 : at + 16 + 8 * tiles, :] = own[: 8 * tiles, :]


def pack_x(phase, solute, own, y_lo, y_hi, after):
    _, tiles, edge, _, depth = phase.shape
    low = pl.BlockSpec((1, tiles, W, edge, depth), lambda i: (0, 0, 0, 0, 0))
    high = pl.BlockSpec((1, tiles, W, edge, depth), lambda i: (0, 0, edge // W - 1, 0, 0))
    side = pl.BlockSpec((edge + 1, 2 * W, depth), lambda i: (0, 0, 0))
    rows = 2 * W * (tiles * edge + 2 * W) + 8 * (tiles + 2)
    out = jax.ShapeDtypeStruct((rows, depth), jnp.float32)
    whole = pl.BlockSpec((rows, depth), lambda i: (0, 0))
    return pl.pallas_call(
        pack_x_kernel,
        grid=(1,),
        in_specs=[pl.BlockSpec((8 * tiles + 8, depth), lambda i: (0, 0)), low, high, low, high, side, side, pl.BlockSpec(memory_space=pl.ANY)],
        out_specs=[whole, whole],
        out_shape=[out, out],
        compiler_params=pltpu.CompilerParams(vmem_limit_bytes=8 * 1024 * 1024),
        name="pack_x",
    )(own, phase, phase, solute, solute, y_lo, y_hi, after)


def update(near_p, near_v, under, mobile, spread, keep):
    p, p_xl, p_xh, p_yl, p_yh = near_p
    v, v_xl, v_xh, v_yl, v_yh = near_v
    depth = p.shape[-1]
    lane = lax.broadcasted_iota(jnp.int32, p.shape, 1)
    first, last = lane == 0, lane == depth - 1
    p_zl = jnp.where(first, p, pltpu.roll(p, 1, 1))
    p_zh = jnp.where(last, p, pltpu.roll(p, depth - 1, 1))
    v_zl = jnp.where(first, v, pltpu.roll(v, 1, 1))
    v_zh = jnp.where(last, v, pltpu.roll(v, depth - 1, 1))
    dx, dy, dz = p_xh - p_xl, p_yh - p_yl, p_zh - p_zl
    qx, qy, qz = dx * dx, dy * dy, dz * dz
    flat = qx + qy
    total = flat + qz
    pairs = qx * qy + flat * qz
    base = total + 4.0
    guess = pl.reciprocal(base, approx=True)
    inverse = guess * (2.0 - base * guess)
    extra = (aniso_strength * total * total - (8.0 * aniso_strength) * pairs) * (inverse * inverse)
    lap_p = (p_xl + p_xh) + (p_yl + p_yh) + (p_zl + p_zh) - 6.0 * p
    sum_v = (v_xl + v_xh) + (v_yl + v_yh) + (v_zl + v_zh)
    well = 1.0 - p * p
    change = mobile * (lap_p + extra * lap_p + well * (p - well * (under + v)))
    return p + change, keep * v + spread * sum_v + change


KINDS = 4


def cells(src_p, src_u, row, start, coefs):
    near = []
    for src in (src_p, src_u):
        near.append(
            (
                src[row, start : start + 8, :],
                src[row - 1, start : start + 8, :],
                src[row + 1, start : start + 8, :],
                src[row, start - 1 : start + 7, :],
                src[row, start + 1 : start + 9, :],
            )
        )
    return update(near[0], near[1], *coefs)


class Plan:
    def __init__(self, pieces, tiles, edge, depth):
        self.pieces, self.tiles, self.edge, self.depth = pieces, tiles, edge, depth
        self.half = pieces // 2
        self.inner = edge - 2 * W
        self.rows = self.inner // self.half
        self.rows_far = (self.inner - 2 * W) // self.half
        self.rows_near = 2 * W // self.half
        self.middle = edge - 16
        self.size = self.rows * self.middle + self.rows_far * 8

        side = self.half // 2
        self.batches = (list(range(side)), list(range(side, self.half)))

    def batch_rows(self, batch, mine):
        count = self.inner // 2
        side = mine // (self.half // 2)
        return W + (side if batch == 0 else 1 - side) * count, count

    def near_row(self, piece, row, gap):
        index = piece * self.rows_near + row
        return index + jnp.where(index < W, 0, gap)

    def parts(self, far, piece):
        at, found = 0, []
        if far:
            for row in range(self.rows):
                found.append((at, W + piece * self.rows + row, "middle"))
                at += self.middle
            for row in range(self.rows_far):
                found.append((at, 2 * W + piece * self.rows_far + row, "last"))
                at += 8
        else:
            for row in range(self.rows_near):
                found.append((at, self.near_row(piece, row, self.inner), "whole"))
                at += self.edge
            for row in range(self.rows):
                found.append((at, W + piece * self.rows + row, "side"))
                at += 8
            for row in range(self.rows_near):
                found.append((at, W + self.near_row(piece, row, self.inner - 2 * W), "last"))
                at += 8
        assert at == self.size
        return found

    def columns(self, name, tile):
        if name == "whole":
            return 0, self.edge
        if name == "middle":
            return 8, self.middle
        low, high = (tile, 1 - tile) if name == "side" else (1 - tile, tile)
        return low * (self.edge - 8), 8


AUX = 8
UNROLL = 4


def march(count, row_of, starts, source, target, coefs_of):
    def one_row(index, carry):
        row = row_of(index)
        for start in starts:
            new_p, new_u = cells(source[0], source[1], row, start, coefs_of(row, start))
            target[0][row, start : start + 8, :] = new_p
            target[1][row, start : start + 8, :] = new_u
        return carry

    lax.fori_loop(0, count, one_row, 0, unroll=UNROLL)


def inner_kernel(plan, batch, own, phase, solute, *rest):
    tiles, edge, indices = plan.tiles, plan.edge, plan.batches[batch]
    outs, scratch = rest[: len(indices)], rest[len(indices) :]
    pairs = (scratch[:2], scratch[2:])
    mine = lax.rem(lax.axis_index("gy"), plan.half)
    begin, count = plan.batch_rows(batch, mine)
    base = begin - W

    def load_row(row, carry):
        for tile in range(tiles):
            start = PAD + tile * edge
            pairs[0][0][row, start : start + edge, :] = phase[0, tile, base + row]
            pairs[0][1][row, start : start + edge, :] = 2.0 * solute[0, tile, base + row]
        return carry

    lax.fori_loop(0, count + 2 * W, load_row, 0, unroll=UNROLL)

    line = lax.broadcasted_iota(jnp.int32, (8, plan.depth), 0)

    def coefs_of(row, start):
        low, high = (start - PAD) // edge, (start + 7 - PAD) // edge
        rows = [[own[8 * tile + kind : 8 * tile + kind + 1, :] for tile in (low, high)] for kind in range(KINDS)]
        if low == high:
            return tuple(pair[0] for pair in rows)
        return tuple(jnp.where(line < W, *pair) for pair in rows)

    for step in range(NSTEPS):
        margin = 8 if step == NSTEPS - 1 else W
        starts = range(PAD + margin, PAD + tiles * edge - margin, 8)
        rows = count + 2 * W - 2 * (step + 1)
        march(rows, lambda i, step=step: step + 1 + i, starts, pairs[step % 2], pairs[(step + 1) % 2], coefs_of)
    for index, out in zip(indices, outs):
        pack(plan, True, mine ^ index, pairs[NSTEPS % 2], -base, PAD, own, out)


def pack(plan, far, piece, done, row_shift, col_shift, own, out):
    for tile in range(plan.tiles):
        for field, values in enumerate(done):
            begin = (2 * tile + field) * plan.size
            for at, row, name in plan.parts(far, piece):
                col, count = plan.columns(name, tile)
                start = col_shift + tile * plan.edge + col
                cells = values[row + row_shift, start : start + count, :]
                out[begin + at : begin + at + count, :] = 0.5 * cells if field else cells
    tail = 2 * plan.tiles * plan.size
    out[tail : tail + AUX, :] = own[8 * plan.tiles : 8 * plan.tiles + AUX, :]


def run_inner(plan, batch, own, phase, solute):
    rows = plan.batch_rows(batch, 0)[1] + 2 * W
    count = len(plan.batches[batch])
    buffer = pltpu.VMEM((rows, plan.tiles * plan.edge + 2 * PAD, plan.depth), jnp.float32)
    vmem = pl.BlockSpec(memory_space=pltpu.VMEM)
    shape = jax.ShapeDtypeStruct((2 * plan.tiles * plan.size + AUX, plan.depth), jnp.float32)
    return pl.pallas_call(
        functools.partial(inner_kernel, plan, batch),
        in_specs=[vmem] * 3,
        out_specs=[vmem] * count,
        out_shape=[shape] * count,
        scratch_shapes=[buffer] * 4,
        compiler_params=pltpu.CompilerParams(vmem_limit_bytes=16 * 1024 * 1024),
        cost_estimate=pl.CostEstimate(flops=10**8, bytes_accessed=24 * 1024 * 1024, transcendentals=0),
        name="inner",
    )(own, phase, solute)


def outer_kernel(plan, own, phase, solute, y_lo, y_hi, x_lo, x_hi, out, *scratch):
    tiles, edge, depth, half = plan.tiles, plan.edge, plan.depth, plan.half
    pairs, coefs = (scratch[:2], scratch[2:4]), scratch[4]
    cols = tiles * edge
    width = cols + 2 * W
    for zone, source in ((0, x_lo), (1, None), (2, x_hi)):
        for kind in range(KINDS):
            if source is None:
                parts = [y_lo[edge, kind : kind + 1, :]]
                parts += [own[8 * tile + kind : 8 * tile + kind + 1, :] for tile in range(tiles)]
                parts += [y_hi[edge, kind : kind + 1, :]]
            else:
                at = 2 * W * width + kind
                parts = [source[at : at + 1, :]]
                parts += [source[at + 16 + 8 * tile : at + 17 + 8 * tile, :] for tile in range(tiles)]
                parts += [source[at + 8 : at + 9, :]]
            coefs[zone, kind, :W, :] = jnp.broadcast_to(parts[0], (W, depth))
            for tile in range(tiles):
                begin = W + tile * edge
                coefs[zone, kind, begin : begin + edge, :] = jnp.broadcast_to(parts[1 + tile], (edge, depth))
            coefs[zone, kind, width - W :, :] = jnp.broadcast_to(parts[-1], (W, depth))
    for source, first in ((x_lo, 0), (x_hi, edge + W)):
        for row in range(W):
            for field in range(2):
                at = (2 * row + field) * width
                values = source[at : at + width, :]
                pairs[0][field][first + row, PAD : PAD + width, :] = 2.0 * values if field else values

    def load_row(row, carry):
        fill_row(
            pairs[0],
            W + row,
            [phase[0, tile, row] for tile in range(tiles)],
            [solute[0, tile, row] for tile in range(tiles)],
            y_lo[row],
            y_hi[row],
        )
        return carry

    lax.fori_loop(0, edge, load_row, 0, unroll=UNROLL)

    def coefs_of(zone):
        def found(row, start):
            return tuple(coefs[zone(row), kind, start - PAD : start - PAD + 8, :] for kind in range(KINDS))

        return found

    any_zone = coefs_of(lambda row: jnp.where(row < W, 0, jnp.where(row < W + edge, 1, 2)))

    own_zone = coefs_of(lambda row: 1)
    def blocks(first, last):
        low, high = (first + W - shift) // 8 * 8, -(-(last + W - shift) // 8) * 8
        return list(range(PAD + shift + low, PAD + shift + high, 8))

    for step in range(1, NSTEPS + 1):
        source, target = pairs[(step - 1) % 2], pairs[step % 2]
        left = NSTEPS - step
        shift = W if step == NSTEPS else 0
        whole = blocks(-left, cols + left)
        sides = blocks(-left, 8 + left) + blocks(cols - 8 - left, cols + left)
        ends = list(sides)
        for tile in range(tiles):
            col, count = plan.columns("last", tile)
            ends += blocks(tile * edge + col - left, tile * edge + col + count + left)
        strip = W + left

        def two(size, begin):
            mirror = 2 * W + edge - begin - size
            return lambda i: i + jnp.where(i < size, begin, mirror - size)

        march(2 * (strip + left), two(strip + left, W - left), whole, source, target, any_zone)
        march(2 * W, two(W, W + strip), sorted(set(ends)), source, target, own_zone)
        march(edge - 2 * strip - 2 * W, lambda i, strip=strip: i + 2 * W + strip, sides, source, target, own_zone)
    done = pairs[NSTEPS % 2]
    for piece in range(half):
        pack(plan, False, piece, done, W, PAD + W, own, out.at[piece])


def run_outer(plan, own, phase, solute, halos):
    tiles, edge, depth = plan.tiles, plan.edge, plan.depth
    width = tiles * edge + 2 * W
    buffer = pltpu.VMEM((edge + 2 * W, width + 2 * PAD, depth), jnp.float32)
    vmem = pl.BlockSpec(memory_space=pltpu.VMEM)
    near = jax.ShapeDtypeStruct((plan.half, 2 * tiles * plan.size + AUX, depth), jnp.float32)
    return pl.pallas_call(
        functools.partial(outer_kernel, plan),
        in_specs=[vmem] * 7,
        out_specs=vmem,
        out_shape=near,
        scratch_shapes=[buffer] * 4 + [pltpu.VMEM((3, KINDS, width, depth), jnp.float32)],
        compiler_params=pltpu.CompilerParams(vmem_limit_bytes=16 * 1024 * 1024),
        cost_estimate=pl.CostEstimate(flops=10**8, bytes_accessed=40 * 1024 * 1024, transcendentals=0),
        name="outer",
    )(own, phase, solute, *halos)


def route_kernel(plan, near, *refs):
    pieces, tiles, half, size = plan.pieces, plan.tiles, plan.half, 2 * plan.size
    far, near_out, far_outs, table = refs[:half], refs[half], refs[half + 1 : 2 * half + 1], refs[2 * half + 1]
    held, peers, count = refs[2 * half + 2 :]
    me = lax.axis_index("gy")
    base = me - lax.rem(me, half)
    tail = tiles * size
    for tile in range(tiles):
        for piece in range(half):
            peer = lax.rem(near[piece, tail, tile].astype(jnp.int32), pieces)
            peers[(base + piece) * tiles + tile] = peer
        for index in range(half):
            peer = lax.rem(far[index][tail, tile].astype(jnp.int32), pieces)
            peers[(me ^ (half + index)) * tiles + tile] = peer
    for piece in range(half):
        for tile in range(tiles):
            held[(base + piece) * tiles + tile] = near[piece, tile * size : (tile + 1) * size, :]
    for index in range(half):
        for tile in range(tiles):
            held[(me ^ (half + index)) * tiles + tile] = far[index][tile * size : (tile + 1) * size, :]
    for peer in range(pieces):
        count[peer] = 0
    for home in range(pieces * tiles):
        peer = peers[home]
        slot = count[peer]
        table[peer * tiles + slot] = home
        count[peer] = slot + 1
    for index in range(half):
        for slot in range(tiles):
            far_outs[index][slot] = held[table[(me ^ (half + index)) * tiles + slot]]
            near_out[index, slot] = held[table[(base + index) * tiles + slot]]


def route(plan, near, far):
    tiles, half, size, depth = plan.tiles, plan.half, 2 * plan.size, plan.depth
    vmem = pl.BlockSpec(memory_space=pltpu.VMEM)
    one = jax.ShapeDtypeStruct((tiles, size, depth), jnp.float32)
    count = plan.pieces * tiles
    results = pl.pallas_call(
        functools.partial(route_kernel, plan),
        in_specs=[vmem] * (half + 1),
        out_specs=[vmem] * (half + 1) + [pl.BlockSpec(memory_space=pltpu.SMEM)],
        out_shape=[jax.ShapeDtypeStruct((half, tiles, size, depth), jnp.float32)]
        + [one] * half
        + [jax.ShapeDtypeStruct((count,), jnp.int32)],
        scratch_shapes=[
            pltpu.VMEM((count, size, depth), jnp.float32),
            pltpu.SMEM((count,), jnp.int32),
            pltpu.SMEM((plan.pieces,), jnp.int32),
        ],
        compiler_params=pltpu.CompilerParams(vmem_limit_bytes=16 * 1024 * 1024),
        name="route",
    )(near, *far)
    return results[0], results[1 : half + 1], results[-1]


def settle_kernel(plan, table, near, *refs):
    tiles, half = plan.tiles, plan.half
    far, outs, (ready, sems) = refs[:half], refs[half : half + 2], refs[half + 2 :]
    me = lax.axis_index("gy")
    mine = lax.rem(me, half)
    copies = []
    for slot in range(tiles):
        home = table[me * tiles + slot]
        tile = lax.rem(home, tiles)
        at_home = home // (tiles * half) == me // half

        def put(source, piece, is_far, slot=slot, tile=tile):
            for field in range(2):
                for at, row, name in plan.parts(is_far, piece):
                    col, count = plan.columns(name, tile)
                    if not isinstance(col, int):
                        col = pl.multiple_of(col, 8)
                    ready[field, slot, row, pl.ds(col, count), :] = source[
                        slot, field * plan.size + at : field * plan.size + at + count, :
                    ]

        def put_all(same, put=put):
            for index in range(half):
                put(near.at[index], index, not same)
                put(far[index], mine ^ index, same)

        @pl.when(at_home)
        def _(put_all=put_all):
            put_all(True)

        @pl.when(jnp.logical_not(at_home))
        def _(put_all=put_all):
            put_all(False)

        for field, out in enumerate(outs):
            copy = pltpu.make_async_copy(ready.at[field, slot], out.at[0, slot], sems.at[field, slot])
            copy.start()
            copies.append(copy)
    for copy in copies:
        copy.wait()


def settle(plan, table, near, far):
    tiles, edge, depth = plan.tiles, plan.edge, plan.depth
    out = jax.ShapeDtypeStruct((1, tiles, edge, edge, depth), jnp.float32)
    vmem = pl.BlockSpec(memory_space=pltpu.VMEM)
    return pl.pallas_call(
        functools.partial(settle_kernel, plan),
        in_specs=[pl.BlockSpec(memory_space=pltpu.SMEM)] + [vmem] * (plan.half + 1),
        out_specs=[pl.BlockSpec(memory_space=pl.ANY)] * 2,
        out_shape=[out, out],
        scratch_shapes=[
            pltpu.VMEM((2, tiles, edge, edge, depth), jnp.float32),
            pltpu.SemaphoreType.DMA((2, tiles)),
        ],
        compiler_params=pltpu.CompilerParams(vmem_limit_bytes=16 * 1024 * 1024),
        name="settle",
    )(table, near, *far)


def ring(axis, step):
    count = lax.axis_size(axis)
    return [(i, (i + step) % count) for i in range(count)]


def swap(values, mask):
    return lax.ppermute(values, "gy", [(i, i ^ mask) for i in range(lax.axis_size("gy"))])


def among_half(plan, values, together):
    def exchange(values):
        groups = [list(range(plan.half)), list(range(plan.half, plan.pieces))]
        return lax.all_to_all(values, "gy", 0, 0, axis_index_groups=groups, tiled=True)

    return lax.cond(together, exchange, exchange, values)


def in_vmem(values):
    return pltpu.with_memory_space_constraint(values, pltpu.VMEM)


def per_device(phase, solute, undercool, mobility, diffusivity, owner):
    _, tiles, edge, _, depth = phase.shape
    plan = Plan(lax.axis_size("gy"), tiles, edge, depth)
    half = plan.half
    to_prev, to_next, own = pack_y(phase, solute, (undercool, mobility, diffusivity), owner)
    y_lo = lax.ppermute(to_next, "gy", ring("gy", 1))
    y_hi = lax.ppermute(to_prev, "gy", ring("gy", -1))
    far = {}

    def send_far(batch, values):
        for index, value in zip(plan.batches[batch], values):
            far[index] = swap(value, half + index)

    own_here, phase_here, solute_here = own, phase, solute
    first = run_inner(plan, 0, own_here, phase_here, in_vmem(solute_here))
    send_far(0, first)
    to_prev, to_next = pack_x(phase_here, solute_here, own_here, y_lo, y_hi, first[0])
    together = owner[0, 0] >= 0

    def around(low, high, *values):
        return ring_swap(low, high), run_inner(plan, 1, *values)

    def ring_swap(low, high):
        return lax.ppermute(low, "gx", ring("gx", 1)), lax.ppermute(high, "gx", ring("gx", -1))

    (x_lo, x_hi), second = lax.cond(together, around, around, to_next, to_prev, own, phase, solute)
    send_far(1, second)
    near = run_outer(plan, own_here, phase_here, solute_here, (y_lo, y_hi, in_vmem(x_lo), in_vmem(x_hi)))
    far = [in_vmem(far[index]) for index in range(half)]
    near = among_half(plan, near, together)
    near, far, table = route(plan, in_vmem(near), far)
    far = [swap(values, half + index) for index, values in enumerate(far)]
    near = among_half(plan, near, together)
    return tuple(settle(plan, table, near, far))


def solution(mesh):
    tile_spec = P("gx", "gy", None, None, None)
    in_specs = (tile_spec, tile_spec) + (P("gx", "gy"),) * 4
    out_spec = P(("gx", "gy"), None, None, None, None)
    return jax.shard_map(
        per_device, mesh=mesh, in_specs=in_specs, out_specs=(out_spec, out_spec), check_vma=False
    )
```

```python
import functools

import jax
import jax.numpy as jnp
from jax import lax
from jax.experimental import pallas as pl
from jax.experimental.pallas import tpu as pltpu
from jax.sharding import PartitionSpec as P

NSTEPS = 4
W = NSTEPS
PAD = 8

aniso_strength = 0.05


def pack_y_kernel(under, mobile, spread, owner, phase_lo, phase_hi, solute_lo, solute_hi, to_prev, to_next, own):
    edge, depth = phase_lo.shape[2], phase_lo.shape[4]
    tiles = own.shape[0] // 8 - 1
    to_prev[:edge, :W, :] = phase_lo[0, 0, :, :W, :]
    to_prev[:edge, W:, :] = solute_lo[0, 0, :, :W, :]
    to_next[:edge, :W, :] = phase_hi[0, 0, :, W:, :]
    to_next[:edge, W:, :] = solute_hi[0, 0, :, W:, :]
    line = lax.broadcasted_iota(jnp.int32, (8, depth), 0)
    lane = lax.broadcasted_iota(jnp.int32, (8, depth), 1)
    names = jnp.zeros((8, depth), jnp.float32)
    for tile in range(tiles):
        rows = jnp.zeros((8, depth), jnp.float32)
        ready = (2.0 * under[0, tile], mobile[0, tile], spread[0, tile], 1.0 - 6.0 * spread[0, tile])
        for kind, coef in enumerate(ready):
            rows = jnp.where(line == kind, coef, rows)
        own[8 * tile : 8 * tile + 8, :] = rows
        if tile == 0:
            to_prev[edge] = rows
        if tile == tiles - 1:
            to_next[edge] = rows
        names = jnp.where(lane == tile, owner[0, tile].astype(jnp.float32), names)
    own[8 * tiles :, :] = names


def pack_y(phase, solute, coef, owner):
    _, tiles, edge, _, depth = phase.shape
    low = pl.BlockSpec((1, 1, edge, 2 * W, depth), lambda i: (0, 0, 0, 0, 0))
    high = pl.BlockSpec((1, 1, edge, 2 * W, depth), lambda i: (0, tiles - 1, 0, edge // (2 * W) - 1, 0))
    face = jax.ShapeDtypeStruct((edge + 1, 2 * W, depth), jnp.float32)
    own = jax.ShapeDtypeStruct((8 * tiles + 8, depth), jnp.float32)
    whole = pl.BlockSpec((edge + 1, 2 * W, depth), lambda i: (0, 0, 0))
    return pl.pallas_call(
        pack_y_kernel,
        grid=(1,),
        in_specs=[pl.BlockSpec(memory_space=pltpu.SMEM)] * 4 + [low, high, low, high],
        out_specs=[whole, whole, pl.BlockSpec((8 * tiles + 8, depth), lambda i: (0, 0))],
        out_shape=[face, face, own],
        name="pack_y",
    )(*coef, owner, phase, phase, solute, solute)


def fill_row(dst, row, phase_row, solute_row, lo, hi):
    start = PAD
    dst[0][row, start : start + W, :] = lo[:W]
    dst[1][row, start : start + W, :] = 2.0 * lo[W:]
    start += W
    for values in phase_row:
        size = values.shape[0]
        dst[0][row, start : start + size, :] = values
        start += size
    dst[0][row, start : start + W, :] = hi[:W]
    dst[1][row, start : start + W, :] = 2.0 * hi[W:]
    start = PAD + W
    for values in solute_row:
        size = values.shape[0]
        dst[1][row, start : start + size, :] = 2.0 * values
        start += size


def pack_x_kernel(own, phase_lo, phase_hi, solute_lo, solute_hi, y_lo, y_hi, _, to_prev, to_next):
    tiles, edge, depth = phase_lo.shape[1], phase_lo.shape[3], phase_lo.shape[4]
    width = tiles * edge + 2 * W
    for out, phase, solute, first in (
        (to_prev, phase_lo, solute_lo, 0),
        (to_next, phase_hi, solute_hi, edge - W),
    ):
        for row in range(W):
            for field, values, half in ((0, phase, 0), (1, solute, W)):
                at = (2 * row + field) * width
                out[at : at + W, :] = y_lo[first + row, half : half + W, :]
                for tile in range(tiles):
                    begin = at + W + tile * edge
                    out[begin : begin + edge, :] = values[0, tile, row]
                out[at + width - W : at + width, :] = y_hi[first + row, half : half + W, :]
        at = 2 * W * width
        out[at : at + 8, :] = y_lo[edge]
        out[at + 8 : at + 16, :] = y_hi[edge]
        out[at + 16 : at + 16 + 8 * tiles, :] = own[: 8 * tiles, :]


def pack_x(phase, solute, own, y_lo, y_hi, after):
    _, tiles, edge, _, depth = phase.shape
    low = pl.BlockSpec((1, tiles, W, edge, depth), lambda i: (0, 0, 0, 0, 0))
    high = pl.BlockSpec((1, tiles, W, edge, depth), lambda i: (0, 0, edge // W - 1, 0, 0))
    side = pl.BlockSpec((edge + 1, 2 * W, depth), lambda i: (0, 0, 0))
    rows = 2 * W * (tiles * edge + 2 * W) + 8 * (tiles + 2)
    out = jax.ShapeDtypeStruct((rows, depth), jnp.float32)
    whole = pl.BlockSpec((rows, depth), lambda i: (0, 0))
    return pl.pallas_call(
        pack_x_kernel,
        grid=(1,),
        in_specs=[pl.BlockSpec((8 * tiles + 8, depth), lambda i: (0, 0)), low, high, low, high, side, side, pl.BlockSpec(memory_space=pl.ANY)],
        out_specs=[whole, whole],
        out_shape=[out, out],
        compiler_params=pltpu.CompilerParams(vmem_limit_bytes=8 * 1024 * 1024),
        name="pack_x",
    )(own, phase, phase, solute, solute, y_lo, y_hi, after)


def update(near_p, near_v, under, mobile, spread, keep):
    p, p_xl, p_xh, p_yl, p_yh = near_p
    v, v_xl, v_xh, v_yl, v_yh = near_v
    depth = p.shape[-1]
    lane = lax.broadcasted_iota(jnp.int32, p.shape, 1)
    first, last = lane == 0, lane == depth - 1
    p_zl = jnp.where(first, p, pltpu.roll(p, 1, 1))
    p_zh = jnp.where(last, p, pltpu.roll(p, depth - 1, 1))
    v_zl = jnp.where(first, v, pltpu.roll(v, 1, 1))
    v_zh = jnp.where(last, v, pltpu.roll(v, depth - 1, 1))
    dx, dy, dz = p_xh - p_xl, p_yh - p_yl, p_zh - p_zl
    qx, qy, qz = dx * dx, dy * dy, dz * dz
    flat = qx + qy
    total = flat + qz
    pairs = qx * qy + flat * qz
    base = total + 4.0
    guess = pl.reciprocal(base, approx=True)
    inverse = guess * (2.0 - base * guess)
    extra = (aniso_strength * total * total - (8.0 * aniso_strength) * pairs) * (inverse * inverse)
    lap_p = (p_xl + p_xh) + (p_yl + p_yh) + (p_zl + p_zh) - 6.0 * p
    sum_v = (v_xl + v_xh) + (v_yl + v_yh) + (v_zl + v_zh)
    well = 1.0 - p * p
    change = mobile * (lap_p + extra * lap_p + well * (p - well * (under + v)))
    return p + change, keep * v + spread * sum_v + change


KINDS = 4


def cells(src_p, src_u, row, start, coefs):
    near = []
    for src in (src_p, src_u):
        near.append(
            (
                src[row, start : start + 8, :],
                src[row - 1, start : start + 8, :],
                src[row + 1, start : start + 8, :],
                src[row, start - 1 : start + 7, :],
                src[row, start + 1 : start + 9, :],
            )
        )
    return update(near[0], near[1], *coefs)


class Plan:
    def __init__(self, pieces, tiles, edge, depth):
        self.pieces, self.tiles, self.edge, self.depth = pieces, tiles, edge, depth
        self.half = pieces // 2
        self.inner = edge - 2 * W
        self.rows = self.inner // self.half
        self.rows_far = (self.inner - 2 * W) // self.half
        self.rows_near = 2 * W // self.half
        self.middle = edge - 16
        self.size = self.rows * self.middle + self.rows_far * 8

        side = self.half // 2
        self.batches = (list(range(side)), list(range(side, self.half)))

    def batch_rows(self, batch, mine):
        count = self.inner // 2
        side = mine // (self.half // 2)
        return W + (side if batch == 0 else 1 - side) * count, count

    def near_row(self, piece, row, gap):
        index = piece * self.rows_near + row
        return index + jnp.where(index < W, 0, gap)

    def parts(self, far, piece):
        at, found = 0, []
        if far:
            for row in range(self.rows):
                found.append((at, W + piece * self.rows + row, "middle"))
                at += self.middle
            for row in range(self.rows_far):
                found.append((at, 2 * W + piece * self.rows_far + row, "last"))
                at += 8
        else:
            for row in range(self.rows_near):
                found.append((at, self.near_row(piece, row, self.inner), "whole"))
                at += self.edge
            for row in range(self.rows):
                found.append((at, W + piece * self.rows + row, "side"))
                at += 8
            for row in range(self.rows_near):
                found.append((at, W + self.near_row(piece, row, self.inner - 2 * W), "last"))
                at += 8
        assert at == self.size
        return found

    def columns(self, name, tile):
        if name == "whole":
            return 0, self.edge
        if name == "middle":
            return 8, self.middle
        low, high = (tile, 1 - tile) if name == "side" else (1 - tile, tile)
        return low * (self.edge - 8), 8


AUX = 8
UNROLL = 4


def march(count, row_of, starts, source, target, coefs_of, unroll=UNROLL):
    def one_row(index, carry):
        row = row_of(index)
        for start in starts:
            new_p, new_u = cells(source[0], source[1], row, start, coefs_of(row, start))
            target[0][row, start : start + 8, :] = new_p
            target[1][row, start : start + 8, :] = new_u
        return carry

    lax.fori_loop(0, count, one_row, 0, unroll=unroll)


def inner_kernel(plan, batch, own, phase, solute, *rest):
    tiles, edge, indices = plan.tiles, plan.edge, plan.batches[batch]
    outs, scratch = rest[: len(indices)], rest[len(indices) :]
    pairs = (scratch[:2], scratch[2:])
    mine = lax.rem(lax.axis_index("gy"), plan.half)
    begin, count = plan.batch_rows(batch, mine)
    base = begin - W

    def load_row(row, carry):
        for tile in range(tiles):
            start = PAD + tile * edge
            pairs[0][0][row, start : start + edge, :] = phase[0, tile, base + row]
            pairs[0][1][row, start : start + edge, :] = 2.0 * solute[0, tile, base + row]
        return carry

    lax.fori_loop(0, count + 2 * W, load_row, 0, unroll=UNROLL)

    line = lax.broadcasted_iota(jnp.int32, (8, plan.depth), 0)

    def coefs_of(row, start):
        low, high = (start - PAD) // edge, (start + 7 - PAD) // edge
        rows = [[own[8 * tile + kind : 8 * tile + kind + 1, :] for tile in (low, high)] for kind in range(KINDS)]
        if low == high:
            return tuple(pair[0] for pair in rows)
        return tuple(jnp.where(line < W, *pair) for pair in rows)

    for step in range(NSTEPS):
        margin = 8 if step == NSTEPS - 1 else W
        starts = range(PAD + margin, PAD + tiles * edge - margin, 8)
        rows = count + 2 * W - 2 * (step + 1)
        march(rows, lambda i, step=step: step + 1 + i, starts, pairs[step % 2], pairs[(step + 1) % 2], coefs_of, 6)
    for index, out in zip(indices, outs):
        pack(plan, True, mine ^ index, pairs[NSTEPS % 2], -base, PAD, own, out)


def pack(plan, far, piece, done, row_shift, col_shift, own, out):
    for tile in range(plan.tiles):
        for field, values in enumerate(done):
            begin = (2 * tile + field) * plan.size
            for at, row, name in plan.parts(far, piece):
                col, count = plan.columns(name, tile)
                start = col_shift + tile * plan.edge + col
                cells = values[row + row_shift, start : start + count, :]
                out[begin + at : begin + at + count, :] = 0.5 * cells if field else cells
    tail = 2 * plan.tiles * plan.size
    out[tail : tail + AUX, :] = own[8 * plan.tiles : 8 * plan.tiles + AUX, :]


def run_inner(plan, batch, own, phase, solute):
    rows = plan.batch_rows(batch, 0)[1] + 2 * W
    count = len(plan.batches[batch])
    buffer = pltpu.VMEM((rows, plan.tiles * plan.edge + 2 * PAD, plan.depth), jnp.float32)
    vmem = pl.BlockSpec(memory_space=pltpu.VMEM)
    shape = jax.ShapeDtypeStruct((2 * plan.tiles * plan.size + AUX, plan.depth), jnp.float32)
    return pl.pallas_call(
        functools.partial(inner_kernel, plan, batch),
        in_specs=[vmem] * 3,
        out_specs=[vmem] * count,
        out_shape=[shape] * count,
        scratch_shapes=[buffer] * 4,
        compiler_params=pltpu.CompilerParams(vmem_limit_bytes=16 * 1024 * 1024),
        cost_estimate=pl.CostEstimate(flops=10**8, bytes_accessed=24 * 1024 * 1024, transcendentals=0),
        name="inner",
    )(own, phase, solute)


def outer_kernel(plan, own, phase, solute, y_lo, y_hi, x_lo, x_hi, out, *scratch):
    tiles, edge, depth, half = plan.tiles, plan.edge, plan.depth, plan.half
    pairs, coefs = (scratch[:2], scratch[2:4]), scratch[4]
    cols = tiles * edge
    width = cols + 2 * W
    for zone, source in ((0, x_lo), (1, None), (2, x_hi)):
        for kind in range(KINDS):
            if source is None:
                parts = [y_lo[edge, kind : kind + 1, :]]
                parts += [own[8 * tile + kind : 8 * tile + kind + 1, :] for tile in range(tiles)]
                parts += [y_hi[edge, kind : kind + 1, :]]
            else:
                at = 2 * W * width + kind
                parts = [source[at : at + 1, :]]
                parts += [source[at + 16 + 8 * tile : at + 17 + 8 * tile, :] for tile in range(tiles)]
                parts += [source[at + 8 : at + 9, :]]
            coefs[zone, kind, :W, :] = jnp.broadcast_to(parts[0], (W, depth))
            for tile in range(tiles):
                begin = W + tile * edge
                coefs[zone, kind, begin : begin + edge, :] = jnp.broadcast_to(parts[1 + tile], (edge, depth))
            coefs[zone, kind, width - W :, :] = jnp.broadcast_to(parts[-1], (W, depth))
    for source, first in ((x_lo, 0), (x_hi, edge + W)):
        for row in range(W):
            for field in range(2):
                at = (2 * row + field) * width
                values = source[at : at + width, :]
                pairs[0][field][first + row, PAD : PAD + width, :] = 2.0 * values if field else values

    def load_row(row, carry):
        fill_row(
            pairs[0],
            W + row,
            [phase[0, tile, row] for tile in range(tiles)],
            [solute[0, tile, row] for tile in range(tiles)],
            y_lo[row],
            y_hi[row],
        )
        return carry

    lax.fori_loop(0, edge, load_row, 0, unroll=UNROLL)

    def coefs_of(zone):
        def found(row, start):
            return tuple(coefs[zone(row), kind, start - PAD : start - PAD + 8, :] for kind in range(KINDS))

        return found

    any_zone = coefs_of(lambda row: jnp.where(row < W, 0, jnp.where(row < W + edge, 1, 2)))

    own_zone = coefs_of(lambda row: 1)
    def blocks(first, last):
        low, high = (first + W - shift) // 8 * 8, -(-(last + W - shift) // 8) * 8
        return list(range(PAD + shift + low, PAD + shift + high, 8))

    for step in range(1, NSTEPS + 1):
        source, target = pairs[(step - 1) % 2], pairs[step % 2]
        left = NSTEPS - step
        shift = W if step == NSTEPS else 0
        whole = blocks(-left, cols + left)
        sides = blocks(-left, 8 + left) + blocks(cols - 8 - left, cols + left)
        ends = list(sides)
        for tile in range(tiles):
            col, count = plan.columns("last", tile)
            ends += blocks(tile * edge + col - left, tile * edge + col + count + left)
        strip = W + left

        def two(size, begin):
            mirror = 2 * W + edge - begin - size
            return lambda i: i + jnp.where(i < size, begin, mirror - size)

        march(2 * (strip + left), two(strip + left, W - left), whole, source, target, any_zone)
        march(2 * W, two(W, W + strip), sorted(set(ends)), source, target, own_zone)
        march(edge - 2 * strip - 2 * W, lambda i, strip=strip: i + 2 * W + strip, sides, source, target, own_zone)
    done = pairs[NSTEPS % 2]
    for piece in range(half):
        pack(plan, False, piece, done, W, PAD + W, own, out.at[piece])


def run_outer(plan, own, phase, solute, halos):
    tiles, edge, depth = plan.tiles, plan.edge, plan.depth
    width = tiles * edge + 2 * W
    buffer = pltpu.VMEM((edge + 2 * W, width + 2 * PAD, depth), jnp.float32)
    vmem = pl.BlockSpec(memory_space=pltpu.VMEM)
    near = jax.ShapeDtypeStruct((plan.half, 2 * tiles * plan.size + AUX, depth), jnp.float32)
    return pl.pallas_call(
        functools.partial(outer_kernel, plan),
        in_specs=[vmem] * 7,
        out_specs=vmem,
        out_shape=near,
        scratch_shapes=[buffer] * 4 + [pltpu.VMEM((3, KINDS, width, depth), jnp.float32)],
        compiler_params=pltpu.CompilerParams(vmem_limit_bytes=16 * 1024 * 1024),
        cost_estimate=pl.CostEstimate(flops=10**8, bytes_accessed=40 * 1024 * 1024, transcendentals=0),
        name="outer",
    )(own, phase, solute, *halos)


def route_kernel(plan, near, *refs):
    pieces, tiles, half, size = plan.pieces, plan.tiles, plan.half, 2 * plan.size
    far, near_out, far_outs, table = refs[:half], refs[half], refs[half + 1 : 2 * half + 1], refs[2 * half + 1]
    held, peers, count = refs[2 * half + 2 :]
    me = lax.axis_index("gy")
    base = me - lax.rem(me, half)
    tail = tiles * size
    for tile in range(tiles):
        for piece in range(half):
            peer = lax.rem(near[piece, tail, tile].astype(jnp.int32), pieces)
            peers[(base + piece) * tiles + tile] = peer
        for index in range(half):
            peer = lax.rem(far[index][tail, tile].astype(jnp.int32), pieces)
            peers[(me ^ (half + index)) * tiles + tile] = peer
    for piece in range(half):
        for tile in range(tiles):
            held[(base + piece) * tiles + tile] = near[piece, tile * size : (tile + 1) * size, :]
    for index in range(half):
        for tile in range(tiles):
            held[(me ^ (half + index)) * tiles + tile] = far[index][tile * size : (tile + 1) * size, :]
    for peer in range(pieces):
        count[peer] = 0
    for home in range(pieces * tiles):
        peer = peers[home]
        slot = count[peer]
        table[peer * tiles + slot] = home
        count[peer] = slot + 1
    for index in range(half):
        for slot in range(tiles):
            far_outs[index][slot] = held[table[(me ^ (half + index)) * tiles + slot]]
            near_out[index, slot] = held[table[(base + index) * tiles + slot]]


def route(plan, near, far):
    tiles, half, size, depth = plan.tiles, plan.half, 2 * plan.size, plan.depth
    vmem = pl.BlockSpec(memory_space=pltpu.VMEM)
    one = jax.ShapeDtypeStruct((tiles, size, depth), jnp.float32)
    count = plan.pieces * tiles
    results = pl.pallas_call(
        functools.partial(route_kernel, plan),
        in_specs=[vmem] * (half + 1),
        out_specs=[vmem] * (half + 1) + [pl.BlockSpec(memory_space=pltpu.SMEM)],
        out_shape=[jax.ShapeDtypeStruct((half, tiles, size, depth), jnp.float32)]
        + [one] * half
        + [jax.ShapeDtypeStruct((count,), jnp.int32)],
        scratch_shapes=[
            pltpu.VMEM((count, size, depth), jnp.float32),
            pltpu.SMEM((count,), jnp.int32),
            pltpu.SMEM((plan.pieces,), jnp.int32),
        ],
        compiler_params=pltpu.CompilerParams(vmem_limit_bytes=16 * 1024 * 1024),
        name="route",
    )(near, *far)
    return results[0], results[1 : half + 1], results[-1]


def settle_kernel(plan, table, near, *refs):
    tiles, half = plan.tiles, plan.half
    far, outs, (ready, sems) = refs[:half], refs[half : half + 2], refs[half + 2 :]
    me = lax.axis_index("gy")
    mine = lax.rem(me, half)
    copies = []
    for slot in range(tiles):
        home = table[me * tiles + slot]
        tile = lax.rem(home, tiles)
        at_home = home // (tiles * half) == me // half

        def put(source, piece, is_far, slot=slot, tile=tile):
            for field in range(2):
                for at, row, name in plan.parts(is_far, piece):
                    col, count = plan.columns(name, tile)
                    if not isinstance(col, int):
                        col = pl.multiple_of(col, 8)
                    ready[field, slot, row, pl.ds(col, count), :] = source[
                        slot, field * plan.size + at : field * plan.size + at + count, :
                    ]

        def put_all(same, put=put):
            for index in range(half):
                put(near.at[index], index, not same)
                put(far[index], mine ^ index, same)

        @pl.when(at_home)
        def _(put_all=put_all):
            put_all(True)

        @pl.when(jnp.logical_not(at_home))
        def _(put_all=put_all):
            put_all(False)

        for field, out in enumerate(outs):
            copy = pltpu.make_async_copy(ready.at[field, slot], out.at[0, slot], sems.at[field, slot])
            copy.start()
            copies.append(copy)
    for copy in copies:
        copy.wait()


def settle(plan, table, near, far):
    tiles, edge, depth = plan.tiles, plan.edge, plan.depth
    out = jax.ShapeDtypeStruct((1, tiles, edge, edge, depth), jnp.float32)
    vmem = pl.BlockSpec(memory_space=pltpu.VMEM)
    return pl.pallas_call(
        functools.partial(settle_kernel, plan),
        in_specs=[pl.BlockSpec(memory_space=pltpu.SMEM)] + [vmem] * (plan.half + 1),
        out_specs=[pl.BlockSpec(memory_space=pl.ANY)] * 2,
        out_shape=[out, out],
        scratch_shapes=[
            pltpu.VMEM((2, tiles, edge, edge, depth), jnp.float32),
            pltpu.SemaphoreType.DMA((2, tiles)),
        ],
        compiler_params=pltpu.CompilerParams(vmem_limit_bytes=16 * 1024 * 1024),
        name="settle",
    )(table, near, *far)


def ring(axis, step):
    count = lax.axis_size(axis)
    return [(i, (i + step) % count) for i in range(count)]


def swap(values, mask):
    return lax.ppermute(values, "gy", [(i, i ^ mask) for i in range(lax.axis_size("gy"))])


def among_half(plan, values, together):
    def exchange(values):
        groups = [list(range(plan.half)), list(range(plan.half, plan.pieces))]
        return lax.all_to_all(values, "gy", 0, 0, axis_index_groups=groups, tiled=True)

    return lax.cond(together, exchange, exchange, values)


def in_vmem(values):
    return pltpu.with_memory_space_constraint(values, pltpu.VMEM)


def per_device(phase, solute, undercool, mobility, diffusivity, owner):
    _, tiles, edge, _, depth = phase.shape
    plan = Plan(lax.axis_size("gy"), tiles, edge, depth)
    half = plan.half
    to_prev, to_next, own = pack_y(phase, solute, (undercool, mobility, diffusivity), owner)
    y_lo = lax.ppermute(to_next, "gy", ring("gy", 1))
    y_hi = lax.ppermute(to_prev, "gy", ring("gy", -1))
    far = {}

    def send_far(batch, values):
        for index, value in zip(plan.batches[batch], values):
            far[index] = swap(value, half + index)

    own_here, phase_here, solute_here = own, phase, solute
    first = run_inner(plan, 0, own_here, phase_here, in_vmem(solute_here))
    send_far(0, first)
    to_prev, to_next = pack_x(phase_here, solute_here, own_here, y_lo, y_hi, first[0])
    together = owner[0, 0] >= 0

    def around(low, high, *values):
        return ring_swap(low, high), run_inner(plan, 1, *values)

    def ring_swap(low, high):
        return lax.ppermute(low, "gx", ring("gx", 1)), lax.ppermute(high, "gx", ring("gx", -1))

    (x_lo, x_hi), second = lax.cond(together, around, around, to_next, to_prev, own, phase, solute)
    send_far(1, second)
    near = run_outer(plan, own_here, phase_here, solute_here, (y_lo, y_hi, in_vmem(x_lo), in_vmem(x_hi)))
    far = [in_vmem(far[index]) for index in range(half)]
    near = among_half(plan, near, together)
    near, far, table = route(plan, in_vmem(near), far)
    far = [swap(values, half + index) for index, values in enumerate(far)]
    near = among_half(plan, near, together)
    return tuple(settle(plan, table, near, far))


def solution(mesh):
    tile_spec = P("gx", "gy", None, None, None)
    in_specs = (tile_spec, tile_spec) + (P("gx", "gy"),) * 4
    out_spec = P(("gx", "gy"), None, None, None, None)
    return jax.shard_map(
        per_device, mesh=mesh, in_specs=in_specs, out_specs=(out_spec, out_spec), check_vma=False
    )
```

```python
import functools

import jax
import jax.numpy as jnp
from jax import lax
from jax.experimental import pallas as pl
from jax.experimental.pallas import tpu as pltpu
from jax.sharding import PartitionSpec as P

NSTEPS = 4
W = NSTEPS
PAD = 8

aniso_strength = 0.05


def pack_y_kernel(under, mobile, spread, owner, phase_lo, phase_hi, solute_lo, solute_hi, to_prev, to_next, own):
    edge, depth = phase_lo.shape[2], phase_lo.shape[4]
    tiles = own.shape[0] // 8 - 1
    to_prev[:edge, :W, :] = phase_lo[0, 0, :, :W, :]
    to_prev[:edge, W:, :] = solute_lo[0, 0, :, :W, :]
    to_next[:edge, :W, :] = phase_hi[0, 0, :, W:, :]
    to_next[:edge, W:, :] = solute_hi[0, 0, :, W:, :]
    line = lax.broadcasted_iota(jnp.int32, (8, depth), 0)
    lane = lax.broadcasted_iota(jnp.int32, (8, depth), 1)
    names = jnp.zeros((8, depth), jnp.float32)
    for tile in range(tiles):
        rows = jnp.zeros((8, depth), jnp.float32)
        ready = (2.0 * under[0, tile], mobile[0, tile], spread[0, tile], 1.0 - 6.0 * spread[0, tile])
        for kind, coef in enumerate(ready):
            rows = jnp.where(line == kind, coef, rows)
        own[8 * tile : 8 * tile + 8, :] = rows
        if tile == 0:
            to_prev[edge] = rows
        if tile == tiles - 1:
            to_next[edge] = rows
        names = jnp.where(lane == tile, owner[0, tile].astype(jnp.float32), names)
    own[8 * tiles :, :] = names


def pack_y(phase, solute, coef, owner):
    _, tiles, edge, _, depth = phase.shape
    low = pl.BlockSpec((1, 1, edge, 2 * W, depth), lambda i: (0, 0, 0, 0, 0))
    high = pl.BlockSpec((1, 1, edge, 2 * W, depth), lambda i: (0, tiles - 1, 0, edge // (2 * W) - 1, 0))
    face = jax.ShapeDtypeStruct((edge + 1, 2 * W, depth), jnp.float32)
    own = jax.ShapeDtypeStruct((8 * tiles + 8, depth), jnp.float32)
    whole = pl.BlockSpec((edge + 1, 2 * W, depth), lambda i: (0, 0, 0))
    return pl.pallas_call(
        pack_y_kernel,
        grid=(1,),
        in_specs=[pl.BlockSpec(memory_space=pltpu.SMEM)] * 4 + [low, high, low, high],
        out_specs=[whole, whole, pl.BlockSpec((8 * tiles + 8, depth), lambda i: (0, 0))],
        out_shape=[face, face, own],
        name="pack_y",
    )(*coef, owner, phase, phase, solute, solute)


def fill_row(dst, row, phase_row, solute_row, lo, hi):
    start = PAD
    dst[0][row, start : start + W, :] = lo[:W]
    dst[1][row, start : start + W, :] = 2.0 * lo[W:]
    start += W
    for values in phase_row:
        size = values.shape[0]
        dst[0][row, start : start + size, :] = values
        start += size
    dst[0][row, start : start + W, :] = hi[:W]
    dst[1][row, start : start + W, :] = 2.0 * hi[W:]
    start = PAD + W
    for values in solute_row:
        size = values.shape[0]
        dst[1][row, start : start + size, :] = 2.0 * values
        start += size


def pack_x_kernel(own, phase_lo, phase_hi, solute_lo, solute_hi, y_lo, y_hi, _, to_prev, to_next):
    tiles, edge, depth = phase_lo.shape[1], phase_lo.shape[3], phase_lo.shape[4]
    width = tiles * edge + 2 * W
    for out, phase, solute, first in (
        (to_prev, phase_lo, solute_lo, 0),
        (to_next, phase_hi, solute_hi, edge - W),
    ):
        for row in range(W):
            for field, values, half in ((0, phase, 0), (1, solute, W)):
                at = (2 * row + field) * width
                out[at : at + W, :] = y_lo[first + row, half : half + W, :]
                for tile in range(tiles):
                    begin = at + W + tile * edge
                    out[begin : begin + edge, :] = values[0, tile, row]
                out[at + width - W : at + width, :] = y_hi[first + row, half : half + W, :]
        at = 2 * W * width
        out[at : at + 8, :] = y_lo[edge]
        out[at + 8 : at + 16, :] = y_hi[edge]
        out[at + 16 : at + 16 + 8 * tiles, :] = own[: 8 * tiles, :]


def pack_x(phase, solute, own, y_lo, y_hi, after):
    _, tiles, edge, _, depth = phase.shape
    low = pl.BlockSpec((1, tiles, W, edge, depth), lambda i: (0, 0, 0, 0, 0))
    high = pl.BlockSpec((1, tiles, W, edge, depth), lambda i: (0, 0, edge // W - 1, 0, 0))
    side = pl.BlockSpec((edge + 1, 2 * W, depth), lambda i: (0, 0, 0))
    rows = 2 * W * (tiles * edge + 2 * W) + 8 * (tiles + 2)
    out = jax.ShapeDtypeStruct((rows, depth), jnp.float32)
    whole = pl.BlockSpec((rows, depth), lambda i: (0, 0))
    return pl.pallas_call(
        pack_x_kernel,
        grid=(1,),
        in_specs=[pl.BlockSpec((8 * tiles + 8, depth), lambda i: (0, 0)), low, high, low, high, side, side, pl.BlockSpec(memory_space=pl.ANY)],
        out_specs=[whole, whole],
        out_shape=[out, out],
        compiler_params=pltpu.CompilerParams(vmem_limit_bytes=8 * 1024 * 1024),
        name="pack_x",
    )(own, phase, phase, solute, solute, y_lo, y_hi, after)


def update(near_p, near_v, under, mobile, spread, keep):
    p, p_xl, p_xh, p_yl, p_yh = near_p
    v, v_xl, v_xh, v_yl, v_yh = near_v
    depth = p.shape[-1]
    lane = lax.broadcasted_iota(jnp.int32, p.shape, 1)
    first, last = lane == 0, lane == depth - 1
    p_zl = jnp.where(first, p, pltpu.roll(p, 1, 1))
    p_zh = jnp.where(last, p, pltpu.roll(p, depth - 1, 1))
    v_zl = jnp.where(first, v, pltpu.roll(v, 1, 1))
    v_zh = jnp.where(last, v, pltpu.roll(v, depth - 1, 1))
    dx, dy, dz = p_xh - p_xl, p_yh - p_yl, p_zh - p_zl
    qx, qy, qz = dx * dx, dy * dy, dz * dz
    flat = qx + qy
    total = flat + qz
    pairs = qx * qy + flat * qz
    base = total + 4.0
    guess = pl.reciprocal(base, approx=True)
    inverse = guess * (2.0 - base * guess)
    extra = (aniso_strength * total * total - (8.0 * aniso_strength) * pairs) * (inverse * inverse)
    lap_p = (p_xl + p_xh) + (p_yl + p_yh) + (p_zl + p_zh) - 6.0 * p
    sum_v = (v_xl + v_xh) + (v_yl + v_yh) + (v_zl + v_zh)
    well = 1.0 - p * p
    change = mobile * (lap_p + extra * lap_p + well * (p - well * (under + v)))
    return p + change, keep * v + spread * sum_v + change


KINDS = 4


def cells(src_p, src_u, row, start, coefs):
    near = []
    for src in (src_p, src_u):
        near.append(
            (
                src[row, start : start + 8, :],
                src[row - 1, start : start + 8, :],
                src[row + 1, start : start + 8, :],
                src[row, start - 1 : start + 7, :],
                src[row, start + 1 : start + 9, :],
            )
        )
    return update(near[0], near[1], *coefs)


class Plan:
    def __init__(self, pieces, tiles, edge, depth):
        self.pieces, self.tiles, self.edge, self.depth = pieces, tiles, edge, depth
        self.half = pieces // 2
        self.inner = edge - 2 * W
        self.rows = self.inner // self.half
        self.rows_far = (self.inner - 2 * W) // self.half
        self.rows_near = 2 * W // self.half
        self.middle = edge - 16
        self.size = self.rows * self.middle + self.rows_far * 8

        side = self.half // 2
        self.batches = (list(range(side)), list(range(side, self.half)))

    def batch_rows(self, batch, mine):
        count = self.inner // 2
        side = mine // (self.half // 2)
        return W + (side if batch == 0 else 1 - side) * count, count

    def near_row(self, piece, row, gap):
        index = piece * self.rows_near + row
        return index + jnp.where(index < W, 0, gap)

    def parts(self, far, piece):
        at, found = 0, []
        if far:
            for row in range(self.rows):
                found.append((at, W + piece * self.rows + row, "middle"))
                at += self.middle
            for row in range(self.rows_far):
                found.append((at, 2 * W + piece * self.rows_far + row, "last"))
                at += 8
        else:
            for row in range(self.rows_near):
                found.append((at, self.near_row(piece, row, self.inner), "whole"))
                at += self.edge
            for row in range(self.rows):
                found.append((at, W + piece * self.rows + row, "side"))
                at += 8
            for row in range(self.rows_near):
                found.append((at, W + self.near_row(piece, row, self.inner - 2 * W), "last"))
                at += 8
        assert at == self.size
        return found

    def columns(self, name, tile):
        if name == "whole":
            return 0, self.edge
        if name == "middle":
            return 8, self.middle
        low, high = (tile, 1 - tile) if name == "side" else (1 - tile, tile)
        return low * (self.edge - 8), 8


AUX = 8
UNROLL = 4


def march(count, row_of, starts, source, target, coefs_of):
    def one_row(index, carry):
        row = row_of(index)
        for start in starts:
            new_p, new_u = cells(source[0], source[1], row, start, coefs_of(row, start))
            target[0][row, start : start + 8, :] = new_p
            target[1][row, start : start + 8, :] = new_u
        return carry

    lax.fori_loop(0, count, one_row, 0, unroll=UNROLL)


def inner_kernel(plan, batch, own, phase, solute, *rest):
    tiles, edge, indices = plan.tiles, plan.edge, plan.batches[batch]
    outs, scratch = rest[: len(indices)], rest[len(indices) :]
    pairs = (scratch[:2], scratch[2:])
    mine = lax.rem(lax.axis_index("gy"), plan.half)
    begin, count = plan.batch_rows(batch, mine)
    base = begin - W

    def load_row(row, carry):
        for tile in range(tiles):
            start = PAD + tile * edge
            pairs[0][0][row, start : start + edge, :] = phase[0, tile, base + row]
            pairs[0][1][row, start : start + edge, :] = 2.0 * solute[0, tile, base + row]
        return carry

    lax.fori_loop(0, count + 2 * W, load_row, 0, unroll=UNROLL)

    line = lax.broadcasted_iota(jnp.int32, (8, plan.depth), 0)

    def coefs_of(row, start):
        low, high = (start - PAD) // edge, (start + 7 - PAD) // edge
        rows = [[own[8 * tile + kind : 8 * tile + kind + 1, :] for tile in (low, high)] for kind in range(KINDS)]
        if low == high:
            return tuple(pair[0] for pair in rows)
        return tuple(jnp.where(line < W, *pair) for pair in rows)

    for step in range(NSTEPS):
        margin = 8 if step == NSTEPS - 1 else W
        starts = range(PAD + margin, PAD + tiles * edge - margin, 8)
        rows = count + 2 * W - 2 * (step + 1)
        march(rows, lambda i, step=step: step + 1 + i, starts, pairs[step % 2], pairs[(step + 1) % 2], coefs_of)
    for index, out in zip(indices, outs):
        pack(plan, True, mine ^ index, pairs[NSTEPS % 2], -base, PAD, own, out)


def pack(plan, far, piece, done, row_shift, col_shift, own, out):
    for tile in range(plan.tiles):
        for field, values in enumerate(done):
            begin = (2 * tile + field) * plan.size
            for at, row, name in plan.parts(far, piece):
                col, count = plan.columns(name, tile)
                start = col_shift + tile * plan.edge + col
                cells = values[row + row_shift, start : start + count, :]
                out[begin + at : begin + at + count, :] = 0.5 * cells if field else cells
    tail = 2 * plan.tiles * plan.size
    out[tail : tail + AUX, :] = own[8 * plan.tiles : 8 * plan.tiles + AUX, :]


def run_inner(plan, batch, own, phase, solute):
    rows = plan.batch_rows(batch, 0)[1] + 2 * W
    count = len(plan.batches[batch])
    buffer = pltpu.VMEM((rows, plan.tiles * plan.edge + 2 * PAD, plan.depth), jnp.float32)
    vmem = pl.BlockSpec(memory_space=pltpu.VMEM)
    shape = jax.ShapeDtypeStruct((2 * plan.tiles * plan.size + AUX, plan.depth), jnp.float32)
    return pl.pallas_call(
        functools.partial(inner_kernel, plan, batch),
        in_specs=[vmem] * 3,
        out_specs=[vmem] * count,
        out_shape=[shape] * count,
        scratch_shapes=[buffer] * 4,
        compiler_params=pltpu.CompilerParams(vmem_limit_bytes=16 * 1024 * 1024),
        cost_estimate=pl.CostEstimate(flops=10**8, bytes_accessed=24 * 1024 * 1024, transcendentals=0),
        name="inner",
    )(own, phase, solute)


def outer_kernel(plan, own, phase, solute, y_lo, y_hi, x_lo, x_hi, out, *scratch):
    tiles, edge, depth, half = plan.tiles, plan.edge, plan.depth, plan.half
    pairs, coefs = (scratch[:2], scratch[2:4]), scratch[4]
    cols = tiles * edge
    width = cols + 2 * W
    for zone, source in ((0, x_lo), (1, None), (2, x_hi)):
        for kind in range(KINDS):
            if source is None:
                parts = [y_lo[edge, kind : kind + 1, :]]
                parts += [own[8 * tile + kind : 8 * tile + kind + 1, :] for tile in range(tiles)]
                parts += [y_hi[edge, kind : kind + 1, :]]
            else:
                at = 2 * W * width + kind
                parts = [source[at : at + 1, :]]
                parts += [source[at + 16 + 8 * tile : at + 17 + 8 * tile, :] for tile in range(tiles)]
                parts += [source[at + 8 : at + 9, :]]
            coefs[zone, kind, :W, :] = jnp.broadcast_to(parts[0], (W, depth))
            for tile in range(tiles):
                begin = W + tile * edge
                coefs[zone, kind, begin : begin + edge, :] = jnp.broadcast_to(parts[1 + tile], (edge, depth))
            coefs[zone, kind, width - W :, :] = jnp.broadcast_to(parts[-1], (W, depth))
    for source, first in ((x_lo, 0), (x_hi, edge + W)):
        for row in range(W):
            for field in range(2):
                at = (2 * row + field) * width
                values = source[at : at + width, :]
                pairs[0][field][first + row, PAD : PAD + width, :] = 2.0 * values if field else values

    def load_row(row, carry):
        fill_row(
            pairs[0],
            W + row,
            [phase[0, tile, row] for tile in range(tiles)],
            [solute[0, tile, row] for tile in range(tiles)],
            y_lo[row],
            y_hi[row],
        )
        return carry

    lax.fori_loop(0, edge, load_row, 0, unroll=UNROLL)

    def coefs_of(zone):
        def found(row, start):
            return tuple(coefs[zone(row), kind, start - PAD : start - PAD + 8, :] for kind in range(KINDS))

        return found

    any_zone = coefs_of(lambda row: jnp.where(row < W, 0, jnp.where(row < W + edge, 1, 2)))

    own_zone = coefs_of(lambda row: 1)
    def blocks(first, last):
        low, high = (first + W - shift) // 8 * 8, -(-(last + W - shift) // 8) * 8
        return list(range(PAD + shift + low, PAD + shift + high, 8))

    for step in range(1, NSTEPS + 1):
        source, target = pairs[(step - 1) % 2], pairs[step % 2]
        left = NSTEPS - step
        shift = W if step == NSTEPS else 0
        whole = blocks(-left, cols + left)
        sides = blocks(-left, 8 + left) + blocks(cols - 8 - left, cols + left)
        ends = list(sides)
        for tile in range(tiles):
            col, count = plan.columns("last", tile)
            ends += blocks(tile * edge + col - left, tile * edge + col + count + left)
        strip = W + left

        def two(size, begin):
            mirror = 2 * W + edge - begin - size
            return lambda i: i + jnp.where(i < size, begin, mirror - size)

        march(2 * (strip + left), two(strip + left, W - left), whole, source, target, any_zone)
        march(2 * W, two(W, W + strip), sorted(set(ends)), source, target, own_zone)
        march(edge - 2 * strip - 2 * W, lambda i, strip=strip: i + 2 * W + strip, sides, source, target, own_zone)
    done = pairs[NSTEPS % 2]
    for piece in range(half):
        pack(plan, False, piece, done, W, PAD + W, own, out.at[piece])


def run_outer(plan, own, phase, solute, halos):
    tiles, edge, depth = plan.tiles, plan.edge, plan.depth
    width = tiles * edge + 2 * W
    buffer = pltpu.VMEM((edge + 2 * W, width + 2 * PAD, depth), jnp.float32)
    vmem = pl.BlockSpec(memory_space=pltpu.VMEM)
    near = jax.ShapeDtypeStruct((plan.half, 2 * tiles * plan.size + AUX, depth), jnp.float32)
    return pl.pallas_call(
        functools.partial(outer_kernel, plan),
        in_specs=[vmem] * 7,
        out_specs=vmem,
        out_shape=near,
        scratch_shapes=[buffer] * 4 + [pltpu.VMEM((3, KINDS, width, depth), jnp.float32)],
        compiler_params=pltpu.CompilerParams(vmem_limit_bytes=16 * 1024 * 1024),
        cost_estimate=pl.CostEstimate(flops=10**8, bytes_accessed=40 * 1024 * 1024, transcendentals=0),
        name="outer",
    )(own, phase, solute, *halos)


def route_kernel(plan, near, *refs):
    pieces, tiles, half, size = plan.pieces, plan.tiles, plan.half, 2 * plan.size
    far, near_out, far_outs, table = refs[:half], refs[half], refs[half + 1 : 2 * half + 1], refs[2 * half + 1]
    held, peers, count = refs[2 * half + 2 :]
    me = lax.axis_index("gy")
    base = me - lax.rem(me, half)
    tail = tiles * size
    for tile in range(tiles):
        for piece in range(half):
            peer = lax.rem(near[piece, tail, tile].astype(jnp.int32), pieces)
            peers[(base + piece) * tiles + tile] = peer
        for index in range(half):
            peer = lax.rem(far[index][tail, tile].astype(jnp.int32), pieces)
            peers[(me ^ (half + index)) * tiles + tile] = peer
    for piece in range(half):
        for tile in range(tiles):
            held[(base + piece) * tiles + tile] = near[piece, tile * size : (tile + 1) * size, :]
    for index in range(half):
        for tile in range(tiles):
            held[(me ^ (half + index)) * tiles + tile] = far[index][tile * size : (tile + 1) * size, :]
    for peer in range(pieces):
        count[peer] = 0
    for home in range(pieces * tiles):
        peer = peers[home]
        slot = count[peer]
        table[peer * tiles + slot] = home
        count[peer] = slot + 1
    for index in range(half):
        for slot in range(tiles):
            far_outs[index][slot] = held[table[(me ^ (half + index)) * tiles + slot]]
            near_out[index, slot] = held[table[(base + index) * tiles + slot]]


def route(plan, near, far):
    tiles, half, size, depth = plan.tiles, plan.half, 2 * plan.size, plan.depth
    vmem = pl.BlockSpec(memory_space=pltpu.VMEM)
    one = jax.ShapeDtypeStruct((tiles, size, depth), jnp.float32)
    count = plan.pieces * tiles
    results = pl.pallas_call(
        functools.partial(route_kernel, plan),
        in_specs=[vmem] * (half + 1),
        out_specs=[vmem] * (half + 1) + [pl.BlockSpec(memory_space=pltpu.SMEM)],
        out_shape=[jax.ShapeDtypeStruct((half, tiles, size, depth), jnp.float32)]
        + [one] * half
        + [jax.ShapeDtypeStruct((count,), jnp.int32)],
        scratch_shapes=[
            pltpu.VMEM((count, size, depth), jnp.float32),
            pltpu.SMEM((count,), jnp.int32),
            pltpu.SMEM((plan.pieces,), jnp.int32),
        ],
        compiler_params=pltpu.CompilerParams(vmem_limit_bytes=16 * 1024 * 1024),
        name="route",
    )(near, *far)
    return results[0], results[1 : half + 1], results[-1]


def settle_kernel(plan, table, near, *refs):
    tiles, half = plan.tiles, plan.half
    far, outs, (ready, sems) = refs[:half], refs[half : half + 2], refs[half + 2 :]
    me = lax.axis_index("gy")
    mine = lax.rem(me, half)
    copies = []
    for slot in range(tiles):
        home = table[me * tiles + slot]
        tile = lax.rem(home, tiles)
        at_home = home // (tiles * half) == me // half

        def put(source, piece, is_far, slot=slot, tile=tile):
            for field in range(2):
                for at, row, name in plan.parts(is_far, piece):
                    col, count = plan.columns(name, tile)
                    if not isinstance(col, int):
                        col = pl.multiple_of(col, 8)
                    ready[field, slot, row, pl.ds(col, count), :] = source[
                        slot, field * plan.size + at : field * plan.size + at + count, :
                    ]

        def put_all(same, put=put):
            for index in range(half):
                put(near.at[index], index, not same)
                put(far[index], mine ^ index, same)

        @pl.when(at_home)
        def _(put_all=put_all):
            put_all(True)

        @pl.when(jnp.logical_not(at_home))
        def _(put_all=put_all):
            put_all(False)

        for field, out in enumerate(outs):
            copy = pltpu.make_async_copy(ready.at[field, slot], out.at[0, slot], sems.at[field, slot])
            copy.start()
            copies.append(copy)
    for copy in copies:
        copy.wait()


def settle(plan, table, near, far):
    tiles, edge, depth = plan.tiles, plan.edge, plan.depth
    out = jax.ShapeDtypeStruct((1, tiles, edge, edge, depth), jnp.float32)
    vmem = pl.BlockSpec(memory_space=pltpu.VMEM)
    return pl.pallas_call(
        functools.partial(settle_kernel, plan),
        in_specs=[pl.BlockSpec(memory_space=pltpu.SMEM)] + [vmem] * (plan.half + 1),
        out_specs=[pl.BlockSpec(memory_space=pl.ANY)] * 2,
        out_shape=[out, out],
        scratch_shapes=[
            pltpu.VMEM((2, tiles, edge, edge, depth), jnp.float32),
            pltpu.SemaphoreType.DMA((2, tiles)),
        ],
        compiler_params=pltpu.CompilerParams(vmem_limit_bytes=16 * 1024 * 1024),
        name="settle",
    )(table, near, *far)


def ring(axis, step):
    count = lax.axis_size(axis)
    return [(i, (i + step) % count) for i in range(count)]


def swap(values, mask):
    return lax.ppermute(values, "gy", [(i, i ^ mask) for i in range(lax.axis_size("gy"))])


def among_half(plan, values, together):
    def exchange(values):
        groups = [list(range(plan.half)), list(range(plan.half, plan.pieces))]
        return lax.all_to_all(values, "gy", 0, 0, axis_index_groups=groups, tiled=True)

    return lax.cond(together, exchange, exchange, values)


def in_vmem(values):
    return pltpu.with_memory_space_constraint(values, pltpu.VMEM)


def per_device(phase, solute, undercool, mobility, diffusivity, owner):
    _, tiles, edge, _, depth = phase.shape
    plan = Plan(lax.axis_size("gy"), tiles, edge, depth)
    half = plan.half
    to_prev, to_next, own = pack_y(phase, solute, (undercool, mobility, diffusivity), owner)
    y_lo = lax.ppermute(to_next, "gy", ring("gy", 1))
    y_hi = lax.ppermute(to_prev, "gy", ring("gy", -1))
    far = {}

    def send_far(batch, values):
        for index, value in zip(plan.batches[batch], values):
            far[index] = swap(value, half + index)

    own_here, phase_here, solute_here = own, phase, solute
    first = run_inner(plan, 0, own_here, phase_here, in_vmem(solute_here))
    send_far(0, first)
    to_prev, to_next = pack_x(phase_here, solute_here, own_here, y_lo, y_hi, first[0])
    together = owner[0, 0] >= 0

    def around(low, high, *values):
        return ring_swap(low, high), run_inner(plan, 1, *values)

    def ring_swap(low, high):
        return lax.ppermute(low, "gx", ring("gx", 1)), lax.ppermute(high, "gx", ring("gx", -1))

    (x_lo, x_hi), second = lax.cond(together, around, around, to_next, to_prev, own, phase, solute)
    send_far(1, second)
    near = run_outer(plan, own_here, in_vmem(phase_here), solute_here, (y_lo, y_hi, in_vmem(x_lo), in_vmem(x_hi)))
    far = [in_vmem(far[index]) for index in range(half)]
    near = among_half(plan, near, together)
    near, far, table = route(plan, in_vmem(near), far)
    far = [swap(values, half + index) for index, values in enumerate(far)]
    near = among_half(plan, near, together)
    return tuple(settle(plan, table, near, far))


def solution(mesh):
    tile_spec = P("gx", "gy", None, None, None)
    in_specs = (tile_spec, tile_spec) + (P("gx", "gy"),) * 4
    out_spec = P(("gx", "gy"), None, None, None, None)
    return jax.shard_map(
        per_device, mesh=mesh, in_specs=in_specs, out_specs=(out_spec, out_spec), check_vma=False
    )
```
